32 devices in a mesh: wide: 8 (over z, x), narrow: 4 (over y, core).
Axes of the slice: x: 2, y: 2, z: 4, core: 2. Of those that a mesh axis runs over, the one named last changes fastest.
Arguments:
- inputs: bfloat16 [32, 256, 512], P(('wide', 'narrow')), may hold values from -6 to 6
- dense_inputs: bfloat16 [32, 256, 1536], P(('wide', 'narrow')), may hold values from -6 to 6
- lengths: int32 [32], P(('wide', 'narrow')), may hold values from 1 to 256, as said below
- owners: int32 [89], replicated, may hold values from 0 to 7, as said below
- cotangent: bfloat16 [32, 256, 512], P(('wide', 'narrow')), may hold values from -6 to 6
- master: float32 [49152, 512], P(('wide', 'narrow')), may hold values from -0.0625 to 0.0625
- moment_one: float32 [49152, 512], P(('wide', 'narrow')), may hold values from -24 to 24
- moment_two: float32 [49152, 512], P(('wide', 'narrow')), may hold values from 0.65536 to 10.6496
- average: float32 [49152, 512], P(('wide', 'narrow')), may hold values from -0.0625 to 0.0625
- norm_gain: float32 [11, 512], replicated, may hold values from 0.1 to 1.9
- norm_shift: float32 [11, 512], replicated, may hold values from -3 to 3
- norm_one: float32 [2, 11, 512], replicated, may hold values from -24 to 24
- norm_two: float32 [2, 11, 512], replicated, may hold values from 0.65536 to 10.6496
Outputs:
- block_out: bfloat16 [32, 256, 512], P(('wide', 'narrow'))
- input_grad: float32 [32, 256, 512], P(('wide', 'narrow'))
- dense_grad: float32 [32, 256, 1536], P(('wide', 'narrow'))
- weight_grad: float32 [49152, 512], P(('wide', 'narrow'))
- weight_one: float32 [49152, 512], P(('wide', 'narrow'))
- weight_two: float32 [49152, 512], P(('wide', 'narrow'))
- weight_new: float32 [49152, 512], P(('wide', 'narrow'))
- weight_average: float32 [49152, 512], P(('wide', 'narrow'))
- weight_copy: bfloat16 [49152, 512], P(('wide', 'narrow'))
- norm_grad: float32 [2, 11, 512], replicated
- norm_one_new: float32 [2, 11, 512], replicated
- norm_two_new: float32 [2, 11, 512], replicated
- norm_new: float32 [2, 11, 512], replicated
The draws below stay inside these ranges and needn't reach their ends.
Inputs may be any that keep to these rules, and one draw needn't show every extreme that they name: `lengths`: the last utterance has exactly 256 true frames. `owners`: no owner names more than 12 matrices, and one owner names exactly 12.
All inputs are finite; a program needn't handle non-finite values.
Results may differ from the reference program's by a relative error of at most 0.014.
Values may be sent and summed in bfloat16 or wider, within the bound.
A program may use at most 512 MiB of HBM per device.

```python
import math
import jax
import jax.numpy as jnp
from jax import lax

C = 512
WLOW = 256
WMID = 384
K = 17
SUBS = 5
PAD = 256
UTT_DEV = 1
STEP = 10
UTTS = 32
DENSE = 1536
NORMS = 11
MATS = 89
SLOTS = 12
BANK_ROWS = 49152
N_WIDE = 8
N_NARROW = 4


def draw_lengths(key, part):
    key = jax.random.fold_in(key, 11)
    positions = jnp.arange(UTTS, dtype=jnp.int32)
    device_id = positions // UTT_DEV
    wide_pos = device_id // N_NARROW
    narrow_pos = device_id % N_NARROW
    ramp_level = wide_pos * (N_NARROW - 1) + narrow_pos * (N_WIDE - 1)
    top_level = 2 * (N_WIDE - 1) * (N_NARROW - 1)
    upper_len = PAD // 3 + (PAD - PAD // 3) * ramp_level // top_level
    lower_len = jnp.maximum(1, upper_len * 3 // 4)
    random_len = jax.random.randint(key, (UTTS,), 0, 1 << 20) % (upper_len - lower_len + 1) + lower_len
    return jnp.where(positions == UTTS - 1, PAD, random_len).astype(jnp.int32)


def draw_owners(key, part):
    key = jax.random.fold_in(key, 23)
    key_one, key_two, key_three = jax.random.split(key, 3)
    slot_total = N_WIDE * SLOTS
    ranking = jax.random.permutation(key_one, slot_total)
    chosen_owner = jax.random.randint(key_two, (), 0, N_WIDE)
    scores = jnp.where(ranking // SLOTS == chosen_owner, ranking - slot_total, ranking)
    sorted_slots = ranking[jnp.argsort(scores, stable=True)]
    picked = sorted_slots[:MATS]
    shuffled = picked[jax.random.permutation(key_three, MATS)]
    return (shuffled // SLOTS).astype(jnp.int32)


def shard_levels(own_key, extent, pieces, smallest, top_value):
    def one(axis_at, blocks):
        draws = jax.random.uniform(jax.random.fold_in(jax.random.fold_in(own_key, 6), axis_at), (blocks,), jnp.float32, smallest / len(pieces), top_value / len(pieces))
        return jnp.repeat(jnp.exp(draws), extent[axis_at] // blocks).reshape((-1,) + (1,) * (len(extent) - axis_at - 1))

    level = one(*pieces[0])
    for cut in pieces[1:]:
        level = level * one(*cut)
    return level


def noise(rng, dims, scale, reach, shards=(), kind=jnp.bfloat16):
    values = scale * jax.random.normal(rng, dims, jnp.float32)
    if shards:
        values = values * shard_levels(rng, dims, shards, -0.22, 0.18)
    return jnp.clip(values, -reach, reach).astype(kind)


def setup_inputs(seed: int = 0) -> dict:
    key_list = jax.random.split(jax.random.key(seed), 14)
    return {
        "inputs": noise(key_list[0], (UTTS, PAD, C), 1.0, 6.0, ((0, 32),)),
        "dense_inputs": noise(key_list[1], (UTTS, PAD, DENSE), 1.0, 6.0, ((0, 32),)),
        "lengths": draw_lengths(jax.random.fold_in(key_list[13], 71), 0),
        "owners": draw_owners(jax.random.fold_in(key_list[13], 71), 0),
        "cotangent": noise(key_list[4], (UTTS, PAD, C), 1.0, 6.0, ((0, 32),)),
        "master": noise(key_list[5], (BANK_ROWS, C), (K * C) ** -0.5, 0.0625, ((0, 32),), jnp.float32),
        "moment_one": noise(key_list[6], (BANK_ROWS, C), (0.045 * (UTTS * PAD) ** 0.5), 24.0, ((0, 32),), jnp.float32),
        "moment_two": jnp.clip(jnp.exp(math.log(10.6496) - 2.7880929 * jax.random.uniform(key_list[7], (BANK_ROWS, C), jnp.float32) ** shard_levels(key_list[7], (BANK_ROWS, C), ((0, 32),), -0.2, 0.2)), 0.65536, 10.6496),
        "average": noise(key_list[8], (BANK_ROWS, C), (K * C) ** -0.5, 0.0625, ((0, 32),), jnp.float32),
        "norm_gain": jnp.clip(1.0 + 0.18 * jax.random.normal(key_list[9], (NORMS, C), jnp.float32), 0.1, 1.9),
        "norm_shift": noise(key_list[10], (NORMS, C), 0.5, 3.0, (), jnp.float32),
        "norm_one": noise(key_list[11], (2, NORMS, C), (0.045 * (UTTS * PAD) ** 0.5), 24.0, (), jnp.float32),
        "norm_two": jnp.clip(jnp.exp(jax.random.uniform(key_list[12], (2, NORMS, C), jnp.float32, math.log(0.65536), math.log(10.6496))), 0.65536, 10.6496),
    }


@jax.custom_vjp
def low(v):
    return lax.optimization_barrier(v.astype(jnp.bfloat16)).astype(jnp.float32)

@jax.custom_vjp
def low_back(v):
    return v

def low_keep(v):
    return (low(v), None)

def low_pass(kept, grad):
    return (grad,)

def back_keep(v):
    return (v, None)

def back_low(kept, grad):
    return (low(grad),)
low.defvjp(low_keep, low_pass)
low_back.defvjp(back_keep, back_low)
norm_eps = 1e-05
beta_one = 0.9
beta_two = 0.999
adam_eps = 1e-08
rate_main = 0.02
rate_norm = 0.15
decay_main = 0.01
ema_keep = 0.8

def slot_table(owners, capacity):
    number = owners.shape[0]
    same_owner = owners[:, None] == owners[None, :]
    earlier = jnp.arange(number)[None, :] < jnp.arange(number)[:, None]
    ranking = lax.optimization_barrier(jnp.sum(jnp.where(same_owner & earlier, 1, 0), axis=1))
    return (owners * capacity + ranking).astype(jnp.int32)

def convolve(active, kernel):
    margin = K // 2
    frames = active.shape[1]
    padded = jnp.pad(active, ((0, 0), (margin, margin), (0, 0)))
    result = jnp.zeros((active.shape[0], frames, kernel.shape[2]), jnp.float32)
    for offset in range(K):
        result = result + jnp.einsum('utc,cd->utd', padded[:, offset:offset + frames], kernel[offset], precision=lax.Precision.HIGHEST)
    return result

def source_widths():
    return [WLOW, WLOW, WLOW, WMID, WMID]

def forward(values, dense_values, master, norm_gain, norm_shift, valid, frame_total, places):
    width = values.shape[2]
    weights = low(jnp.take(master.reshape(-1, width, width), places, axis=0))
    residual = weights[SUBS * K:SUBS * K + 4].reshape(4 * width, width)
    active = low(values * valid[..., None])
    dense_active = low(dense_values * valid[..., None])
    sources = []
    start = 0
    for piece_width in source_widths():
        sources.append((dense_active[..., start:start + piece_width], start, piece_width))
        start = start + piece_width
    sources.append((active, start, width))
    hidden = active
    for section in range(SUBS):
        branches = [low_back(convolve(active, weights[section * K:(section + 1) * K]))]
        if section == SUBS - 1:
            for source, begin, piece_width in sources:
                branches.append(low_back(jnp.einsum('utc,cd->utd', source, residual[begin:begin + piece_width], precision=lax.Precision.HIGHEST)))
        before = jnp.zeros(branches[0].shape, jnp.float32)
        for member, branch in enumerate(branches):
            channel_mean = lax.optimization_barrier(jnp.sum(branch * valid[..., None], axis=(0, 1))) / frame_total
            spread = (branch - channel_mean) * valid[..., None]
            variance = lax.optimization_barrier(jnp.sum(spread * spread, axis=(0, 1))) / frame_total
            normed = (branch - channel_mean) * lax.rsqrt(variance + norm_eps)
            before = before + norm_gain[section + member] * normed + norm_shift[section + member]
        hidden = jax.nn.silu(before) * valid[..., None]
        active = low(hidden)
    return hidden

def adamw(gradient, params, first_moment, second_moment, rate, decay):
    moment_new = beta_one * first_moment + (1.0 - beta_one) * gradient
    second_new = beta_two * second_moment + (1.0 - beta_two) * gradient * gradient
    direction = moment_new / (1.0 - beta_one ** STEP) / (jnp.sqrt(second_new / (1.0 - beta_two ** STEP)) + adam_eps)
    return (moment_new, second_new, params - rate * (direction + decay * params))

def reference(inputs, dense_inputs, lengths, owners, cotangent, master, moment_one, moment_two, average, norm_gain, norm_shift, norm_one, norm_two):
    frames = inputs.shape[1]
    width = inputs.shape[2]
    valid = (jnp.arange(frames, dtype=jnp.int32)[None, :] < lengths[:, None]).astype(jnp.float32)
    frame_total = jnp.sum(valid)
    capacity = master.shape[0] // (N_WIDE * width)
    places = slot_table(owners, capacity)

    def closed(values, dense_values, weights_in, gain_in, shift_in):
        return forward(values, dense_values, weights_in, gain_in, shift_in, valid, frame_total, places)
    outputs, pullback = jax.vjp(closed, inputs.astype(jnp.float32), dense_inputs.astype(jnp.float32), master, norm_gain, norm_shift)
    input_grad, dense_grad, weight_grad, gain_grad, shift_grad = pullback(cotangent.astype(jnp.float32))
    weight_one, weight_two, weight_new = adamw(weight_grad, master, moment_one, moment_two, rate_main, decay_main)
    weight_average = ema_keep * average + (1.0 - ema_keep) * weight_new
    norm_grad = jnp.stack([gain_grad, shift_grad])
    norm_params = jnp.stack([norm_gain, norm_shift])
    norm_one_new, norm_two_new, norm_new = adamw(norm_grad, norm_params, norm_one, norm_two, rate_norm, 0.0)
    return (outputs.astype(jnp.bfloat16), input_grad, dense_grad, weight_grad, weight_one, weight_two, weight_new, weight_average, weight_new.astype(jnp.bfloat16), norm_grad, norm_one_new, norm_two_new, norm_new)
```

```python
import functools

import jax
import jax.numpy as jnp
from jax import lax
from jax.experimental import pallas as pl
from jax.experimental.pallas import tpu as pltpu
from jax.sharding import PartitionSpec as P

WLOW = 256
WMID = 384
K = 17
SUBS = 5
SOURCES = 6
STEP = 10
MARGIN = K // 2
EDGE = 16
UNIT = 64
F32 = jnp.float32
BF16 = jnp.bfloat16
MESH = pl.DeviceIdType.MESH
AXES = ("wide", "narrow")

norm_eps = 1e-05
beta_one = 0.9
beta_two = 0.999
adam_eps = 1e-08
rate_main = 0.02
rate_norm = 0.15
decay_main = 0.01
ema_keep = 0.8

NT = (((1,), (1,)), ((), ()))


def slot_table(owners, capacity):
    number = owners.shape[0]
    same_owner = owners[:, None] == owners[None, :]
    earlier = jnp.arange(number)[None, :] < jnp.arange(number)[:, None]
    ranking = jnp.sum(jnp.where(same_owner & earlier, 1, 0), axis=1)
    return (owners * capacity + ranking).astype(jnp.int32)


def source_pieces(half):
    pieces = []
    start = 0
    for width in (WLOW, WLOW, WLOW, WMID, WMID):
        parts = []
        stop = start + width
        while start < stop:
            chunk, lane = divmod(start, half)
            lanes = min(half - lane, stop - start)
            parts.append((chunk, lane, lanes))
            start += lanes
        pieces.append(parts)
    return pieces


class Place:
    def __init__(self, depth):
        wide = lax.axis_index("wide")
        narrow = lax.axis_index("narrow")
        self.depth = depth
        self.core = lax.rem(narrow, 2)
        self.y = narrow // 2
        self.x = lax.rem(wide, 2)
        self.z = wide // 2
        self.groups = depth * 4
        self.me = wide * 2 + self.y

    def at(self, z, x, y, core):
        return (z * 2 + x, y * 2 + core)

    def partner(self):
        return self.at(self.z, self.x, self.y, 1 - self.core)

    def over_x(self):
        return self.at(self.z, 1 - self.x, self.y, self.core)

    def over_y(self):
        return self.at(self.z, self.x, 1 - self.y, self.core)

    def up(self):
        return self.at(self.z + 1, self.x, self.y, self.core)

    def down(self):
        return self.at(self.z - 1, self.x, self.y, self.core)

    def peer(self, offset):
        other = lax.rem(self.me + offset, self.groups)
        return (other // 2, lax.rem(other, 2) * 2 + self.core)

    def enter(self):
        barrier = pltpu.get_barrier_semaphore()
        pl.semaphore_signal(barrier, inc=1, device_id=self.partner(), device_id_type=MESH)

        def greet(offset, carry):
            pl.semaphore_signal(barrier, inc=1, device_id=self.peer(offset), device_id_type=MESH)
            return carry

        lax.fori_loop(1, self.groups, greet, 0)
        pl.semaphore_wait(barrier, self.groups)


def remote(src, dst, send_sem, recv_sem, device):
    return pltpu.make_async_remote_copy(
        src_ref=src,
        dst_ref=dst,
        send_sem=send_sem,
        recv_sem=recv_sem,
        device_id=device,
        device_id_type=MESH,
    )


def when(cond, action):
    if cond is None:
        action()
    else:
        pl.when(cond)(action)


def cut(block):
    small = block // 8
    large = (block - 2 * small) // 2
    return large, small


def steps(depth, body, first=0):
    if depth <= 4:
        for step in range(first, depth):
            body(step)
    else:
        def looped(step, carry):
            body(step)
            return carry

        if first == 0:
            body(0)
        lax.fori_loop(max(first, 1), depth, looped, 0)


def gather_bank(place, bank, block, sems):
    depth, z, x, y = place.depth, place.z, place.x, place.y
    large, small = cut(block)
    (zab_s, zab_r, zcd_s, zcd_r, ax_s, ax_r, ay_s, ay_r, by_s, by_r, bx_s, bx_r, cd_s, cd_r) = sems

    def rows(zz, xx, yy, first, count):
        begin = ((zz * 2 + xx) * 2 + yy) * (block // UNIT) + first // UNIT
        return bank.at[pl.ds(begin, count // UNIT)]

    def move(zz, xx, yy, first, count, send_sem, recv_sem, device):
        ref = rows(zz, xx, yy, first, count)
        return remote(ref, ref, send_sem, recv_sem, device)

    start_b, start_c, start_d = large, 2 * large, 2 * large + small
    over_x, over_y, up, down = place.over_x(), place.over_y(), place.up(), place.down()

    def sides(step):
        out = [(z - step, z - step >= 0)]
        if not (isinstance(step, int) and step == 0):
            out.append((z + step, z + step < depth))
        return out

    def z_moves(step, kind):
        out = []
        low, high = z - step, z + step
        for level, cond, device, way in (
            (low, (low >= 0) & (z + 1 < depth), up, 0),
            (high, (high < depth) & (z >= 1), down, 1),
        ):
            if kind == "ab":
                out.append(
                    (cond, move(level, x, y, 0, 2 * large, zab_s.at[level, way], zab_r.at[level], device))
                )
            else:
                for xx in range(2):
                    for yy in range(2):
                        out.append(
                            (
                                cond,
                                move(
                                    level, xx, yy, start_c, 2 * small,
                                    zcd_s.at[level, way, xx * 2 + yy],
                                    zcd_r.at[level, xx * 2 + yy], device,
                                ),
                            )
                        )
        return out

    def ax(level):
        return move(level, x, y, 0, large, ax_s.at[level], ax_r.at[level], over_x)

    def by(level):
        return move(level, x, y, start_b, large, by_s.at[level], by_r.at[level], over_y)

    def ay(level, other):
        xx = 1 - x if other else x
        return move(level, xx, y, 0, large, ay_s.at[level, other], ay_r.at[level, other], over_y)

    def bx(level, other):
        yy = 1 - y if other else y
        return move(level, x, yy, start_b, large, bx_s.at[level, other], bx_r.at[level, other], over_x)

    plane = [
        move(z, x, y, start_c, small, cd_s.at[0], cd_r.at[0], over_x),
        move(z, x, y, start_d, small, cd_s.at[1], cd_r.at[1], over_y),
        move(z, x, y, start_c, small, cd_s.at[2], cd_r.at[2], over_y),
        move(z, 1 - x, y, start_c, small, cd_s.at[3], cd_r.at[3], over_y),
        move(z, x, y, start_d, small, cd_s.at[4], cd_r.at[4], over_x),
        move(z, x, 1 - y, start_d, small, cd_s.at[5], cd_r.at[5], over_x),
    ]

    def run(step):
        if isinstance(step, int) and step == 0:
            plane[0].start()
            plane[1].start()
        else:
            for level, cond in sides(step):
                when(cond, move(level, x, y, 0, 2 * large, zab_s.at[level, 0], zab_r.at[level], up).wait_recv)
        for cond, copy in z_moves(step, "ab"):
            when(cond, copy.start)
        for level, cond in sides(step):
            def begin(level=level):
                ax(level).start()
                by(level).start()
                ay(level, 0).start()
                bx(level, 0).start()

            when(cond, begin)
        if isinstance(step, int) and step == 0:
            plane[2].start()
            plane[4].start()
            plane[0].wait_recv()
            plane[3].start()
            plane[1].wait_recv()
            plane[5].start()
            for copy in plane[2:]:
                copy.wait_recv()
            for cond, copy in z_moves(0, "cd"):
                when(cond, copy.start)
        for level, cond in sides(step):
            def across(level=level):
                ax(level).wait_recv()
                ay(level, 1).start()
                by(level).wait_recv()
                bx(level, 1).start()

            when(cond, across)
        if not (isinstance(step, int) and step == 0):
            for level, cond in sides(step):
                def arrived(level=level):
                    for part in range(4):
                        move(
                            level, x, y, start_c, 2 * small, zcd_s.at[level, 0, part],
                            zcd_r.at[level, part], up,
                        ).wait_recv()

                when(cond, arrived)
            for cond, copy in z_moves(step, "cd"):
                when(cond, copy.start)

    steps(depth, run)

    def drain(step):
        for level, cond in sides(step):
            def finish(level=level):
                for other in range(2):
                    ay(level, other).wait_recv()
                    bx(level, other).wait_recv()
                    ay(level, other).wait_send()
                    bx(level, other).wait_send()
                ax(level).wait_send()
                by(level).wait_send()

            when(cond, finish)
        for kind in ("ab", "cd"):
            for cond, copy in z_moves(step, kind):
                when(cond, copy.wait_send)

    steps(depth, drain)
    for copy in plane:
        copy.wait_send()


def chain_kernel(
    depth, block,
    slot_ref, own_mats, own_x, own_dense, own_mask, own_cot, gain_ref, shift_ref,
    act_out, dcv_out, dsd_out, dense_out, blk_out, ig_out, dg_out, nrm_out,
    bank, act, dense, mask, cot, hat, side, pre4, acc, upsend, uprecv, dcv, dsd, dgrecv, igacc, igrecv,
    nrm, blk, blksend, keep, ex_side, ex_last, ex_sub,
    load_sem, swap_s, swap_r, act_s, act_r, up_s, up_r, ex_s, ex_r, out_sem, *tree,
):
    place = Place(depth)
    core, other = place.core, 1 - place.core
    partner = place.partner()
    half = bank.shape[2]
    width = 2 * half
    frames = own_mask.shape[0]
    rows = 2 * frames
    peers = place.groups - 1
    chunks = own_dense.shape[0]
    pieces = source_pieces(half)
    inner = pl.ds(EDGE, frames)

    place.enter()
    own_rows = block // 2
    base = place.me * (block // UNIT) + core * (own_rows // UNIT)
    mine = bank.at[pl.ds(base, own_rows // UNIT)]
    send_mats = remote(own_mats.at[other], mine, swap_s.at[0], swap_r.at[0], partner)
    send_mats.start()
    keep_mats = pltpu.make_async_copy(own_mats.at[core], mine, load_sem.at[0])
    keep_mats.start()
    edge_zero = jnp.zeros((EDGE, half), BF16)

    def clear(section, carry):
        for u in range(2):
            for h in range(2):
                act[section, h, u, pl.ds(0, EDGE)] = edge_zero
                act[section, h, u, pl.ds(EDGE + frames, EDGE)] = edge_zero
            dcv[section, u, pl.ds(0, EDGE)] = edge_zero
            dcv[section, u, pl.ds(EDGE + frames, EDGE)] = edge_zero
        return carry

    lax.fori_loop(0, SUBS, clear, 0)
    loads = [
        pltpu.make_async_copy(own_x, act.at[0, :, core, inner], load_sem.at[1]),
        pltpu.make_async_copy(own_dense, dense.at[:, core], load_sem.at[2]),
        pltpu.make_async_copy(own_mask, mask.at[core], load_sem.at[3]),
        pltpu.make_async_copy(own_cot.at[core], cot.at[core], load_sem.at[4]),
    ]
    swaps = [
        remote(own_x, act.at[0, :, core, inner], swap_s.at[1], swap_r.at[1], partner),
        remote(own_dense, dense.at[:, core], swap_s.at[2], swap_r.at[2], partner),
        remote(own_mask, mask.at[core], swap_s.at[3], swap_r.at[3], partner),
        remote(own_cot.at[other], cot.at[core], swap_s.at[4], swap_r.at[4], partner),
    ]
    keep_mats.wait()
    send_mats.wait()
    for copy in loads + swaps:
        copy.start()
    gather_bank(place, bank, block, tree)
    for copy in loads + swaps:
        copy.wait()

    outs = []

    def put(src, dst):
        copy = pltpu.make_async_copy(src, dst, out_sem.at[len(outs)])
        copy.start()
        outs.append(copy)

    put(dense, dense_out)

    def weight(matrix, first, count):
        begin = slot_ref[matrix] * (width // UNIT) + first // UNIT
        return jnp.concatenate([bank[begin + i] for i in range(count // UNIT)], axis=0)

    def valid():
        column = mask[...].reshape(rows, 128)
        return jnp.concatenate([column] * (half // 128), axis=1)

    def share(buffer, index, values):
        buffer[place.me] = values

        def go(offset, carry):
            remote(
                buffer.at[place.me], buffer.at[place.me], ex_s.at[index], ex_r.at[index],
                place.peer(offset),
            ).start()
            return carry

        lax.fori_loop(1, place.groups, go, 0, unroll=place.groups <= 16)

    def shared(buffer, index):
        everyone = buffer.at[pl.ds(0, peers)]
        copy = remote(everyone, everyone, ex_s.at[index], ex_r.at[index], place.peer(1))
        copy.wait_recv()
        copy.wait_send()
        return buffer[...]

    def moments(values, valid_now, count):
        total = jnp.sum(values * valid_now, axis=0, keepdims=True)
        spread = (values - total / count) * valid_now
        return total, jnp.sum(spread * spread, axis=0, keepdims=True)

    def merge(count, total, squares):
        frame_total = jnp.sum(count, axis=0)
        mean = jnp.sum(total, axis=0) / frame_total
        shift = total / count - mean[None]
        variance = jnp.sum(squares + count * shift * shift, axis=0) / frame_total
        return mean, lax.rsqrt(variance + norm_eps), frame_total

    valid_now = valid()
    count = jnp.sum(valid_now, axis=0, keepdims=True)
    totals, squares = [], []
    for index in range(SOURCES):
        if index < SOURCES - 1:
            value = None
            for chunk, lane, lanes in pieces[index]:
                left = dense[chunk].reshape(rows, half)[:, lane : lane + lanes]
                right = weight(SUBS * K + chunk // 2, (chunk % 2) * half + lane, lanes)
                term = jnp.dot(left, right, preferred_element_type=F32)
                value = term if value is None else value + term
        else:
            value = None
            for h in range(2):
                left = jnp.concatenate([act[0, h, u, inner] for u in range(2)], axis=0)
                term = jnp.dot(left, weight(SUBS * K + 3, h * half, half), preferred_element_type=F32)
                value = term if value is None else value + term
        side[index] = value
        total, square = moments(value, valid_now, count)
        totals.append(total)
        squares.append(square)
    fill = jnp.zeros((3, half), F32)
    share(ex_side, 0, jnp.concatenate([count] + totals + squares + [fill], axis=0))

    def convolve(section, h):
        value = None
        for k in range(K):
            left = jnp.concatenate(
                [act[section, h, u, pl.ds(EDGE - MARGIN + k, frames)] for u in range(2)], axis=0
            )
            term = jnp.dot(
                left, weight(section * K + k, h * half, half), preferred_element_type=F32
            )
            value = term if value is None else value + term
            if k % 2 == 1 or k == K - 1:
                acc[...] += value
                value = None

    def swap_act(section):
        own = act.at[section, core, :, inner]
        return remote(own, own, act_s.at[section], act_r.at[section], partner)

    def forward(section, last):
        acc[...] = jnp.zeros_like(acc)
        convolve(section, core)
        if isinstance(section, int):
            if section > 0:
                swap_act(section).wait_recv()
        else:
            pl.when(section > 0)(swap_act(section).wait_recv)
        convolve(section, other)
        valid_now = valid()
        values = acc[...]
        count = jnp.sum(valid_now, axis=0, keepdims=True)
        total, square = moments(values, valid_now, count)
        share(
            ex_sub.at[lax.rem(section, 2)], 1 + section,
            jnp.concatenate([count, total, square, jnp.zeros_like(count)], axis=0),
        )
        parts = shared(ex_sub.at[lax.rem(section, 2)], 1 + section)
        mean, inverse, frame_total = merge(parts[:, 0], parts[:, 1], parts[:, 2])
        normed = (values - mean[None]) * inverse[None]
        hat[section] = normed
        keep[pl.ds(section, 1)] = inverse[None]
        before = normed * gain_ref[pl.ds(section, 1)] + shift_ref[pl.ds(section, 1)]
        if last:
            before = before + pre4[...]
            pre4[...] = before
        hidden = (before * jax.nn.sigmoid(before) * valid()).astype(BF16)
        if last:
            hidden = hidden.reshape(2, frames, half)
            for u in range(2):
                @pl.when(core == u)
                def _(u=u):
                    blk[core] = hidden[u]
                    blksend[...] = hidden[1 - u]
        else:
            for u in range(2):
                act[section + 1, core, u, inner] = hidden[u * frames : (u + 1) * frames]
            swap_act(section + 1).start()
        return frame_total

    def looped(section, carry):
        forward(section, False)

        @pl.when(section == 0)
        def _():
            parts = shared(ex_side, 0)
            before = None
            for index in range(SOURCES):
                mean, inverse, _ = merge(
                    parts[:, 0], parts[:, 1 + index], parts[:, 1 + SOURCES + index]
                )
                normed = (side[index] - mean[None]) * inverse[None]
                side[index] = normed
                keep[pl.ds(SUBS + index, 1)] = inverse[None]
                term = (
                    normed * gain_ref[pl.ds(SUBS + index, 1)] + shift_ref[pl.ds(SUBS + index, 1)]
                )
                before = term if before is None else before + term
            pre4[...] = before

        return carry

    lax.fori_loop(0, SUBS - 1, looped, 0)
    frame_total = forward(SUBS - 1, True)[None]
    blk_copy = remote(blksend, blk.at[core], swap_s.at[5], swap_r.at[5], partner)
    blk_copy.start()
    for section in range(1, SUBS):
        swap_act(section).wait_send()
    put(act, act_out)

    def slope_of(section, upstream, before):
        sigmoid = jax.nn.sigmoid(before)
        return upstream * valid() * (sigmoid * (1.0 + before * (1.0 - sigmoid)))

    def branch(slope, normed, index, shift_sum, gain_sum):
        scale = gain_ref[pl.ds(index, 1)] * keep[pl.ds(index, 1)]
        return (
            valid() * scale * (slope - shift_sum / frame_total - normed * (gain_sum / frame_total))
        ).astype(BF16)

    def store_branch(section, value):
        for u in range(2):
            dcv[section, u, inner] = value[u * frames : (u + 1) * frames]

    def back_half(section, h):
        total = None
        value = None
        for k in range(K):
            left = jnp.concatenate(
                [dcv[section, u, pl.ds(EDGE + MARGIN - k, frames)] for u in range(2)], axis=0
            )
            term = lax.dot_general(
                left, weight(section * K + k, h * half, half), NT, preferred_element_type=F32
            )
            value = term if value is None else value + term
            if k % 2 == 1 or k == K - 1:
                total = value if total is None else total + value
                value = None
        return total

    def up_copy(section):
        slot = lax.rem(section, 2)
        return remote(upsend, uprecv.at[slot], up_s.at[slot], up_r.at[slot], partner)

    def backward(section):
        upsend[...] = back_half(section, other)
        up_copy(section).start()
        acc[...] = back_half(section, core)

    def joined(section):
        copy = up_copy(section)
        copy.wait()
        return acc[...] + uprecv[lax.rem(section, 2)]

    before = pre4[...]
    slope = slope_of(SUBS - 1, cot[...].reshape(rows, half).astype(F32), before)
    sums = [jnp.sum(slope, axis=0, keepdims=True)]
    sums.append(jnp.sum(slope * hat[SUBS - 1], axis=0, keepdims=True))
    for index in range(SOURCES):
        sums.append(jnp.sum(slope * side[index], axis=0, keepdims=True))
    share(ex_last, SUBS + 1, jnp.concatenate(sums, axis=0))
    pre4[...] = slope
    sums = jnp.sum(shared(ex_last, SUBS + 1), axis=0)
    slope = pre4[...]
    shift_sum = sums[0:1]
    store_branch(SUBS - 1, branch(slope, hat[SUBS - 1], SUBS - 1, shift_sum, sums[1:2]))
    nrm[core] = jnp.zeros_like(nrm[0])
    nrm[core, pl.ds(SUBS - 1, 1 + SOURCES)] = sums[1:]
    nrm[core, pl.ds(SUBS + SOURCES + SUBS - 1, 1)] = shift_sum
    backward(SUBS - 1)
    for index in range(SOURCES):
        dsd[index] = branch(slope, side[index], SUBS + index, shift_sum, sums[2 + index : 3 + index])
    put(dsd, dsd_out)
    for index in range(SOURCES - 1):
        for chunk, lane, lanes in pieces[index]:
            right = weight(SUBS * K + chunk // 2, (chunk % 2) * half + lane, lanes)
            side[chunk, :, pl.ds(lane, lanes)] = lax.dot_general(
                dsd[index], right, NT, preferred_element_type=F32
            )
    theirs = pl.multiple_of(other * frames, frames)
    ours = pl.multiple_of(core * frames, frames)
    dg_copy = remote(
        side.at[:, pl.ds(theirs, frames)], dgrecv, swap_s.at[6], swap_r.at[6], partner
    )
    dg_copy.start()

    def looped_back(turn, carry):
        section = SUBS - 2 - turn
        upstream = joined(section + 1)
        normed = hat[section]
        before = normed * gain_ref[pl.ds(section, 1)] + shift_ref[pl.ds(section, 1)]
        slope = slope_of(section, upstream, before)
        zero = jnp.zeros((2, half), F32)
        share(
            ex_sub.at[lax.rem(section, 2)], SUBS + 2 + section,
            jnp.concatenate(
                [
                    jnp.sum(slope, axis=0, keepdims=True),
                    jnp.sum(slope * normed, axis=0, keepdims=True),
                    zero,
                ],
                axis=0,
            ),
        )
        sums = jnp.sum(shared(ex_sub.at[lax.rem(section, 2)], SUBS + 2 + section), axis=0)
        store_branch(section, branch(slope, normed, section, sums[0:1], sums[1:2]))
        nrm[core, pl.ds(section, 1)] = sums[1:2]
        nrm[core, pl.ds(SUBS + SOURCES + section, 1)] = sums[0:1]

        @pl.when(section > 0)
        def _():
            backward(section)

        return carry

    lax.fori_loop(0, SUBS - 1, looped_back, 0)
    put(dcv, dcv_out)
    nrm_copy = remote(nrm.at[core], nrm.at[core], swap_s.at[7], swap_r.at[7], partner)
    nrm_copy.start()
    for h in range(2):
        value = back_half(0, h) + lax.dot_general(
            dsd[SOURCES - 1], weight(SUBS * K + 3, h * half, half), NT, preferred_element_type=F32
        )
        igacc[h] = value
    ig_copy = remote(
        igacc.at[:, pl.ds(theirs, frames)], igrecv, swap_s.at[8], swap_r.at[8], partner
    )
    ig_copy.start()
    own_valid = jnp.concatenate([mask[core]] * (half // 128), axis=1)
    dg_copy.wait()
    for chunk in range(chunks):
        dgrecv[chunk] = (dgrecv[chunk] + side[chunk, pl.ds(ours, frames)]) * own_valid
    put(dgrecv, dg_out)
    blk_copy.wait()
    put(blk, blk_out)
    nrm_copy.wait()
    put(nrm, nrm_out)
    ig_copy.wait()
    for h in range(2):
        igrecv[h] = (igrecv[h] + igacc[h, pl.ds(ours, frames)]) * own_valid
    put(igrecv, ig_out)
    for copy in outs:
        copy.wait()


def run_chain(depth, block, places, own_mats, own_x, own_dense, own_mask, own_cot, gains, shifts):
    frames = own_mask.shape[0]
    half = own_mats.shape[3]
    rows = 2 * frames
    chunks = own_dense.shape[0]
    padded = frames + 2 * EDGE
    groups = depth * 4
    dma = pltpu.SemaphoreType.DMA
    anywhere = pl.BlockSpec(memory_space=pl.ANY)
    vmem = pl.BlockSpec(memory_space=pltpu.VMEM)
    out_shape = [
        jax.ShapeDtypeStruct((SUBS, 2, 2, padded, half), BF16),
        jax.ShapeDtypeStruct((SUBS, 2, padded, half), BF16),
        jax.ShapeDtypeStruct((SOURCES, rows, half), BF16),
        jax.ShapeDtypeStruct((chunks, 2, frames, half), BF16),
        jax.ShapeDtypeStruct((2, frames, half), BF16),
        jax.ShapeDtypeStruct((2, frames, half), F32),
        jax.ShapeDtypeStruct((chunks, frames, half), F32),
        jax.ShapeDtypeStruct((2, 16, half), F32),
    ]
    scratch = [
        pltpu.VMEM((groups * block // UNIT, UNIT, half), BF16),
        pltpu.VMEM((SUBS, 2, 2, padded, half), BF16),
        pltpu.VMEM((chunks, 2, frames, half), BF16),
        pltpu.VMEM((2, frames, 128), F32),
        pltpu.VMEM((2, frames, half), BF16),
        pltpu.VMEM((SUBS, rows, half), F32),
        pltpu.VMEM((SOURCES, rows, half), F32),
        pltpu.VMEM((rows, half), F32),
        pltpu.VMEM((rows, half), F32),
        pltpu.VMEM((rows, half), F32),
        pltpu.VMEM((2, rows, half), F32),
        pltpu.VMEM((SUBS, 2, padded, half), BF16),
        pltpu.VMEM((SOURCES, rows, half), BF16),
        pltpu.VMEM((chunks, frames, half), F32),
        pltpu.VMEM((2, rows, half), F32),
        pltpu.VMEM((2, frames, half), F32),
        pltpu.VMEM((2, 16, half), F32),
        pltpu.VMEM((2, frames, half), BF16),
        pltpu.VMEM((frames, half), BF16),
        pltpu.VMEM((16, half), F32),
        pltpu.VMEM((groups, 16, half), F32),
        pltpu.VMEM((groups, 8, half), F32),
        pltpu.VMEM((2, groups, 4, half), F32),
        dma((5,)),
        dma((9,)), dma((9,)),
        dma((SUBS,)), dma((SUBS,)),
        dma((2,)), dma((2,)),
        dma((2 * SUBS + 1,)), dma((2 * SUBS + 1,)),
        dma((8,)),
    ] + [
        dma((depth, 2)), dma((depth,)), dma((depth, 2, 4)), dma((depth, 4)),
        dma((depth,)), dma((depth,)), dma((depth, 2)), dma((depth, 2)),
        dma((depth,)), dma((depth,)), dma((depth, 2)), dma((depth, 2)),
        dma((6,)), dma((6,)),
    ]
    return pl.pallas_call(
        functools.partial(chain_kernel, depth, block),
        out_shape=out_shape,
        in_specs=[pl.BlockSpec(memory_space=pltpu.SMEM)] + [anywhere] * 5 + [vmem] * 2,
        out_specs=[anywhere] * len(out_shape),
        scratch_shapes=scratch,
        compiler_params=pltpu.CompilerParams(
            collective_id=1, has_side_effects=True, vmem_limit_bytes=63 << 20
        ),
        cost_estimate=pl.CostEstimate(
            flops=4 * SUBS * K * rows * 2 * half * half, bytes_accessed=16 << 20, transcendentals=0
        ),
        name="chain",
    )(places, own_mats, own_x, own_dense, own_mask, own_cot, gains, shifts)


def grad_kernel(slot_ref, act_ref, dcv_ref, dense_ref, dsd_ref, out_ref, left, stage, sems):
    section = pl.program_id(0)
    half = act_ref.shape[4]
    width = 2 * half
    frames = act_ref.shape[3] - 2 * EDGE
    rows = 2 * frames
    inner = pl.ds(EDGE, frames)
    depth = stage.shape[0]
    for h in range(2):
        left[pl.ds(h * half, half), :] = jnp.concatenate(
            [act_ref[0, h, u, inner] for u in range(2)], axis=0
        ).T

    def emit(turn, matrix, value):
        place = turn % depth
        out = out_ref.at[pl.ds(pl.multiple_of(slot_ref[matrix] * width, 16), width)]
        copy = pltpu.make_async_copy(stage.at[place], out, sems.at[place])
        if turn >= depth:
            copy.wait()
        stage[place] = value.astype(BF16)
        copy.start()
        return copy

    def finish(turns):
        for turn in range(max(0, turns - depth), turns):
            place = turn % depth
            pltpu.make_async_copy(
                stage.at[place], out_ref.at[pl.ds(0, width)], sems.at[place]
            ).wait()

    for k in range(K):
        right = jnp.concatenate(
            [dcv_ref[0, u, pl.ds(EDGE + MARGIN - k, frames)] for u in range(2)], axis=0
        )
        emit(k, section * K + k, jnp.dot(left[...], right, preferred_element_type=F32))
    finish(K)

    @pl.when(section == 0)
    def _():
        pieces = source_pieces(half)
        chunk_rows = [[] for _ in range(dense_ref.shape[0])]
        for index, parts in enumerate(pieces):
            for chunk, lane, lanes in parts:
                chunk_rows[chunk].append((lane, lanes, index))
        for matrix in range(4):
            if matrix < 3:
                out = []
                for chunk in (2 * matrix, 2 * matrix + 1):
                    turned = dense_ref[chunk].reshape(rows, half).T
                    for lane, lanes, index in chunk_rows[chunk]:
                        out.append(
                            jnp.dot(
                                turned[lane : lane + lanes], dsd_ref[index],
                                preferred_element_type=F32,
                            )
                        )
                value = jnp.concatenate(out, axis=0)
            else:
                value = jnp.dot(left[...], dsd_ref[SOURCES - 1], preferred_element_type=F32)
            emit(matrix, SUBS * K + matrix, value)
        finish(4)


def run_grads(total_rows, places, act, dcv, dense, dsd):
    half = act.shape[4]
    grid_spec = pltpu.PrefetchScalarGridSpec(
        num_scalar_prefetch=1,
        grid=(SUBS,),
        in_specs=[
            pl.BlockSpec((1,) + act.shape[1:], lambda s, t: (s, 0, 0, 0, 0)),
            pl.BlockSpec((1,) + dcv.shape[1:], lambda s, t: (s, 0, 0, 0)),
            pl.BlockSpec(dense.shape, lambda s, t: (0, 0, 0, 0)),
            pl.BlockSpec(dsd.shape, lambda s, t: (0, 0, 0)),
        ],
        out_specs=pl.BlockSpec(memory_space=pl.ANY),
        scratch_shapes=[
            pltpu.VMEM((2 * half, dsd.shape[1]), BF16),
            pltpu.VMEM((4, 2 * half, half), BF16),
            pltpu.SemaphoreType.DMA((4,)),
        ],
    )
    return pl.pallas_call(
        grad_kernel,
        grid_spec=grid_spec,
        out_shape=jax.ShapeDtypeStruct((total_rows, half), BF16),
        compiler_params=pltpu.CompilerParams(vmem_limit_bytes=40 << 20),
        name="weight_grads",
    )(places, act, dcv, dense, dsd)


def reduce_kernel(
    depth, block, grads, out, l_ay, l_ax, l_bx, l_by, l_zab, l_zcd, l_c, l_d, stage, final, result,
    stage_sem, out_sem, swap_s, swap_r, ay_s, ay_r, ax_s, ax_r, bx_s, bx_r, by_s, by_r,
    zab_s, zab_r, zcd_s, zcd_r, cd_s, cd_r,
):
    place = Place(depth)
    z, x, y, core = place.z, place.x, place.y, place.core
    large, small = cut(block)
    start_b, start_c, start_d = large, 2 * large, 2 * large + small
    over_x, over_y, up, down = place.over_x(), place.over_y(), place.up(), place.down()
    place.enter()

    def rows(zz, xx, yy, first, count):
        begin = pl.multiple_of(((zz * 2 + xx) * 2 + yy) * block + first, 16)
        return grads.at[pl.ds(begin, count)]

    def ay(level, other_x):
        xx = 1 - x if other_x else x
        return remote(
            rows(level, xx, 1 - y, 0, large), l_ay.at[level, other_x],
            ay_s.at[level, other_x], ay_r.at[level, other_x], over_y,
        )

    def bx(level, other_y):
        yy = 1 - y if other_y else y
        return remote(
            rows(level, 1 - x, yy, start_b, large), l_bx.at[level, other_y],
            bx_s.at[level, other_y], bx_r.at[level, other_y], over_x,
        )

    def ax(level):
        return remote(l_ay.at[level, 1], l_ax.at[level], ax_s.at[level], ax_r.at[level], over_x)

    def by(level):
        return remote(l_bx.at[level, 1], l_by.at[level], by_s.at[level], by_r.at[level], over_y)

    def fetch(refs):
        copies = []
        first = 0
        for index, ref in enumerate(refs):
            copy = pltpu.make_async_copy(
                ref, stage.at[pl.ds(first, ref.shape[0])], stage_sem.at[index]
            )
            copy.start()
            copies.append(copy)
            first += ref.shape[0]
        return copies

    def add(target, first, count, others, keep=None):
        strip = count
        while strip > 192 or count % strip:
            strip -= 16

        def one(index, carry):
            at = pl.ds(pl.multiple_of(index * strip, 16), strip)
            value = stage[pl.ds(pl.multiple_of(first + index * strip, 16), strip)].astype(F32)
            for ref in [target] + others:
                value = value + ref[at].astype(F32)
            if keep is None:
                target[at] = value.astype(BF16)
            else:
                keep[at] = value
            return carry

        lax.fori_loop(0, count // strip, one, 0)

    def sides(step):
        out = [(z - step, z - step >= 0)]
        if not (isinstance(step, int) and step == 0):
            out.append((z + step, z + step < depth))
        return out

    def backwards(body, first, last):
        if depth <= 4:
            for step in range(first, last - 1, -1):
                body(step)
        else:
            def looped(turn, carry):
                body(first - turn)
                return carry

            lax.fori_loop(0, first - last + 1, looped, 0)

    def leaves(step):
        for level, cond in sides(step):
            def go(level=level):
                for other in (1, 0):
                    ay(level, other).start()
                    bx(level, other).start()

            when(cond, go)

    def zcd(level, way, part):
        device = down if way == 0 else up
        beyond = z + 1 < depth if way == 0 else z >= 1
        at_home = (z - 1 == level) if way == 0 else (z + 1 == level)
        entry = level if way == 0 else level + (depth - level) * at_home.astype(jnp.int32)
        dst = l_zcd.at[entry, part]
        src = rows(level, part // 2, part % 2, start_c, 2 * small)
        send_sem, recv_sem = zcd_s.at[level, part], zcd_r.at[entry, part]
        leaf = remote(src, dst, send_sem, recv_sem, device)
        node = remote(l_zcd.at[level, part], dst, send_sem, recv_sem, device)
        return beyond, leaf, node, src

    def plane_step(step):
        for way, level, cond in ((0, z - step, z - step >= 0), (1, z + step, z + step < depth)):
            def go(way=way, level=level):
                hops = [zcd(level, way, part) for part in range(4)]
                beyond = hops[0][0]

                @pl.when(beyond)
                def _():
                    copies = fetch([hop[3] for hop in hops])
                    for part, (_, leaf, node, src) in enumerate(hops):
                        remote(
                            l_zcd.at[level, part], l_zcd.at[level, part], zcd_s.at[level, part],
                            zcd_r.at[level, part], up,
                        ).wait_recv()
                        copies[part].wait()
                        add(l_zcd.at[level, part], part * 2 * small, 2 * small, [])
                        node.start()

                @pl.when(jnp.logical_not(beyond))
                def _():
                    for _, leaf, node, src in hops:
                        leaf.start()

            when(cond, go)

    def zab(level, way):
        device = down if way == 0 else up
        beyond = z + 1 < depth if way == 0 else z >= 1
        at_home = (z - 1 == level) if way == 0 else (z + 1 == level)
        entry = level if way == 0 else level + (depth - level) * at_home.astype(jnp.int32)
        copies = []
        for index, landing in enumerate((l_ax, l_by)):
            copies.append(
                remote(
                    landing.at[level], l_zab.at[entry, index], zab_s.at[level, index],
                    zab_r.at[entry, index], device,
                )
            )
        return beyond, copies

    def zab_arrived(entry, index):
        remote(
            l_zab.at[entry, index], l_zab.at[entry, index], zab_s.at[entry, index],
            zab_r.at[entry, index], up,
        ).wait_recv()

    def across(level):
        copies = fetch([rows(level, 1 - x, y, 0, large), rows(level, x, 1 - y, start_b, large)])
        ay(level, 1).wait_recv()
        copies[0].wait()
        add(l_ay.at[level, 1], 0, large, [])
        ax(level).start()
        bx(level, 1).wait_recv()
        copies[1].wait()
        add(l_bx.at[level, 1], large, large, [])
        by(level).start()

    def line_step(step):
        for way, level, cond in ((0, z - step, z - step >= 0), (1, z + step, z + step < depth)):
            def go(way=way, level=level):
                copies = fetch([rows(level, x, y, 0, 2 * large)])
                beyond, hops = zab(level, way)
                ay(level, 0).wait_recv()
                ax(level).wait_recv()
                copies[0].wait()

                @pl.when(beyond)
                def _():
                    zab_arrived(level, 0)
                    add(l_ax.at[level], 0, large, [l_ay.at[level, 0], l_zab.at[level, 0]])

                @pl.when(jnp.logical_not(beyond))
                def _():
                    add(l_ax.at[level], 0, large, [l_ay.at[level, 0]])

                hops[0].start()
                bx(level, 0).wait_recv()
                by(level).wait_recv()

                @pl.when(beyond)
                def _():
                    zab_arrived(level, 1)
                    add(l_by.at[level], large, large, [l_bx.at[level, 0], l_zab.at[level, 1]])

                @pl.when(jnp.logical_not(beyond))
                def _():
                    add(l_by.at[level], large, large, [l_bx.at[level, 0]])

                hops[1].start()

            when(cond, go)

    def both(step, action):
        for level, cond in sides(step):
            when(cond, functools.partial(action, level))

    backwards(leaves, depth - 1, 0)

    def turn(step):
        plane_step(step)
        both(step, across)
        line_step(step)

    backwards(turn, depth - 1, 1)

    def home(entry, part, cond):
        def go():
            remote(
                l_zcd.at[entry, part], l_zcd.at[entry, part], zcd_s.at[0, part],
                zcd_r.at[entry, part], up,
            ).wait_recv()

        when(cond, go)

    above, below = z + 1 < depth, z >= 1
    copies = fetch([rows(z, part // 2, part % 2, start_c, 2 * small) for part in range(4)])
    for part in range(4):
        home(z, part, above)
        home(depth, part, below)
        copies[part].wait()

        @pl.when(above & below)
        def _(part=part):
            add(l_zcd.at[z, part], part * 2 * small, 2 * small, [l_zcd.at[depth, part]])

        @pl.when(above & jnp.logical_not(below))
        def _(part=part):
            add(l_zcd.at[z, part], part * 2 * small, 2 * small, [])

        @pl.when(jnp.logical_not(above))
        def _(part=part):
            strip = 2 * small
            value = stage[pl.ds(part * strip, strip)].astype(F32) + l_zcd[depth, part].astype(F32)
            l_zcd[z, part] = value.astype(BF16)

    def block_at(xx, yy, first):
        return l_zcd.at[z, xx * 2 + yy, pl.ds(first, small)]

    plane = [
        remote(block_at(1 - x, 1 - y, 0), l_c.at[1], cd_s.at[0], cd_r.at[0], over_y),
        remote(block_at(x, 1 - y, 0), l_c.at[0], cd_s.at[1], cd_r.at[1], over_y),
        remote(block_at(1 - x, 1 - y, small), l_d.at[1], cd_s.at[2], cd_r.at[2], over_x),
        remote(block_at(1 - x, y, small), l_d.at[0], cd_s.at[3], cd_r.at[3], over_x),
        remote(l_c.at[1], l_c.at[2], cd_s.at[4], cd_r.at[4], over_x),
        remote(l_d.at[1], l_d.at[2], cd_s.at[5], cd_r.at[5], over_y),
    ]
    for copy in plane[:4]:
        copy.start()
    both(0, across)
    plane[0].wait_recv()
    l_c[1] = (l_c[1].astype(F32) + l_zcd[z, (1 - x) * 2 + y, pl.ds(0, small)].astype(F32)).astype(BF16)
    plane[4].start()
    plane[2].wait_recv()
    l_d[1] = (l_d[1].astype(F32) + l_zcd[z, x * 2 + 1 - y, pl.ds(small, small)].astype(F32)).astype(BF16)
    plane[5].start()

    copies = fetch([rows(z, x, y, 0, 2 * large)])
    copies[0].wait()
    for index, (first_hop, second_hop, first_land, second_land, begin) in enumerate(
        ((ay, ax, l_ay, l_ax, 0), (bx, by, l_bx, l_by, start_b))
    ):
        first_hop(z, 0).wait_recv()
        second_hop(z).wait_recv()
        base = [second_land.at[z], first_land.at[z, 0]]
        target = final.at[pl.ds(begin, large)]

        @pl.when(above)
        def _(index=index):
            zab_arrived(z, index)

        @pl.when(below)
        def _(index=index):
            zab_arrived(depth, index)

        for cond, more in (
            (above & below, [z, depth]),
            (above & jnp.logical_not(below), [z]),
            (jnp.logical_not(above), [depth]),
        ):
            @pl.when(cond)
            def _(more=more, base=base, target=target, begin=begin, index=index):
                add(
                    base[0], begin, large,
                    base[1:] + [l_zab.at[entry, index] for entry in more], keep=target,
                )

    for copy in (plane[1], plane[3], plane[4], plane[5]):
        copy.wait_recv()
    here = x * 2 + y
    final[pl.ds(start_c, small)] = (
        l_zcd[z, here, pl.ds(0, small)].astype(F32) + l_c[0].astype(F32) + l_c[2].astype(F32)
    )
    final[pl.ds(start_d, small)] = (
        l_zcd[z, here, pl.ds(small, small)].astype(F32) + l_d[0].astype(F32) + l_d[2].astype(F32)
    )
    own_rows = block // 2
    theirs = final.at[pl.ds(pl.multiple_of((1 - core) * own_rows, 16), own_rows)]
    mine = final.at[pl.ds(pl.multiple_of(core * own_rows, 16), own_rows)]
    cross = remote(theirs, result, swap_s.at[0], swap_r.at[0], place.partner())
    cross.start()
    local = pltpu.make_async_copy(mine, out.at[core], out_sem.at[0])
    local.start()

    def drain(step):
        for level, cond in sides(step):
            def go(level=level):
                for other in range(2):
                    ay(level, other).wait_send()
                    bx(level, other).wait_send()
                ax(level).wait_send()
                by(level).wait_send()

            when(cond, go)
        if not (isinstance(step, int) and step == 0):
            for way, level, cond in ((0, z - step, z - step >= 0), (1, z + step, z + step < depth)):
                def go(way=way, level=level):
                    for part in range(4):
                        zcd(level, way, part)[2].wait_send()
                    for copy in zab(level, way)[1]:
                        copy.wait_send()

                when(cond, go)

    steps(depth, drain)
    for copy in plane:
        copy.wait_send()
    cross.wait()
    fetched = pltpu.make_async_copy(result, out.at[1 - core], out_sem.at[1])
    fetched.start()
    fetched.wait()
    local.wait()


def run_reduce(depth, block, grads):
    half = grads.shape[1]
    large, small = cut(block)
    dma = pltpu.SemaphoreType.DMA
    anywhere = pl.BlockSpec(memory_space=pl.ANY)
    scratch = [
        pltpu.VMEM((depth, 2, large, half), BF16),
        pltpu.VMEM((depth, large, half), BF16),
        pltpu.VMEM((depth, 2, large, half), BF16),
        pltpu.VMEM((depth, large, half), BF16),
        pltpu.VMEM((depth + 1, 2, large, half), BF16),
        pltpu.VMEM((depth + 1, 4, 2 * small, half), BF16),
        pltpu.VMEM((3, small, half), BF16),
        pltpu.VMEM((3, small, half), BF16),
        pltpu.VMEM((max(2 * large, 8 * small), half), BF16),
        pltpu.VMEM((block, half), F32),
        pltpu.VMEM((block // 2, half), F32),
        dma((4,)), dma((2,)), dma((1,)), dma((1,)),
        dma((depth, 2)), dma((depth, 2)), dma((depth,)), dma((depth,)),
        dma((depth, 2)), dma((depth, 2)), dma((depth,)), dma((depth,)),
        dma((depth + 1, 2)), dma((depth + 1, 2)),
        dma((depth + 1, 4)), dma((depth + 1, 4)),
        dma((6,)), dma((6,)),
    ]
    return pl.pallas_call(
        functools.partial(reduce_kernel, depth, block),
        out_shape=jax.ShapeDtypeStruct((2, block // 2, half), F32),
        in_specs=[anywhere],
        out_specs=anywhere,
        scratch_shapes=scratch,
        compiler_params=pltpu.CompilerParams(
            collective_id=2, has_side_effects=True, vmem_limit_bytes=62 << 20
        ),
        name="reduce",
    )(grads)


def adamw(gradient, params, first_moment, second_moment, rate, decay):
    moment_new = beta_one * first_moment + (1.0 - beta_one) * gradient
    second_new = beta_two * second_moment + (1.0 - beta_two) * gradient * gradient
    direction = (
        moment_new
        / (1.0 - beta_one**STEP)
        / (jnp.sqrt(second_new / (1.0 - beta_two**STEP)) + adam_eps)
    )
    return (moment_new, second_new, params - rate * (direction + decay * params))


def body(
    inputs,
    dense_inputs,
    lengths,
    owners,
    cotangent,
    master,
    moment_one,
    moment_two,
    average,
    norm_gain,
    norm_shift,
    norm_one,
    norm_two,
):
    _, frames, width = inputs.shape
    half = width // 2
    wides, narrows = lax.axis_size("wide"), lax.axis_size("narrow")
    depth = wides // 2
    own_rows = master.shape[0]
    block = 2 * own_rows
    capacity = own_rows * narrows // width
    places = slot_table(owners, capacity)
    valid = (jnp.arange(frames, dtype=jnp.int32) < lengths[0]).astype(F32)
    low_valid = valid[:, None].astype(BF16)

    def by_halves(values):
        return values.reshape(values.shape[0], -1, half).transpose(1, 0, 2)

    core = lax.rem(lax.axis_index("narrow"), 2)
    gains = lax.dynamic_slice(norm_gain, (0, core * half), (norm_gain.shape[0], half))
    shifts = lax.dynamic_slice(norm_shift, (0, core * half), (norm_shift.shape[0], half))
    act, dcv, dsd, dense, blk, input_grad, dense_grad, sums = run_chain(
        depth, block, places,
        by_halves(master.astype(BF16)).reshape(2, -1, UNIT, half),
        by_halves(inputs[0] * low_valid),
        by_halves(dense_inputs[0] * low_valid),
        jnp.broadcast_to(valid[:, None], (frames, 128)),
        by_halves(cotangent[0]),
        gains, shifts,
    )
    grads = run_grads(wides * narrows * own_rows, places, act, dcv, dense, dsd)
    reduced = run_reduce(depth, block, grads)

    def joined(values):
        return values.transpose(1, 0, 2).reshape(values.shape[1], -1)

    mine = (lax.axis_index("wide") * narrows + lax.axis_index("narrow")) * own_rows
    slot_of_row = (mine + jnp.arange(own_rows, dtype=jnp.int32)) // width
    filled = jnp.any(places[None, :] == slot_of_row[:, None], axis=1)
    weight_grad = jnp.where(filled[:, None], joined(reduced), 0.0)
    weight_one, weight_two, weight_new = adamw(
        weight_grad, master, moment_one, moment_two, rate_main, decay_main
    )
    weight_average = ema_keep * average + (1.0 - ema_keep) * weight_new
    sums = joined(sums)
    branches = SUBS + SOURCES
    shift_rows = sums[branches : branches + SUBS]
    norm_grad = jnp.stack(
        [
            sums[:branches],
            jnp.concatenate([shift_rows] + [shift_rows[SUBS - 1 :]] * SOURCES, axis=0),
        ]
    )
    norm_params = jnp.stack([norm_gain, norm_shift])
    norm_one_new, norm_two_new, norm_new = adamw(
        norm_grad, norm_params, norm_one, norm_two, rate_norm, 0.0
    )
    return (
        joined(blk)[None],
        joined(input_grad)[None],
        joined(dense_grad)[None],
        weight_grad,
        weight_one,
        weight_two,
        weight_new,
        weight_average,
        weight_new.astype(BF16),
        norm_grad,
        norm_one_new,
        norm_two_new,
        norm_new,
    )


def solution(mesh):
    rows = P(AXES, None)
    utterances = P(AXES, None, None)
    in_specs = (
        utterances, utterances, P(AXES), P(), utterances, rows, rows, rows, rows,
        P(), P(), P(), P(),
    )
    out_specs = (
        utterances, utterances, utterances, rows, rows, rows, rows, rows, rows,
        P(), P(), P(), P(),
    )
    return jax.shard_map(body, mesh=mesh, in_specs=in_specs, out_specs=out_specs, check_vma=False)
```

```python
import functools

import jax
import jax.numpy as jnp
from jax import lax
from jax.experimental import pallas as pl
from jax.experimental.pallas import tpu as pltpu
from jax.sharding import PartitionSpec as P

WLOW = 256
WMID = 384
K = 17
SUBS = 5
SOURCES = 6
STEP = 10
MARGIN = K // 2
EDGE = 16
UNIT = 64
F32 = jnp.float32
BF16 = jnp.bfloat16
MESH = pl.DeviceIdType.MESH
AXES = ("wide", "narrow")

norm_eps = 1e-05
beta_one = 0.9
beta_two = 0.999
adam_eps = 1e-08
rate_main = 0.02
rate_norm = 0.15
decay_main = 0.01
ema_keep = 0.8

NT = (((1,), (1,)), ((), ()))


def slot_table(owners, capacity):
    number = owners.shape[0]
    same_owner = owners[:, None] == owners[None, :]
    earlier = jnp.arange(number)[None, :] < jnp.arange(number)[:, None]
    ranking = jnp.sum(jnp.where(same_owner & earlier, 1, 0), axis=1)
    return (owners * capacity + ranking).astype(jnp.int32)


def source_pieces(half):
    pieces = []
    start = 0
    for width in (WLOW, WLOW, WLOW, WMID, WMID):
        parts = []
        stop = start + width
        while start < stop:
            chunk, lane = divmod(start, half)
            lanes = min(half - lane, stop - start)
            parts.append((chunk, lane, lanes))
            start += lanes
        pieces.append(parts)
    return pieces


class Place:
    def __init__(self, depth):
        wide = lax.axis_index("wide")
        narrow = lax.axis_index("narrow")
        self.depth = depth
        self.core = lax.rem(narrow, 2)
        self.y = narrow // 2
        self.x = lax.rem(wide, 2)
        self.z = wide // 2
        self.groups = depth * 4
        self.me = wide * 2 + self.y

    def at(self, z, x, y, core):
        return (z * 2 + x, y * 2 + core)

    def beside(self):
        return self.at(self.z + 1 - 2 * lax.rem(self.z, 2), self.x, self.y, self.core)

    def partner(self):
        return self.at(self.z, self.x, self.y, 1 - self.core)

    def over_x(self):
        return self.at(self.z, 1 - self.x, self.y, self.core)

    def over_y(self):
        return self.at(self.z, self.x, 1 - self.y, self.core)

    def up(self):
        return self.at(self.z + 1, self.x, self.y, self.core)

    def down(self):
        return self.at(self.z - 1, self.x, self.y, self.core)

    def peer(self, offset):
        other = lax.rem(self.me + offset, self.groups)
        return (other // 2, lax.rem(other, 2) * 2 + self.core)

    def enter(self):
        barrier = pltpu.get_barrier_semaphore()
        pl.semaphore_signal(barrier, inc=1, device_id=self.partner(), device_id_type=MESH)

        def greet(offset, carry):
            pl.semaphore_signal(barrier, inc=1, device_id=self.peer(offset), device_id_type=MESH)
            return carry

        lax.fori_loop(1, self.groups, greet, 0)
        pl.semaphore_wait(barrier, self.groups)


class QuadPlace(Place):
    def __init__(self, depth):
        super().__init__(depth)
        self.parity = lax.rem(self.z, 2)
        self.z = self.z // 2

    def at(self, z, x, y, core):
        return ((2 * z + self.parity) * 2 + x, y * 2 + core)

    def enter(self):
        barrier = pltpu.get_barrier_semaphore()

        def greet(device):
            pl.semaphore_signal(barrier, inc=1, device_id=device, device_id_type=MESH)

        for device in (self.partner(), self.over_x(), self.over_y()):
            greet(device)
        above, below = self.z + 1 < self.depth, self.z >= 1
        pl.when(above)(functools.partial(greet, self.up()))
        pl.when(below)(functools.partial(greet, self.down()))
        met = 3 + above.astype(jnp.int32) + below.astype(jnp.int32)
        pl.semaphore_wait(barrier, met)


def remote(src, dst, send_sem, recv_sem, device):
    return pltpu.make_async_remote_copy(
        src_ref=src,
        dst_ref=dst,
        send_sem=send_sem,
        recv_sem=recv_sem,
        device_id=device,
        device_id_type=MESH,
    )


def when(cond, action):
    if cond is None:
        action()
    else:
        pl.when(cond)(action)


def cut(block, share):
    units = block // UNIT
    small = max(1, units // share)
    return (units - 2 * small) // 2 * UNIT, small * UNIT


def steps(depth, body, first=0):
    if depth <= 4:
        for step in range(first, depth):
            body(step)
    else:
        def looped(step, carry):
            body(step)
            return carry

        if first == 0:
            body(0)
        lax.fori_loop(max(first, 1), depth, looped, 0)


def tree_sems(depth):
    dma = pltpu.SemaphoreType.DMA
    return [
        dma((depth, 2)), dma((depth,)), dma((depth, 2, 4)), dma((depth, 4)),
        dma((depth,)), dma((depth,)), dma((depth, 2)), dma((depth, 2)),
        dma((depth,)), dma((depth,)), dma((depth, 2)), dma((depth, 2)),
        dma((6,)), dma((6,)),
    ]


def gather_bank(place, bank, block, sems, meanwhile=lambda: None):
    depth, z, x, y = place.depth, place.z, place.x, place.y
    large, small = cut(block, 9)
    (zab_s, zab_r, zcd_s, zcd_r, ax_s, ax_r, ay_s, ay_r, by_s, by_r, bx_s, bx_r, cd_s, cd_r) = sems

    def rows(zz, xx, yy, first, count):
        begin = ((zz * 2 + xx) * 2 + yy) * (block // UNIT) + first // UNIT
        return bank.at[pl.ds(begin, count // UNIT)]

    def move(zz, xx, yy, first, count, send_sem, recv_sem, device):
        ref = rows(zz, xx, yy, first, count)
        return remote(ref, ref, send_sem, recv_sem, device)

    start_b, start_c, start_d = large, 2 * large, 2 * large + small
    over_x, over_y, up, down = place.over_x(), place.over_y(), place.up(), place.down()

    def sides(step):
        out = [(z - step, z - step >= 0)]
        if not (isinstance(step, int) and step == 0):
            out.append((z + step, z + step < depth))
        return out

    def z_moves(step, kind):
        out = []
        low, high = z - step, z + step
        for level, cond, device, way in (
            (low, (low >= 0) & (z + 1 < depth), up, 0),
            (high, (high < depth) & (z >= 1), down, 1),
        ):
            if kind == "ab":
                out.append(
                    (cond, move(level, x, y, 0, 2 * large, zab_s.at[level, way], zab_r.at[level], device))
                )
            else:
                for xx in range(2):
                    for yy in range(2):
                        out.append(
                            (
                                cond,
                                move(
                                    level, xx, yy, start_c, 2 * small,
                                    zcd_s.at[level, way, xx * 2 + yy],
                                    zcd_r.at[level, xx * 2 + yy], device,
                                ),
                            )
                        )
        return out

    def ax(level):
        return move(level, x, y, 0, large, ax_s.at[level], ax_r.at[level], over_x)

    def by(level):
        return move(level, x, y, start_b, large, by_s.at[level], by_r.at[level], over_y)

    def ay(level, other):
        xx = 1 - x if other else x
        return move(level, xx, y, 0, large, ay_s.at[level, other], ay_r.at[level, other], over_y)

    def bx(level, other):
        yy = 1 - y if other else y
        return move(level, x, yy, start_b, large, bx_s.at[level, other], bx_r.at[level, other], over_x)

    plane = [
        move(z, x, y, start_c, small, cd_s.at[0], cd_r.at[0], over_x),
        move(z, x, y, start_d, small, cd_s.at[1], cd_r.at[1], over_y),
        move(z, x, y, start_c, small, cd_s.at[2], cd_r.at[2], over_y),
        move(z, 1 - x, y, start_c, small, cd_s.at[3], cd_r.at[3], over_y),
        move(z, x, y, start_d, small, cd_s.at[4], cd_r.at[4], over_x),
        move(z, x, 1 - y, start_d, small, cd_s.at[5], cd_r.at[5], over_x),
    ]

    def run(step):
        if isinstance(step, int) and step == 0:
            plane[0].start()
            plane[1].start()
        else:
            for level, cond in sides(step):
                when(cond, move(level, x, y, 0, 2 * large, zab_s.at[level, 0], zab_r.at[level], up).wait_recv)
        for cond, copy in z_moves(step, "ab"):
            when(cond, copy.start)
        for level, cond in sides(step):
            def begin(level=level):
                ax(level).start()
                by(level).start()
                ay(level, 0).start()
                bx(level, 0).start()

            when(cond, begin)
        if isinstance(step, int) and step == 0:
            meanwhile()
            plane[2].start()
            plane[4].start()
            plane[0].wait_recv()
            plane[3].start()
            plane[1].wait_recv()
            plane[5].start()
            for copy in plane[2:]:
                copy.wait_recv()
            for cond, copy in z_moves(0, "cd"):
                when(cond, copy.start)
        for level, cond in sides(step):
            def across(level=level):
                ax(level).wait_recv()
                ay(level, 1).start()
                by(level).wait_recv()
                bx(level, 1).start()

            when(cond, across)
        if not (isinstance(step, int) and step == 0):
            for level, cond in sides(step):
                def arrived(level=level):
                    for part in range(4):
                        move(
                            level, x, y, start_c, 2 * small, zcd_s.at[level, 0, part],
                            zcd_r.at[level, part], up,
                        ).wait_recv()

                when(cond, arrived)
            for cond, copy in z_moves(step, "cd"):
                when(cond, copy.start)

    steps(depth, run)

    def drain(step):
        for level, cond in sides(step):
            def finish(level=level):
                for other in range(2):
                    ay(level, other).wait_recv()
                    bx(level, other).wait_recv()
                    ay(level, other).wait_send()
                    bx(level, other).wait_send()
                ax(level).wait_send()
                by(level).wait_send()

            when(cond, finish)
        for kind in ("ab", "cd"):
            for cond, copy in z_moves(step, kind):
                when(cond, copy.wait_send)

    steps(depth, drain)
    for copy in plane:
        copy.wait_send()


def strips(rows, body, carry=0):
    strip = 64

    def one(index, carry):
        return body(pl.ds(pl.multiple_of(index * strip, strip), strip), carry)

    return lax.fori_loop(0, rows // strip, one, carry)


def fold(values):
    return jnp.sum(values.reshape(-1, 8, values.shape[1]), axis=0)


def chain_kernel(
    depth, block,
    slot_ref, length_ref, master, own_x, own_dense, own_cot, gain_ref, shift_ref,
    act_out, dcv_out, res_out, blk_out, ig_out, dg_out, nrm_out,
    bank, act, dense, mask, cot, raw, side, pre4, slope, upown, upsend, uprecv, dcv, dsd, res, dgrecv,
    igrecv, stage, nrm, blk, blksend, keep, ex_side, ex_last, ex_sub,
    load_sem, swap_s, swap_r, act_s, act_r, up_s, up_r, ex_s, ex_r, out_sem, far_s, far_r, near_s, near_r,
    *tree,
):
    place = Place(depth)
    core, other = place.core, 1 - place.core
    partner, beside = place.partner(), place.beside()
    half = bank.shape[2]
    width = 2 * half
    frames = mask.shape[1]
    rows = 2 * frames
    peers = place.groups - 1
    chunks = dense.shape[0]
    pieces = source_pieces(half)
    inner = pl.ds(EDGE, frames)
    own_rows = block // 2
    load_rows = min(own_rows, rows)
    loads_of = own_rows // load_rows

    mats_in = []
    for part in range(loads_of):
        for h in range(2):
            mats_in.append(
                pltpu.make_async_copy(
                    master.at[pl.ds(part * load_rows, load_rows), pl.ds(h * half, half)],
                    side.at[part * 2 + h, pl.ds(0, load_rows)],
                    load_sem.at[part * 2 + h],
                )
            )
    x_in = [
        pltpu.make_async_copy(
            own_x.at[0, :, pl.ds(h * half, half)], act.at[0, h, core, inner], load_sem.at[6 + h]
        )
        for h in range(2)
    ]
    dense_in = [
        pltpu.make_async_copy(
            own_dense.at[0, :, pl.ds(chunk * half, half)], dense.at[chunk, core], load_sem.at[8 + chunk]
        )
        for chunk in range(chunks)
    ]
    ours_lanes = pl.ds(pl.multiple_of(core * half, half), half)
    theirs_lanes = pl.ds(pl.multiple_of(other * half, half), half)
    cot_in = pltpu.make_async_copy(own_cot.at[0, :, ours_lanes], cot.at[core], load_sem.at[8 + chunks])
    for copy in mats_in + x_in + dense_in + [cot_in]:
        copy.start()
    place.enter()
    base = place.me * (block // UNIT) + core * (own_rows // UNIT)
    units = load_rows // UNIT
    for copy in mats_in:
        copy.wait()
    for part in range(loads_of):
        def narrow(unit, carry, part=part):
            at = pl.ds(pl.multiple_of(unit * UNIT, UNIT), UNIT)
            stage[part * units + unit] = side[part * 2 + other, at].astype(BF16)
            bank[base + part * units + unit] = side[part * 2 + core, at].astype(BF16)
            return carry

        lax.fori_loop(0, units, narrow, 0)
    send_mats = remote(stage, bank.at[pl.ds(base, own_rows // UNIT)], swap_s.at[0], swap_r.at[0], partner)
    send_mats.start()
    mask[core] = (
        lax.broadcasted_iota(jnp.int32, (frames, 128), 0) < length_ref[0]
    ).astype(F32)
    edge_zero = jnp.zeros((EDGE, half), BF16)

    def clear(section, carry):
        for u in range(2):
            for h in range(2):
                act[section, h, u, pl.ds(0, EDGE)] = edge_zero
                act[section, h, u, pl.ds(EDGE + frames, EDGE)] = edge_zero
            dcv[section, u, pl.ds(0, EDGE)] = edge_zero
            dcv[section, u, pl.ds(EDGE + frames, EDGE)] = edge_zero
        return carry

    lax.fori_loop(0, SUBS, clear, 0)
    send_mats.wait()

    def prepare():
        for copy in x_in + dense_in + [cot_in]:
            copy.wait()
        low_mask = jnp.concatenate([mask[core].astype(BF16)] * (half // 128), axis=1)
        for h in range(2):
            act[0, h, core, inner] = act[0, h, core, inner] * low_mask
        for chunk in range(chunks):
            dense[chunk, core] = dense[chunk, core] * low_mask
        own = act.at[0, :, core, inner]
        swaps = [
            remote(own, own, swap_s.at[1], swap_r.at[1], partner),
            remote(dense.at[:, core], dense.at[:, core], swap_s.at[2], swap_r.at[2], partner),
            remote(mask.at[core], mask.at[core], swap_s.at[3], swap_r.at[3], partner),
            remote(own_cot.at[0, :, theirs_lanes], cot.at[core], swap_s.at[4], swap_r.at[4], partner),
        ]
        for copy in swaps:
            copy.start()
        return swaps

    swaps = []
    gather_bank(place, bank, block, tree, lambda: swaps.extend(prepare()))
    for copy in swaps:
        copy.wait()

    outs = []

    def put(src, dst):
        copy = pltpu.make_async_copy(src, dst, out_sem.at[len(outs)])
        copy.start()
        outs.append(copy)

    def far_act(section):
        return remote(
            act.at[section, core, :, inner], act_out.at[section, 1, core],
            far_s.at[section], far_r.at[section], beside,
        )

    def near_act(section):
        ref = act_out.at[section, 1, core]
        return remote(ref, ref, near_s.at[section], near_r.at[section], partner)

    def far_dcv(section):
        return remote(
            dcv.at[section], dcv_out.at[section, 1],
            far_s.at[SUBS + section], far_r.at[SUBS + section], beside,
        )

    def far_res(index):
        return remote(
            res.at[index], res_out.at[1, index],
            far_s.at[2 * SUBS + index], far_r.at[2 * SUBS + index], beside,
        )

    far_act(0).start()

    def weight(matrix, first, count):
        begin = slot_ref[matrix] * (width // UNIT) + first // UNIT
        return jnp.concatenate([bank[begin + i] for i in range(count // UNIT)], axis=0)

    def valid(at):
        return jnp.concatenate([mask_rows(at)] * (half // 128), axis=1)

    def mask_rows(at):
        return mask[at.start // frames, pl.ds(pl.multiple_of(lax.rem(at.start, frames), 64), at.size)]

    def gain(index):
        return gain_ref[pl.ds(index, 1), ours_lanes]

    def bias(index):
        return shift_ref[pl.ds(index, 1), ours_lanes]

    def share(buffer, index, values):
        buffer[place.me] = values

        def go(offset, carry):
            remote(
                buffer.at[place.me], buffer.at[place.me], ex_s.at[index], ex_r.at[index],
                place.peer(offset),
            ).start()
            return carry

        lax.fori_loop(1, place.groups, go, 0, unroll=place.groups <= 16)

    def shared(buffer, index):
        everyone = buffer.at[pl.ds(0, peers)]
        copy = remote(everyone, everyone, ex_s.at[index], ex_r.at[index], place.peer(1))
        copy.wait_recv()
        copy.wait_send()
        return buffer[...]

    def total_of(values):
        return jnp.sum(values, axis=0, keepdims=True)

    def counted():
        def add(at, carry):
            return carry + fold(valid(at))

        return total_of(strips(rows, add, jnp.zeros((8, half), F32)))

    def moments(load, count):
        pivot = load(pl.ds(0, 8))[0:1]

        def add(at, carry):
            first, second = carry
            valid_now = valid(at)
            off = (load(at) - pivot) * valid_now
            return first + fold(off), second + fold(off * off)

        zero = jnp.zeros((8, half), F32)
        first, second = strips(rows, add, (zero, zero))
        first, second = total_of(first), total_of(second)
        return first + count * pivot, jnp.maximum(second - first * first / count, 0.0)

    def merge(count, total, squares):
        frame_total = jnp.sum(count, axis=0)
        mean = jnp.sum(total, axis=0) / frame_total
        shift = total / count - mean[None]
        variance = jnp.sum(squares + count * shift * shift, axis=0) / frame_total
        return mean[None], lax.rsqrt(variance + norm_eps)[None], frame_total[None]

    def save(index, mean, inverse):
        scale = gain(index) * inverse
        keep[0, pl.ds(index, 1)] = inverse
        keep[1, pl.ds(index, 1)] = mean * inverse
        keep[2, pl.ds(index, 1)] = scale
        keep[3, pl.ds(index, 1)] = bias(index) - mean * scale

    def kept(row, index):
        return keep[row, pl.ds(index, 1)]

    count = counted()
    totals, squares = [], []
    for index in range(SOURCES):
        value = None
        if index < SOURCES - 1:
            for chunk, lane, lanes in pieces[index]:
                left = dense[chunk].reshape(rows, half)[:, lane : lane + lanes]
                right = weight(SUBS * K + chunk // 2, (chunk % 2) * half + lane, lanes)
                term = jnp.dot(left, right, preferred_element_type=F32)
                value = term if value is None else value + term
        else:
            for h in range(2):
                left = jnp.concatenate([act[0, h, u, inner] for u in range(2)], axis=0)
                term = jnp.dot(left, weight(SUBS * K + 3, h * half, half), preferred_element_type=F32)
                value = term if value is None else value + term
        side[index] = value
        total, square = moments(lambda at, index=index: side[index, at], count)
        totals.append(total)
        squares.append(square)
    fill = jnp.zeros((3, half), F32)
    share(ex_side, 0, jnp.concatenate([count] + totals + squares + [fill], axis=0))

    def convolve(section, h, first):
        value = None
        for k in range(K):
            left = jnp.concatenate(
                [act[section, h, u, pl.ds(EDGE - MARGIN + k, frames)] for u in range(2)], axis=0
            )
            term = jnp.dot(
                left, weight(section * K + k, h * half, half), preferred_element_type=F32
            )
            value = term if value is None else value + term
            if k % 2 == 1 or k == K - 1:
                if first and k == 1:
                    raw[section] = value
                else:
                    raw[section] += value
                value = None

    def swap_act(section):
        own = act.at[section, core, :, inner]
        return remote(own, own, act_s.at[section], act_r.at[section], partner)

    def forward(section, last):
        convolve(section, core, True)
        if isinstance(section, int):
            if section > 0:
                swap_act(section).wait_recv()
        else:
            pl.when(section > 0)(swap_act(section).wait_recv)
        convolve(section, other, False)
        total, square = moments(lambda at: raw[section, at], count)
        buffer = ex_sub.at[lax.rem(section, 2)]
        share(buffer, 1 + section, jnp.concatenate([count, total, square, jnp.zeros_like(count)], axis=0))
        parts = shared(buffer, 1 + section)
        mean, inverse, frame_total = merge(parts[:, 0], parts[:, 1], parts[:, 2])
        save(section, mean, inverse)
        scale, offset = kept(2, section), kept(3, section)

        def activate(at, carry):
            before = raw[section, at] * scale + offset
            if last:
                before = before + pre4[at]
                pre4[at] = before
            hidden = (before * jax.nn.sigmoid(before) * valid(at)).astype(BF16)
            u = at.start // frames
            first = pl.multiple_of(lax.rem(at.start, frames), 64)
            if last:
                @pl.when(u == core)
                def _():
                    blk[core, pl.ds(first, at.size)] = hidden

                @pl.when(u != core)
                def _():
                    blksend[pl.ds(first, at.size)] = hidden
            else:
                act[section + 1, core, u, pl.ds(pl.multiple_of(first + EDGE, EDGE), at.size)] = hidden
            return carry

        strips(rows, activate)
        if not last:
            swap_act(section + 1).start()
            far_act(section + 1).start()
            far_act(section).wait_recv()
            near_act(section).start()
        return frame_total

    def looped(section, carry):
        forward(section, False)

        @pl.when(section == 0)
        def _():
            parts = shared(ex_side, 0)
            for index in range(SOURCES):
                mean, inverse, _ = merge(
                    parts[:, 0], parts[:, 1 + index], parts[:, 1 + SOURCES + index]
                )
                save(SUBS + index, mean, inverse)
            scales = [kept(2, SUBS + index) for index in range(SOURCES)]
            offset = sum(kept(3, SUBS + index) for index in range(SOURCES))

            def add(at, carry):
                before = offset
                for index in range(SOURCES):
                    before = before + side[index, at] * scales[index]
                pre4[at] = before
                return carry

            strips(rows, add)

        return carry

    lax.fori_loop(0, SUBS - 1, looped, 0)
    frame_total = forward(SUBS - 1, True)
    blk_copy = remote(blksend, blk.at[core], swap_s.at[5], swap_r.at[5], partner)
    blk_copy.start()
    for section in range(1, SUBS):
        swap_act(section).wait_send()
    for h in range(2):
        put(act.at[:, h, :, inner], act_out.at[:, 0, h])
    far_act(SUBS - 1).wait_recv()
    near_act(SUBS - 1).start()

    def hat_of(values, index):
        return values * kept(0, index) - kept(1, index)

    def back_half(section, h):
        total = None
        value = None
        for k in range(K):
            left = jnp.concatenate(
                [dcv[section, u, pl.ds(EDGE + MARGIN - k, frames)] for u in range(2)], axis=0
            )
            term = lax.dot_general(
                left, weight(section * K + k, h * half, half), NT, preferred_element_type=F32
            )
            value = term if value is None else value + term
            if k % 2 == 1 or k == K - 1:
                total = value if total is None else total + value
                value = None
        return total

    def up_copy(section):
        slot = lax.rem(section, 2)
        return remote(upsend, uprecv.at[slot], up_s.at[slot], up_r.at[slot], partner)

    def backward(section):
        upsend[...] = back_half(section, other)
        up_copy(section).start()
        upown[...] = back_half(section, core)

    def slopes(section, upstream, before_of, others):
        sources = [(lambda at: raw[section, at], section)] + others

        def one(at, carry):
            before = before_of(at)
            sigmoid = jax.nn.sigmoid(before)
            now = upstream(at) * valid(at) * (sigmoid * (1.0 + before * (1.0 - sigmoid)))
            slope[at] = now
            out = [carry[0] + fold(now)]
            for (load, index), so_far in zip(sources, carry[1:]):
                out.append(so_far + fold(now * hat_of(load(at), index)))
            return tuple(out)

        zero = jnp.zeros((8, half), F32)
        return [total_of(value) for value in strips(rows, one, (zero,) * (1 + len(sources)))]

    def branch(load, index, shift_sum, gain_sum, store):
        scale = kept(2, index)
        shift_mean, gain_mean = shift_sum / frame_total, gain_sum / frame_total

        def one(at, carry):
            value = slope[at] - shift_mean - hat_of(load(at), index) * gain_mean
            store(at, (valid(at) * scale * value).astype(BF16))
            return carry

        strips(rows, one)

    def conv_branch(section, shift_sum, gain_sum):
        def store(at, value):
            first = pl.multiple_of(lax.rem(at.start, frames) + EDGE, EDGE)
            dcv[section, at.start // frames, pl.ds(first, at.size)] = value

        branch(lambda at: raw[section, at], section, shift_sum, gain_sum, store)
        far_dcv(section).start()

    def cot_at(at):
        return cot[
            at.start // frames, pl.ds(pl.multiple_of(lax.rem(at.start, frames), 64), at.size)
        ].astype(F32)

    sums = slopes(
        SUBS - 1, cot_at, lambda at: pre4[at],
        [(lambda at, index=index: side[index, at], SUBS + index) for index in range(SOURCES)],
    )
    share(ex_last, SUBS + 1, jnp.concatenate(sums, axis=0))
    sums = jnp.sum(shared(ex_last, SUBS + 1), axis=0)
    shift_sum = sums[0:1]
    conv_branch(SUBS - 1, shift_sum, sums[1:2])
    nrm[core] = jnp.zeros_like(nrm[0])
    nrm[core, pl.ds(SUBS - 1, 1 + SOURCES)] = sums[1:]
    nrm[core, pl.ds(SUBS + SOURCES + SUBS - 1, 1)] = shift_sum
    backward(SUBS - 1)
    for index in range(SOURCES):
        def store(at, value, index=index):
            dsd[index, at] = value

        branch(
            lambda at, index=index: side[index, at], SUBS + index, shift_sum,
            sums[2 + index : 3 + index], store,
        )
    theirs = pl.multiple_of(other * frames, frames)
    ours = pl.multiple_of(core * frames, frames)
    dg_copy = remote(
        side.at[:, pl.ds(theirs, frames)], dgrecv, swap_s.at[6], swap_r.at[6], partner
    )

    def dense_grads():
        for index in range(SOURCES - 1):
            for chunk, lane, lanes in pieces[index]:
                right = weight(SUBS * K + chunk // 2, (chunk % 2) * half + lane, lanes)
                side[chunk, :, pl.ds(lane, lanes)] = lax.dot_general(
                    dsd[index], right, NT, preferred_element_type=F32
                )
        dg_copy.start()

    def residual_grads():
        rows_of = [[] for _ in range(chunks)]
        for index, parts in enumerate(pieces):
            for chunk, lane, lanes in parts:
                rows_of[chunk].append((lane, lanes, index))
        for chunk in range(chunks):
            turned = dense[chunk].reshape(rows, half).T
            for lane, lanes, index in rows_of[chunk]:
                res[chunk // 2, pl.ds((chunk % 2) * half + lane, lanes)] = jnp.dot(
                    turned[lane : lane + lanes], dsd[index], preferred_element_type=F32
                ).astype(BF16)
        for h in range(2):
            turned = jnp.concatenate([act[0, h, u, inner] for u in range(2)], axis=0).T
            res[3, pl.ds(h * half, half)] = jnp.dot(
                turned, dsd[SOURCES - 1], preferred_element_type=F32
            ).astype(BF16)

    def looped_back(turn, carry):
        section = SUBS - 2 - turn
        copy = up_copy(section + 1)
        copy.wait()
        slot = lax.rem(section + 1, 2)
        scale, offset = kept(2, section), kept(3, section)
        sums = slopes(
            section, lambda at: upown[at] + uprecv[slot, at],
            lambda at: raw[section, at] * scale + offset, [],
        )
        zero = jnp.zeros((2, half), F32)
        buffer = ex_sub.at[lax.rem(section, 2)]
        share(buffer, SUBS + 2 + section, jnp.concatenate(sums + [zero], axis=0))

        @pl.when(section == SUBS - 2)
        def _():
            residual_grads()
            dense_grads()

        sums = jnp.sum(shared(buffer, SUBS + 2 + section), axis=0)
        far_res(turn).start()
        conv_branch(section, sums[0:1], sums[1:2])
        nrm[core, pl.ds(section, 1)] = sums[1:2]
        nrm[core, pl.ds(SUBS + SOURCES + section, 1)] = sums[0:1]

        @pl.when(section > 0)
        def _():
            backward(section)

        return carry

    lax.fori_loop(0, SUBS - 1, looped_back, 0)
    put(dcv, dcv_out.at[:, 0])
    put(res, res_out.at[0])
    nrm_copy = remote(nrm.at[core], nrm.at[core], swap_s.at[7], swap_r.at[7], partner)
    nrm_copy.start()
    for h in range(2):
        uprecv[h] = back_half(0, h) + lax.dot_general(
            dsd[SOURCES - 1], weight(SUBS * K + 3, h * half, half), NT, preferred_element_type=F32
        )
    ig_copy = remote(
        uprecv.at[:, pl.ds(theirs, frames)], igrecv, swap_s.at[8], swap_r.at[8], partner
    )
    ig_copy.start()
    own_valid = jnp.concatenate([mask[core]] * (half // 128), axis=1)
    dg_copy.wait()
    for chunk in range(chunks):
        dgrecv[chunk] = (dgrecv[chunk] + side[chunk, pl.ds(ours, frames)]) * own_valid
        put(dgrecv.at[chunk], dg_out.at[0, :, pl.ds(chunk * half, half)])
    blk_copy.wait()
    nrm_copy.wait()
    put(nrm, nrm_out)
    ig_copy.wait()
    for h in range(2):
        igrecv[h] = (igrecv[h] + uprecv[h, pl.ds(ours, frames)]) * own_valid
        put(igrecv.at[h], ig_out.at[0, :, pl.ds(h * half, half)])
        put(blk.at[h], blk_out.at[0, :, pl.ds(h * half, half)])
    for section in range(SUBS):
        near_act(section).wait()
        far_act(section).wait_send()
        far_dcv(section).wait()
    for index in range(4):
        far_res(index).wait()
    for copy in outs:
        copy.wait()


def run_chain(depth, block, places, lengths, master, x, dense, cot, gains, shifts):
    frames, width = x.shape[1:]
    half = width // 2
    rows = 2 * frames
    chunks = dense.shape[2] // half
    padded = frames + 2 * EDGE
    groups = depth * 4
    dma = pltpu.SemaphoreType.DMA
    anywhere = pl.BlockSpec(memory_space=pl.ANY)
    vmem = pl.BlockSpec(memory_space=pltpu.VMEM)
    smem = pl.BlockSpec(memory_space=pltpu.SMEM)
    out_shape = [
        jax.ShapeDtypeStruct((SUBS, 2, 2, 2, frames, half), BF16),
        jax.ShapeDtypeStruct((SUBS, 2, 2, padded, half), BF16),
        jax.ShapeDtypeStruct((2, 4, width, half), BF16),
        jax.ShapeDtypeStruct(x.shape, BF16),
        jax.ShapeDtypeStruct(x.shape, F32),
        jax.ShapeDtypeStruct(dense.shape, F32),
        jax.ShapeDtypeStruct((2, 16, half), F32),
    ]
    scratch = [
        pltpu.VMEM((groups * block // UNIT, UNIT, half), BF16),
        pltpu.VMEM((SUBS, 2, 2, padded, half), BF16),
        pltpu.VMEM((chunks, 2, frames, half), BF16),
        pltpu.VMEM((2, frames, 128), F32),
        pltpu.VMEM((2, frames, half), BF16),
        pltpu.VMEM((SUBS, rows, half), F32),
        pltpu.VMEM((SOURCES, rows, half), F32),
        pltpu.VMEM((rows, half), F32),
        pltpu.VMEM((rows, half), F32),
        pltpu.VMEM((rows, half), F32),
        pltpu.VMEM((rows, half), F32),
        pltpu.VMEM((2, rows, half), F32),
        pltpu.VMEM((SUBS, 2, padded, half), BF16),
        pltpu.VMEM((SOURCES, rows, half), BF16),
        pltpu.VMEM((4, width, half), BF16),
        pltpu.VMEM((chunks, frames, half), F32),
        pltpu.VMEM((2, frames, half), F32),
        pltpu.VMEM((block // 2 // UNIT, UNIT, half), BF16),
        pltpu.VMEM((2, 16, half), F32),
        pltpu.VMEM((2, frames, half), BF16),
        pltpu.VMEM((frames, half), BF16),
        pltpu.VMEM((4, 16, half), F32),
        pltpu.VMEM((groups, 16, half), F32),
        pltpu.VMEM((groups, 8, half), F32),
        pltpu.VMEM((2, groups, 4, half), F32),
        dma((9 + chunks,)),
        dma((9,)), dma((9,)),
        dma((SUBS,)), dma((SUBS,)),
        dma((2,)), dma((2,)),
        dma((2 * SUBS + 1,)), dma((2 * SUBS + 1,)),
        dma((10 + chunks,)),
        dma((2 * SUBS + 4,)), dma((2 * SUBS + 4,)),
        dma((SUBS,)), dma((SUBS,)),
    ] + tree_sems(depth)
    return pl.pallas_call(
        functools.partial(chain_kernel, depth, block),
        out_shape=out_shape,
        in_specs=[smem] * 2 + [anywhere] * 4 + [vmem] * 2,
        out_specs=[anywhere] * len(out_shape),
        scratch_shapes=scratch,
        compiler_params=pltpu.CompilerParams(
            collective_id=1, has_side_effects=True, vmem_limit_bytes=63 << 20
        ),
        cost_estimate=pl.CostEstimate(
            flops=4 * SUBS * K * rows * width * half, bytes_accessed=16 << 20, transcendentals=0
        ),
        name="chain",
    )(places, lengths, master, x, dense, cot, gains, shifts)


def grad_kernel(slot_ref, act_ref, dcv_ref, res_ref, out_ref, left, stage, count, sems):
    section = pl.program_id(0)
    half = act_ref.shape[5]
    width = 2 * half
    frames = act_ref.shape[4]
    rows = 2 * frames
    ring = stage.shape[0]
    for pair in range(2):
        for h in range(2):
            left[pl.ds(h * half, half), pl.ds(pair * rows, rows)] = (
                act_ref[0, pair, h].reshape(rows, half).T
            )

    @pl.when(section == 0)
    def _():
        count[0] = 0

    def slot_copy(place, slot):
        out = out_ref.at[pl.ds(pl.multiple_of(slot * width, 16), width)]
        return pltpu.make_async_copy(stage.at[place], out, sems.at[place])

    def emit(matrix, compute):
        slot = slot_ref[matrix]

        @pl.when(slot >= 0)
        def _():
            turn = count[0]
            place = lax.rem(turn, ring)
            pl.when(turn >= ring)(slot_copy(place, 0).wait)
            stage[place] = compute().astype(BF16)
            slot_copy(place, slot).start()
            count[0] = turn + 1

    for k in range(K):
        def conv(k=k):
            right = jnp.concatenate(
                [
                    dcv_ref[0, pair, u, pl.ds(EDGE + MARGIN - k, frames)]
                    for pair in range(2)
                    for u in range(2)
                ],
                axis=0,
            )
            return jnp.dot(left[...], right, preferred_element_type=F32)

        emit(section * K + k, conv)

    @pl.when(section == SUBS - 1)
    def _():
        for index in range(4):
            emit(
                SUBS * K + index,
                lambda index=index: res_ref[0, index].astype(F32) + res_ref[1, index].astype(F32),
            )
        turns = count[0]

        def finish(place, carry):
            pl.when(place < turns)(slot_copy(place, 0).wait)
            return carry

        lax.fori_loop(0, ring, finish, 0)


def run_grads(total_rows, places, act, dcv, res):
    half = act.shape[5]
    frames = act.shape[4]
    ring = 8
    grid_spec = pltpu.PrefetchScalarGridSpec(
        num_scalar_prefetch=1,
        grid=(SUBS,),
        in_specs=[
            pl.BlockSpec((1,) + act.shape[1:], lambda s, t: (s, 0, 0, 0, 0, 0)),
            pl.BlockSpec((1,) + dcv.shape[1:], lambda s, t: (s, 0, 0, 0, 0)),
            pl.BlockSpec(res.shape, lambda s, t: (0, 0, 0, 0)),
        ],
        out_specs=pl.BlockSpec(memory_space=pl.ANY),
        scratch_shapes=[
            pltpu.VMEM((2 * half, 4 * frames), BF16),
            pltpu.VMEM((ring, 2 * half, half), BF16),
            pltpu.SMEM((1,), jnp.int32),
            pltpu.SemaphoreType.DMA((ring,)),
        ],
    )
    return pl.pallas_call(
        grad_kernel,
        grid_spec=grid_spec,
        out_shape=jax.ShapeDtypeStruct((total_rows, half), BF16),
        compiler_params=pltpu.CompilerParams(vmem_limit_bytes=60 << 20),
        name="weight_grads",
    )(places, act, dcv, res)


def reduce_kernel(
    depth, block, grads, out, l_ay, l_ax, l_bx, l_by, l_zab, l_zcd, l_c, l_d, stage, final, result,
    stage_sem, out_sem, swap_s, swap_r, ay_s, ay_r, ax_s, ax_r, bx_s, bx_r, by_s, by_r,
    zab_s, zab_r, zcd_s, zcd_r, cd_s, cd_r,
):
    place = QuadPlace(depth)
    z, x, y, core = place.z, place.x, place.y, place.core
    large, small = cut(block, 16)
    start_b, start_c, start_d = large, 2 * large, 2 * large + small
    over_x, over_y, up, down = place.over_x(), place.over_y(), place.up(), place.down()
    place.enter()

    def rows(zz, xx, yy, first, count):
        begin = pl.multiple_of(((zz * 2 + xx) * 2 + yy) * block + first, 16)
        return grads.at[pl.ds(begin, count)]

    def ay(level, other_x):
        xx = 1 - x if other_x else x
        return remote(
            rows(level, xx, 1 - y, 0, large), l_ay.at[level, other_x],
            ay_s.at[level, other_x], ay_r.at[level, other_x], over_y,
        )

    def bx(level, other_y):
        yy = 1 - y if other_y else y
        return remote(
            rows(level, 1 - x, yy, start_b, large), l_bx.at[level, other_y],
            bx_s.at[level, other_y], bx_r.at[level, other_y], over_x,
        )

    def ax(level):
        return remote(l_ay.at[level, 1], l_ax.at[level], ax_s.at[level], ax_r.at[level], over_x)

    def by(level):
        return remote(l_bx.at[level, 1], l_by.at[level], by_s.at[level], by_r.at[level], over_y)

    def fetch(refs):
        copies = []
        first = 0
        for index, ref in enumerate(refs):
            copy = pltpu.make_async_copy(
                ref, stage.at[pl.ds(first, ref.shape[0])], stage_sem.at[index]
            )
            copy.start()
            copies.append(copy)
            first += ref.shape[0]
        return copies

    def add(target, first, count, others, keep=None):
        strip = count
        while strip > 192 or count % strip:
            strip -= 16

        def one(index, carry):
            at = pl.ds(pl.multiple_of(index * strip, 16), strip)
            value = stage[pl.ds(pl.multiple_of(first + index * strip, 16), strip)].astype(F32)
            for ref in [target] + others:
                value = value + ref[at].astype(F32)
            if keep is None:
                target[at] = value.astype(BF16)
            else:
                keep[at] = value
            return carry

        lax.fori_loop(0, count // strip, one, 0)

    def sides(step):
        out = [(z - step, z - step >= 0)]
        if not (isinstance(step, int) and step == 0):
            out.append((z + step, z + step < depth))
        return out

    def backwards(body, first, last):
        if depth <= 4:
            for step in range(first, last - 1, -1):
                body(step)
        else:
            def looped(turn, carry):
                body(first - turn)
                return carry

            lax.fori_loop(0, first - last + 1, looped, 0)

    def leaves(step):
        for level, cond in sides(step):
            def go(level=level):
                for other in (1, 0):
                    ay(level, other).start()
                    bx(level, other).start()

            when(cond, go)

    def zcd(level, way, part):
        device = down if way == 0 else up
        beyond = z + 1 < depth if way == 0 else z >= 1
        at_home = (z - 1 == level) if way == 0 else (z + 1 == level)
        entry = level if way == 0 else level + (depth - level) * at_home.astype(jnp.int32)
        dst = l_zcd.at[entry, part]
        src = rows(level, part // 2, part % 2, start_c, 2 * small)
        send_sem, recv_sem = zcd_s.at[level, part], zcd_r.at[entry, part]
        leaf = remote(src, dst, send_sem, recv_sem, device)
        node = remote(l_zcd.at[level, part], dst, send_sem, recv_sem, device)
        return beyond, leaf, node, src

    def plane_step(step):
        for way, level, cond in ((0, z - step, z - step >= 0), (1, z + step, z + step < depth)):
            def go(way=way, level=level):
                hops = [zcd(level, way, part) for part in range(4)]
                beyond = hops[0][0]

                @pl.when(beyond)
                def _():
                    copies = fetch([hop[3] for hop in hops])
                    for part, (_, leaf, node, src) in enumerate(hops):
                        remote(
                            l_zcd.at[level, part], l_zcd.at[level, part], zcd_s.at[level, part],
                            zcd_r.at[level, part], up,
                        ).wait_recv()
                        copies[part].wait()
                        add(l_zcd.at[level, part], part * 2 * small, 2 * small, [])
                        node.start()

                @pl.when(jnp.logical_not(beyond))
                def _():
                    for _, leaf, node, src in hops:
                        leaf.start()

            when(cond, go)

    def zab(level, way):
        device = down if way == 0 else up
        beyond = z + 1 < depth if way == 0 else z >= 1
        at_home = (z - 1 == level) if way == 0 else (z + 1 == level)
        entry = level if way == 0 else level + (depth - level) * at_home.astype(jnp.int32)
        copies = []
        for index, landing in enumerate((l_ax, l_by)):
            copies.append(
                remote(
                    landing.at[level], l_zab.at[entry, index], zab_s.at[level, index],
                    zab_r.at[entry, index], device,
                )
            )
        return beyond, copies

    def zab_arrived(entry, index):
        remote(
            l_zab.at[entry, index], l_zab.at[entry, index], zab_s.at[entry, index],
            zab_r.at[entry, index], up,
        ).wait_recv()

    def across(level):
        copies = fetch([rows(level, 1 - x, y, 0, large), rows(level, x, 1 - y, start_b, large)])
        ay(level, 1).wait_recv()
        copies[0].wait()
        add(l_ay.at[level, 1], 0, large, [])
        ax(level).start()
        bx(level, 1).wait_recv()
        copies[1].wait()
        add(l_bx.at[level, 1], large, large, [])
        by(level).start()

    def line_step(step):
        for way, level, cond in ((0, z - step, z - step >= 0), (1, z + step, z + step < depth)):
            def go(way=way, level=level):
                copies = fetch([rows(level, x, y, 0, 2 * large)])
                beyond, hops = zab(level, way)
                ay(level, 0).wait_recv()
                ax(level).wait_recv()
                copies[0].wait()

                @pl.when(beyond)
                def _():
                    zab_arrived(level, 0)
                    add(l_ax.at[level], 0, large, [l_ay.at[level, 0], l_zab.at[level, 0]])

                @pl.when(jnp.logical_not(beyond))
                def _():
                    add(l_ax.at[level], 0, large, [l_ay.at[level, 0]])

                hops[0].start()
                bx(level, 0).wait_recv()
                by(level).wait_recv()

                @pl.when(beyond)
                def _():
                    zab_arrived(level, 1)
                    add(l_by.at[level], large, large, [l_bx.at[level, 0], l_zab.at[level, 1]])

                @pl.when(jnp.logical_not(beyond))
                def _():
                    add(l_by.at[level], large, large, [l_bx.at[level, 0]])

                hops[1].start()

            when(cond, go)

    def both(step, action):
        for level, cond in sides(step):
            when(cond, functools.partial(action, level))

    def turn(step):
        leaves(step)
        plane_step(step)
        both(step, across)
        line_step(step)

    backwards(turn, depth - 1, 1)
    leaves(0)

    def home(entry, part, cond):
        def go():
            remote(
                l_zcd.at[entry, part], l_zcd.at[entry, part], zcd_s.at[0, part],
                zcd_r.at[entry, part], up,
            ).wait_recv()

        when(cond, go)

    above, below = z + 1 < depth, z >= 1
    copies = fetch([rows(z, part // 2, part % 2, start_c, 2 * small) for part in range(4)])
    for part in range(4):
        home(z, part, above)
        home(depth, part, below)
        copies[part].wait()

        @pl.when(above & below)
        def _(part=part):
            add(l_zcd.at[z, part], part * 2 * small, 2 * small, [l_zcd.at[depth, part]])

        @pl.when(above & jnp.logical_not(below))
        def _(part=part):
            add(l_zcd.at[z, part], part * 2 * small, 2 * small, [])

        @pl.when(jnp.logical_not(above))
        def _(part=part):
            strip = 2 * small
            value = stage[pl.ds(part * strip, strip)].astype(F32) + l_zcd[depth, part].astype(F32)
            l_zcd[z, part] = value.astype(BF16)

    def block_at(xx, yy, first):
        return l_zcd.at[z, xx * 2 + yy, pl.ds(first, small)]

    plane = [
        remote(block_at(1 - x, 1 - y, 0), l_c.at[1], cd_s.at[0], cd_r.at[0], over_y),
        remote(block_at(x, 1 - y, 0), l_c.at[0], cd_s.at[1], cd_r.at[1], over_y),
        remote(block_at(1 - x, 1 - y, small), l_d.at[1], cd_s.at[2], cd_r.at[2], over_x),
        remote(block_at(1 - x, y, small), l_d.at[0], cd_s.at[3], cd_r.at[3], over_x),
        remote(l_c.at[1], l_c.at[2], cd_s.at[4], cd_r.at[4], over_x),
        remote(l_d.at[1], l_d.at[2], cd_s.at[5], cd_r.at[5], over_y),
    ]
    for copy in plane[:4]:
        copy.start()
    both(0, across)
    plane[0].wait_recv()
    l_c[1] = (l_c[1].astype(F32) + l_zcd[z, (1 - x) * 2 + y, pl.ds(0, small)].astype(F32)).astype(BF16)
    plane[4].start()
    plane[2].wait_recv()
    l_d[1] = (l_d[1].astype(F32) + l_zcd[z, x * 2 + 1 - y, pl.ds(small, small)].astype(F32)).astype(BF16)
    plane[5].start()

    copies = fetch([rows(z, x, y, 0, 2 * large)])
    copies[0].wait()
    for index, (first_hop, second_hop, first_land, second_land, begin) in enumerate(
        ((ay, ax, l_ay, l_ax, 0), (bx, by, l_bx, l_by, start_b))
    ):
        first_hop(z, 0).wait_recv()
        second_hop(z).wait_recv()
        base = [second_land.at[z], first_land.at[z, 0]]
        target = final.at[pl.ds(begin, large)]

        @pl.when(above)
        def _(index=index):
            zab_arrived(z, index)

        @pl.when(below)
        def _(index=index):
            zab_arrived(depth, index)

        for cond, more in (
            (above & below, [z, depth]),
            (above & jnp.logical_not(below), [z]),
            (jnp.logical_not(above), [depth]),
        ):
            @pl.when(cond)
            def _(more=more, base=base, target=target, begin=begin, index=index):
                add(
                    base[0], begin, large,
                    base[1:] + [l_zab.at[entry, index] for entry in more], keep=target,
                )

    for copy in (plane[1], plane[3], plane[4], plane[5]):
        copy.wait_recv()
    here = x * 2 + y
    final[pl.ds(start_c, small)] = (
        l_zcd[z, here, pl.ds(0, small)].astype(F32) + l_c[0].astype(F32) + l_c[2].astype(F32)
    )
    final[pl.ds(start_d, small)] = (
        l_zcd[z, here, pl.ds(small, small)].astype(F32) + l_d[0].astype(F32) + l_d[2].astype(F32)
    )
    own_rows = block // 2
    theirs = final.at[pl.ds(pl.multiple_of((1 - core) * own_rows, 16), own_rows)]
    mine = final.at[pl.ds(pl.multiple_of(core * own_rows, 16), own_rows)]
    cross = remote(theirs, result, swap_s.at[0], swap_r.at[0], place.partner())
    cross.start()
    local = pltpu.make_async_copy(mine, out.at[core], out_sem.at[0])
    local.start()

    def drain(step):
        for level, cond in sides(step):
            def go(level=level):
                for other in range(2):
                    ay(level, other).wait_send()
                    bx(level, other).wait_send()
                ax(level).wait_send()
                by(level).wait_send()

            when(cond, go)
        if not (isinstance(step, int) and step == 0):
            for way, level, cond in ((0, z - step, z - step >= 0), (1, z + step, z + step < depth)):
                def go(way=way, level=level):
                    for part in range(4):
                        zcd(level, way, part)[2].wait_send()
                    for copy in zab(level, way)[1]:
                        copy.wait_send()

                when(cond, go)

    steps(depth, drain)
    for copy in plane:
        copy.wait_send()
    cross.wait()
    fetched = pltpu.make_async_copy(result, out.at[1 - core], out_sem.at[1])
    fetched.start()
    fetched.wait()
    local.wait()


def run_reduce(depth, block, grads):
    half = grads.shape[1]
    large, small = cut(block, 16)
    dma = pltpu.SemaphoreType.DMA
    anywhere = pl.BlockSpec(memory_space=pl.ANY)
    scratch = [
        pltpu.VMEM((depth, 2, large, half), BF16),
        pltpu.VMEM((depth, large, half), BF16),
        pltpu.VMEM((depth, 2, large, half), BF16),
        pltpu.VMEM((depth, large, half), BF16),
        pltpu.VMEM((depth + 1, 2, large, half), BF16),
        pltpu.VMEM((depth + 1, 4, 2 * small, half), BF16),
        pltpu.VMEM((3, small, half), BF16),
        pltpu.VMEM((3, small, half), BF16),
        pltpu.VMEM((max(2 * large, 8 * small), half), BF16),
        pltpu.VMEM((block, half), F32),
        pltpu.VMEM((block // 2, half), F32),
        dma((4,)), dma((2,)), dma((1,)), dma((1,)),
        dma((depth, 2)), dma((depth, 2)), dma((depth,)), dma((depth,)),
        dma((depth, 2)), dma((depth, 2)), dma((depth,)), dma((depth,)),
        dma((depth + 1, 2)), dma((depth + 1, 2)),
        dma((depth + 1, 4)), dma((depth + 1, 4)),
        dma((6,)), dma((6,)),
    ]
    return pl.pallas_call(
        functools.partial(reduce_kernel, depth, block),
        out_shape=jax.ShapeDtypeStruct((2, block // 2, half), F32),
        in_specs=[anywhere],
        out_specs=anywhere,
        scratch_shapes=scratch,
        compiler_params=pltpu.CompilerParams(
            collective_id=2, has_side_effects=True, vmem_limit_bytes=62 << 20
        ),
        name="reduce",
    )(grads)


def adamw(gradient, params, first_moment, second_moment, rate, decay):
    moment_new = beta_one * first_moment + (1.0 - beta_one) * gradient
    second_new = beta_two * second_moment + (1.0 - beta_two) * gradient * gradient
    direction = (
        moment_new
        / (1.0 - beta_one**STEP)
        / (jnp.sqrt(second_new / (1.0 - beta_two**STEP)) + adam_eps)
    )
    return (moment_new, second_new, params - rate * (direction + decay * params))


def update_kernel(
    filled_ref, sums_ref, master_ref, one_ref, two_ref, average_ref,
    grad_ref, one_out, two_out, new_ref, average_out, copy_ref,
):
    filled = filled_ref[pl.program_id(0)] > 0
    half = sums_ref.shape[2]
    strip = 32

    def one(index, carry):
        at = pl.ds(pl.multiple_of(index * strip, strip), strip)
        for h in range(2):
            lanes = pl.ds(h * half, half)
            gradient = jnp.where(filled, sums_ref[h, at], 0.0)
            master = master_ref[at, lanes]
            moment, second, new = adamw(
                gradient, master, one_ref[at, lanes], two_ref[at, lanes], rate_main, decay_main
            )
            grad_ref[at, lanes] = gradient
            one_out[at, lanes] = moment
            two_out[at, lanes] = second
            new_ref[at, lanes] = new
            average_out[at, lanes] = ema_keep * average_ref[at, lanes] + (1.0 - ema_keep) * new
            copy_ref[at, lanes] = new.astype(BF16)
        return carry

    lax.fori_loop(0, master_ref.shape[0] // strip, one, 0)


def run_update(filled, sums, master, moment_one, moment_two, average):
    rows, width = master.shape
    step = rows // filled.shape[0]
    spec = pl.BlockSpec((step, width), lambda i, t: (i, 0))
    grid_spec = pltpu.PrefetchScalarGridSpec(
        num_scalar_prefetch=1,
        grid=(rows // step,),
        in_specs=[pl.BlockSpec((2, step, sums.shape[2]), lambda i, t: (0, i, 0))] + [spec] * 4,
        out_specs=[spec] * 6,
    )
    full = jax.ShapeDtypeStruct(master.shape, F32)
    return pl.pallas_call(
        update_kernel,
        grid_spec=grid_spec,
        out_shape=[full] * 5 + [jax.ShapeDtypeStruct(master.shape, BF16)],
        compiler_params=pltpu.CompilerParams(vmem_limit_bytes=60 << 20),
        name="update",
    )(filled, sums, master, moment_one, moment_two, average)


def body(
    inputs,
    dense_inputs,
    lengths,
    owners,
    cotangent,
    master,
    moment_one,
    moment_two,
    average,
    norm_gain,
    norm_shift,
    norm_one,
    norm_two,
):
    width = inputs.shape[2]
    wides, narrows = lax.axis_size("wide"), lax.axis_size("narrow")
    depth = wides // 2
    own_rows = master.shape[0]
    block = 2 * own_rows
    capacity = own_rows * narrows // width
    places = slot_table(owners, capacity)
    act, dcv, res, block_out, input_grad, dense_grad, sums = run_chain(
        depth, block, places, lengths, master, inputs, dense_inputs, cotangent, norm_gain, norm_shift
    )
    owner = places // capacity
    compact = ((owner // 4) * 2 + owner % 2) * capacity + places % capacity
    parity = (lax.axis_index("wide") // 2) % 2
    handled = jnp.where((owner // 2) % 2 == parity, compact, -1).astype(jnp.int32)
    grads = run_grads(wides * narrows * own_rows // 2, handled, act, dcv, res)
    reduced = run_reduce(depth // 2, block, grads)

    step = min(own_rows, 256)
    first = (lax.axis_index("wide") * narrows + lax.axis_index("narrow")) * own_rows
    slot_of_step = (first + step * jnp.arange(own_rows // step, dtype=jnp.int32)) // width
    filled = jnp.any(places[None, :] == slot_of_step[:, None], axis=1).astype(jnp.int32)
    updated = run_update(filled, reduced, master, moment_one, moment_two, average)
    sums = sums.transpose(1, 0, 2).reshape(sums.shape[1], -1)
    branches = SUBS + SOURCES
    shift_rows = sums[branches : branches + SUBS]
    norm_grad = jnp.stack(
        [
            sums[:branches],
            jnp.concatenate([shift_rows] + [shift_rows[SUBS - 1 :]] * SOURCES, axis=0),
        ]
    )
    norm_params = jnp.stack([norm_gain, norm_shift])
    norm_one_new, norm_two_new, norm_new = adamw(
        norm_grad, norm_params, norm_one, norm_two, rate_norm, 0.0
    )
    return (
        block_out,
        input_grad,
        dense_grad,
        *updated,
        norm_grad,
        norm_one_new,
        norm_two_new,
        norm_new,
    )


def solution(mesh):
    rows = P(AXES, None)
    utterances = P(AXES, None, None)
    in_specs = (
        utterances, utterances, P(AXES), P(), utterances, rows, rows, rows, rows,
        P(), P(), P(), P(),
    )
    out_specs = (
        utterances, utterances, utterances, rows, rows, rows, rows, rows, rows,
        P(), P(), P(), P(),
    )
    return jax.shard_map(body, mesh=mesh, in_specs=in_specs, out_specs=out_specs, check_vma=False)
```

```python
import functools

import jax
import jax.numpy as jnp
from jax import lax
from jax.experimental import pallas as pl
from jax.experimental.pallas import tpu as pltpu
from jax.sharding import PartitionSpec as P

WLOW = 256
WMID = 384
K = 17
SUBS = 5
SOURCES = 6
STEP = 10
MARGIN = K // 2
EDGE = 16
UNIT = 64
F32 = jnp.float32
BF16 = jnp.bfloat16
MESH = pl.DeviceIdType.MESH
AXES = ("wide", "narrow")

norm_eps = 1e-05
beta_one = 0.9
beta_two = 0.999
adam_eps = 1e-08
rate_main = 0.02
rate_norm = 0.15
decay_main = 0.01
ema_keep = 0.8

NT = (((1,), (1,)), ((), ()))


def slot_table(owners, capacity):
    number = owners.shape[0]
    same_owner = owners[:, None] == owners[None, :]
    earlier = jnp.arange(number)[None, :] < jnp.arange(number)[:, None]
    ranking = jnp.sum(jnp.where(same_owner & earlier, 1, 0), axis=1)
    return (owners * capacity + ranking).astype(jnp.int32)


def source_pieces(half):
    pieces = []
    start = 0
    for width in (WLOW, WLOW, WLOW, WMID, WMID):
        parts = []
        stop = start + width
        while start < stop:
            chunk, lane = divmod(start, half)
            lanes = min(half - lane, stop - start)
            parts.append((chunk, lane, lanes))
            start += lanes
        pieces.append(parts)
    return pieces


class Place:
    def __init__(self, depth):
        wide = lax.axis_index("wide")
        narrow = lax.axis_index("narrow")
        self.depth = depth
        self.core = lax.rem(narrow, 2)
        self.y = narrow // 2
        self.x = lax.rem(wide, 2)
        self.z = wide // 2
        self.groups = depth * 4
        self.me = wide * 2 + self.y

    def at(self, z, x, y, core):
        return (z * 2 + x, y * 2 + core)

    def beside(self):
        return self.at(self.z + 1 - 2 * lax.rem(self.z, 2), self.x, self.y, self.core)

    def partner(self):
        return self.at(self.z, self.x, self.y, 1 - self.core)

    def over_x(self):
        return self.at(self.z, 1 - self.x, self.y, self.core)

    def over_y(self):
        return self.at(self.z, self.x, 1 - self.y, self.core)

    def up(self):
        return self.at(self.z + 1, self.x, self.y, self.core)

    def down(self):
        return self.at(self.z - 1, self.x, self.y, self.core)

    def peer(self, offset):
        other = lax.rem(self.me + offset, self.groups)
        return (other // 2, lax.rem(other, 2) * 2 + self.core)

    def enter(self):
        barrier = pltpu.get_barrier_semaphore()
        pl.semaphore_signal(barrier, inc=1, device_id=self.partner(), device_id_type=MESH)

        def greet(offset, carry):
            pl.semaphore_signal(barrier, inc=1, device_id=self.peer(offset), device_id_type=MESH)
            return carry

        lax.fori_loop(1, self.groups, greet, 0)
        pl.semaphore_wait(barrier, self.groups)


class QuadPlace(Place):
    def __init__(self, depth):
        super().__init__(depth)
        self.parity = lax.rem(self.z, 2)
        self.z = self.z // 2

    def at(self, z, x, y, core):
        return ((2 * z + self.parity) * 2 + x, y * 2 + core)

    def enter(self):
        barrier = pltpu.get_barrier_semaphore()

        def greet(device):
            pl.semaphore_signal(barrier, inc=1, device_id=device, device_id_type=MESH)

        for device in (self.partner(), self.over_x(), self.over_y()):
            greet(device)
        above, below = self.z + 1 < self.depth, self.z >= 1
        pl.when(above)(functools.partial(greet, self.up()))
        pl.when(below)(functools.partial(greet, self.down()))
        met = 3 + above.astype(jnp.int32) + below.astype(jnp.int32)
        pl.semaphore_wait(barrier, met)


def remote(src, dst, send_sem, recv_sem, device):
    return pltpu.make_async_remote_copy(
        src_ref=src,
        dst_ref=dst,
        send_sem=send_sem,
        recv_sem=recv_sem,
        device_id=device,
        device_id_type=MESH,
    )


def when(cond, action):
    if cond is None:
        action()
    else:
        pl.when(cond)(action)


def cut(block, share):
    units = block // UNIT
    small = max(1, units // share)
    return (units - 2 * small) // 2 * UNIT, small * UNIT


def steps(depth, body, first=0):
    if depth <= 4:
        for step in range(first, depth):
            body(step)
    else:
        def looped(step, carry):
            body(step)
            return carry

        if first == 0:
            body(0)
        lax.fori_loop(max(first, 1), depth, looped, 0)


def tree_sems(depth):
    dma = pltpu.SemaphoreType.DMA
    return [
        dma((depth, 2)), dma((depth,)), dma((depth, 2, 4)), dma((depth, 4)),
        dma((depth,)), dma((depth,)), dma((depth, 2)), dma((depth, 2)),
        dma((depth,)), dma((depth,)), dma((depth, 2)), dma((depth, 2)),
        dma((6,)), dma((6,)),
    ]


def gather_bank(place, bank, block, sems, first_idle=lambda: None, second_idle=lambda: None):
    depth, z, x, y = place.depth, place.z, place.x, place.y
    large, small = cut(block, 9)
    (zab_s, zab_r, zcd_s, zcd_r, ax_s, ax_r, ay_s, ay_r, by_s, by_r, bx_s, bx_r, cd_s, cd_r) = sems

    def rows(zz, xx, yy, first, count):
        begin = ((zz * 2 + xx) * 2 + yy) * (block // UNIT) + first // UNIT
        return bank.at[pl.ds(begin, count // UNIT)]

    def move(zz, xx, yy, first, count, send_sem, recv_sem, device):
        ref = rows(zz, xx, yy, first, count)
        return remote(ref, ref, send_sem, recv_sem, device)

    start_b, start_c, start_d = large, 2 * large, 2 * large + small
    over_x, over_y, up, down = place.over_x(), place.over_y(), place.up(), place.down()

    def sides(step):
        out = [(z - step, z - step >= 0)]
        if not (isinstance(step, int) and step == 0):
            out.append((z + step, z + step < depth))
        return out

    def z_moves(step, kind):
        out = []
        low, high = z - step, z + step
        for level, cond, device, way in (
            (low, (low >= 0) & (z + 1 < depth), up, 0),
            (high, (high < depth) & (z >= 1), down, 1),
        ):
            if kind == "ab":
                out.append(
                    (cond, move(level, x, y, 0, 2 * large, zab_s.at[level, way], zab_r.at[level], device))
                )
            else:
                for xx in range(2):
                    for yy in range(2):
                        out.append(
                            (
                                cond,
                                move(
                                    level, xx, yy, start_c, 2 * small,
                                    zcd_s.at[level, way, xx * 2 + yy],
                                    zcd_r.at[level, xx * 2 + yy], device,
                                ),
                            )
                        )
        return out

    def ax(level):
        return move(level, x, y, 0, large, ax_s.at[level], ax_r.at[level], over_x)

    def by(level):
        return move(level, x, y, start_b, large, by_s.at[level], by_r.at[level], over_y)

    def ay(level, other):
        xx = 1 - x if other else x
        return move(level, xx, y, 0, large, ay_s.at[level, other], ay_r.at[level, other], over_y)

    def bx(level, other):
        yy = 1 - y if other else y
        return move(level, x, yy, start_b, large, bx_s.at[level, other], bx_r.at[level, other], over_x)

    plane = [
        move(z, x, y, start_c, small, cd_s.at[0], cd_r.at[0], over_x),
        move(z, x, y, start_d, small, cd_s.at[1], cd_r.at[1], over_y),
        move(z, x, y, start_c, small, cd_s.at[2], cd_r.at[2], over_y),
        move(z, 1 - x, y, start_c, small, cd_s.at[3], cd_r.at[3], over_y),
        move(z, x, y, start_d, small, cd_s.at[4], cd_r.at[4], over_x),
        move(z, x, 1 - y, start_d, small, cd_s.at[5], cd_r.at[5], over_x),
    ]

    def run(step):
        if isinstance(step, int) and step == 0:
            plane[0].start()
            plane[1].start()
        else:
            for level, cond in sides(step):
                when(cond, move(level, x, y, 0, 2 * large, zab_s.at[level, 0], zab_r.at[level], up).wait_recv)
        for cond, copy in z_moves(step, "ab"):
            when(cond, copy.start)
        for level, cond in sides(step):
            def begin(level=level):
                ax(level).start()
                by(level).start()

            when(cond, begin)
        if isinstance(step, int) and step == 0:
            first_idle()
            plane[2].start()
            plane[4].start()
            plane[0].wait_recv()
            plane[3].start()
            plane[1].wait_recv()
            plane[5].start()
            for copy in plane[2:]:
                copy.wait_recv()
            for cond, copy in z_moves(0, "cd"):
                when(cond, copy.start)
        for level, cond in sides(step):
            def across(level=level):
                ay(level, 0).start()
                bx(level, 0).start()
                ax(level).wait_recv()
                ay(level, 1).start()
                by(level).wait_recv()
                bx(level, 1).start()

            when(cond, across)
        if isinstance(step, int) and step == 0:
            second_idle()
        if not (isinstance(step, int) and step == 0):
            for level, cond in sides(step):
                def arrived(level=level):
                    for part in range(4):
                        move(
                            level, x, y, start_c, 2 * small, zcd_s.at[level, 0, part],
                            zcd_r.at[level, part], up,
                        ).wait_recv()

                when(cond, arrived)
            for cond, copy in z_moves(step, "cd"):
                when(cond, copy.start)

    steps(depth, run)

    def drain(step):
        for level, cond in sides(step):
            def finish(level=level):
                for other in range(2):
                    ay(level, other).wait_recv()
                    bx(level, other).wait_recv()
                    ay(level, other).wait_send()
                    bx(level, other).wait_send()
                ax(level).wait_send()
                by(level).wait_send()

            when(cond, finish)
        for kind in ("ab", "cd"):
            for cond, copy in z_moves(step, kind):
                when(cond, copy.wait_send)

    steps(depth, drain)
    for copy in plane:
        copy.wait_send()


def strips(rows, body, carry=0):
    strip = 64

    def one(index, carry):
        return body(pl.ds(pl.multiple_of(index * strip, strip), strip), carry)

    return lax.fori_loop(0, rows // strip, one, carry, unroll=True)


def fold(values):
    return jnp.sum(values.reshape(-1, 8, values.shape[1]), axis=0)


def chain_kernel(
    depth, block,
    slot_ref, length_ref, master, own_x, own_dense, own_cot, gain_ref, shift_ref,
    act_out, dcv_out, res_out, blk_out, ig_out, dg_out, nrm_out,
    bank, act, dense, mask, cot, raw, side, pre4, slope, upown, upsend, uprecv, dcv, dsd, res, res_x, res_y, dgrecv,
    igrecv, stage, turned, nrm, blk, blksend, keep, ex_side, ex_last, ex_sub,
    load_sem, swap_s, swap_r, act_s, act_r, up_s, up_r, ex_s, ex_r, out_sem, far_s, far_r, near_s, near_r, own_sem,
    *tree,
):
    place = Place(depth)
    core, other = place.core, 1 - place.core
    partner, beside = place.partner(), place.beside()
    half = bank.shape[2]
    width = 2 * half
    frames = mask.shape[1]
    rows = 2 * frames
    peers = place.groups - 1
    chunks = dense.shape[0]
    pieces = source_pieces(half)
    inner = pl.ds(EDGE, frames)
    own_rows = block // 2
    load_rows = min(own_rows, rows)
    loads_of = own_rows // load_rows

    mats_in = []
    for part in range(loads_of):
        for h in range(2):
            mats_in.append(
                pltpu.make_async_copy(
                    master.at[pl.ds(part * load_rows, load_rows), pl.ds(h * half, half)],
                    side.at[part * 2 + h, pl.ds(0, load_rows)],
                    load_sem.at[part * 2 + h],
                )
            )
    x_in = [
        pltpu.make_async_copy(
            own_x.at[0, :, pl.ds(h * half, half)], act.at[0, h, core, inner], load_sem.at[6 + h]
        )
        for h in range(2)
    ]
    dense_in = [
        pltpu.make_async_copy(
            own_dense.at[0, :, pl.ds(chunk * half, half)], dense.at[chunk, core], load_sem.at[8 + chunk]
        )
        for chunk in range(chunks)
    ]
    ours_lanes = pl.ds(pl.multiple_of(core * half, half), half)
    theirs_lanes = pl.ds(pl.multiple_of(other * half, half), half)
    cot_in = pltpu.make_async_copy(own_cot.at[0, :, ours_lanes], cot.at[core], load_sem.at[8 + chunks])
    for copy in mats_in + x_in + dense_in + [cot_in]:
        copy.start()
    place.enter()
    base = place.me * (block // UNIT) + core * (own_rows // UNIT)
    units = load_rows // UNIT
    for copy in mats_in:
        copy.wait()
    for part in range(loads_of):
        def narrow(unit, carry, part=part):
            at = pl.ds(pl.multiple_of(unit * UNIT, UNIT), UNIT)
            stage[part * units + unit] = side[part * 2 + other, at].astype(BF16)
            bank[base + part * units + unit] = side[part * 2 + core, at].astype(BF16)
            return carry

        lax.fori_loop(0, units, narrow, 0)
    send_mats = remote(stage, bank.at[pl.ds(base, own_rows // UNIT)], swap_s.at[0], swap_r.at[0], partner)
    send_mats.start()
    mask[core] = (
        lax.broadcasted_iota(jnp.int32, (frames, 128), 0) < length_ref[0]
    ).astype(F32)
    edge_zero = jnp.zeros((EDGE, half), BF16)

    def clear(section, carry):
        for u in range(2):
            for h in range(2):
                act[section, h, u, pl.ds(0, EDGE)] = edge_zero
                act[section, h, u, pl.ds(EDGE + frames, EDGE)] = edge_zero
            dcv[section, u, pl.ds(0, EDGE)] = edge_zero
            dcv[section, u, pl.ds(EDGE + frames, EDGE)] = edge_zero
        return carry

    lax.fori_loop(0, SUBS, clear, 0)
    send_mats.wait()

    def prepare():
        for copy in x_in + dense_in + [cot_in]:
            copy.wait()
        low_mask = jnp.concatenate([mask[core].astype(BF16)] * (half // 128), axis=1)
        for h in range(2):
            act[0, h, core, inner] = act[0, h, core, inner] * low_mask
        for chunk in range(chunks):
            dense[chunk, core] = dense[chunk, core] * low_mask
        own = act.at[0, :, core, inner]
        swaps = [
            remote(own, own, swap_s.at[1], swap_r.at[1], partner),
            remote(dense.at[:, core], dense.at[:, core], swap_s.at[2], swap_r.at[2], partner),
            remote(mask.at[core], mask.at[core], swap_s.at[3], swap_r.at[3], partner),
            remote(own_cot.at[0, :, theirs_lanes], cot.at[core], swap_s.at[4], swap_r.at[4], partner),
        ]
        for copy in swaps:
            copy.start()
        return swaps

    def own_act(section):
        half_of = turned.at[lax.rem(section, 2)]
        return [
            pltpu.make_async_copy(half_of, act_out.at[section, 0, core], own_sem.at[section]),
            remote(
                half_of, act_out.at[section, 0, core], near_s.at[section], near_r.at[section], partner
            ),
            remote(
                half_of, act_out.at[section, 1, core], far_s.at[section], far_r.at[section], beside
            ),
        ]

    def pass_act(section):
        ref = act_out.at[section, 1, core]
        return remote(ref, ref, near_s.at[SUBS + section], near_r.at[SUBS + section], partner)

    def turn_act(section):
        turned[lax.rem(section, 2)] = jnp.concatenate(
            [act[section, core, u, inner] for u in range(2)], axis=0
        ).T
        for copy in own_act(section):
            copy.start()

    def free_turned(section):
        copies = own_act(section)
        copies[0].wait()
        copies[1].wait_send()
        copies[2].wait_send()

    swaps = []

    def arrived():
        for copy in swaps:
            copy.wait()
        turn_act(0)

    gather_bank(place, bank, block, tree, lambda: swaps.extend(prepare()), arrived)

    outs = []

    def put(src, dst):
        copy = pltpu.make_async_copy(src, dst, out_sem.at[len(outs)])
        copy.start()
        outs.append(copy)

    def far_dcv(section):
        return remote(
            dcv.at[section], dcv_out.at[section, 1],
            far_s.at[SUBS + section], far_r.at[SUBS + section], beside,
        )

    def keep_dcv(section):
        return pltpu.make_async_copy(
            dcv.at[section], dcv_out.at[section, 0], own_sem.at[SUBS + section]
        )

    def res_over(step):
        if step == 0:
            src, dst, device = res.at[pl.ds(2 * (1 - place.x), 2)], res_x, place.over_x()
        elif step == 1:
            src, dst, device = res_x.at[1 - place.y], res_y, place.over_y()
        else:
            src, dst, device = res_y, res_out.at[1], beside
        at = 2 * SUBS + step
        return remote(src, dst, far_s.at[at], far_r.at[at], device)

    def weight(matrix, first, count):
        begin = slot_ref[matrix] * (width // UNIT) + first // UNIT
        return jnp.concatenate([bank[begin + i] for i in range(count // UNIT)], axis=0)

    def valid(at):
        return jnp.concatenate([mask_rows(at)] * (half // 128), axis=1)

    def mask_rows(at):
        return mask[at.start // frames, pl.ds(pl.multiple_of(lax.rem(at.start, frames), 64), at.size)]

    def gain(index):
        return gain_ref[pl.ds(index, 1), ours_lanes]

    def bias(index):
        return shift_ref[pl.ds(index, 1), ours_lanes]

    def share(buffer, index, values):
        buffer[place.me] = values

        def go(offset, carry):
            remote(
                buffer.at[place.me], buffer.at[place.me], ex_s.at[index], ex_r.at[index],
                place.peer(offset),
            ).start()
            return carry

        lax.fori_loop(1, place.groups, go, 0, unroll=place.groups <= 16)

    def shared(buffer, index):
        everyone = buffer.at[pl.ds(0, peers)]
        copy = remote(everyone, everyone, ex_s.at[index], ex_r.at[index], place.peer(1))
        copy.wait_recv()
        copy.wait_send()
        return buffer[...]

    def total_of(values):
        return jnp.sum(values, axis=0, keepdims=True)

    def counted():
        def add(at, carry):
            return carry + fold(valid(at))

        return total_of(strips(rows, add, jnp.zeros((8, half), F32)))

    def moments(load, count):
        pivot = load(pl.ds(0, 8))[0:1]

        def add(at, carry):
            first, second = carry
            valid_now = valid(at)
            off = (load(at) - pivot) * valid_now
            return first + fold(off), second + fold(off * off)

        zero = jnp.zeros((8, half), F32)
        first, second = strips(rows, add, (zero, zero))
        first, second = total_of(first), total_of(second)
        return first + count * pivot, jnp.maximum(second - first * first / count, 0.0)

    def merge(count, total, squares):
        frame_total = jnp.sum(count, axis=0)
        mean = jnp.sum(total, axis=0) / frame_total
        shift = total / count - mean[None]
        variance = jnp.sum(squares + count * shift * shift, axis=0) / frame_total
        return mean[None], lax.rsqrt(variance + norm_eps)[None], frame_total[None]

    def save(index, mean, inverse):
        scale = gain(index) * inverse
        keep[0, pl.ds(index, 1)] = inverse
        keep[1, pl.ds(index, 1)] = mean * inverse
        keep[2, pl.ds(index, 1)] = scale
        keep[3, pl.ds(index, 1)] = bias(index) - mean * scale

    def kept(row, index):
        return keep[row, pl.ds(index, 1)]

    count = counted()
    totals, squares = [], []
    for index in range(SOURCES):
        value = None
        if index < SOURCES - 1:
            for chunk, lane, lanes in pieces[index]:
                left = dense[chunk].reshape(rows, half)[:, lane : lane + lanes]
                right = weight(SUBS * K + chunk // 2, (chunk % 2) * half + lane, lanes)
                term = jnp.dot(left, right, preferred_element_type=F32)
                value = term if value is None else value + term
        else:
            for h in range(2):
                left = jnp.concatenate([act[0, h, u, inner] for u in range(2)], axis=0)
                term = jnp.dot(left, weight(SUBS * K + 3, h * half, half), preferred_element_type=F32)
                value = term if value is None else value + term
        side[index] = value
        total, square = moments(lambda at, index=index: side[index, at], count)
        totals.append(total)
        squares.append(square)
    fill = jnp.zeros((3, half), F32)
    share(ex_side, 0, jnp.concatenate([count] + totals + squares + [fill], axis=0))

    def convolve(section, h, first):
        value = None
        for k in range(K):
            left = jnp.concatenate(
                [act[section, h, u, pl.ds(EDGE - MARGIN + k, frames)] for u in range(2)], axis=0
            )
            term = jnp.dot(
                left, weight(section * K + k, h * half, half), preferred_element_type=F32
            )
            value = term if value is None else value + term
            if k % 2 == 1 or k == K - 1:
                if first and k == 1:
                    raw[section] = value
                else:
                    raw[section] += value
                value = None

    def swap_act(section):
        own = act.at[section, core, :, inner]
        return remote(own, own, act_s.at[section], act_r.at[section], partner)

    def forward(section, last):
        convolve(section, core, True)
        if isinstance(section, int):
            if section > 0:
                swap_act(section).wait_recv()
        else:
            pl.when(section > 0)(swap_act(section).wait_recv)
        convolve(section, other, False)
        total, square = moments(lambda at: raw[section, at], count)
        buffer = ex_sub.at[lax.rem(section, 2)]
        share(buffer, 1 + section, jnp.concatenate([count, total, square, jnp.zeros_like(count)], axis=0))

        def background():
            own_act(section - 1)[2].wait_recv()
            pass_act(section - 1).start()
            if isinstance(section, int):
                free_turned(section - 2)
            else:
                pl.when(section > 1)(functools.partial(free_turned, section - 2))
            turn_act(section)

        if isinstance(section, int):
            background()
        else:
            pl.when(section > 0)(background)
        parts = shared(buffer, 1 + section)
        mean, inverse, frame_total = merge(parts[:, 0], parts[:, 1], parts[:, 2])
        save(section, mean, inverse)
        scale, offset = kept(2, section), kept(3, section)

        def activate(at, carry):
            before = raw[section, at] * scale + offset
            if last:
                before = before + pre4[at]
                pre4[at] = before
            hidden = (before * jax.nn.sigmoid(before) * valid(at)).astype(BF16)
            u = at.start // frames
            first = pl.multiple_of(lax.rem(at.start, frames), 64)
            if last:
                @pl.when(u == core)
                def _():
                    blk[core, pl.ds(first, at.size)] = hidden

                @pl.when(u != core)
                def _():
                    blksend[pl.ds(first, at.size)] = hidden
            else:
                act[section + 1, core, u, pl.ds(pl.multiple_of(first + EDGE, EDGE), at.size)] = hidden
            return carry

        strips(rows, activate)
        if not last:
            swap_act(section + 1).start()
        return frame_total

    def looped(section, carry):
        forward(section, False)

        @pl.when(section == 0)
        def _():
            parts = shared(ex_side, 0)
            for index in range(SOURCES):
                mean, inverse, _ = merge(
                    parts[:, 0], parts[:, 1 + index], parts[:, 1 + SOURCES + index]
                )
                save(SUBS + index, mean, inverse)
            scales = [kept(2, SUBS + index) for index in range(SOURCES)]
            offset = sum(kept(3, SUBS + index) for index in range(SOURCES))

            def add(at, carry):
                before = offset
                for index in range(SOURCES):
                    before = before + side[index, at] * scales[index]
                pre4[at] = before
                return carry

            strips(rows, add)

        return carry

    lax.fori_loop(0, SUBS - 1, looped, 0)
    frame_total = forward(SUBS - 1, True)
    blk_copy = remote(blksend, blk.at[core], swap_s.at[5], swap_r.at[5], partner)
    blk_copy.start()
    for section in range(1, SUBS):
        swap_act(section).wait_send()
    for section in (SUBS - 2, SUBS - 1):
        free_turned(section)

    def hat_of(values, index):
        return values * kept(0, index) - kept(1, index)

    def back_half(section, h):
        total = None
        value = None
        for k in range(K):
            left = jnp.concatenate(
                [dcv[section, u, pl.ds(EDGE + MARGIN - k, frames)] for u in range(2)], axis=0
            )
            term = lax.dot_general(
                left, weight(section * K + k, h * half, half), NT, preferred_element_type=F32
            )
            value = term if value is None else value + term
            if k % 2 == 1 or k == K - 1:
                total = value if total is None else total + value
                value = None
        return total

    def up_copy(section):
        slot = lax.rem(section, 2)
        return remote(upsend, uprecv.at[slot], up_s.at[slot], up_r.at[slot], partner)

    def backward(section):
        upsend[...] = back_half(section, other)
        up_copy(section).start()
        upown[...] = back_half(section, core)

    def slopes(section, upstream, before_of, others):
        sources = [(lambda at: raw[section, at], section)] + others

        def one(at, carry):
            before = before_of(at)
            sigmoid = jax.nn.sigmoid(before)
            now = upstream(at) * valid(at) * (sigmoid * (1.0 + before * (1.0 - sigmoid)))
            slope[at] = now
            out = [carry[0] + fold(now)]
            for (load, index), so_far in zip(sources, carry[1:]):
                out.append(so_far + fold(now * hat_of(load(at), index)))
            return tuple(out)

        zero = jnp.zeros((8, half), F32)
        return [total_of(value) for value in strips(rows, one, (zero,) * (1 + len(sources)))]

    def branch(load, index, shift_sum, gain_sum, store):
        scale = kept(2, index)
        shift_mean, gain_mean = shift_sum / frame_total, gain_sum / frame_total

        def one(at, carry):
            value = slope[at] - shift_mean - hat_of(load(at), index) * gain_mean
            store(at, (valid(at) * scale * value).astype(BF16))
            return carry

        strips(rows, one)

    def conv_branch(section, shift_sum, gain_sum):
        def store(at, value):
            first = pl.multiple_of(lax.rem(at.start, frames) + EDGE, EDGE)
            dcv[section, at.start // frames, pl.ds(first, at.size)] = value

        branch(lambda at: raw[section, at], section, shift_sum, gain_sum, store)
        far_dcv(section).start()
        keep_dcv(section).start()

    def cot_at(at):
        return cot[
            at.start // frames, pl.ds(pl.multiple_of(lax.rem(at.start, frames), 64), at.size)
        ].astype(F32)

    sums = slopes(
        SUBS - 1, cot_at, lambda at: pre4[at],
        [(lambda at, index=index: side[index, at], SUBS + index) for index in range(SOURCES)],
    )
    share(ex_last, SUBS + 1, jnp.concatenate(sums, axis=0))
    sums = jnp.sum(shared(ex_last, SUBS + 1), axis=0)
    shift_sum = sums[0:1]
    conv_branch(SUBS - 1, shift_sum, sums[1:2])
    nrm[core] = jnp.zeros_like(nrm[0])
    nrm[core, pl.ds(SUBS - 1, 1 + SOURCES)] = sums[1:]
    nrm[core, pl.ds(SUBS + SOURCES + SUBS - 1, 1)] = shift_sum
    backward(SUBS - 1)
    for index in range(SOURCES):
        def store(at, value, index=index):
            dsd[index, at] = value

        branch(
            lambda at, index=index: side[index, at], SUBS + index, shift_sum,
            sums[2 + index : 3 + index], store,
        )
    theirs = pl.multiple_of(other * frames, frames)
    ours = pl.multiple_of(core * frames, frames)
    dg_copy = remote(
        side.at[:, pl.ds(theirs, frames)], dgrecv, swap_s.at[6], swap_r.at[6], partner
    )

    def dense_grads():
        for index in range(SOURCES - 1):
            for chunk, lane, lanes in pieces[index]:
                right = weight(SUBS * K + chunk // 2, (chunk % 2) * half + lane, lanes)
                side[chunk, :, pl.ds(lane, lanes)] = lax.dot_general(
                    dsd[index], right, NT, preferred_element_type=F32
                )
        dg_copy.start()

    def residual_grads():
        rows_of = [[] for _ in range(chunks)]
        for index, parts in enumerate(pieces):
            for chunk, lane, lanes in parts:
                rows_of[chunk].append((lane, lanes, index))
        for chunk in range(chunks):
            turned = dense[chunk].reshape(rows, half).T
            for lane, lanes, index in rows_of[chunk]:
                res[chunk // 2, pl.ds((chunk % 2) * half + lane, lanes)] = jnp.dot(
                    turned[lane : lane + lanes], dsd[index], preferred_element_type=F32
                ).astype(BF16)
        for h in range(2):
            turned = jnp.concatenate([act[0, h, u, inner] for u in range(2)], axis=0).T
            res[3, pl.ds(h * half, half)] = jnp.dot(
                turned, dsd[SOURCES - 1], preferred_element_type=F32
            ).astype(BF16)

    dg_puts = [
        pltpu.make_async_copy(
            dgrecv.at[chunk], dg_out.at[0, :, pl.ds(chunk * half, half)], load_sem.at[chunk]
        )
        for chunk in range(chunks)
    ]

    def finish_dense():
        dg_copy.wait()
        own_valid = jnp.concatenate([mask[core]] * (half // 128), axis=1)
        for chunk in range(chunks):
            dgrecv[chunk] = (dgrecv[chunk] + side[chunk, pl.ds(ours, frames)]) * own_valid
            dg_puts[chunk].start()

    def looped_back(turn, carry):
        section = SUBS - 2 - turn
        copy = up_copy(section + 1)
        copy.wait()
        slot = lax.rem(section + 1, 2)
        scale, offset = kept(2, section), kept(3, section)
        sums = slopes(
            section, lambda at: upown[at] + uprecv[slot, at],
            lambda at: raw[section, at] * scale + offset, [],
        )
        zero = jnp.zeros((2, half), F32)
        buffer = ex_sub.at[lax.rem(section, 2)]
        share(buffer, SUBS + 2 + section, jnp.concatenate(sums + [zero], axis=0))

        @pl.when(section == SUBS - 2)
        def _():
            residual_grads()
            res_over(0).start()
            dense_grads()

        @pl.when(section == SUBS - 3)
        def _():
            res_over(0).wait_recv()
            for index in range(2):
                total = res[2 * place.x + index].astype(F32) + res_x[index].astype(F32)
                res_x[index] = total.astype(BF16)
            res_over(1).start()
            finish_dense()
            own_act(SUBS - 1)[2].wait_recv()
            pass_act(SUBS - 1).start()

        @pl.when(section == SUBS - 4)
        def _():
            res_over(1).wait_recv()
            res_y[...] = (res_y[...].astype(F32) + res_x[place.y].astype(F32)).astype(BF16)

        sums = jnp.sum(shared(buffer, SUBS + 2 + section), axis=0)
        pl.when(section == SUBS - 4)(lambda: res_over(2).start())
        conv_branch(section, sums[0:1], sums[1:2])
        nrm[core, pl.ds(section, 1)] = sums[1:2]
        nrm[core, pl.ds(SUBS + SOURCES + section, 1)] = sums[0:1]

        @pl.when(section > 0)
        def _():
            backward(section)

        return carry

    lax.fori_loop(0, SUBS - 1, looped_back, 0)
    put(res_y, res_out.at[0])
    nrm_copy = remote(nrm.at[core], nrm.at[core], swap_s.at[7], swap_r.at[7], partner)
    nrm_copy.start()
    for h in range(2):
        uprecv[h] = back_half(0, h) + lax.dot_general(
            dsd[SOURCES - 1], weight(SUBS * K + 3, h * half, half), NT, preferred_element_type=F32
        )
    ig_copy = remote(
        uprecv.at[:, pl.ds(theirs, frames)], igrecv, swap_s.at[8], swap_r.at[8], partner
    )
    ig_copy.start()
    own_valid = jnp.concatenate([mask[core]] * (half // 128), axis=1)
    blk_copy.wait()
    nrm_copy.wait()
    put(nrm, nrm_out)
    ig_copy.wait()
    for h in range(2):
        igrecv[h] = (igrecv[h] + uprecv[h, pl.ds(ours, frames)]) * own_valid
        put(igrecv.at[h], ig_out.at[0, :, pl.ds(h * half, half)])
        put(blk.at[h], blk_out.at[0, :, pl.ds(h * half, half)])
    for section in range(SUBS):
        own_act(section)[1].wait_recv()
        pass_act(section).wait()
        far_dcv(section).wait()
        keep_dcv(section).wait()
    res_over(0).wait_send()
    res_over(1).wait_send()
    res_over(2).wait()
    for copy in outs + dg_puts:
        copy.wait()


def run_chain(depth, block, places, lengths, master, x, dense, cot, gains, shifts):
    frames, width = x.shape[1:]
    half = width // 2
    rows = 2 * frames
    chunks = dense.shape[2] // half
    padded = frames + 2 * EDGE
    groups = depth * 4
    dma = pltpu.SemaphoreType.DMA
    anywhere = pl.BlockSpec(memory_space=pl.ANY)
    vmem = pl.BlockSpec(memory_space=pltpu.VMEM)
    smem = pl.BlockSpec(memory_space=pltpu.SMEM)
    out_shape = [
        jax.ShapeDtypeStruct((SUBS, 2, 2, half, rows), BF16),
        jax.ShapeDtypeStruct((SUBS, 2, 2, padded, half), BF16),
        jax.ShapeDtypeStruct((2, width, half), BF16),
        jax.ShapeDtypeStruct(x.shape, BF16),
        jax.ShapeDtypeStruct(x.shape, F32),
        jax.ShapeDtypeStruct(dense.shape, F32),
        jax.ShapeDtypeStruct((2, 16, half), F32),
    ]
    scratch = [
        pltpu.VMEM((groups * block // UNIT, UNIT, half), BF16),
        pltpu.VMEM((SUBS, 2, 2, padded, half), BF16),
        pltpu.VMEM((chunks, 2, frames, half), BF16),
        pltpu.VMEM((2, frames, 128), F32),
        pltpu.VMEM((2, frames, half), BF16),
        pltpu.VMEM((SUBS, rows, half), F32),
        pltpu.VMEM((SOURCES, rows, half), F32),
        pltpu.VMEM((rows, half), F32),
        pltpu.VMEM((rows, half), F32),
        pltpu.VMEM((rows, half), F32),
        pltpu.VMEM((rows, half), F32),
        pltpu.VMEM((2, rows, half), F32),
        pltpu.VMEM((SUBS, 2, padded, half), BF16),
        pltpu.VMEM((SOURCES, rows, half), BF16),
        pltpu.VMEM((4, width, half), BF16),
        pltpu.VMEM((2, width, half), BF16),
        pltpu.VMEM((width, half), BF16),
        pltpu.VMEM((chunks, frames, half), F32),
        pltpu.VMEM((2, frames, half), F32),
        pltpu.VMEM((block // 2 // UNIT, UNIT, half), BF16),
        pltpu.VMEM((2, half, rows), BF16),
        pltpu.VMEM((2, 16, half), F32),
        pltpu.VMEM((2, frames, half), BF16),
        pltpu.VMEM((frames, half), BF16),
        pltpu.VMEM((4, 16, half), F32),
        pltpu.VMEM((groups, 16, half), F32),
        pltpu.VMEM((groups, 8, half), F32),
        pltpu.VMEM((2, groups, 4, half), F32),
        dma((9 + chunks,)),
        dma((9,)), dma((9,)),
        dma((SUBS,)), dma((SUBS,)),
        dma((2,)), dma((2,)),
        dma((2 * SUBS + 1,)), dma((2 * SUBS + 1,)),
        dma((10 + chunks,)),
        dma((2 * SUBS + 3,)), dma((2 * SUBS + 3,)),
        dma((2 * SUBS,)), dma((2 * SUBS,)),
        dma((2 * SUBS,)),
    ] + tree_sems(depth)
    return pl.pallas_call(
        functools.partial(chain_kernel, depth, block),
        out_shape=out_shape,
        in_specs=[smem] * 2 + [anywhere] * 4 + [vmem] * 2,
        out_specs=[anywhere] * len(out_shape),
        scratch_shapes=scratch,
        compiler_params=pltpu.CompilerParams(
            collective_id=1, has_side_effects=True, vmem_limit_bytes=63 << 20
        ),
        cost_estimate=pl.CostEstimate(
            flops=4 * SUBS * K * rows * width * half, bytes_accessed=16 << 20, transcendentals=0
        ),
        name="chain",
    )(places, lengths, master, x, dense, cot, gains, shifts)


def grad_kernel(slot_ref, act_ref, dcv_ref, res_ref, out_ref, stage, count, sems):
    section = pl.program_id(0)
    half = act_ref.shape[3]
    width = 2 * half
    frames = act_ref.shape[4] // 2
    ring = stage.shape[0]

    @pl.when(section == 0)
    def _():
        count[0] = 0

    def slot_copy(place, slot):
        out = out_ref.at[pl.ds(pl.multiple_of(slot * width, 16), width)]
        return pltpu.make_async_copy(stage.at[place], out, sems.at[place])

    def emit(matrix, compute):
        slot = slot_ref[matrix]

        @pl.when(slot >= 0)
        def _():
            turn = count[0]
            place = lax.rem(turn, ring)
            pl.when(turn >= ring)(slot_copy(place, 0).wait)
            stage[place] = compute().astype(BF16)
            slot_copy(place, slot).start()
            count[0] = turn + 1

    for k in range(K):
        def conv(k=k):
            total = None
            for pair in range(2):
                right = jnp.concatenate(
                    [dcv_ref[0, pair, u, pl.ds(EDGE + MARGIN - k, frames)] for u in range(2)], axis=0
                )
                left = act_ref[0, pair].reshape(width, 2 * frames)
                term = jnp.dot(left, right, preferred_element_type=F32)
                total = term if total is None else total + term
            return total

        emit(section * K + k, conv)

    @pl.when(section == SUBS - 1)
    def _():
        for index in range(4):
            here = slot_ref[SUBS * K + 4] == index
            emit(
                SUBS * K + index,
                lambda here=here: jnp.where(
                    here, res_ref[0].astype(F32) + res_ref[1].astype(F32), 0.0
                ),
            )
        turns = count[0]

        def finish(place, carry):
            pl.when(place < turns)(slot_copy(place, 0).wait)
            return carry

        lax.fori_loop(0, ring, finish, 0)


def run_grads(total_rows, places, act, dcv, res):
    half = act.shape[3]
    ring = 8
    grid_spec = pltpu.PrefetchScalarGridSpec(
        num_scalar_prefetch=1,
        grid=(SUBS,),
        in_specs=[
            pl.BlockSpec((1,) + act.shape[1:], lambda s, t: (s, 0, 0, 0, 0)),
            pl.BlockSpec((1,) + dcv.shape[1:], lambda s, t: (s, 0, 0, 0, 0)),
            pl.BlockSpec(res.shape, lambda s, t: (0, 0, 0)),
        ],
        out_specs=pl.BlockSpec(memory_space=pl.ANY),
        scratch_shapes=[
            pltpu.VMEM((ring, 2 * half, half), BF16),
            pltpu.SMEM((1,), jnp.int32),
            pltpu.SemaphoreType.DMA((ring,)),
        ],
    )
    return pl.pallas_call(
        grad_kernel,
        grid_spec=grid_spec,
        out_shape=jax.ShapeDtypeStruct((total_rows, half), BF16),
        compiler_params=pltpu.CompilerParams(vmem_limit_bytes=60 << 20),
        name="weight_grads",
    )(places, act, dcv, res)


def shares(rows, number):
    units = rows // UNIT
    out = []
    first = 0
    for index in range(number):
        count = units // number + (1 if index < units % number else 0)
        if count:
            out.append((first * UNIT, count * UNIT))
        first += count
    return out


def reduce_kernel(
    depth, block, grads, out, l_ay, l_ax, l_bx, l_by, l_zab, l_zcd, l_c, l_d,
    o_cross, o_line, o_plane, final, result,
    cross_sem, line_sem, plane_sem, out_sem, swap_s, swap_r, ay_s, ay_r, ax_s, ax_r, bx_s, bx_r, by_s, by_r,
    zab_s, zab_r, zcd_s, zcd_r, cd_s, cd_r,
):
    place = QuadPlace(depth)
    z, x, y, core = place.z, place.x, place.y, place.core
    large, small = cut(block, 16)
    start_b, start_c, start_d = large, 2 * large, 2 * large + small
    over_x, over_y, up, down = place.over_x(), place.over_y(), place.up(), place.down()
    pieces = shares(large, 2)
    runs = range(len(pieces))

    def rows(zz, xx, yy, first, count):
        begin = pl.multiple_of(((zz * 2 + xx) * 2 + yy) * block + first, 16)
        return grads.at[pl.ds(begin, count)]

    def part(run):
        return pl.ds(*pieces[run])

    def ay(level, other_x, run):
        xx = 1 - x if other_x else x
        first, count = pieces[run]
        return remote(
            rows(level, xx, 1 - y, first, count), l_ay.at[level, other_x, part(run)],
            ay_s.at[level, other_x, run], ay_r.at[level, other_x, run], over_y,
        )

    def bx(level, other_y, run):
        yy = 1 - y if other_y else y
        first, count = pieces[run]
        return remote(
            rows(level, 1 - x, yy, start_b + first, count), l_bx.at[level, other_y, part(run)],
            bx_s.at[level, other_y, run], bx_r.at[level, other_y, run], over_x,
        )

    def ax(level, run):
        return remote(
            l_ay.at[level, 1, part(run)], l_ax.at[level, part(run)],
            ax_s.at[level, run], ax_r.at[level, run], over_x,
        )

    def by(level, run):
        return remote(
            l_bx.at[level, 1, part(run)], l_by.at[level, part(run)],
            by_s.at[level, run], by_r.at[level, run], over_y,
        )

    def own_cross(level):
        return [
            pltpu.make_async_copy(rows(level, 1 - x, y, 0, large), o_cross.at[level, 0], cross_sem.at[level, 0]),
            pltpu.make_async_copy(rows(level, x, 1 - y, start_b, large), o_cross.at[level, 1], cross_sem.at[level, 1]),
        ]

    def own_line(level):
        return [
            pltpu.make_async_copy(rows(level, x, y, index * large, large), o_line.at[level, index], line_sem.at[level, index])
            for index in range(2)
        ]

    def own_plane(level):
        return [
            pltpu.make_async_copy(
                rows(level, index // 2, index % 2, start_c, 2 * small),
                o_plane.at[level, index], plane_sem.at[level, index],
            )
            for index in range(4)
        ]

    def add(target, others, count, keep=None):
        strip = UNIT

        def one(index, carry):
            at = pl.ds(pl.multiple_of(index * strip, strip), strip)
            value = target[at].astype(F32)
            for ref in others:
                value = value + ref[at].astype(F32)
            if keep is None:
                target[at] = value.astype(BF16)
            else:
                keep[at] = value
            return carry

        lax.fori_loop(0, count // strip, one, 0)

    def sides(step):
        out = [(z - step, z - step >= 0)]
        if not (isinstance(step, int) and step == 0):
            out.append((z + step, z + step < depth))
        return out

    def both(step, action):
        for level, cond in sides(step):
            when(cond, functools.partial(action, level))

    def backwards(body, first, last):
        if depth <= 4:
            for step in range(first, last - 1, -1):
                body(step)
        else:
            def looped(turn, carry):
                body(first - turn)
                return carry

            lax.fori_loop(0, first - last + 1, looped, 0)

    def leaf(step, other, run):
        def go(level):
            ay(level, other, run).start()
            bx(level, other, run).start()

        both(step, go)

    def fetch(step):
        def go(level):
            for copy in own_cross(level) + own_line(level):
                copy.start()

        both(step, go)

    def entry_of(level, way):
        at_home = (z - 1 == level) if way == 0 else (z + 1 == level)
        return level if way == 0 else level + (depth - level) * at_home.astype(jnp.int32)

    def beyond(way):
        return z + 1 < depth if way == 0 else z >= 1

    def zcd(level, way, index, leaf_copy):
        entry = entry_of(level, way)
        if leaf_copy:
            src = rows(level, index // 2, index % 2, start_c, 2 * small)
        else:
            src = l_zcd.at[level, index]
        return remote(
            src, l_zcd.at[entry, index], zcd_s.at[level, index], zcd_r.at[entry, index],
            down if way == 0 else up,
        )

    def zcd_arrived(entry, index):
        ref = l_zcd.at[entry, index]
        remote(ref, ref, zcd_s.at[0, index], zcd_r.at[entry, index], up).wait_recv()

    def lines(step):
        return ((0, z - step, z - step >= 0), (1, z + step, z + step < depth))

    def plane_step(step):
        for way, level, cond in lines(step):
            def go(way=way, level=level):
                @pl.when(beyond(way))
                def _():
                    copies = own_plane(level)
                    for copy in copies:
                        copy.start()
                    for index in range(4):
                        zcd_arrived(level, index)
                        copies[index].wait()
                        add(l_zcd.at[level, index], [o_plane.at[level, index]], 2 * small)
                        zcd(level, way, index, False).start()

                @pl.when(jnp.logical_not(beyond(way)))
                def _():
                    for index in range(4):
                        zcd(level, way, index, True).start()

            when(cond, go)

    def zab(level, way, run):
        entry = entry_of(level, way)
        return [
            remote(
                landing.at[level, part(run)], l_zab.at[entry, index, part(run)],
                zab_s.at[level, index, run], zab_r.at[entry, index, run], down if way == 0 else up,
            )
            for index, landing in enumerate((l_ax, l_by))
        ]

    def zab_arrived(entry, index, run):
        ref = l_zab.at[entry, index, part(run)]
        remote(ref, ref, zab_s.at[0, index, run], zab_r.at[entry, index, run], up).wait_recv()

    def across(run):
        def go(level):
            count = pieces[run][1]
            copies = own_cross(level)
            ay(level, 1, run).wait_recv()
            if run == 0:
                copies[0].wait()
            add(l_ay.at[level, 1, part(run)], [o_cross.at[level, 0, part(run)]], count)
            ax(level, run).start()
            bx(level, 1, run).wait_recv()
            if run == 0:
                copies[1].wait()
            add(l_bx.at[level, 1, part(run)], [o_cross.at[level, 1, part(run)]], count)
            by(level, run).start()

        return go

    def line_step(step, run):
        count = pieces[run][1]
        for way, level, cond in lines(step):
            def go(way=way, level=level):
                copies = own_line(level)
                hops = zab(level, way, run)
                for index, (first_hop, second_hop, first_land, second_land) in enumerate(
                    ((ay, ax, l_ay, l_ax), (bx, by, l_bx, l_by))
                ):
                    first_hop(level, 0, run).wait_recv()
                    second_hop(level, run).wait_recv()
                    if run == 0:
                        copies[index].wait()
                    target = second_land.at[level, part(run)]
                    terms = [first_land.at[level, 0, part(run)], o_line.at[level, index, part(run)]]

                    @pl.when(beyond(way))
                    def _(index=index, target=target, terms=terms):
                        zab_arrived(level, index, run)
                        add(target, terms + [l_zab.at[level, index, part(run)]], count)

                    @pl.when(jnp.logical_not(beyond(way)))
                    def _(target=target, terms=terms):
                        add(target, terms, count)

                    hops[index].start()

            when(cond, go)

    unrolled = depth <= 4
    place.enter()
    for run in runs:
        leaf(depth - 1, 1, run)
    if not unrolled:
        for run in runs:
            leaf(depth - 1, 0, run)
    fetch(depth - 1)

    def turn(step):
        plane_step(step)
        for run in runs:
            if unrolled and step == depth - 1:
                leaf(step, 0, run)
            both(step, across(run))
        for run in runs:
            leaf(step - 1, 1, run)
        fetch(step - 1)
        for run in runs:
            line_step(step, run)
            leaf(step - 1, 0, run)

    backwards(turn, depth - 1, 1)

    above, below = z + 1 < depth, z >= 1
    copies = own_plane(z)
    for copy in copies:
        copy.start()
    for index in range(4):
        pl.when(above)(functools.partial(zcd_arrived, z, index))
        pl.when(below)(functools.partial(zcd_arrived, depth, index))
        copies[index].wait()
        target = o_plane.at[z, index]
        for cond, entries in (
            (above & below, (z, depth)), (above & jnp.logical_not(below), (z,)), (jnp.logical_not(above), (depth,))
        ):
            @pl.when(cond)
            def _(entries=entries, target=target, index=index):
                add(target, [l_zcd.at[entry, index] for entry in entries], 2 * small)

    def block_at(xx, yy, first):
        return o_plane.at[z, xx * 2 + yy, pl.ds(first, small)]

    plane = [
        remote(block_at(1 - x, 1 - y, 0), l_c.at[1], cd_s.at[0], cd_r.at[0], over_y),
        remote(block_at(x, 1 - y, 0), l_c.at[0], cd_s.at[1], cd_r.at[1], over_y),
        remote(block_at(1 - x, 1 - y, small), l_d.at[1], cd_s.at[2], cd_r.at[2], over_x),
        remote(block_at(1 - x, y, small), l_d.at[0], cd_s.at[3], cd_r.at[3], over_x),
        remote(l_c.at[1], l_c.at[2], cd_s.at[4], cd_r.at[4], over_x),
        remote(l_d.at[1], l_d.at[2], cd_s.at[5], cd_r.at[5], over_y),
    ]
    for copy in plane[:4]:
        copy.start()
    for run in runs:
        both(0, across(run))
    plane[0].wait_recv()
    add(l_c.at[1], [block_at(1 - x, y, 0)], small)
    plane[4].start()
    plane[2].wait_recv()
    add(l_d.at[1], [block_at(x, 1 - y, small)], small)
    plane[5].start()

    copies = own_line(z)
    for run in runs:
        first, count = pieces[run]
        for index, (first_hop, second_hop, first_land, second_land) in enumerate(
            ((ay, ax, l_ay, l_ax), (bx, by, l_bx, l_by))
        ):
            first_hop(z, 0, run).wait_recv()
            second_hop(z, run).wait_recv()
            if run == 0:
                copies[index].wait()
            terms = [first_land.at[z, 0, part(run)], o_line.at[z, index, part(run)]]
            target = final.at[pl.ds(index * large + first, count)]
            pl.when(above)(functools.partial(zab_arrived, z, index, run))
            pl.when(below)(functools.partial(zab_arrived, depth, index, run))
            for cond, entries in (
                (above & below, (z, depth)), (above & jnp.logical_not(below), (z,)), (jnp.logical_not(above), (depth,))
            ):
                @pl.when(cond)
                def _(entries=entries, terms=terms, target=target, index=index, land=second_land, run=run, count=count):
                    more = [l_zab.at[entry, index, part(run)] for entry in entries]
                    add(land.at[z, part(run)], terms + more, count, keep=target)

    for copy in (plane[1], plane[3], plane[4], plane[5]):
        copy.wait_recv()
    add(block_at(x, y, 0), [l_c.at[0], l_c.at[2]], small, keep=final.at[pl.ds(start_c, small)])
    add(block_at(x, y, small), [l_d.at[0], l_d.at[2]], small, keep=final.at[pl.ds(start_d, small)])
    own_rows = block // 2
    theirs = final.at[pl.ds(pl.multiple_of((1 - core) * own_rows, 16), own_rows)]
    mine = final.at[pl.ds(pl.multiple_of(core * own_rows, 16), own_rows)]
    cross = remote(theirs, result, swap_s.at[0], swap_r.at[0], place.partner())
    cross.start()
    local = pltpu.make_async_copy(mine, out.at[core], out_sem.at[0])
    local.start()

    def drain(step):
        def go(level):
            for run in runs:
                for other in range(2):
                    ay(level, other, run).wait_send()
                    bx(level, other, run).wait_send()
                ax(level, run).wait_send()
                by(level, run).wait_send()

        both(step, go)
        if not (isinstance(step, int) and step == 0):
            for way, level, cond in lines(step):
                def along(way=way, level=level):
                    for index in range(4):
                        zcd(level, way, index, False).wait_send()
                    for run in runs:
                        for copy in zab(level, way, run):
                            copy.wait_send()

                when(cond, along)

    steps(depth, drain)
    for copy in plane:
        copy.wait_send()
    cross.wait()
    fetched = pltpu.make_async_copy(result, out.at[1 - core], out_sem.at[1])
    fetched.start()
    fetched.wait()
    local.wait()


def run_reduce(depth, block, grads):
    half = grads.shape[1]
    large, small = cut(block, 16)
    dma = pltpu.SemaphoreType.DMA
    anywhere = pl.BlockSpec(memory_space=pl.ANY)
    scratch = [
        pltpu.VMEM((depth, 2, large, half), BF16),
        pltpu.VMEM((depth, large, half), BF16),
        pltpu.VMEM((depth, 2, large, half), BF16),
        pltpu.VMEM((depth, large, half), BF16),
        pltpu.VMEM((depth + 1, 2, large, half), BF16),
        pltpu.VMEM((depth + 1, 4, 2 * small, half), BF16),
        pltpu.VMEM((3, small, half), BF16),
        pltpu.VMEM((3, small, half), BF16),
        pltpu.VMEM((depth, 2, large, half), BF16),
        pltpu.VMEM((depth, 2, large, half), BF16),
        pltpu.VMEM((depth, 4, 2 * small, half), BF16),
        pltpu.VMEM((block, half), F32),
        pltpu.VMEM((block // 2, half), F32),
        dma((depth, 2)), dma((depth, 2)), dma((depth, 4)), dma((2,)), dma((1,)), dma((1,)),
        dma((depth, 2, 2)), dma((depth, 2, 2)), dma((depth, 2)), dma((depth, 2)),
        dma((depth, 2, 2)), dma((depth, 2, 2)), dma((depth, 2)), dma((depth, 2)),
        dma((depth + 1, 2, 2)), dma((depth + 1, 2, 2)),
        dma((depth + 1, 4)), dma((depth + 1, 4)),
        dma((6,)), dma((6,)),
    ]
    return pl.pallas_call(
        functools.partial(reduce_kernel, depth, block),
        out_shape=jax.ShapeDtypeStruct((2, block // 2, half), F32),
        in_specs=[anywhere],
        out_specs=anywhere,
        scratch_shapes=scratch,
        compiler_params=pltpu.CompilerParams(
            collective_id=2, has_side_effects=True, vmem_limit_bytes=51 << 20
        ),
        name="reduce",
    )(grads)


def adamw(gradient, params, first_moment, second_moment, rate, decay):
    moment_new = beta_one * first_moment + (1.0 - beta_one) * gradient
    second_new = beta_two * second_moment + (1.0 - beta_two) * gradient * gradient
    direction = (
        moment_new
        / (1.0 - beta_one**STEP)
        / (jnp.sqrt(second_new / (1.0 - beta_two**STEP)) + adam_eps)
    )
    return (moment_new, second_new, params - rate * (direction + decay * params))


def update_kernel(
    filled_ref, sums_ref, master_ref, one_ref, two_ref, average_ref,
    nrm_ref, gain_ref, shift_ref, norm_one_ref, norm_two_ref,
    grad_ref, one_out, two_out, new_ref, average_out, copy_ref,
    norm_grad_ref, norm_one_out, norm_two_out, norm_new_ref,
):
    @pl.when(pl.program_id(0) == 0)
    def _():
        branches = SUBS + SOURCES
        sums = jnp.concatenate([nrm_ref[0], nrm_ref[1]], axis=1)
        shifts = sums[branches : branches + SUBS]
        both = (
            sums[:branches],
            jnp.concatenate([shifts] + [shifts[SUBS - 1 :]] * SOURCES, axis=0),
        )
        for index, (gradient, params) in enumerate(zip(both, (gain_ref, shift_ref))):
            moment, second, new = adamw(
                gradient, params[...], norm_one_ref[:, index], norm_two_ref[:, index], rate_norm, 0.0
            )
            norm_grad_ref[:, index] = gradient
            norm_one_out[:, index] = moment
            norm_two_out[:, index] = second
            norm_new_ref[:, index] = new

    filled = filled_ref[pl.program_id(0)] > 0
    half = sums_ref.shape[2]
    strip = 32

    def one(index, carry):
        at = pl.ds(pl.multiple_of(index * strip, strip), strip)
        for h in range(2):
            lanes = pl.ds(h * half, half)
            gradient = jnp.where(filled, sums_ref[h, at], 0.0)
            master = master_ref[at, lanes]
            moment, second, new = adamw(
                gradient, master, one_ref[at, lanes], two_ref[at, lanes], rate_main, decay_main
            )
            grad_ref[at, lanes] = gradient
            one_out[at, lanes] = moment
            two_out[at, lanes] = second
            new_ref[at, lanes] = new
            average_out[at, lanes] = ema_keep * average_ref[at, lanes] + (1.0 - ema_keep) * new
            copy_ref[at, lanes] = new.astype(BF16)
        return carry

    lax.fori_loop(0, master_ref.shape[0] // strip, one, 0)


def run_update(filled, sums, master, moment_one, moment_two, average, nrm, gains, shifts, norm_one, norm_two):
    rows, width = master.shape
    step = rows // filled.shape[0]
    spec = pl.BlockSpec((step, width), lambda i, t: (i, 0))

    def whole(array):
        return pl.BlockSpec(array.shape, lambda i, t: (0,) * array.ndim)

    grid_spec = pltpu.PrefetchScalarGridSpec(
        num_scalar_prefetch=1,
        grid=(rows // step,),
        in_specs=[pl.BlockSpec((2, step, sums.shape[2]), lambda i, t: (0, i, 0))] + [spec] * 4
        + [whole(array) for array in (nrm, gains, shifts, norm_one, norm_two)],
        out_specs=[spec] * 6 + [whole(norm_one)] * 4,
    )
    full = jax.ShapeDtypeStruct(master.shape, F32)
    return pl.pallas_call(
        update_kernel,
        grid_spec=grid_spec,
        out_shape=[full] * 5 + [jax.ShapeDtypeStruct(master.shape, BF16)]
        + [jax.ShapeDtypeStruct(norm_one.shape, F32)] * 4,
        compiler_params=pltpu.CompilerParams(vmem_limit_bytes=24 << 20),
        name="update",
    )(filled, sums, master, moment_one, moment_two, average, nrm, gains, shifts, norm_one, norm_two)


def body(
    inputs,
    dense_inputs,
    lengths,
    owners,
    cotangent,
    master,
    moment_one,
    moment_two,
    average,
    norm_gain,
    norm_shift,
    norm_one,
    norm_two,
):
    width = inputs.shape[2]
    wides, narrows = lax.axis_size("wide"), lax.axis_size("narrow")
    depth = wides // 2
    own_rows = master.shape[0]
    block = 2 * own_rows
    capacity = own_rows * narrows // width
    places = slot_table(owners, capacity)
    act, dcv, res, block_out, input_grad, dense_grad, sums = run_chain(
        depth, block, places, lengths, master, inputs, dense_inputs, cotangent, norm_gain, norm_shift
    )
    owner = places // capacity
    compact = ((owner // 4) * 2 + owner % 2) * capacity + places % capacity
    parity = (lax.axis_index("wide") // 2) % 2
    handled = jnp.where((owner // 2) % 2 == parity, compact, -1).astype(jnp.int32)
    kept = 2 * (lax.axis_index("wide") % 2) + lax.axis_index("narrow") // 2
    handled = jnp.concatenate([handled, kept.astype(jnp.int32)[None]])
    grads = run_grads(wides * narrows * own_rows // 2, handled, act, dcv, res)
    reduced = run_reduce(depth // 2, block, grads)

    step = min(own_rows, 256)
    first = (lax.axis_index("wide") * narrows + lax.axis_index("narrow")) * own_rows
    slot_of_step = (first + step * jnp.arange(own_rows // step, dtype=jnp.int32)) // width
    filled = jnp.any(places[None, :] == slot_of_step[:, None], axis=1).astype(jnp.int32)
    updated = run_update(
        filled, reduced, master, moment_one, moment_two, average,
        sums, norm_gain, norm_shift, norm_one.transpose(1, 0, 2), norm_two.transpose(1, 0, 2),
    )
    return (
        block_out,
        input_grad,
        dense_grad,
        *updated[:6],
        *(values.transpose(1, 0, 2) for values in updated[6:]),
    )


def solution(mesh):
    rows = P(AXES, None)
    utterances = P(AXES, None, None)
    in_specs = (
        utterances, utterances, P(AXES), P(), utterances, rows, rows, rows, rows,
        P(), P(), P(), P(),
    )
    out_specs = (
        utterances, utterances, utterances, rows, rows, rows, rows, rows, rows,
        P(), P(), P(), P(),
    )
    return jax.shard_map(body, mesh=mesh, in_specs=in_specs, out_specs=out_specs, check_vma=False)
```

```python
import functools

import jax
import jax.numpy as jnp
from jax import lax
from jax.experimental import pallas as pl
from jax.experimental.pallas import tpu as pltpu
from jax.sharding import PartitionSpec as P

WLOW = 256
WMID = 384
K = 17
SUBS = 5
SOURCES = 6
STEP = 10
MARGIN = K // 2
EDGE = 16
UNIT = 64
F32 = jnp.float32
BF16 = jnp.bfloat16
MESH = pl.DeviceIdType.MESH
AXES = ("wide", "narrow")

norm_eps = 1e-05
beta_one = 0.9
beta_two = 0.999
adam_eps = 1e-08
rate_main = 0.02
rate_norm = 0.15
decay_main = 0.01
ema_keep = 0.8

NT = (((1,), (1,)), ((), ()))


def slot_table(owners, capacity):
    number = owners.shape[0]
    same_owner = owners[:, None] == owners[None, :]
    earlier = jnp.arange(number)[None, :] < jnp.arange(number)[:, None]
    ranking = jnp.sum(jnp.where(same_owner & earlier, 1, 0), axis=1)
    return (owners * capacity + ranking).astype(jnp.int32)


def source_pieces(half):
    pieces = []
    start = 0
    for width in (WLOW, WLOW, WLOW, WMID, WMID):
        parts = []
        stop = start + width
        while start < stop:
            chunk, lane = divmod(start, half)
            lanes = min(half - lane, stop - start)
            parts.append((chunk, lane, lanes))
            start += lanes
        pieces.append(parts)
    return pieces


class Place:
    def __init__(self, depth):
        wide = lax.axis_index("wide")
        narrow = lax.axis_index("narrow")
        self.depth = depth
        self.core = lax.rem(narrow, 2)
        self.y = narrow // 2
        self.x = lax.rem(wide, 2)
        self.z = wide // 2
        self.groups = depth * 4
        self.me = wide * 2 + self.y

    def at(self, z, x, y, core):
        return (z * 2 + x, y * 2 + core)

    def beside(self):
        return self.at(self.z + 1 - 2 * lax.rem(self.z, 2), self.x, self.y, self.core)

    def partner(self):
        return self.at(self.z, self.x, self.y, 1 - self.core)

    def over_x(self):
        return self.at(self.z, 1 - self.x, self.y, self.core)

    def over_y(self):
        return self.at(self.z, self.x, 1 - self.y, self.core)

    def up(self):
        return self.at(self.z + 1, self.x, self.y, self.core)

    def down(self):
        return self.at(self.z - 1, self.x, self.y, self.core)

    def far(self, turn):
        z = lax.rem(self.z + 1 + turn // 4, self.depth)
        return self.at(z, lax.rem(turn // 2, 2), lax.rem(turn, 2), self.core)

    def near(self):
        return (
            self.over_x(), self.over_y(), self.at(self.z, 1 - self.x, 1 - self.y, self.core)
        )

    def enter(self):
        barrier = pltpu.get_barrier_semaphore()

        def greet(device):
            pl.semaphore_signal(barrier, inc=1, device_id=device, device_id_type=MESH)

        for device in (self.partner(), self.over_x(), self.over_y()):
            greet(device)
        above, below = self.z + 1 < self.depth, self.z >= 1
        pl.when(above)(functools.partial(greet, self.up()))
        pl.when(below)(functools.partial(greet, self.down()))
        met = 3 + above.astype(jnp.int32) + below.astype(jnp.int32)
        pl.semaphore_wait(barrier, met)


class QuadPlace(Place):
    def __init__(self, depth):
        super().__init__(depth)
        self.parity = lax.rem(self.z, 2)
        self.z = self.z // 2

    def at(self, z, x, y, core):
        return ((2 * z + self.parity) * 2 + x, y * 2 + core)


def remote(src, dst, send_sem, recv_sem, device):
    return pltpu.make_async_remote_copy(
        src_ref=src,
        dst_ref=dst,
        send_sem=send_sem,
        recv_sem=recv_sem,
        device_id=device,
        device_id_type=MESH,
    )


def when(cond, action):
    if cond is None:
        action()
    else:
        pl.when(cond)(action)


def cut(block, share):
    units = block // UNIT
    small = max(1, units // share)
    return (units - 2 * small) // 2 * UNIT, small * UNIT


def steps(depth, body, first=0):
    if depth <= 4:
        for step in range(first, depth):
            body(step)
    else:
        def looped(step, carry):
            body(step)
            return carry

        if first == 0:
            body(0)
        lax.fori_loop(max(first, 1), depth, looped, 0)


def shares(rows, number):
    units = rows // UNIT
    out = []
    first = 0
    for index in range(number):
        count = units // number + (1 if index < units % number else 0)
        if count:
            out.append((first * UNIT, count * UNIT))
        first += count
    return out


def tree_sems(depth):
    dma = pltpu.SemaphoreType.DMA
    return [
        dma((depth, 2, 2)), dma((depth, 2)), dma((depth, 2, 4)), dma((depth, 4)),
        dma((depth, 2)), dma((depth, 2)), dma((depth, 2, 2)), dma((depth, 2, 2)),
        dma((depth, 2)), dma((depth, 2)), dma((depth, 2, 2)), dma((depth, 2, 2)),
        dma((6,)), dma((6,)),
    ]


def gather_bank(place, bank, block, sems, first_idle=lambda: None, second_idle=lambda: None):
    depth, z, x, y = place.depth, place.z, place.x, place.y
    large, small = cut(block, 9)
    (zab_s, zab_r, zcd_s, zcd_r, ax_s, ax_r, ay_s, ay_r, by_s, by_r, bx_s, bx_r, cd_s, cd_r) = sems
    pieces = shares(large, 2)
    runs = range(len(pieces))

    def rows(zz, xx, yy, first, count):
        begin = ((zz * 2 + xx) * 2 + yy) * (block // UNIT) + first // UNIT
        return bank.at[pl.ds(begin, count // UNIT)]

    def move(zz, xx, yy, first, count, send_sem, recv_sem, device):
        ref = rows(zz, xx, yy, first, count)
        return remote(ref, ref, send_sem, recv_sem, device)

    start_c, start_d = 2 * large, 2 * large + small
    over_x, over_y, up, down = place.over_x(), place.over_y(), place.up(), place.down()

    def sides(step):
        out = [(z - step, z - step >= 0)]
        if not (isinstance(step, int) and step == 0):
            out.append((z + step, z + step < depth))
        return out

    def both(step, action):
        for level, cond in sides(step):
            when(cond, functools.partial(action, level))

    def z_moves(step, run):
        out = []
        low, high = z - step, z + step
        for level, cond, device, way in (
            (low, (low >= 0) & (z + 1 < depth), up, 0),
            (high, (high < depth) & (z >= 1), down, 1),
        ):
            if run is not None:
                first, count = pieces[run]
                copy = move(
                    level, x, y, 2 * first, 2 * count, zab_s.at[level, way, run], zab_r.at[level, run], device
                )
                out.append((cond, copy))
                continue
            for index in range(4):
                copy = move(
                    level, index // 2, index % 2, start_c, 2 * small, zcd_s.at[level, way, index],
                    zcd_r.at[level, index], device,
                )
                out.append((cond, copy))
        return out

    def ax(level, run):
        first, count = pieces[run]
        return move(level, x, y, 2 * first, count, ax_s.at[level, run], ax_r.at[level, run], over_x)

    def by(level, run):
        first, count = pieces[run]
        return move(level, x, y, 2 * first + count, count, by_s.at[level, run], by_r.at[level, run], over_y)

    def ay(level, run, other):
        first, count = pieces[run]
        xx = 1 - x if other else x
        return move(level, xx, y, 2 * first, count, ay_s.at[level, run, other], ay_r.at[level, run, other], over_y)

    def bx(level, run, other):
        first, count = pieces[run]
        yy = 1 - y if other else y
        return move(
            level, x, yy, 2 * first + count, count, bx_s.at[level, run, other], bx_r.at[level, run, other], over_x
        )

    plane = [
        move(z, x, y, start_c, small, cd_s.at[0], cd_r.at[0], over_x),
        move(z, x, y, start_d, small, cd_s.at[1], cd_r.at[1], over_y),
        move(z, x, y, start_c, small, cd_s.at[2], cd_r.at[2], over_y),
        move(z, 1 - x, y, start_c, small, cd_s.at[3], cd_r.at[3], over_y),
        move(z, x, y, start_d, small, cd_s.at[4], cd_r.at[4], over_x),
        move(z, x, 1 - y, start_d, small, cd_s.at[5], cd_r.at[5], over_x),
    ]

    def run_step(step):
        home = isinstance(step, int) and step == 0
        if home:
            plane[0].start()
            plane[1].start()
        for run in runs:
            first, count = pieces[run]
            if not home:
                both(
                    step,
                    lambda level, run=run, first=first, count=count: move(
                        level, x, y, 2 * first, 2 * count, zab_s.at[level, 0, run], zab_r.at[level, run], up
                    ).wait_recv(),
                )
            for cond, copy in z_moves(step, run):
                when(cond, copy.start)

            def begin(level, run=run):
                ax(level, run).start()
                by(level, run).start()

            both(step, begin)
        if home:
            first_idle()
            plane[2].start()
            plane[4].start()
            plane[0].wait_recv()
            plane[3].start()
            plane[1].wait_recv()
            plane[5].start()
            for copy in plane[2:]:
                copy.wait_recv()
            for cond, copy in z_moves(step, None):
                when(cond, copy.start)
        for run in runs:
            def across(level, run=run):
                ay(level, run, 0).start()
                bx(level, run, 0).start()
                ax(level, run).wait_recv()
                ay(level, run, 1).start()
                by(level, run).wait_recv()
                bx(level, run, 1).start()

            both(step, across)
        if not home:
            def arrived(level):
                for index in range(4):
                    move(
                        level, x, y, start_c, 2 * small, zcd_s.at[level, 0, index],
                        zcd_r.at[level, index], up,
                    ).wait_recv()

            both(step, arrived)
            for cond, copy in z_moves(step, None):
                when(cond, copy.start)
        if home:
            second_idle()

    steps(depth, run_step)

    def drain(step):
        def finish(level):
            for run in runs:
                for other in range(2):
                    ay(level, run, other).wait_recv()
                    bx(level, run, other).wait_recv()
                    ay(level, run, other).wait_send()
                    bx(level, run, other).wait_send()
                ax(level, run).wait_send()
                by(level, run).wait_send()

        both(step, finish)
        for kind in list(runs) + [None]:
            for cond, copy in z_moves(step, kind):
                when(cond, copy.wait_send)

    steps(depth, drain)
    for copy in plane:
        copy.wait_send()


def strips(rows, body, carry=0):
    strip = 64

    def one(index, carry):
        return body(pl.ds(pl.multiple_of(index * strip, strip), strip), carry)

    return lax.fori_loop(0, rows // strip, one, carry, unroll=True)


def fold(values):
    return jnp.sum(values.reshape(-1, 8, values.shape[1]), axis=0)


def chain_kernel(
    depth, block,
    slot_ref, length_ref, master, own_x, own_dense, own_cot, gain_ref, shift_ref,
    act_out, dcv_out, res_out, blk_out, ig_out, dg_out, nrm_out,
    bank, act, dense, mask, cot, raw, side, pre4, slope, upown, upsend, uprecv, dcv, dsd, res, res_x, res_y, dgrecv,
    igrecv, stage, turned, nrm, blk, blksend, keep, ex_side, ex_last, ex_sub,
    load_sem, swap_s, swap_r, act_s, act_r, up_s, up_r, ex_s, ex_r, out_sem, far_s, far_r, near_s, near_r, own_sem,
    *tree,
):
    place = Place(depth)
    core, other = place.core, 1 - place.core
    partner, beside = place.partner(), place.beside()
    half = bank.shape[2]
    width = 2 * half
    frames = mask.shape[1]
    rows = 2 * frames
    chunks = dense.shape[0]
    pieces = source_pieces(half)
    inner = pl.ds(EDGE, frames)
    own_rows = block // 2
    load_rows = min(own_rows, rows)
    loads_of = own_rows // load_rows

    mats_in = []
    for part in range(loads_of):
        for h in range(2):
            mats_in.append(
                pltpu.make_async_copy(
                    master.at[pl.ds(part * load_rows, load_rows), pl.ds(h * half, half)],
                    side.at[part * 2 + h, pl.ds(0, load_rows)],
                    load_sem.at[part * 2 + h],
                )
            )
    x_in = [
        pltpu.make_async_copy(
            own_x.at[0, :, pl.ds(h * half, half)], act.at[0, h, core, inner], load_sem.at[6 + h]
        )
        for h in range(2)
    ]
    dense_in = [
        pltpu.make_async_copy(
            own_dense.at[0, :, pl.ds(chunk * half, half)], dense.at[chunk, core], load_sem.at[8 + chunk]
        )
        for chunk in range(chunks)
    ]
    ours_lanes = pl.ds(pl.multiple_of(core * half, half), half)
    theirs_lanes = pl.ds(pl.multiple_of(other * half, half), half)
    cot_in = pltpu.make_async_copy(own_cot.at[0, :, ours_lanes], cot.at[core], load_sem.at[8 + chunks])
    for copy in mats_in + x_in + dense_in + [cot_in]:
        copy.start()
    place.enter()
    base = place.me * (block // UNIT) + core * (own_rows // UNIT)
    units = load_rows // UNIT
    send_mats = []
    for part in range(loads_of):
        def narrow(unit, carry, part=part):
            at = pl.ds(pl.multiple_of(unit * UNIT, UNIT), UNIT)
            stage[part * units + unit] = side[part * 2 + other, at].astype(BF16)
            return carry

        def keep_own(unit, carry, part=part):
            at = pl.ds(pl.multiple_of(unit * UNIT, UNIT), UNIT)
            bank[base + part * units + unit] = side[part * 2 + core, at].astype(BF16)
            return carry

        mats_in[2 * part].wait()
        mats_in[2 * part + 1].wait()
        lax.fori_loop(0, units, narrow, 0, unroll=2)
        copy = remote(
            stage.at[pl.ds(part * units, units)], bank.at[pl.ds(base + part * units, units)],
            swap_s.at[9 + part], swap_r.at[9 + part], partner,
        )
        copy.start()
        send_mats.append(copy)
        lax.fori_loop(0, units, keep_own, 0, unroll=2)
    mask[core] = (
        lax.broadcasted_iota(jnp.int32, (frames, 128), 0) < length_ref[0]
    ).astype(F32)
    edge_zero = jnp.zeros((EDGE, half), BF16)

    def clear(section, carry):
        for u in range(2):
            for h in range(2):
                act[section, h, u, pl.ds(0, EDGE)] = edge_zero
                act[section, h, u, pl.ds(EDGE + frames, EDGE)] = edge_zero
            dcv[section, u, pl.ds(0, EDGE)] = edge_zero
            dcv[section, u, pl.ds(EDGE + frames, EDGE)] = edge_zero
        return carry

    lax.fori_loop(0, SUBS, clear, 0)
    for copy in send_mats:
        copy.wait()

    def prepare():
        for copy in x_in + dense_in + [cot_in]:
            copy.wait()
        low_mask = jnp.concatenate([mask[core].astype(BF16)] * (half // 128), axis=1)
        for h in range(2):
            act[0, h, core, inner] = act[0, h, core, inner] * low_mask
        for chunk in range(chunks):
            dense[chunk, core] = dense[chunk, core] * low_mask
        own = act.at[0, :, core, inner]
        swaps = [
            remote(own, own, swap_s.at[1], swap_r.at[1], partner),
            remote(dense.at[:, core], dense.at[:, core], swap_s.at[2], swap_r.at[2], partner),
            remote(mask.at[core], mask.at[core], swap_s.at[3], swap_r.at[3], partner),
            remote(own_cot.at[0, :, theirs_lanes], cot.at[core], swap_s.at[4], swap_r.at[4], partner),
        ]
        for copy in swaps:
            copy.start()
        return swaps

    def own_act(section):
        half_of = turned.at[lax.rem(section, 2)]
        return [
            pltpu.make_async_copy(half_of, act_out.at[section, 0, core], own_sem.at[section]),
            remote(
                half_of, act_out.at[section, 0, core], near_s.at[section], near_r.at[section], partner
            ),
            remote(
                half_of, act_out.at[section, 1, core], far_s.at[section], far_r.at[section], beside
            ),
        ]

    def pass_act(section):
        ref = act_out.at[section, 1, core]
        return remote(ref, ref, near_s.at[SUBS + section], near_r.at[SUBS + section], partner)

    def turn_act(section):
        turned[lax.rem(section, 2)] = jnp.concatenate(
            [act[section, core, u, inner] for u in range(2)], axis=0
        ).T
        for copy in own_act(section)[:2]:
            copy.start()

    def free_turned(section):
        copies = own_act(section)
        copies[0].wait()
        copies[1].wait_send()
        copies[2].wait_send()

    swaps = []

    def arrived():
        for copy in swaps:
            copy.wait()
        turn_act(0)
        own_act(0)[2].start()

    gather_bank(place, bank, block, tree, lambda: swaps.extend(prepare()), arrived)

    outs = []

    def put(src, dst):
        copy = pltpu.make_async_copy(src, dst, out_sem.at[len(outs)])
        copy.start()
        outs.append(copy)

    def far_dcv(section):
        return remote(
            dcv.at[section], dcv_out.at[section, 1],
            far_s.at[SUBS + section], far_r.at[SUBS + section], beside,
        )

    def keep_dcv(section):
        return pltpu.make_async_copy(
            dcv.at[section], dcv_out.at[section, 0], own_sem.at[SUBS + section]
        )

    def res_over(step):
        if step == 0:
            src, dst, device = res.at[pl.ds(2 * (1 - place.x), 2)], res_x, place.over_x()
        elif step == 1:
            src, dst, device = res_x.at[1 - place.y], res_y, place.over_y()
        else:
            src, dst, device = res_y, res_out.at[1], beside
        at = 2 * SUBS + step
        return remote(src, dst, far_s.at[at], far_r.at[at], device)

    def weight(matrix, first, count):
        begin = slot_ref[matrix] * (width // UNIT) + first // UNIT
        return jnp.concatenate([bank[begin + i] for i in range(count // UNIT)], axis=0)

    def valid(at):
        return jnp.concatenate([mask_rows(at)] * (half // 128), axis=1)

    def mask_rows(at):
        return mask[at.start // frames, pl.ds(pl.multiple_of(lax.rem(at.start, frames), 64), at.size)]

    def gain(index):
        return gain_ref[pl.ds(index, 1), ours_lanes]

    def bias(index):
        return shift_ref[pl.ds(index, 1), ours_lanes]

    def share(buffer, index, values):
        buffer[place.me] = values
        mine = buffer.at[place.me]

        def go(turn, carry):
            remote(mine, mine, ex_s.at[index, 1], ex_r.at[index, 1], place.far(turn)).start()
            return carry

        lax.fori_loop(0, place.groups - 4, go, 0, unroll=place.groups <= 16)
        for device in place.near():
            remote(mine, mine, ex_s.at[index, 0], ex_r.at[index, 0], device).start()

    def shared(buffer, index, between=lambda: None):
        for kind, number in ((0, 3), (1, place.groups - 4)):
            some = buffer.at[pl.ds(0, number)]
            copy = remote(some, some, ex_s.at[index, kind], ex_r.at[index, kind], place.over_x())
            copy.wait_recv()
            copy.wait_send()
            if kind == 0:
                between()
        return buffer[...]

    def total_of(values):
        return jnp.sum(values, axis=0, keepdims=True)

    def counted():
        def add(at, carry):
            return carry + fold(valid(at))

        return total_of(strips(rows, add, jnp.zeros((8, half), F32)))

    def moments(load, count):
        pivot = load(pl.ds(0, 8))[0:1]

        def add(at, carry):
            first, second = carry
            valid_now = valid(at)
            off = (load(at) - pivot) * valid_now
            return first + fold(off), second + fold(off * off)

        zero = jnp.zeros((8, half), F32)
        first, second = strips(rows, add, (zero, zero))
        first, second = total_of(first), total_of(second)
        return first + count * pivot, jnp.maximum(second - first * first / count, 0.0)

    def merge(count, total, squares):
        frame_total = jnp.sum(count, axis=0)
        mean = jnp.sum(total, axis=0) / frame_total
        shift = total / count - mean[None]
        variance = jnp.sum(squares + count * shift * shift, axis=0) / frame_total
        return mean[None], lax.rsqrt(variance + norm_eps)[None], frame_total[None]

    def save(index, mean, inverse):
        scale = gain(index) * inverse
        keep[0, pl.ds(index, 1)] = inverse
        keep[1, pl.ds(index, 1)] = mean * inverse
        keep[2, pl.ds(index, 1)] = scale
        keep[3, pl.ds(index, 1)] = bias(index) - mean * scale

    def kept(row, index):
        return keep[row, pl.ds(index, 1)]

    count = counted()
    def side_branches():
        totals, squares = [], []
        for index in range(SOURCES):
            value = None
            if index < SOURCES - 1:
                for chunk, lane, lanes in pieces[index]:
                    left = dense[chunk].reshape(rows, half)[:, lane : lane + lanes]
                    right = weight(SUBS * K + chunk // 2, (chunk % 2) * half + lane, lanes)
                    term = jnp.dot(left, right, preferred_element_type=F32)
                    value = term if value is None else value + term
            else:
                for h in range(2):
                    left = jnp.concatenate([act[0, h, u, inner] for u in range(2)], axis=0)
                    term = jnp.dot(left, weight(SUBS * K + 3, h * half, half), preferred_element_type=F32)
                    value = term if value is None else value + term
            side[index] = value
            total, square = moments(lambda at, index=index: side[index, at], count)
            totals.append(total)
            squares.append(square)
        fill = jnp.zeros((3, half), F32)
        share(ex_side, 0, jnp.concatenate([count] + totals + squares + [fill], axis=0))

    def convolve(section, h, first):
        value = None
        for k in range(K):
            left = jnp.concatenate(
                [act[section, h, u, pl.ds(EDGE - MARGIN + k, frames)] for u in range(2)], axis=0
            )
            term = jnp.dot(
                left, weight(section * K + k, h * half, half), preferred_element_type=F32
            )
            value = term if value is None else value + term
            if k % 2 == 1 or k == K - 1:
                if first and k == 1:
                    raw[section] = value
                else:
                    raw[section] += value
                value = None

    def swap_act(section):
        own = act.at[section, core, :, inner]
        return remote(own, own, act_s.at[section], act_r.at[section], partner)

    def forward(section, last):
        convolve(section, core, True)
        if isinstance(section, int):
            if section > 0:
                swap_act(section).wait_recv()
        else:
            pl.when(section > 0)(swap_act(section).wait_recv)
        convolve(section, other, False)
        total, square = moments(lambda at: raw[section, at], count)
        buffer = ex_sub.at[lax.rem(section, 2)]
        share(buffer, 1 + section, jnp.concatenate([count, total, square, jnp.zeros_like(count)], axis=0))

        def pre_side():
            parts = shared(ex_side, 0)
            for index in range(SOURCES):
                mean, inverse, _ = merge(
                    parts[:, 0], parts[:, 1 + index], parts[:, 1 + SOURCES + index]
                )
                save(SUBS + index, mean, inverse)
            scales = [kept(2, SUBS + index) for index in range(SOURCES)]
            offset = sum(kept(3, SUBS + index) for index in range(SOURCES))

            def add(at, carry):
                before = offset
                for index in range(SOURCES):
                    before = before + side[index, at] * scales[index]
                pre4[at] = before
                return carry

            strips(rows, add)

        def background():
            own_act(section - 1)[2].wait_recv()
            pass_act(section - 1).start()
            if isinstance(section, int):
                free_turned(section - 2)
            else:
                pl.when(section > 1)(functools.partial(free_turned, section - 2))
            turn_act(section)

        if isinstance(section, int):
            background()
            parts = shared(buffer, 1 + section, own_act(section)[2].start)
        else:
            pl.when(section == 0)(side_branches)
            pl.when(section > 0)(background)
            pl.when(section == 1)(pre_side)
            parts = shared(
                buffer, 1 + section, lambda: pl.when(section > 0)(own_act(section)[2].start)
            )
        mean, inverse, frame_total = merge(parts[:, 0], parts[:, 1], parts[:, 2])
        save(section, mean, inverse)
        scale, offset = kept(2, section), kept(3, section)

        def activate(at, carry):
            before = raw[section, at] * scale + offset
            if last:
                before = before + pre4[at]
                pre4[at] = before
            hidden = (before * jax.nn.sigmoid(before) * valid(at)).astype(BF16)
            u = at.start // frames
            first = pl.multiple_of(lax.rem(at.start, frames), 64)
            if last:
                @pl.when(u == core)
                def _():
                    blk[core, pl.ds(first, at.size)] = hidden

                @pl.when(u != core)
                def _():
                    blksend[pl.ds(first, at.size)] = hidden
            else:
                act[section + 1, core, u, pl.ds(pl.multiple_of(first + EDGE, EDGE), at.size)] = hidden
            return carry

        strips(rows, activate)
        if not last:
            swap_act(section + 1).start()
        return frame_total

    def looped(section, carry):
        forward(section, False)
        return carry

    lax.fori_loop(0, SUBS - 1, looped, 0)
    frame_total = forward(SUBS - 1, True)
    blk_copy = remote(blksend, blk.at[core], swap_s.at[5], swap_r.at[5], partner)
    blk_copy.start()
    for section in range(1, SUBS):
        swap_act(section).wait_send()
    for section in (SUBS - 2, SUBS - 1):
        free_turned(section)

    def hat_of(values, index):
        return values * kept(0, index) - kept(1, index)

    def back_half(section, h):
        total = None
        value = None
        for k in range(K):
            left = jnp.concatenate(
                [dcv[section, u, pl.ds(EDGE + MARGIN - k, frames)] for u in range(2)], axis=0
            )
            term = lax.dot_general(
                left, weight(section * K + k, h * half, half), NT, preferred_element_type=F32
            )
            value = term if value is None else value + term
            if k % 2 == 1 or k == K - 1:
                total = value if total is None else total + value
                value = None
        return total

    def up_copy(section):
        slot = lax.rem(section, 2)
        return remote(upsend, uprecv.at[slot], up_s.at[slot], up_r.at[slot], partner)

    def backward(section):
        upsend[...] = back_half(section, other)
        up_copy(section).start()
        upown[...] = back_half(section, core)

    def slopes(section, upstream, before_of, others, target):
        sources = [(lambda at: raw[section, at], section)] + others

        def one(at, carry):
            before = before_of(at)
            sigmoid = jax.nn.sigmoid(before)
            now = upstream(at) * valid(at) * (sigmoid * (1.0 + before * (1.0 - sigmoid)))
            target[at] = now
            out = [carry[0] + fold(now)]
            for (load, index), so_far in zip(sources, carry[1:]):
                out.append(so_far + fold(now * hat_of(load(at), index)))
            return tuple(out)

        zero = jnp.zeros((8, half), F32)
        return [total_of(value) for value in strips(rows, one, (zero,) * (1 + len(sources)))]

    def branch(source, load, index, shift_sum, gain_sum, store):
        scale = kept(2, index)
        shift_mean, gain_mean = shift_sum / frame_total, gain_sum / frame_total

        def one(at, carry):
            value = source[at] - shift_mean - hat_of(load(at), index) * gain_mean
            store(at, (valid(at) * scale * value).astype(BF16))
            return carry

        strips(rows, one)

    def conv_branch(source, section, shift_sum, gain_sum):
        def store(at, value):
            first = pl.multiple_of(lax.rem(at.start, frames) + EDGE, EDGE)
            dcv[section, at.start // frames, pl.ds(first, at.size)] = value

        branch(source, lambda at: raw[section, at], section, shift_sum, gain_sum, store)
        far_dcv(section).start()
        keep_dcv(section).start()

    def cot_at(at):
        return cot[
            at.start // frames, pl.ds(pl.multiple_of(lax.rem(at.start, frames), 64), at.size)
        ].astype(F32)

    sums = slopes(
        SUBS - 1, cot_at, lambda at: pre4[at],
        [(lambda at, index=index: side[index, at], SUBS + index) for index in range(SOURCES)],
        pre4,
    )
    share(ex_last, SUBS + 1, jnp.concatenate(sums, axis=0))
    sums = jnp.sum(shared(ex_last, SUBS + 1), axis=0)
    shift_sum = sums[0:1]
    conv_branch(pre4, SUBS - 1, shift_sum, sums[1:2])
    nrm[core] = jnp.zeros_like(nrm[0])
    nrm[core, pl.ds(SUBS - 1, 1 + SOURCES)] = sums[1:]
    nrm[core, pl.ds(SUBS + SOURCES + SUBS - 1, 1)] = shift_sum
    backward(SUBS - 1)

    def side_grads():
        for index in range(SOURCES):
            def store(at, value, index=index):
                dsd[index, at] = value

            branch(
                pre4, lambda at, index=index: side[index, at], SUBS + index, shift_sum,
                sums[2 + index : 3 + index], store,
            )

    theirs = pl.multiple_of(other * frames, frames)
    ours = pl.multiple_of(core * frames, frames)
    dg_copy = remote(
        side.at[:, pl.ds(theirs, frames)], dgrecv, swap_s.at[6], swap_r.at[6], partner
    )

    def dense_grads():
        for index in range(SOURCES - 1):
            for chunk, lane, lanes in pieces[index]:
                right = weight(SUBS * K + chunk // 2, (chunk % 2) * half + lane, lanes)
                side[chunk, :, pl.ds(lane, lanes)] = lax.dot_general(
                    dsd[index], right, NT, preferred_element_type=F32
                )
        dg_copy.start()

    def residual_grads():
        rows_of = [[] for _ in range(chunks)]
        for index, parts in enumerate(pieces):
            for chunk, lane, lanes in parts:
                rows_of[chunk].append((lane, lanes, index))
        for chunk in range(chunks):
            turned = dense[chunk].reshape(rows, half).T
            for lane, lanes, index in rows_of[chunk]:
                res[chunk // 2, pl.ds((chunk % 2) * half + lane, lanes)] = jnp.dot(
                    turned[lane : lane + lanes], dsd[index], preferred_element_type=F32
                ).astype(BF16)
        for h in range(2):
            turned = jnp.concatenate([act[0, h, u, inner] for u in range(2)], axis=0).T
            res[3, pl.ds(h * half, half)] = jnp.dot(
                turned, dsd[SOURCES - 1], preferred_element_type=F32
            ).astype(BF16)

    dg_puts = [
        pltpu.make_async_copy(
            dgrecv.at[chunk], dg_out.at[0, :, pl.ds(chunk * half, half)], load_sem.at[chunk]
        )
        for chunk in range(chunks)
    ]

    def finish_dense():
        dg_copy.wait()
        own_valid = jnp.concatenate([mask[core]] * (half // 128), axis=1)
        for chunk in range(chunks):
            dgrecv[chunk] = (dgrecv[chunk] + side[chunk, pl.ds(ours, frames)]) * own_valid
            dg_puts[chunk].start()

    def looped_back(turn, carry):
        section = SUBS - 2 - turn
        copy = up_copy(section + 1)
        copy.wait()
        slot = lax.rem(section + 1, 2)
        scale, offset = kept(2, section), kept(3, section)
        sums_now = slopes(
            section, lambda at: upown[at] + uprecv[slot, at],
            lambda at: raw[section, at] * scale + offset, [], slope,
        )
        zero = jnp.zeros((2, half), F32)
        buffer = ex_sub.at[lax.rem(section, 2)]
        share(buffer, SUBS + 2 + section, jnp.concatenate(sums_now + [zero], axis=0))

        @pl.when(section == SUBS - 2)
        def _():
            side_grads()
            residual_grads()
            res_over(0).start()
            dense_grads()

        @pl.when(section == SUBS - 3)
        def _():
            res_over(0).wait_recv()
            for index in range(2):
                total = res[2 * place.x + index].astype(F32) + res_x[index].astype(F32)
                res_x[index] = total.astype(BF16)
            res_over(1).start()
            finish_dense()
            own_act(SUBS - 1)[2].wait_recv()
            pass_act(SUBS - 1).start()

        @pl.when(section == SUBS - 4)
        def _():
            res_over(1).wait_recv()
            res_y[...] = (res_y[...].astype(F32) + res_x[place.y].astype(F32)).astype(BF16)

        sums_now = jnp.sum(shared(buffer, SUBS + 2 + section), axis=0)
        pl.when(section == SUBS - 4)(lambda: res_over(2).start())
        conv_branch(slope, section, sums_now[0:1], sums_now[1:2])
        nrm[core, pl.ds(section, 1)] = sums_now[1:2]
        nrm[core, pl.ds(SUBS + SOURCES + section, 1)] = sums_now[0:1]

        @pl.when(section > 0)
        def _():
            backward(section)

        return carry

    lax.fori_loop(0, SUBS - 1, looped_back, 0)
    put(res_y, res_out.at[0])
    nrm_copy = remote(nrm.at[core], nrm.at[core], swap_s.at[7], swap_r.at[7], partner)
    nrm_copy.start()
    for h in range(2):
        uprecv[h] = back_half(0, h) + lax.dot_general(
            dsd[SOURCES - 1], weight(SUBS * K + 3, h * half, half), NT, preferred_element_type=F32
        )
    ig_copy = remote(
        uprecv.at[:, pl.ds(theirs, frames)], igrecv, swap_s.at[8], swap_r.at[8], partner
    )
    ig_copy.start()
    own_valid = jnp.concatenate([mask[core]] * (half // 128), axis=1)
    blk_copy.wait()
    nrm_copy.wait()
    put(nrm, nrm_out)
    ig_copy.wait()
    for h in range(2):
        igrecv[h] = (igrecv[h] + uprecv[h, pl.ds(ours, frames)]) * own_valid
        put(igrecv.at[h], ig_out.at[0, :, pl.ds(h * half, half)])
        put(blk.at[h], blk_out.at[0, :, pl.ds(h * half, half)])
    for section in range(SUBS):
        own_act(section)[1].wait_recv()
        pass_act(section).wait()
        far_dcv(section).wait()
        keep_dcv(section).wait()
    res_over(0).wait_send()
    res_over(1).wait_send()
    res_over(2).wait()
    for copy in outs + dg_puts:
        copy.wait()


def run_chain(depth, block, places, lengths, master, x, dense, cot, gains, shifts):
    frames, width = x.shape[1:]
    half = width // 2
    rows = 2 * frames
    chunks = dense.shape[2] // half
    padded = frames + 2 * EDGE
    groups = depth * 4
    dma = pltpu.SemaphoreType.DMA
    anywhere = pl.BlockSpec(memory_space=pl.ANY)
    vmem = pl.BlockSpec(memory_space=pltpu.VMEM)
    smem = pl.BlockSpec(memory_space=pltpu.SMEM)
    out_shape = [
        jax.ShapeDtypeStruct((SUBS, 2, 2, half, rows), BF16),
        jax.ShapeDtypeStruct((SUBS, 2, 2, padded, half), BF16),
        jax.ShapeDtypeStruct((2, width, half), BF16),
        jax.ShapeDtypeStruct(x.shape, BF16),
        jax.ShapeDtypeStruct(x.shape, F32),
        jax.ShapeDtypeStruct(dense.shape, F32),
        jax.ShapeDtypeStruct((2, 16, half), F32),
    ]
    scratch = [
        pltpu.VMEM((groups * block // UNIT, UNIT, half), BF16),
        pltpu.VMEM((SUBS, 2, 2, padded, half), BF16),
        pltpu.VMEM((chunks, 2, frames, half), BF16),
        pltpu.VMEM((2, frames, 128), F32),
        pltpu.VMEM((2, frames, half), BF16),
        pltpu.VMEM((SUBS, rows, half), F32),
        pltpu.VMEM((SOURCES, rows, half), F32),
        pltpu.VMEM((rows, half), F32),
        pltpu.VMEM((rows, half), F32),
        pltpu.VMEM((rows, half), F32),
        pltpu.VMEM((rows, half), F32),
        pltpu.VMEM((2, rows, half), F32),
        pltpu.VMEM((SUBS, 2, padded, half), BF16),
        pltpu.VMEM((SOURCES, rows, half), BF16),
        pltpu.VMEM((4, width, half), BF16),
        pltpu.VMEM((2, width, half), BF16),
        pltpu.VMEM((width, half), BF16),
        pltpu.VMEM((chunks, frames, half), F32),
        pltpu.VMEM((2, frames, half), F32),
        pltpu.VMEM((block // 2 // UNIT, UNIT, half), BF16),
        pltpu.VMEM((2, half, rows), BF16),
        pltpu.VMEM((2, 16, half), F32),
        pltpu.VMEM((2, frames, half), BF16),
        pltpu.VMEM((frames, half), BF16),
        pltpu.VMEM((4, 16, half), F32),
        pltpu.VMEM((groups, 16, half), F32),
        pltpu.VMEM((groups, 8, half), F32),
        pltpu.VMEM((2, groups, 4, half), F32),
        dma((9 + chunks,)),
        dma((12,)), dma((12,)),
        dma((SUBS,)), dma((SUBS,)),
        dma((2,)), dma((2,)),
        dma((2 * SUBS + 1, 2)), dma((2 * SUBS + 1, 2)),
        dma((10 + chunks,)),
        dma((2 * SUBS + 3,)), dma((2 * SUBS + 3,)),
        dma((2 * SUBS,)), dma((2 * SUBS,)),
        dma((2 * SUBS,)),
    ] + tree_sems(depth)
    return pl.pallas_call(
        functools.partial(chain_kernel, depth, block),
        out_shape=out_shape,
        in_specs=[smem] * 2 + [anywhere] * 4 + [vmem] * 2,
        out_specs=[anywhere] * len(out_shape),
        scratch_shapes=scratch,
        compiler_params=pltpu.CompilerParams(
            collective_id=1, has_side_effects=True, vmem_limit_bytes=63 << 20
        ),
        cost_estimate=pl.CostEstimate(
            flops=4 * SUBS * K * rows * width * half, bytes_accessed=16 << 20, transcendentals=0
        ),
        name="chain",
    )(places, lengths, master, x, dense, cot, gains, shifts)


def grad_kernel(slot_ref, act_ref, dcv_ref, res_ref, out_ref, stage, count, sems):
    section = pl.program_id(0)
    half = act_ref.shape[3]
    width = 2 * half
    frames = act_ref.shape[4] // 2
    ring = stage.shape[0]

    @pl.when(section == 0)
    def _():
        count[0] = 0

    def slot_copy(place, slot):
        out = out_ref.at[pl.ds(pl.multiple_of(slot * width, 16), width)]
        return pltpu.make_async_copy(stage.at[place], out, sems.at[place])

    def emit(matrix, compute):
        slot = slot_ref[matrix]

        @pl.when(slot >= 0)
        def _():
            turn = count[0]
            place = lax.rem(turn, ring)
            pl.when(turn >= ring)(slot_copy(place, 0).wait)
            stage[place] = compute().astype(BF16)
            slot_copy(place, slot).start()
            count[0] = turn + 1

    for k in range(K):
        def conv(k=k):
            total = None
            for pair in range(2):
                right = jnp.concatenate(
                    [dcv_ref[0, pair, u, pl.ds(EDGE + MARGIN - k, frames)] for u in range(2)], axis=0
                )
                left = act_ref[0, pair].reshape(width, 2 * frames)
                term = jnp.dot(left, right, preferred_element_type=F32)
                total = term if total is None else total + term
            return total

        emit(section * K + k, conv)

    @pl.when(section == SUBS - 1)
    def _():
        for index in range(4):
            here = slot_ref[SUBS * K + 4] == index
            emit(
                SUBS * K + index,
                lambda here=here: jnp.where(
                    here, res_ref[0].astype(F32) + res_ref[1].astype(F32), 0.0
                ),
            )
        turns = count[0]

        def finish(place, carry):
            pl.when(place < turns)(slot_copy(place, 0).wait)
            return carry

        lax.fori_loop(0, ring, finish, 0)


def run_grads(total_rows, places, act, dcv, res):
    half = act.shape[3]
    ring = 8
    grid_spec = pltpu.PrefetchScalarGridSpec(
        num_scalar_prefetch=1,
        grid=(SUBS,),
        in_specs=[
            pl.BlockSpec((1,) + act.shape[1:], lambda s, t: (s, 0, 0, 0, 0)),
            pl.BlockSpec((1,) + dcv.shape[1:], lambda s, t: (s, 0, 0, 0, 0)),
            pl.BlockSpec(res.shape, lambda s, t: (0, 0, 0)),
        ],
        out_specs=pl.BlockSpec(memory_space=pl.ANY),
        scratch_shapes=[
            pltpu.VMEM((ring, 2 * half, half), BF16),
            pltpu.SMEM((1,), jnp.int32),
            pltpu.SemaphoreType.DMA((ring,)),
        ],
    )
    return pl.pallas_call(
        grad_kernel,
        grid_spec=grid_spec,
        out_shape=jax.ShapeDtypeStruct((total_rows, half), BF16),
        compiler_params=pltpu.CompilerParams(vmem_limit_bytes=60 << 20),
        name="weight_grads",
    )(places, act, dcv, res)


def reduce_kernel(
    depth, block, grads, out, l_ay, l_ax, l_bx, l_by, l_zab, l_zcd, l_c, l_d,
    o_cross, o_line, o_plane, final, result,
    cross_sem, line_sem, plane_sem, out_sem, swap_s, swap_r, ay_s, ay_r, ax_s, ax_r, bx_s, bx_r, by_s, by_r,
    zab_s, zab_r, zcd_s, zcd_r, cd_s, cd_r,
):
    place = QuadPlace(depth)
    z, x, y, core = place.z, place.x, place.y, place.core
    large, small = cut(block, 16)
    start_b, start_c, start_d = large, 2 * large, 2 * large + small
    over_x, over_y, up, down = place.over_x(), place.over_y(), place.up(), place.down()
    pieces = shares(large, 2)
    runs = range(len(pieces))

    def rows(zz, xx, yy, first, count):
        begin = pl.multiple_of(((zz * 2 + xx) * 2 + yy) * block + first, 16)
        return grads.at[pl.ds(begin, count)]

    def part(run):
        return pl.ds(*pieces[run])

    def ay(level, other_x, run):
        xx = 1 - x if other_x else x
        first, count = pieces[run]
        return remote(
            rows(level, xx, 1 - y, first, count), l_ay.at[level, other_x, part(run)],
            ay_s.at[level, other_x, run], ay_r.at[level, other_x, run], over_y,
        )

    def bx(level, other_y, run):
        yy = 1 - y if other_y else y
        first, count = pieces[run]
        return remote(
            rows(level, 1 - x, yy, start_b + first, count), l_bx.at[level, other_y, part(run)],
            bx_s.at[level, other_y, run], bx_r.at[level, other_y, run], over_x,
        )

    def ax(level, run):
        return remote(
            l_ay.at[level, 1, part(run)], l_ax.at[level, part(run)],
            ax_s.at[level, run], ax_r.at[level, run], over_x,
        )

    def by(level, run):
        return remote(
            l_bx.at[level, 1, part(run)], l_by.at[level, part(run)],
            by_s.at[level, run], by_r.at[level, run], over_y,
        )

    def own_cross(level):
        return [
            pltpu.make_async_copy(rows(level, 1 - x, y, 0, large), o_cross.at[level, 0], cross_sem.at[level, 0]),
            pltpu.make_async_copy(rows(level, x, 1 - y, start_b, large), o_cross.at[level, 1], cross_sem.at[level, 1]),
        ]

    def own_line(level):
        return [
            pltpu.make_async_copy(rows(level, x, y, index * large, large), o_line.at[level, index], line_sem.at[level, index])
            for index in range(2)
        ]

    def own_plane(level):
        return [
            pltpu.make_async_copy(
                rows(level, index // 2, index % 2, start_c, 2 * small),
                o_plane.at[level, index], plane_sem.at[level, index],
            )
            for index in range(4)
        ]

    def add(target, others, count, keep=None):
        strip = UNIT

        def one(index, carry):
            at = pl.ds(pl.multiple_of(index * strip, strip), strip)
            value = target[at].astype(F32)
            for ref in others:
                value = value + ref[at].astype(F32)
            if keep is None:
                target[at] = value.astype(BF16)
            else:
                keep[at] = value
            return carry

        lax.fori_loop(0, count // strip, one, 0)

    def sides(step):
        out = [(z - step, z - step >= 0)]
        if not (isinstance(step, int) and step == 0):
            out.append((z + step, z + step < depth))
        return out

    def both(step, action):
        for level, cond in sides(step):
            when(cond, functools.partial(action, level))

    def backwards(body, first, last):
        if depth <= 4:
            for step in range(first, last - 1, -1):
                body(step)
        else:
            def looped(turn, carry):
                body(first - turn)
                return carry

            lax.fori_loop(0, first - last + 1, looped, 0)

    def leaf(step, other, run):
        def go(level):
            ay(level, other, run).start()
            bx(level, other, run).start()

        both(step, go)

    def fetch(step):
        def go(level):
            for copy in own_cross(level) + own_line(level):
                copy.start()

        both(step, go)

    def entry_of(level, way):
        at_home = (z - 1 == level) if way == 0 else (z + 1 == level)
        return level if way == 0 else level + (depth - level) * at_home.astype(jnp.int32)

    def beyond(way):
        return z + 1 < depth if way == 0 else z >= 1

    def zcd(level, way, index, leaf_copy):
        entry = entry_of(level, way)
        if leaf_copy:
            src = rows(level, index // 2, index % 2, start_c, 2 * small)
        else:
            src = l_zcd.at[level, index]
        return remote(
            src, l_zcd.at[entry, index], zcd_s.at[level, index], zcd_r.at[entry, index],
            down if way == 0 else up,
        )

    def zcd_arrived(entry, index):
        ref = l_zcd.at[entry, index]
        remote(ref, ref, zcd_s.at[0, index], zcd_r.at[entry, index], up).wait_recv()

    def lines(step):
        return ((0, z - step, z - step >= 0), (1, z + step, z + step < depth))

    def plane_step(step):
        for way, level, cond in lines(step):
            def go(way=way, level=level):
                @pl.when(beyond(way))
                def _():
                    copies = own_plane(level)
                    for copy in copies:
                        copy.start()
                    for index in range(4):
                        zcd_arrived(level, index)
                        copies[index].wait()
                        add(l_zcd.at[level, index], [o_plane.at[level, index]], 2 * small)
                        zcd(level, way, index, False).start()

                @pl.when(jnp.logical_not(beyond(way)))
                def _():
                    for index in range(4):
                        zcd(level, way, index, True).start()

            when(cond, go)

    def zab(level, way, run):
        entry = entry_of(level, way)
        return [
            remote(
                landing.at[level, part(run)], l_zab.at[entry, index, part(run)],
                zab_s.at[level, index, run], zab_r.at[entry, index, run], down if way == 0 else up,
            )
            for index, landing in enumerate((l_ax, l_by))
        ]

    def zab_arrived(entry, index, run):
        ref = l_zab.at[entry, index, part(run)]
        remote(ref, ref, zab_s.at[0, index, run], zab_r.at[entry, index, run], up).wait_recv()

    def across(run):
        def go(level):
            count = pieces[run][1]
            copies = own_cross(level)
            ay(level, 1, run).wait_recv()
            if run == 0:
                copies[0].wait()
            add(l_ay.at[level, 1, part(run)], [o_cross.at[level, 0, part(run)]], count)
            ax(level, run).start()
            bx(level, 1, run).wait_recv()
            if run == 0:
                copies[1].wait()
            add(l_bx.at[level, 1, part(run)], [o_cross.at[level, 1, part(run)]], count)
            by(level, run).start()

        return go

    def line_step(step, run):
        count = pieces[run][1]
        for way, level, cond in lines(step):
            def go(way=way, level=level):
                copies = own_line(level)
                hops = zab(level, way, run)
                for index, (first_hop, second_hop, first_land, second_land) in enumerate(
                    ((ay, ax, l_ay, l_ax), (bx, by, l_bx, l_by))
                ):
                    first_hop(level, 0, run).wait_recv()
                    second_hop(level, run).wait_recv()
                    if run == 0:
                        copies[index].wait()
                    target = second_land.at[level, part(run)]
                    terms = [first_land.at[level, 0, part(run)], o_line.at[level, index, part(run)]]

                    @pl.when(beyond(way))
                    def _(index=index, target=target, terms=terms):
                        zab_arrived(level, index, run)
                        add(target, terms + [l_zab.at[level, index, part(run)]], count)

                    @pl.when(jnp.logical_not(beyond(way)))
                    def _(target=target, terms=terms):
                        add(target, terms, count)

                    hops[index].start()

            when(cond, go)

    unrolled = depth <= 4
    place.enter()
    for run in runs:
        leaf(depth - 1, 1, run)
    if not unrolled:
        for run in runs:
            leaf(depth - 1, 0, run)
    fetch(depth - 1)

    def turn(step):
        plane_step(step)
        for run in runs:
            if unrolled and step == depth - 1:
                leaf(step, 0, run)
            both(step, across(run))
        for run in runs:
            leaf(step - 1, 1, run)
        fetch(step - 1)
        for run in runs:
            line_step(step, run)
            leaf(step - 1, 0, run)

    backwards(turn, depth - 1, 1)

    above, below = z + 1 < depth, z >= 1
    copies = own_plane(z)
    for copy in copies:
        copy.start()
    for index in range(4):
        pl.when(above)(functools.partial(zcd_arrived, z, index))
        pl.when(below)(functools.partial(zcd_arrived, depth, index))
        copies[index].wait()
        target = o_plane.at[z, index]
        for cond, entries in (
            (above & below, (z, depth)), (above & jnp.logical_not(below), (z,)), (jnp.logical_not(above), (depth,))
        ):
            @pl.when(cond)
            def _(entries=entries, target=target, index=index):
                add(target, [l_zcd.at[entry, index] for entry in entries], 2 * small)

    def block_at(xx, yy, first):
        return o_plane.at[z, xx * 2 + yy, pl.ds(first, small)]

    plane = [
        remote(block_at(1 - x, 1 - y, 0), l_c.at[1], cd_s.at[0], cd_r.at[0], over_y),
        remote(block_at(x, 1 - y, 0), l_c.at[0], cd_s.at[1], cd_r.at[1], over_y),
        remote(block_at(1 - x, 1 - y, small), l_d.at[1], cd_s.at[2], cd_r.at[2], over_x),
        remote(block_at(1 - x, y, small), l_d.at[0], cd_s.at[3], cd_r.at[3], over_x),
        remote(l_c.at[1], l_c.at[2], cd_s.at[4], cd_r.at[4], over_x),
        remote(l_d.at[1], l_d.at[2], cd_s.at[5], cd_r.at[5], over_y),
    ]
    for copy in plane[:4]:
        copy.start()
    for run in runs:
        both(0, across(run))
    plane[0].wait_recv()
    add(l_c.at[1], [block_at(1 - x, y, 0)], small)
    plane[4].start()
    plane[2].wait_recv()
    add(l_d.at[1], [block_at(x, 1 - y, small)], small)
    plane[5].start()

    copies = own_line(z)
    for run in runs:
        first, count = pieces[run]
        for index, (first_hop, second_hop, first_land, second_land) in enumerate(
            ((ay, ax, l_ay, l_ax), (bx, by, l_bx, l_by))
        ):
            first_hop(z, 0, run).wait_recv()
            second_hop(z, run).wait_recv()
            if run == 0:
                copies[index].wait()
            terms = [first_land.at[z, 0, part(run)], o_line.at[z, index, part(run)]]
            target = final.at[pl.ds(index * large + first, count)]
            pl.when(above)(functools.partial(zab_arrived, z, index, run))
            pl.when(below)(functools.partial(zab_arrived, depth, index, run))
            for cond, entries in (
                (above & below, (z, depth)), (above & jnp.logical_not(below), (z,)), (jnp.logical_not(above), (depth,))
            ):
                @pl.when(cond)
                def _(entries=entries, terms=terms, target=target, index=index, land=second_land, run=run, count=count):
                    more = [l_zab.at[entry, index, part(run)] for entry in entries]
                    add(land.at[z, part(run)], terms + more, count, keep=target)

    for copy in (plane[1], plane[3], plane[4], plane[5]):
        copy.wait_recv()
    add(block_at(x, y, 0), [l_c.at[0], l_c.at[2]], small, keep=final.at[pl.ds(start_c, small)])
    add(block_at(x, y, small), [l_d.at[0], l_d.at[2]], small, keep=final.at[pl.ds(start_d, small)])
    own_rows = block // 2
    theirs = final.at[pl.ds(pl.multiple_of((1 - core) * own_rows, 16), own_rows)]
    mine = final.at[pl.ds(pl.multiple_of(core * own_rows, 16), own_rows)]
    cross = remote(theirs, result, swap_s.at[0], swap_r.at[0], place.partner())
    cross.start()
    local = pltpu.make_async_copy(mine, out.at[core], out_sem.at[0])
    local.start()

    def drain(step):
        def go(level):
            for run in runs:
                for other in range(2):
                    ay(level, other, run).wait_send()
                    bx(level, other, run).wait_send()
                ax(level, run).wait_send()
                by(level, run).wait_send()

        both(step, go)
        if not (isinstance(step, int) and step == 0):
            for way, level, cond in lines(step):
                def along(way=way, level=level):
                    for index in range(4):
                        zcd(level, way, index, False).wait_send()
                    for run in runs:
                        for copy in zab(level, way, run):
                            copy.wait_send()

                when(cond, along)

    steps(depth, drain)
    for copy in plane:
        copy.wait_send()
    cross.wait()
    fetched = pltpu.make_async_copy(result, out.at[1 - core], out_sem.at[1])
    fetched.start()
    fetched.wait()
    local.wait()


def run_reduce(depth, block, grads):
    half = grads.shape[1]
    large, small = cut(block, 16)
    dma = pltpu.SemaphoreType.DMA
    anywhere = pl.BlockSpec(memory_space=pl.ANY)
    scratch = [
        pltpu.VMEM((depth, 2, large, half), BF16),
        pltpu.VMEM((depth, large, half), BF16),
        pltpu.VMEM((depth, 2, large, half), BF16),
        pltpu.VMEM((depth, large, half), BF16),
        pltpu.VMEM((depth + 1, 2, large, half), BF16),
        pltpu.VMEM((depth + 1, 4, 2 * small, half), BF16),
        pltpu.VMEM((3, small, half), BF16),
        pltpu.VMEM((3, small, half), BF16),
        pltpu.VMEM((depth, 2, large, half), BF16),
        pltpu.VMEM((depth, 2, large, half), BF16),
        pltpu.VMEM((depth, 4, 2 * small, half), BF16),
        pltpu.VMEM((block, half), F32),
        pltpu.VMEM((block // 2, half), F32),
        dma((depth, 2)), dma((depth, 2)), dma((depth, 4)), dma((2,)), dma((1,)), dma((1,)),
        dma((depth, 2, 2)), dma((depth, 2, 2)), dma((depth, 2)), dma((depth, 2)),
        dma((depth, 2, 2)), dma((depth, 2, 2)), dma((depth, 2)), dma((depth, 2)),
        dma((depth + 1, 2, 2)), dma((depth + 1, 2, 2)),
        dma((depth + 1, 4)), dma((depth + 1, 4)),
        dma((6,)), dma((6,)),
    ]
    return pl.pallas_call(
        functools.partial(reduce_kernel, depth, block),
        out_shape=jax.ShapeDtypeStruct((2, block // 2, half), F32),
        in_specs=[anywhere],
        out_specs=anywhere,
        scratch_shapes=scratch,
        compiler_params=pltpu.CompilerParams(
            collective_id=2, has_side_effects=True, vmem_limit_bytes=51 << 20
        ),
        name="reduce",
    )(grads)


def adamw(gradient, params, first_moment, second_moment, rate, decay):
    moment_new = beta_one * first_moment + (1.0 - beta_one) * gradient
    second_new = beta_two * second_moment + (1.0 - beta_two) * gradient * gradient
    direction = (
        moment_new
        / (1.0 - beta_one**STEP)
        / (jnp.sqrt(second_new / (1.0 - beta_two**STEP)) + adam_eps)
    )
    return (moment_new, second_new, params - rate * (direction + decay * params))


def update_kernel(
    filled_ref, sums_ref, master_ref, one_ref, two_ref, average_ref,
    nrm_ref, gain_ref, shift_ref, norm_one_ref, norm_two_ref,
    grad_ref, one_out, two_out, new_ref, average_out, copy_ref,
    norm_grad_ref, norm_one_out, norm_two_out, norm_new_ref,
):
    @pl.when(pl.program_id(0) == 0)
    def _():
        branches = SUBS + SOURCES
        sums = jnp.concatenate([nrm_ref[0], nrm_ref[1]], axis=1)
        shifts = sums[branches : branches + SUBS]
        both = (
            sums[:branches],
            jnp.concatenate([shifts] + [shifts[SUBS - 1 :]] * SOURCES, axis=0),
        )
        for index, (gradient, params) in enumerate(zip(both, (gain_ref, shift_ref))):
            moment, second, new = adamw(
                gradient, params[...], norm_one_ref[:, index], norm_two_ref[:, index], rate_norm, 0.0
            )
            norm_grad_ref[:, index] = gradient
            norm_one_out[:, index] = moment
            norm_two_out[:, index] = second
            norm_new_ref[:, index] = new

    filled = filled_ref[pl.program_id(0)] > 0
    half = sums_ref.shape[2]
    strip = 32

    def one(index, carry):
        at = pl.ds(pl.multiple_of(index * strip, strip), strip)
        for h in range(2):
            lanes = pl.ds(h * half, half)
            gradient = jnp.where(filled, sums_ref[h, at], 0.0)
            master = master_ref[at, lanes]
            moment, second, new = adamw(
                gradient, master, one_ref[at, lanes], two_ref[at, lanes], rate_main, decay_main
            )
            grad_ref[at, lanes] = gradient
            one_out[at, lanes] = moment
            two_out[at, lanes] = second
            new_ref[at, lanes] = new
            average_out[at, lanes] = ema_keep * average_ref[at, lanes] + (1.0 - ema_keep) * new
            copy_ref[at, lanes] = new.astype(BF16)
        return carry

    lax.fori_loop(0, master_ref.shape[0] // strip, one, 0)


def run_update(filled, sums, master, moment_one, moment_two, average, nrm, gains, shifts, norm_one, norm_two):
    rows, width = master.shape
    step = rows // filled.shape[0]
    spec = pl.BlockSpec((step, width), lambda i, t: (i, 0))

    def whole(array):
        return pl.BlockSpec(array.shape, lambda i, t: (0,) * array.ndim)

    grid_spec = pltpu.PrefetchScalarGridSpec(
        num_scalar_prefetch=1,
        grid=(rows // step,),
        in_specs=[pl.BlockSpec((2, step, sums.shape[2]), lambda i, t: (0, i, 0))] + [spec] * 4
        + [whole(array) for array in (nrm, gains, shifts, norm_one, norm_two)],
        out_specs=[spec] * 6 + [whole(norm_one)] * 4,
    )
    full = jax.ShapeDtypeStruct(master.shape, F32)
    return pl.pallas_call(
        update_kernel,
        grid_spec=grid_spec,
        out_shape=[full] * 5 + [jax.ShapeDtypeStruct(master.shape, BF16)]
        + [jax.ShapeDtypeStruct(norm_one.shape, F32)] * 4,
        compiler_params=pltpu.CompilerParams(vmem_limit_bytes=24 << 20),
        name="update",
    )(filled, sums, master, moment_one, moment_two, average, nrm, gains, shifts, norm_one, norm_two)


def body(
    inputs,
    dense_inputs,
    lengths,
    owners,
    cotangent,
    master,
    moment_one,
    moment_two,
    average,
    norm_gain,
    norm_shift,
    norm_one,
    norm_two,
):
    width = inputs.shape[2]
    wides, narrows = lax.axis_size("wide"), lax.axis_size("narrow")
    depth = wides // 2
    own_rows = master.shape[0]
    block = 2 * own_rows
    capacity = own_rows * narrows // width
    places = slot_table(owners, capacity)
    act, dcv, res, block_out, input_grad, dense_grad, sums = run_chain(
        depth, block, places, lengths, master, inputs, dense_inputs, cotangent, norm_gain, norm_shift
    )
    owner = places // capacity
    compact = ((owner // 4) * 2 + owner % 2) * capacity + places % capacity
    parity = (lax.axis_index("wide") // 2) % 2
    handled = jnp.where((owner // 2) % 2 == parity, compact, -1).astype(jnp.int32)
    kept = 2 * (lax.axis_index("wide") % 2) + lax.axis_index("narrow") // 2
    handled = jnp.concatenate([handled, kept.astype(jnp.int32)[None]])
    grads = run_grads(wides * narrows * own_rows // 2, handled, act, dcv, res)
    reduced = run_reduce(depth // 2, block, grads)

    step = min(own_rows, 256)
    first = (lax.axis_index("wide") * narrows + lax.axis_index("narrow")) * own_rows
    slot_of_step = (first + step * jnp.arange(own_rows // step, dtype=jnp.int32)) // width
    filled = jnp.any(places[None, :] == slot_of_step[:, None], axis=1).astype(jnp.int32)
    updated = run_update(
        filled, reduced, master, moment_one, moment_two, average,
        sums, norm_gain, norm_shift, norm_one.transpose(1, 0, 2), norm_two.transpose(1, 0, 2),
    )
    return (
        block_out,
        input_grad,
        dense_grad,
        *updated[:6],
        *(values.transpose(1, 0, 2) for values in updated[6:]),
    )


def solution(mesh):
    rows = P(AXES, None)
    utterances = P(AXES, None, None)
    in_specs = (
        utterances, utterances, P(AXES), P(), utterances, rows, rows, rows, rows,
        P(), P(), P(), P(),
    )
    out_specs = (
        utterances, utterances, utterances, rows, rows, rows, rows, rows, rows,
        P(), P(), P(), P(),
    )
    return jax.shard_map(body, mesh=mesh, in_specs=in_specs, out_specs=out_specs, check_vma=False)
```

```python
import functools

import jax
import jax.numpy as jnp
from jax import lax
from jax.experimental import pallas as pl
from jax.experimental.pallas import tpu as pltpu
from jax.sharding import PartitionSpec as P

WLOW = 256
WMID = 384
K = 17
SUBS = 5
SOURCES = 6
STEP = 10
MARGIN = K // 2
EDGE = 16
UNIT = 64
F32 = jnp.float32
BF16 = jnp.bfloat16
MESH = pl.DeviceIdType.MESH
AXES = ("wide", "narrow")

norm_eps = 1e-05
beta_one = 0.9
beta_two = 0.999
adam_eps = 1e-08
rate_main = 0.02
rate_norm = 0.15
decay_main = 0.01
ema_keep = 0.8

NT = (((1,), (1,)), ((), ()))


def slot_table(owners, capacity):
    number = owners.shape[0]
    same_owner = owners[:, None] == owners[None, :]
    earlier = jnp.arange(number)[None, :] < jnp.arange(number)[:, None]
    ranking = jnp.sum(jnp.where(same_owner & earlier, 1, 0), axis=1)
    return (owners * capacity + ranking).astype(jnp.int32), ranking.astype(jnp.int32)


def source_pieces(half):
    pieces = []
    start = 0
    for width in (WLOW, WLOW, WLOW, WMID, WMID):
        parts = []
        stop = start + width
        while start < stop:
            chunk, lane = divmod(start, half)
            lanes = min(half - lane, stop - start)
            parts.append((chunk, lane, lanes))
            start += lanes
        pieces.append(parts)
    return pieces


class Place:
    def __init__(self, depth):
        wide = lax.axis_index("wide")
        narrow = lax.axis_index("narrow")
        self.depth = depth
        self.core = lax.rem(narrow, 2)
        self.y = narrow // 2
        self.x = lax.rem(wide, 2)
        self.z = wide // 2
        self.groups = depth * 4
        self.me = wide * 2 + self.y

    def at(self, z, x, y, core):
        return (z * 2 + x, y * 2 + core)

    def beside(self):
        return self.at(self.z + 1 - 2 * lax.rem(self.z, 2), self.x, self.y, self.core)

    def partner(self):
        return self.at(self.z, self.x, self.y, 1 - self.core)

    def over_x(self):
        return self.at(self.z, 1 - self.x, self.y, self.core)

    def over_y(self):
        return self.at(self.z, self.x, 1 - self.y, self.core)

    def up(self):
        return self.at(self.z + 1, self.x, self.y, self.core)

    def down(self):
        return self.at(self.z - 1, self.x, self.y, self.core)

    def far(self, turn):
        z = lax.rem(self.z + 1 + turn // 4, self.depth)
        return self.at(z, lax.rem(turn // 2, 2), lax.rem(turn, 2), self.core)

    def near(self):
        return (
            self.over_x(), self.over_y(), self.at(self.z, 1 - self.x, 1 - self.y, self.core)
        )

    def enter(self):
        barrier = pltpu.get_barrier_semaphore()

        def greet(device):
            pl.semaphore_signal(barrier, inc=1, device_id=device, device_id_type=MESH)

        for device in (self.partner(), self.over_x(), self.over_y()):
            greet(device)
        above, below = self.z + 1 < self.depth, self.z >= 1
        pl.when(above)(functools.partial(greet, self.up()))
        pl.when(below)(functools.partial(greet, self.down()))
        met = 3 + above.astype(jnp.int32) + below.astype(jnp.int32)
        pl.semaphore_wait(barrier, met)


class QuadPlace(Place):
    def __init__(self, depth):
        super().__init__(depth)
        self.parity = lax.rem(self.z, 2)
        self.z = self.z // 2

    def at(self, z, x, y, core):
        return ((2 * z + self.parity) * 2 + x, y * 2 + core)


def remote(src, dst, send_sem, recv_sem, device):
    return pltpu.make_async_remote_copy(
        src_ref=src,
        dst_ref=dst,
        send_sem=send_sem,
        recv_sem=recv_sem,
        device_id=device,
        device_id_type=MESH,
    )


def when(cond, action):
    if cond is None:
        action()
    else:
        pl.when(cond)(action)


def cut(block, share):
    units = block // UNIT
    small = max(1, units // share)
    return (units - 2 * small) // 2 * UNIT, small * UNIT


def steps(depth, body, first=0):
    if depth <= 4:
        for step in range(first, depth):
            body(step)
    else:
        def looped(step, carry):
            body(step)
            return carry

        if first == 0:
            body(0)
        lax.fori_loop(max(first, 1), depth, looped, 0)


def shares(rows, number):
    units = rows // UNIT
    out = []
    first = 0
    for index in range(number):
        count = units // number + (1 if index < units % number else 0)
        if count:
            out.append((first * UNIT, count * UNIT))
        first += count
    return out


def tree_sems(depth):
    dma = pltpu.SemaphoreType.DMA
    return [
        dma((depth, 2, 2)), dma((depth, 2)), dma((depth, 2, 4)), dma((depth, 4)),
        dma((depth, 2)), dma((depth, 2)), dma((depth, 2, 2)), dma((depth, 2, 2)),
        dma((depth, 2)), dma((depth, 2)), dma((depth, 2, 2)), dma((depth, 2, 2)),
        dma((6,)), dma((6,)),
    ]


def gather_bank(place, bank, block, sems, first_idle=lambda: None, second_idle=lambda: None):
    depth, z, x, y = place.depth, place.z, place.x, place.y
    large, small = cut(block, 9)
    (zab_s, zab_r, zcd_s, zcd_r, ax_s, ax_r, ay_s, ay_r, by_s, by_r, bx_s, bx_r, cd_s, cd_r) = sems
    pieces = shares(large, 2)
    runs = range(len(pieces))

    def rows(zz, xx, yy, first, count):
        begin = ((zz * 2 + xx) * 2 + yy) * (block // UNIT) + first // UNIT
        return bank.at[pl.ds(begin, count // UNIT)]

    def move(zz, xx, yy, first, count, send_sem, recv_sem, device):
        ref = rows(zz, xx, yy, first, count)
        return remote(ref, ref, send_sem, recv_sem, device)

    start_c, start_d = 2 * large, 2 * large + small
    over_x, over_y, up, down = place.over_x(), place.over_y(), place.up(), place.down()

    def sides(step):
        out = [(z - step, z - step >= 0)]
        if not (isinstance(step, int) and step == 0):
            out.append((z + step, z + step < depth))
        return out

    def both(step, action):
        for level, cond in sides(step):
            when(cond, functools.partial(action, level))

    def z_moves(step, run):
        out = []
        low, high = z - step, z + step
        for level, cond, device, way in (
            (low, (low >= 0) & (z + 1 < depth), up, 0),
            (high, (high < depth) & (z >= 1), down, 1),
        ):
            if run is not None:
                first, count = pieces[run]
                copy = move(
                    level, x, y, 2 * first, 2 * count, zab_s.at[level, way, run], zab_r.at[level, run], device
                )
                out.append((cond, copy))
                continue
            for index in range(4):
                copy = move(
                    level, index // 2, index % 2, start_c, 2 * small, zcd_s.at[level, way, index],
                    zcd_r.at[level, index], device,
                )
                out.append((cond, copy))
        return out

    def ax(level, run):
        first, count = pieces[run]
        return move(level, x, y, 2 * first, count, ax_s.at[level, run], ax_r.at[level, run], over_x)

    def by(level, run):
        first, count = pieces[run]
        return move(level, x, y, 2 * first + count, count, by_s.at[level, run], by_r.at[level, run], over_y)

    def ay(level, run, other):
        first, count = pieces[run]
        xx = 1 - x if other else x
        return move(level, xx, y, 2 * first, count, ay_s.at[level, run, other], ay_r.at[level, run, other], over_y)

    def bx(level, run, other):
        first, count = pieces[run]
        yy = 1 - y if other else y
        return move(
            level, x, yy, 2 * first + count, count, bx_s.at[level, run, other], bx_r.at[level, run, other], over_x
        )

    plane = [
        move(z, x, y, start_c, small, cd_s.at[0], cd_r.at[0], over_x),
        move(z, x, y, start_d, small, cd_s.at[1], cd_r.at[1], over_y),
        move(z, x, y, start_c, small, cd_s.at[2], cd_r.at[2], over_y),
        move(z, 1 - x, y, start_c, small, cd_s.at[3], cd_r.at[3], over_y),
        move(z, x, y, start_d, small, cd_s.at[4], cd_r.at[4], over_x),
        move(z, x, 1 - y, start_d, small, cd_s.at[5], cd_r.at[5], over_x),
    ]

    def run_step(step):
        home = isinstance(step, int) and step == 0
        if home:
            plane[0].start()
            plane[1].start()
        for run in runs:
            first, count = pieces[run]
            if not home:
                both(
                    step,
                    lambda level, run=run, first=first, count=count: move(
                        level, x, y, 2 * first, 2 * count, zab_s.at[level, 0, run], zab_r.at[level, run], up
                    ).wait_recv(),
                )
            for cond, copy in z_moves(step, run):
                when(cond, copy.start)

            def begin(level, run=run):
                ax(level, run).start()
                by(level, run).start()

            both(step, begin)
        if home:
            first_idle()
            plane[2].start()
            plane[4].start()
            plane[0].wait_recv()
            plane[3].start()
            plane[1].wait_recv()
            plane[5].start()
            for copy in plane[2:]:
                copy.wait_recv()
            for cond, copy in z_moves(step, None):
                when(cond, copy.start)
        for run in runs:
            def across(level, run=run):
                ay(level, run, 0).start()
                bx(level, run, 0).start()
                ax(level, run).wait_recv()
                ay(level, run, 1).start()
                by(level, run).wait_recv()
                bx(level, run, 1).start()

            both(step, across)
        if not home:
            def arrived(level):
                for index in range(4):
                    move(
                        level, x, y, start_c, 2 * small, zcd_s.at[level, 0, index],
                        zcd_r.at[level, index], up,
                    ).wait_recv()

            both(step, arrived)
            for cond, copy in z_moves(step, None):
                when(cond, copy.start)
        if home:
            second_idle()

    steps(depth, run_step)

    def drain(step):
        def finish(level):
            for run in runs:
                for other in range(2):
                    ay(level, run, other).wait_recv()
                    bx(level, run, other).wait_recv()
                    ay(level, run, other).wait_send()
                    bx(level, run, other).wait_send()
                ax(level, run).wait_send()
                by(level, run).wait_send()

        both(step, finish)
        for kind in list(runs) + [None]:
            for cond, copy in z_moves(step, kind):
                when(cond, copy.wait_send)

    steps(depth, drain)
    for copy in plane:
        copy.wait_send()


def strips(rows, body, carry=0):
    strip = 64

    def one(index, carry):
        return body(pl.ds(pl.multiple_of(index * strip, strip), strip), carry)

    return lax.fori_loop(0, rows // strip, one, carry, unroll=True)


def fold(values):
    return jnp.sum(values.reshape(-1, 8, values.shape[1]), axis=0)


def chain_kernel(
    depth, block,
    slot_ref, length_ref, master, own_x, own_dense, own_cot, gain_ref, shift_ref,
    act_out, dcv_out, res_out, blk_out, ig_out, dg_out, nrm_out,
    bank, act, dense, mask, cot, raw, side, pre4, slope, upown, upsend, uprecv, dcv, dsd, res, res_x, res_y, dgrecv,
    igrecv, stage, turned, nrm, blk, blksend, keep, ex_side, ex_last, ex_sub,
    load_sem, swap_s, swap_r, act_s, act_r, up_s, up_r, ex_s, ex_r, out_sem, far_s, far_r, near_s, near_r, own_sem,
    *tree,
):
    place = Place(depth)
    core, other = place.core, 1 - place.core
    partner, beside = place.partner(), place.beside()
    half = bank.shape[2]
    width = 2 * half
    frames = mask.shape[1]
    rows = 2 * frames
    chunks = dense.shape[0]
    pieces = source_pieces(half)
    inner = pl.ds(EDGE, frames)
    own_rows = block // 2
    load_rows = min(own_rows, rows)
    loads_of = own_rows // load_rows

    mats_in = []
    for part in range(loads_of):
        for h in range(2):
            mats_in.append(
                pltpu.make_async_copy(
                    master.at[pl.ds(part * load_rows, load_rows), pl.ds(h * half, half)],
                    side.at[part * 2 + h, pl.ds(0, load_rows)],
                    load_sem.at[part * 2 + h],
                )
            )
    x_in = [
        pltpu.make_async_copy(
            own_x.at[0, :, pl.ds(h * half, half)], act.at[0, h, core, inner], load_sem.at[6 + h]
        )
        for h in range(2)
    ]
    dense_in = [
        pltpu.make_async_copy(
            own_dense.at[0, :, pl.ds(chunk * half, half)], dense.at[chunk, core], load_sem.at[8 + chunk]
        )
        for chunk in range(chunks)
    ]
    ours_lanes = pl.ds(pl.multiple_of(core * half, half), half)
    theirs_lanes = pl.ds(pl.multiple_of(other * half, half), half)
    cot_in = pltpu.make_async_copy(own_cot.at[0, :, ours_lanes], cot.at[core], load_sem.at[8 + chunks])
    for copy in mats_in + x_in + dense_in + [cot_in]:
        copy.start()
    place.enter()
    base = place.me * (block // UNIT) + core * (own_rows // UNIT)
    units = load_rows // UNIT
    send_mats = []
    for part in range(loads_of):
        def narrow(unit, carry, part=part):
            at = pl.ds(pl.multiple_of(unit * UNIT, UNIT), UNIT)
            stage[part * units + unit] = side[part * 2 + other, at].astype(BF16)
            return carry

        def keep_own(unit, carry, part=part):
            at = pl.ds(pl.multiple_of(unit * UNIT, UNIT), UNIT)
            bank[base + part * units + unit] = side[part * 2 + core, at].astype(BF16)
            return carry

        mats_in[2 * part].wait()
        mats_in[2 * part + 1].wait()
        lax.fori_loop(0, units, narrow, 0, unroll=2)
        copy = remote(
            stage.at[pl.ds(part * units, units)], bank.at[pl.ds(base + part * units, units)],
            swap_s.at[9 + part], swap_r.at[9 + part], partner,
        )
        copy.start()
        send_mats.append(copy)
        lax.fori_loop(0, units, keep_own, 0, unroll=2)
    mask[core] = (
        lax.broadcasted_iota(jnp.int32, (frames, 128), 0) < length_ref[0]
    ).astype(F32)
    edge_zero = jnp.zeros((EDGE, half), BF16)

    def clear(section, carry):
        for u in range(2):
            for h in range(2):
                act[section, h, u, pl.ds(0, EDGE)] = edge_zero
                act[section, h, u, pl.ds(EDGE + frames, EDGE)] = edge_zero
            dcv[section, u, pl.ds(0, EDGE)] = edge_zero
            dcv[section, u, pl.ds(EDGE + frames, EDGE)] = edge_zero
        return carry

    lax.fori_loop(0, SUBS, clear, 0)
    for copy in send_mats:
        copy.wait()

    def prepare():
        for copy in x_in + dense_in + [cot_in]:
            copy.wait()
        low_mask = jnp.concatenate([mask[core].astype(BF16)] * (half // 128), axis=1)
        for h in range(2):
            act[0, h, core, inner] = act[0, h, core, inner] * low_mask
        for chunk in range(chunks):
            dense[chunk, core] = dense[chunk, core] * low_mask
        own = act.at[0, :, core, inner]
        swaps = [
            remote(own, own, swap_s.at[1], swap_r.at[1], partner),
            remote(dense.at[:, core], dense.at[:, core], swap_s.at[2], swap_r.at[2], partner),
            remote(mask.at[core], mask.at[core], swap_s.at[3], swap_r.at[3], partner),
            remote(own_cot.at[0, :, theirs_lanes], cot.at[core], swap_s.at[4], swap_r.at[4], partner),
        ]
        for copy in swaps:
            copy.start()
        return swaps

    def own_act(section):
        half_of = turned.at[lax.rem(section, 2)]
        return [
            pltpu.make_async_copy(half_of, act_out.at[section, 0, core], own_sem.at[section]),
            remote(
                half_of, act_out.at[section, 0, core], near_s.at[section], near_r.at[section], partner
            ),
            remote(
                half_of, act_out.at[section, 1, core], far_s.at[section], far_r.at[section], beside
            ),
        ]

    def pass_act(section):
        ref = act_out.at[section, 1, core]
        return remote(ref, ref, near_s.at[SUBS + section], near_r.at[SUBS + section], partner)

    def turn_act(section):
        turned[lax.rem(section, 2)] = jnp.concatenate(
            [act[section, core, u, inner] for u in range(2)], axis=0
        ).T
        for copy in own_act(section)[:2]:
            copy.start()

    def free_turned(section):
        copies = own_act(section)
        copies[0].wait()
        copies[1].wait_send()
        copies[2].wait_send()

    swaps = []

    def arrived():
        for copy in swaps:
            copy.wait()
        turn_act(0)
        own_act(0)[2].start()

    gather_bank(place, bank, block, tree, lambda: swaps.extend(prepare()), arrived)

    outs = []

    def put(src, dst):
        copy = pltpu.make_async_copy(src, dst, out_sem.at[len(outs)])
        copy.start()
        outs.append(copy)

    def far_dcv(section):
        return remote(
            dcv.at[section], dcv_out.at[section, 1],
            far_s.at[SUBS + section], far_r.at[SUBS + section], beside,
        )

    def keep_dcv(section):
        return pltpu.make_async_copy(
            dcv.at[section], dcv_out.at[section, 0], own_sem.at[SUBS + section]
        )

    def res_over(step):
        if step == 0:
            src, dst, device = res.at[pl.ds(2 * (1 - place.x), 2)], res_x, place.over_x()
        elif step == 1:
            src, dst, device = res_x.at[1 - place.y], res_y, place.over_y()
        else:
            src, dst, device = res_y, res_out.at[1], beside
        at = 2 * SUBS + step
        return remote(src, dst, far_s.at[at], far_r.at[at], device)

    def weight(matrix, first, count):
        begin = slot_ref[matrix] * (width // UNIT) + first // UNIT
        return jnp.concatenate([bank[begin + i] for i in range(count // UNIT)], axis=0)

    def valid(at):
        return jnp.concatenate([mask_rows(at)] * (half // 128), axis=1)

    def mask_rows(at):
        return mask[at.start // frames, pl.ds(pl.multiple_of(lax.rem(at.start, frames), 64), at.size)]

    def gain(index):
        return gain_ref[pl.ds(index, 1), ours_lanes]

    def bias(index):
        return shift_ref[pl.ds(index, 1), ours_lanes]

    def share(buffer, index, values):
        buffer[place.me] = values
        mine = buffer.at[place.me]

        def go(turn, carry):
            remote(mine, mine, ex_s.at[index, 1], ex_r.at[index, 1], place.far(turn)).start()
            return carry

        lax.fori_loop(0, place.groups - 4, go, 0, unroll=place.groups <= 16)
        for device in place.near():
            remote(mine, mine, ex_s.at[index, 0], ex_r.at[index, 0], device).start()

    def shared(buffer, index, between=lambda: None):
        for kind, number in ((0, 3), (1, place.groups - 4)):
            some = buffer.at[pl.ds(0, number)]
            copy = remote(some, some, ex_s.at[index, kind], ex_r.at[index, kind], place.over_x())
            copy.wait_recv()
            copy.wait_send()
            if kind == 0:
                between()
        return buffer[...]

    def total_of(values):
        return jnp.sum(values, axis=0, keepdims=True)

    def counted():
        def add(at, carry):
            return carry + fold(valid(at))

        return total_of(strips(rows, add, jnp.zeros((8, half), F32)))

    def moments(load, count):
        pivot = load(pl.ds(0, 8))[0:1]

        def add(at, carry):
            first, second = carry
            valid_now = valid(at)
            off = (load(at) - pivot) * valid_now
            return first + fold(off), second + fold(off * off)

        zero = jnp.zeros((8, half), F32)
        first, second = strips(rows, add, (zero, zero))
        first, second = total_of(first), total_of(second)
        return first + count * pivot, jnp.maximum(second - first * first / count, 0.0)

    def merge(count, total, squares):
        frame_total = jnp.sum(count, axis=0)
        mean = jnp.sum(total, axis=0) / frame_total
        shift = total / count - mean[None]
        variance = jnp.sum(squares + count * shift * shift, axis=0) / frame_total
        return mean[None], lax.rsqrt(variance + norm_eps)[None], frame_total[None]

    def save(index, mean, inverse):
        scale = gain(index) * inverse
        keep[0, pl.ds(index, 1)] = inverse
        keep[1, pl.ds(index, 1)] = mean * inverse
        keep[2, pl.ds(index, 1)] = scale
        keep[3, pl.ds(index, 1)] = bias(index) - mean * scale

    def kept(row, index):
        return keep[row, pl.ds(index, 1)]

    count = counted()
    def side_branches():
        totals, squares = [], []
        for index in range(SOURCES):
            value = None
            if index < SOURCES - 1:
                for chunk, lane, lanes in pieces[index]:
                    left = dense[chunk].reshape(rows, half)[:, lane : lane + lanes]
                    right = weight(SUBS * K + chunk // 2, (chunk % 2) * half + lane, lanes)
                    term = jnp.dot(left, right, preferred_element_type=F32)
                    value = term if value is None else value + term
            else:
                for h in range(2):
                    left = jnp.concatenate([act[0, h, u, inner] for u in range(2)], axis=0)
                    term = jnp.dot(left, weight(SUBS * K + 3, h * half, half), preferred_element_type=F32)
                    value = term if value is None else value + term
            side[index] = value
            total, square = moments(lambda at, index=index: side[index, at], count)
            totals.append(total)
            squares.append(square)
        fill = jnp.zeros((3, half), F32)
        share(ex_side, 0, jnp.concatenate([count] + totals + squares + [fill], axis=0))

    def convolve(section, h, first):
        value = None
        for k in range(K):
            left = jnp.concatenate(
                [act[section, h, u, pl.ds(EDGE - MARGIN + k, frames)] for u in range(2)], axis=0
            )
            term = jnp.dot(
                left, weight(section * K + k, h * half, half), preferred_element_type=F32
            )
            value = term if value is None else value + term
            if k % 2 == 1 or k == K - 1:
                if first and k == 1:
                    raw[section] = value
                else:
                    raw[section] += value
                value = None

    def swap_act(section):
        own = act.at[section, core, :, inner]
        return remote(own, own, act_s.at[section], act_r.at[section], partner)

    def forward(section, last):
        convolve(section, core, True)
        if isinstance(section, int):
            if section > 0:
                swap_act(section).wait_recv()
        else:
            pl.when(section > 0)(swap_act(section).wait_recv)
        convolve(section, other, False)
        total, square = moments(lambda at: raw[section, at], count)
        buffer = ex_sub.at[lax.rem(section, 2)]
        share(buffer, 1 + section, jnp.concatenate([count, total, square, jnp.zeros_like(count)], axis=0))

        def pre_side():
            parts = shared(ex_side, 0)
            for index in range(SOURCES):
                mean, inverse, _ = merge(
                    parts[:, 0], parts[:, 1 + index], parts[:, 1 + SOURCES + index]
                )
                save(SUBS + index, mean, inverse)
            scales = [kept(2, SUBS + index) for index in range(SOURCES)]
            offset = sum(kept(3, SUBS + index) for index in range(SOURCES))

            def add(at, carry):
                before = offset
                for index in range(SOURCES):
                    before = before + side[index, at] * scales[index]
                pre4[at] = before
                return carry

            strips(rows, add)

        def background():
            own_act(section - 1)[2].wait_recv()
            pass_act(section - 1).start()
            if isinstance(section, int):
                free_turned(section - 2)
            else:
                pl.when(section > 1)(functools.partial(free_turned, section - 2))
            turn_act(section)

        if isinstance(section, int):
            background()
            parts = shared(buffer, 1 + section, own_act(section)[2].start)
        else:
            pl.when(section == 0)(side_branches)
            pl.when(section > 0)(background)
            pl.when(section == 1)(pre_side)
            parts = shared(
                buffer, 1 + section, lambda: pl.when(section > 0)(own_act(section)[2].start)
            )
        mean, inverse, frame_total = merge(parts[:, 0], parts[:, 1], parts[:, 2])
        save(section, mean, inverse)
        scale, offset = kept(2, section), kept(3, section)

        def activate(at, carry):
            before = raw[section, at] * scale + offset
            if last:
                before = before + pre4[at]
                pre4[at] = before
            hidden = (before * jax.nn.sigmoid(before) * valid(at)).astype(BF16)
            u = at.start // frames
            first = pl.multiple_of(lax.rem(at.start, frames), 64)
            if last:
                @pl.when(u == core)
                def _():
                    blk[core, pl.ds(first, at.size)] = hidden

                @pl.when(u != core)
                def _():
                    blksend[pl.ds(first, at.size)] = hidden
            else:
                act[section + 1, core, u, pl.ds(pl.multiple_of(first + EDGE, EDGE), at.size)] = hidden
            return carry

        strips(rows, activate)
        if not last:
            swap_act(section + 1).start()
        return frame_total

    def looped(section, carry):
        forward(section, False)
        return carry

    lax.fori_loop(0, SUBS - 1, looped, 0)
    frame_total = forward(SUBS - 1, True)
    blk_copy = remote(blksend, blk.at[core], swap_s.at[5], swap_r.at[5], partner)
    blk_copy.start()
    for section in range(1, SUBS):
        swap_act(section).wait_send()
    for section in (SUBS - 2, SUBS - 1):
        free_turned(section)

    def hat_of(values, index):
        return values * kept(0, index) - kept(1, index)

    def back_half(section, h):
        total = None
        value = None
        for k in range(K):
            left = jnp.concatenate(
                [dcv[section, u, pl.ds(EDGE + MARGIN - k, frames)] for u in range(2)], axis=0
            )
            term = lax.dot_general(
                left, weight(section * K + k, h * half, half), NT, preferred_element_type=F32
            )
            value = term if value is None else value + term
            if k % 2 == 1 or k == K - 1:
                total = value if total is None else total + value
                value = None
        return total

    def up_copy(section):
        slot = lax.rem(section, 2)
        return remote(upsend, uprecv.at[slot], up_s.at[slot], up_r.at[slot], partner)

    def backward(section):
        upsend[...] = back_half(section, other)
        up_copy(section).start()
        upown[...] = back_half(section, core)

    def slopes(section, upstream, before_of, others, target):
        sources = [(lambda at: raw[section, at], section)] + others

        def one(at, carry):
            before = before_of(at)
            sigmoid = jax.nn.sigmoid(before)
            now = upstream(at) * valid(at) * (sigmoid * (1.0 + before * (1.0 - sigmoid)))
            target[at] = now
            out = [carry[0] + fold(now)]
            for (load, index), so_far in zip(sources, carry[1:]):
                out.append(so_far + fold(now * hat_of(load(at), index)))
            return tuple(out)

        zero = jnp.zeros((8, half), F32)
        return [total_of(value) for value in strips(rows, one, (zero,) * (1 + len(sources)))]

    def branch(source, load, index, shift_sum, gain_sum, store):
        scale = kept(2, index)
        shift_mean, gain_mean = shift_sum / frame_total, gain_sum / frame_total

        def one(at, carry):
            value = source[at] - shift_mean - hat_of(load(at), index) * gain_mean
            store(at, (valid(at) * scale * value).astype(BF16))
            return carry

        strips(rows, one)

    def conv_branch(source, section, shift_sum, gain_sum):
        def store(at, value):
            first = pl.multiple_of(lax.rem(at.start, frames) + EDGE, EDGE)
            dcv[section, at.start // frames, pl.ds(first, at.size)] = value

        branch(source, lambda at: raw[section, at], section, shift_sum, gain_sum, store)
        far_dcv(section).start()
        keep_dcv(section).start()

    def cot_at(at):
        return cot[
            at.start // frames, pl.ds(pl.multiple_of(lax.rem(at.start, frames), 64), at.size)
        ].astype(F32)

    sums = slopes(
        SUBS - 1, cot_at, lambda at: pre4[at],
        [(lambda at, index=index: side[index, at], SUBS + index) for index in range(SOURCES)],
        pre4,
    )
    share(ex_last, SUBS + 1, jnp.concatenate(sums, axis=0))
    sums = jnp.sum(shared(ex_last, SUBS + 1), axis=0)
    shift_sum = sums[0:1]
    conv_branch(pre4, SUBS - 1, shift_sum, sums[1:2])
    nrm[core] = jnp.zeros_like(nrm[0])
    nrm[core, pl.ds(SUBS - 1, 1 + SOURCES)] = sums[1:]
    nrm[core, pl.ds(SUBS + SOURCES + SUBS - 1, 1)] = shift_sum
    backward(SUBS - 1)

    def side_grads():
        for index in range(SOURCES):
            def store(at, value, index=index):
                dsd[index, at] = value

            branch(
                pre4, lambda at, index=index: side[index, at], SUBS + index, shift_sum,
                sums[2 + index : 3 + index], store,
            )

    theirs = pl.multiple_of(other * frames, frames)
    ours = pl.multiple_of(core * frames, frames)
    dg_copy = remote(
        side.at[:, pl.ds(theirs, frames)], dgrecv, swap_s.at[6], swap_r.at[6], partner
    )

    def dense_grads():
        for index in range(SOURCES - 1):
            for chunk, lane, lanes in pieces[index]:
                right = weight(SUBS * K + chunk // 2, (chunk % 2) * half + lane, lanes)
                side[chunk, :, pl.ds(lane, lanes)] = lax.dot_general(
                    dsd[index], right, NT, preferred_element_type=F32
                )
        dg_copy.start()

    def residual_grads():
        rows_of = [[] for _ in range(chunks)]
        for index, parts in enumerate(pieces):
            for chunk, lane, lanes in parts:
                rows_of[chunk].append((lane, lanes, index))
        for chunk in range(chunks):
            turned = dense[chunk].reshape(rows, half).T
            for lane, lanes, index in rows_of[chunk]:
                res[chunk // 2, pl.ds((chunk % 2) * half + lane, lanes)] = jnp.dot(
                    turned[lane : lane + lanes], dsd[index], preferred_element_type=F32
                ).astype(BF16)
        for h in range(2):
            turned = jnp.concatenate([act[0, h, u, inner] for u in range(2)], axis=0).T
            res[3, pl.ds(h * half, half)] = jnp.dot(
                turned, dsd[SOURCES - 1], preferred_element_type=F32
            ).astype(BF16)

    dg_puts = [
        pltpu.make_async_copy(
            dgrecv.at[chunk], dg_out.at[0, :, pl.ds(chunk * half, half)], load_sem.at[chunk]
        )
        for chunk in range(chunks)
    ]

    def finish_dense():
        dg_copy.wait()
        own_valid = jnp.concatenate([mask[core]] * (half // 128), axis=1)
        for chunk in range(chunks):
            dgrecv[chunk] = (dgrecv[chunk] + side[chunk, pl.ds(ours, frames)]) * own_valid
            dg_puts[chunk].start()

    def looped_back(turn, carry):
        section = SUBS - 2 - turn
        copy = up_copy(section + 1)
        copy.wait()
        slot = lax.rem(section + 1, 2)
        scale, offset = kept(2, section), kept(3, section)
        sums_now = slopes(
            section, lambda at: upown[at] + uprecv[slot, at],
            lambda at: raw[section, at] * scale + offset, [], slope,
        )
        zero = jnp.zeros((2, half), F32)
        buffer = ex_sub.at[lax.rem(section, 2)]
        share(buffer, SUBS + 2 + section, jnp.concatenate(sums_now + [zero], axis=0))

        @pl.when(section == SUBS - 2)
        def _():
            side_grads()
            residual_grads()
            res_over(0).start()
            dense_grads()

        @pl.when(section == SUBS - 3)
        def _():
            res_over(0).wait_recv()
            for index in range(2):
                total = res[2 * place.x + index].astype(F32) + res_x[index].astype(F32)
                res_x[index] = total.astype(BF16)
            res_over(1).start()
            finish_dense()
            own_act(SUBS - 1)[2].wait_recv()
            pass_act(SUBS - 1).start()

        @pl.when(section == SUBS - 4)
        def _():
            res_over(1).wait_recv()
            res_y[...] = (res_y[...].astype(F32) + res_x[place.y].astype(F32)).astype(BF16)

        sums_now = jnp.sum(shared(buffer, SUBS + 2 + section), axis=0)
        pl.when(section == SUBS - 4)(lambda: res_over(2).start())
        conv_branch(slope, section, sums_now[0:1], sums_now[1:2])
        nrm[core, pl.ds(section, 1)] = sums_now[1:2]
        nrm[core, pl.ds(SUBS + SOURCES + section, 1)] = sums_now[0:1]

        @pl.when(section > 0)
        def _():
            backward(section)

        return carry

    lax.fori_loop(0, SUBS - 1, looped_back, 0)
    put(res_y, res_out.at[0])
    nrm_copy = remote(nrm.at[core], nrm.at[core], swap_s.at[7], swap_r.at[7], partner)
    nrm_copy.start()
    for h in range(2):
        uprecv[h] = back_half(0, h) + lax.dot_general(
            dsd[SOURCES - 1], weight(SUBS * K + 3, h * half, half), NT, preferred_element_type=F32
        )
    ig_copy = remote(
        uprecv.at[:, pl.ds(theirs, frames)], igrecv, swap_s.at[8], swap_r.at[8], partner
    )
    ig_copy.start()
    own_valid = jnp.concatenate([mask[core]] * (half // 128), axis=1)
    blk_copy.wait()
    nrm_copy.wait()
    put(nrm, nrm_out)
    ig_copy.wait()
    for h in range(2):
        igrecv[h] = (igrecv[h] + uprecv[h, pl.ds(ours, frames)]) * own_valid
        put(igrecv.at[h], ig_out.at[0, :, pl.ds(h * half, half)])
        put(blk.at[h], blk_out.at[0, :, pl.ds(h * half, half)])
    for section in range(SUBS):
        own_act(section)[1].wait_recv()
        pass_act(section).wait()
        far_dcv(section).wait()
        keep_dcv(section).wait()
    res_over(0).wait_send()
    res_over(1).wait_send()
    res_over(2).wait()
    for copy in outs + dg_puts:
        copy.wait()


def run_chain(depth, block, places, lengths, master, x, dense, cot, gains, shifts):
    frames, width = x.shape[1:]
    half = width // 2
    rows = 2 * frames
    chunks = dense.shape[2] // half
    padded = frames + 2 * EDGE
    groups = depth * 4
    dma = pltpu.SemaphoreType.DMA
    anywhere = pl.BlockSpec(memory_space=pl.ANY)
    vmem = pl.BlockSpec(memory_space=pltpu.VMEM)
    smem = pl.BlockSpec(memory_space=pltpu.SMEM)
    out_shape = [
        jax.ShapeDtypeStruct((SUBS, 2, 2, half, rows), BF16),
        jax.ShapeDtypeStruct((SUBS, 2, 2, padded, half), BF16),
        jax.ShapeDtypeStruct((2, width, half), BF16),
        jax.ShapeDtypeStruct(x.shape, BF16),
        jax.ShapeDtypeStruct(x.shape, F32),
        jax.ShapeDtypeStruct(dense.shape, F32),
        jax.ShapeDtypeStruct((2, 16, half), F32),
    ]
    scratch = [
        pltpu.VMEM((groups * block // UNIT, UNIT, half), BF16),
        pltpu.VMEM((SUBS, 2, 2, padded, half), BF16),
        pltpu.VMEM((chunks, 2, frames, half), BF16),
        pltpu.VMEM((2, frames, 128), F32),
        pltpu.VMEM((2, frames, half), BF16),
        pltpu.VMEM((SUBS, rows, half), F32),
        pltpu.VMEM((SOURCES, rows, half), F32),
        pltpu.VMEM((rows, half), F32),
        pltpu.VMEM((rows, half), F32),
        pltpu.VMEM((rows, half), F32),
        pltpu.VMEM((rows, half), F32),
        pltpu.VMEM((2, rows, half), F32),
        pltpu.VMEM((SUBS, 2, padded, half), BF16),
        pltpu.VMEM((SOURCES, rows, half), BF16),
        pltpu.VMEM((4, width, half), BF16),
        pltpu.VMEM((2, width, half), BF16),
        pltpu.VMEM((width, half), BF16),
        pltpu.VMEM((chunks, frames, half), F32),
        pltpu.VMEM((2, frames, half), F32),
        pltpu.VMEM((block // 2 // UNIT, UNIT, half), BF16),
        pltpu.VMEM((2, half, rows), BF16),
        pltpu.VMEM((2, 16, half), F32),
        pltpu.VMEM((2, frames, half), BF16),
        pltpu.VMEM((frames, half), BF16),
        pltpu.VMEM((4, 16, half), F32),
        pltpu.VMEM((groups, 16, half), F32),
        pltpu.VMEM((groups, 8, half), F32),
        pltpu.VMEM((2, groups, 4, half), F32),
        dma((9 + chunks,)),
        dma((12,)), dma((12,)),
        dma((SUBS,)), dma((SUBS,)),
        dma((2,)), dma((2,)),
        dma((2 * SUBS + 1, 2)), dma((2 * SUBS + 1, 2)),
        dma((10 + chunks,)),
        dma((2 * SUBS + 3,)), dma((2 * SUBS + 3,)),
        dma((2 * SUBS,)), dma((2 * SUBS,)),
        dma((2 * SUBS,)),
    ] + tree_sems(depth)
    return pl.pallas_call(
        functools.partial(chain_kernel, depth, block),
        out_shape=out_shape,
        in_specs=[smem] * 2 + [anywhere] * 4 + [vmem] * 2,
        out_specs=[anywhere] * len(out_shape),
        scratch_shapes=scratch,
        compiler_params=pltpu.CompilerParams(
            collective_id=1, has_side_effects=True, vmem_limit_bytes=63 << 20
        ),
        cost_estimate=pl.CostEstimate(
            flops=4 * SUBS * K * rows * width * half, bytes_accessed=16 << 20, transcendentals=0
        ),
        name="chain",
    )(places, lengths, master, x, dense, cot, gains, shifts)


def grad_kernel(slot_ref, act_ref, dcv_ref, res_ref, out_ref, stage, count, sems):
    section = pl.program_id(0)
    half = act_ref.shape[3]
    width = 2 * half
    frames = act_ref.shape[4] // 2
    ring = stage.shape[0]

    @pl.when(section == 0)
    def _():
        count[0] = 0

    def slot_copy(place, slot):
        out = out_ref.at[pl.ds(pl.multiple_of(slot * width, 16), width)]
        return pltpu.make_async_copy(stage.at[place], out, sems.at[place])

    def emit(matrix, compute):
        slot = slot_ref[matrix]

        @pl.when(slot >= 0)
        def _():
            turn = count[0]
            place = lax.rem(turn, ring)
            pl.when(turn >= ring)(slot_copy(place, 0).wait)
            stage[place] = compute().astype(BF16)
            slot_copy(place, slot).start()
            count[0] = turn + 1

    for k in range(K):
        def conv(k=k):
            total = None
            for pair in range(2):
                right = jnp.concatenate(
                    [dcv_ref[0, pair, u, pl.ds(EDGE + MARGIN - k, frames)] for u in range(2)], axis=0
                )
                left = act_ref[0, pair].reshape(width, 2 * frames)
                term = jnp.dot(left, right, preferred_element_type=F32)
                total = term if total is None else total + term
            return total

        emit(section * K + k, conv)

    @pl.when(section == SUBS - 1)
    def _():
        for index in range(4):
            here = slot_ref[SUBS * K + 4] == index
            emit(
                SUBS * K + index,
                lambda here=here: jnp.where(
                    here, res_ref[0].astype(F32) + res_ref[1].astype(F32), 0.0
                ),
            )
        turns = count[0]

        def finish(place, carry):
            pl.when(place < turns)(slot_copy(place, 0).wait)
            return carry

        lax.fori_loop(0, ring, finish, 0)


def run_grads(total_rows, places, act, dcv, res):
    half = act.shape[3]
    ring = 8
    grid_spec = pltpu.PrefetchScalarGridSpec(
        num_scalar_prefetch=1,
        grid=(SUBS,),
        in_specs=[
            pl.BlockSpec((1,) + act.shape[1:], lambda s, t: (s, 0, 0, 0, 0)),
            pl.BlockSpec((1,) + dcv.shape[1:], lambda s, t: (s, 0, 0, 0, 0)),
            pl.BlockSpec(res.shape, lambda s, t: (0, 0, 0)),
        ],
        out_specs=pl.BlockSpec(memory_space=pl.ANY),
        scratch_shapes=[
            pltpu.VMEM((ring, 2 * half, half), BF16),
            pltpu.SMEM((1,), jnp.int32),
            pltpu.SemaphoreType.DMA((ring,)),
        ],
    )
    return pl.pallas_call(
        grad_kernel,
        grid_spec=grid_spec,
        out_shape=jax.ShapeDtypeStruct((total_rows, half), BF16),
        compiler_params=pltpu.CompilerParams(vmem_limit_bytes=60 << 20),
        name="weight_grads",
    )(places, act, dcv, res)


def reduce_kernel(
    depth, block, grads, out, l_ay, l_ax, l_bx, l_by, l_zab, l_zcd, l_c, l_d,
    o_cross, o_line, o_plane, final, result,
    cross_sem, line_sem, plane_sem, out_sem, swap_s, swap_r, ay_s, ay_r, ax_s, ax_r, bx_s, bx_r, by_s, by_r,
    zab_s, zab_r, zcd_s, zcd_r, cd_s, cd_r,
):
    place = QuadPlace(depth)
    z, x, y, core = place.z, place.x, place.y, place.core
    large, small = cut(block, 16)
    start_b, start_c, start_d = large, 2 * large, 2 * large + small
    over_x, over_y, up, down = place.over_x(), place.over_y(), place.up(), place.down()
    pieces = shares(large, 2)
    runs = range(len(pieces))

    def rows(zz, xx, yy, first, count):
        begin = pl.multiple_of(((zz * 2 + xx) * 2 + yy) * block + first, 16)
        return grads.at[pl.ds(begin, count)]

    def part(run):
        return pl.ds(*pieces[run])

    def ay(level, other_x, run):
        xx = 1 - x if other_x else x
        first, count = pieces[run]
        return remote(
            rows(level, xx, 1 - y, first, count), l_ay.at[level, other_x, part(run)],
            ay_s.at[level, other_x, run], ay_r.at[level, other_x, run], over_y,
        )

    def bx(level, other_y, run):
        yy = 1 - y if other_y else y
        first, count = pieces[run]
        return remote(
            rows(level, 1 - x, yy, start_b + first, count), l_bx.at[level, other_y, part(run)],
            bx_s.at[level, other_y, run], bx_r.at[level, other_y, run], over_x,
        )

    def ax(level, run):
        return remote(
            l_ay.at[level, 1, part(run)], l_ax.at[level, part(run)],
            ax_s.at[level, run], ax_r.at[level, run], over_x,
        )

    def by(level, run):
        return remote(
            l_bx.at[level, 1, part(run)], l_by.at[level, part(run)],
            by_s.at[level, run], by_r.at[level, run], over_y,
        )

    def own_cross(level):
        return [
            pltpu.make_async_copy(rows(level, 1 - x, y, 0, large), o_cross.at[level, 0], cross_sem.at[level, 0]),
            pltpu.make_async_copy(rows(level, x, 1 - y, start_b, large), o_cross.at[level, 1], cross_sem.at[level, 1]),
        ]

    def own_line(level):
        return [
            pltpu.make_async_copy(rows(level, x, y, index * large, large), o_line.at[level, index], line_sem.at[level, index])
            for index in range(2)
        ]

    def own_plane(level):
        return [
            pltpu.make_async_copy(
                rows(level, index // 2, index % 2, start_c, 2 * small),
                o_plane.at[level, index], plane_sem.at[level, index],
            )
            for index in range(4)
        ]

    def add(target, others, count, keep=None):
        strip = UNIT

        def one(index, carry):
            at = pl.ds(pl.multiple_of(index * strip, strip), strip)
            value = target[at].astype(F32)
            for ref in others:
                value = value + ref[at].astype(F32)
            if keep is None:
                target[at] = value.astype(BF16)
            else:
                keep[at] = value
            return carry

        lax.fori_loop(0, count // strip, one, 0)

    def sides(step):
        out = [(z - step, z - step >= 0)]
        if not (isinstance(step, int) and step == 0):
            out.append((z + step, z + step < depth))
        return out

    def both(step, action):
        for level, cond in sides(step):
            when(cond, functools.partial(action, level))

    def backwards(body, first, last):
        if depth <= 4:
            for step in range(first, last - 1, -1):
                body(step)
        else:
            def looped(turn, carry):
                body(first - turn)
                return carry

            lax.fori_loop(0, first - last + 1, looped, 0)

    def leaf(step, other, run):
        def go(level):
            ay(level, other, run).start()
            bx(level, other, run).start()

        both(step, go)

    def fetch(step):
        def go(level):
            for copy in own_cross(level) + own_line(level):
                copy.start()

        both(step, go)

    def entry_of(level, way):
        at_home = (z - 1 == level) if way == 0 else (z + 1 == level)
        return level if way == 0 else level + (depth - level) * at_home.astype(jnp.int32)

    def beyond(way):
        return z + 1 < depth if way == 0 else z >= 1

    def zcd(level, way, index, leaf_copy):
        entry = entry_of(level, way)
        if leaf_copy:
            src = rows(level, index // 2, index % 2, start_c, 2 * small)
        else:
            src = l_zcd.at[level, index]
        return remote(
            src, l_zcd.at[entry, index], zcd_s.at[level, index], zcd_r.at[entry, index],
            down if way == 0 else up,
        )

    def zcd_arrived(entry, index):
        ref = l_zcd.at[entry, index]
        remote(ref, ref, zcd_s.at[0, index], zcd_r.at[entry, index], up).wait_recv()

    def lines(step):
        return ((0, z - step, z - step >= 0), (1, z + step, z + step < depth))

    def plane_step(step):
        for way, level, cond in lines(step):
            def go(way=way, level=level):
                @pl.when(beyond(way))
                def _():
                    copies = own_plane(level)
                    for copy in copies:
                        copy.start()
                    for index in range(4):
                        zcd_arrived(level, index)
                        copies[index].wait()
                        add(l_zcd.at[level, index], [o_plane.at[level, index]], 2 * small)
                        zcd(level, way, index, False).start()

                @pl.when(jnp.logical_not(beyond(way)))
                def _():
                    for index in range(4):
                        zcd(level, way, index, True).start()

            when(cond, go)

    def zab(level, way, run):
        entry = entry_of(level, way)
        return [
            remote(
                landing.at[level, part(run)], l_zab.at[entry, index, part(run)],
                zab_s.at[level, index, run], zab_r.at[entry, index, run], down if way == 0 else up,
            )
            for index, landing in enumerate((l_ax, l_by))
        ]

    def zab_arrived(entry, index, run):
        ref = l_zab.at[entry, index, part(run)]
        remote(ref, ref, zab_s.at[0, index, run], zab_r.at[entry, index, run], up).wait_recv()

    def across(run):
        def go(level):
            count = pieces[run][1]
            copies = own_cross(level)
            ay(level, 1, run).wait_recv()
            if run == 0:
                copies[0].wait()
            add(l_ay.at[level, 1, part(run)], [o_cross.at[level, 0, part(run)]], count)
            ax(level, run).start()
            bx(level, 1, run).wait_recv()
            if run == 0:
                copies[1].wait()
            add(l_bx.at[level, 1, part(run)], [o_cross.at[level, 1, part(run)]], count)
            by(level, run).start()

        return go

    def line_step(step, run):
        count = pieces[run][1]
        for way, level, cond in lines(step):
            def go(way=way, level=level):
                copies = own_line(level)
                hops = zab(level, way, run)
                for index, (first_hop, second_hop, first_land, second_land) in enumerate(
                    ((ay, ax, l_ay, l_ax), (bx, by, l_bx, l_by))
                ):
                    first_hop(level, 0, run).wait_recv()
                    second_hop(level, run).wait_recv()
                    if run == 0:
                        copies[index].wait()
                    target = second_land.at[level, part(run)]
                    terms = [first_land.at[level, 0, part(run)], o_line.at[level, index, part(run)]]

                    @pl.when(beyond(way))
                    def _(index=index, target=target, terms=terms):
                        zab_arrived(level, index, run)
                        add(target, terms + [l_zab.at[level, index, part(run)]], count)

                    @pl.when(jnp.logical_not(beyond(way)))
                    def _(target=target, terms=terms):
                        add(target, terms, count)

                    hops[index].start()

            when(cond, go)

    unrolled = depth <= 4
    place.enter()
    for run in runs:
        leaf(depth - 1, 1, run)
    if not unrolled:
        for run in runs:
            leaf(depth - 1, 0, run)
    fetch(depth - 1)

    def turn(step):
        plane_step(step)
        for run in runs:
            if unrolled and step == depth - 1:
                leaf(step, 0, run)
            both(step, across(run))
        for run in runs:
            leaf(step - 1, 1, run)
        fetch(step - 1)
        for run in runs:
            line_step(step, run)
            leaf(step - 1, 0, run)

    backwards(turn, depth - 1, 1)

    above, below = z + 1 < depth, z >= 1
    copies = own_plane(z)
    for copy in copies:
        copy.start()
    for index in range(4):
        pl.when(above)(functools.partial(zcd_arrived, z, index))
        pl.when(below)(functools.partial(zcd_arrived, depth, index))
        copies[index].wait()
        target = o_plane.at[z, index]
        for cond, entries in (
            (above & below, (z, depth)), (above & jnp.logical_not(below), (z,)), (jnp.logical_not(above), (depth,))
        ):
            @pl.when(cond)
            def _(entries=entries, target=target, index=index):
                add(target, [l_zcd.at[entry, index] for entry in entries], 2 * small)

    def block_at(xx, yy, first):
        return o_plane.at[z, xx * 2 + yy, pl.ds(first, small)]

    plane = [
        remote(block_at(1 - x, 1 - y, 0), l_c.at[1], cd_s.at[0], cd_r.at[0], over_y),
        remote(block_at(x, 1 - y, 0), l_c.at[0], cd_s.at[1], cd_r.at[1], over_y),
        remote(block_at(1 - x, 1 - y, small), l_d.at[1], cd_s.at[2], cd_r.at[2], over_x),
        remote(block_at(1 - x, y, small), l_d.at[0], cd_s.at[3], cd_r.at[3], over_x),
        remote(l_c.at[1], l_c.at[2], cd_s.at[4], cd_r.at[4], over_x),
        remote(l_d.at[1], l_d.at[2], cd_s.at[5], cd_r.at[5], over_y),
    ]
    for copy in plane[:4]:
        copy.start()
    for run in runs:
        both(0, across(run))
    plane[0].wait_recv()
    add(l_c.at[1], [block_at(1 - x, y, 0)], small)
    plane[4].start()
    plane[2].wait_recv()
    add(l_d.at[1], [block_at(x, 1 - y, small)], small)
    plane[5].start()

    copies = own_line(z)
    for run in runs:
        first, count = pieces[run]
        for index, (first_hop, second_hop, first_land, second_land) in enumerate(
            ((ay, ax, l_ay, l_ax), (bx, by, l_bx, l_by))
        ):
            first_hop(z, 0, run).wait_recv()
            second_hop(z, run).wait_recv()
            if run == 0:
                copies[index].wait()
            terms = [first_land.at[z, 0, part(run)], o_line.at[z, index, part(run)]]
            target = final.at[pl.ds(index * large + first, count)]
            pl.when(above)(functools.partial(zab_arrived, z, index, run))
            pl.when(below)(functools.partial(zab_arrived, depth, index, run))
            for cond, entries in (
                (above & below, (z, depth)), (above & jnp.logical_not(below), (z,)), (jnp.logical_not(above), (depth,))
            ):
                @pl.when(cond)
                def _(entries=entries, terms=terms, target=target, index=index, land=second_land, run=run, count=count):
                    more = [l_zab.at[entry, index, part(run)] for entry in entries]
                    add(land.at[z, part(run)], terms + more, count, keep=target)

    for copy in (plane[1], plane[3], plane[4], plane[5]):
        copy.wait_recv()
    add(block_at(x, y, 0), [l_c.at[0], l_c.at[2]], small, keep=final.at[pl.ds(start_c, small)])
    add(block_at(x, y, small), [l_d.at[0], l_d.at[2]], small, keep=final.at[pl.ds(start_d, small)])
    own_rows = block // 2
    theirs = final.at[pl.ds(pl.multiple_of((1 - core) * own_rows, 16), own_rows)]
    mine = final.at[pl.ds(pl.multiple_of(core * own_rows, 16), own_rows)]
    cross = remote(theirs, result, swap_s.at[0], swap_r.at[0], place.partner())
    cross.start()
    local = pltpu.make_async_copy(mine, out.at[core], out_sem.at[0])
    local.start()

    def drain(step):
        def go(level):
            for run in runs:
                for other in range(2):
                    ay(level, other, run).wait_send()
                    bx(level, other, run).wait_send()
                ax(level, run).wait_send()
                by(level, run).wait_send()

        both(step, go)
        if not (isinstance(step, int) and step == 0):
            for way, level, cond in lines(step):
                def along(way=way, level=level):
                    for index in range(4):
                        zcd(level, way, index, False).wait_send()
                    for run in runs:
                        for copy in zab(level, way, run):
                            copy.wait_send()

                when(cond, along)

    steps(depth, drain)
    for copy in plane:
        copy.wait_send()
    cross.wait()
    fetched = pltpu.make_async_copy(result, out.at[1 - core], out_sem.at[1])
    fetched.start()
    fetched.wait()
    local.wait()


def run_reduce(depth, block, grads):
    half = grads.shape[1]
    large, small = cut(block, 16)
    dma = pltpu.SemaphoreType.DMA
    anywhere = pl.BlockSpec(memory_space=pl.ANY)
    scratch = [
        pltpu.VMEM((depth, 2, large, half), BF16),
        pltpu.VMEM((depth, large, half), BF16),
        pltpu.VMEM((depth, 2, large, half), BF16),
        pltpu.VMEM((depth, large, half), BF16),
        pltpu.VMEM((depth + 1, 2, large, half), BF16),
        pltpu.VMEM((depth + 1, 4, 2 * small, half), BF16),
        pltpu.VMEM((3, small, half), BF16),
        pltpu.VMEM((3, small, half), BF16),
        pltpu.VMEM((depth, 2, large, half), BF16),
        pltpu.VMEM((depth, 2, large, half), BF16),
        pltpu.VMEM((depth, 4, 2 * small, half), BF16),
        pltpu.VMEM((block, half), F32),
        pltpu.VMEM((block // 2, half), F32),
        dma((depth, 2)), dma((depth, 2)), dma((depth, 4)), dma((2,)), dma((1,)), dma((1,)),
        dma((depth, 2, 2)), dma((depth, 2, 2)), dma((depth, 2)), dma((depth, 2)),
        dma((depth, 2, 2)), dma((depth, 2, 2)), dma((depth, 2)), dma((depth, 2)),
        dma((depth + 1, 2, 2)), dma((depth + 1, 2, 2)),
        dma((depth + 1, 4)), dma((depth + 1, 4)),
        dma((6,)), dma((6,)),
    ]
    return pl.pallas_call(
        functools.partial(reduce_kernel, depth, block),
        out_shape=jax.ShapeDtypeStruct((2, block // 2, half), F32),
        in_specs=[anywhere],
        out_specs=anywhere,
        scratch_shapes=scratch,
        compiler_params=pltpu.CompilerParams(
            collective_id=2, has_side_effects=True, vmem_limit_bytes=48 << 20
        ),
        name="reduce",
    )(grads)


def adamw(gradient, params, first_moment, second_moment, rate, decay):
    moment_new = beta_one * first_moment + (1.0 - beta_one) * gradient
    second_new = beta_two * second_moment + (1.0 - beta_two) * gradient * gradient
    direction = (
        moment_new
        / (1.0 - beta_one**STEP)
        / (jnp.sqrt(second_new / (1.0 - beta_two**STEP)) + adam_eps)
    )
    return (moment_new, second_new, params - rate * (direction + decay * params))


def update_kernel(
    filled_ref, sums_ref, master_ref, one_ref, two_ref, average_ref,
    nrm_ref, gain_ref, shift_ref, norm_one_ref, norm_two_ref,
    grad_ref, one_out, two_out, new_ref, average_out, copy_ref,
    norm_grad_ref, norm_one_out, norm_two_out, norm_new_ref,
):
    @pl.when(pl.program_id(0) == 0)
    def _():
        branches = SUBS + SOURCES
        sums = jnp.concatenate([nrm_ref[0], nrm_ref[1]], axis=1)
        shifts = sums[branches : branches + SUBS]
        both = (
            sums[:branches],
            jnp.concatenate([shifts] + [shifts[SUBS - 1 :]] * SOURCES, axis=0),
        )
        for index, (gradient, params) in enumerate(zip(both, (gain_ref, shift_ref))):
            moment, second, new = adamw(
                gradient, params[...], norm_one_ref[:, index], norm_two_ref[:, index], rate_norm, 0.0
            )
            norm_grad_ref[:, index] = gradient
            norm_one_out[:, index] = moment
            norm_two_out[:, index] = second
            norm_new_ref[:, index] = new

    filled = filled_ref[pl.program_id(0)] > 0
    half = sums_ref.shape[2]
    strip = 32

    def one(index, carry):
        at = pl.ds(pl.multiple_of(index * strip, strip), strip)
        for h in range(2):
            lanes = pl.ds(h * half, half)
            gradient = jnp.where(filled, sums_ref[h, at], 0.0)
            master = master_ref[at, lanes]
            moment, second, new = adamw(
                gradient, master, one_ref[at, lanes], two_ref[at, lanes], rate_main, decay_main
            )
            grad_ref[at, lanes] = gradient
            one_out[at, lanes] = moment
            two_out[at, lanes] = second
            new_ref[at, lanes] = new
            average_out[at, lanes] = ema_keep * average_ref[at, lanes] + (1.0 - ema_keep) * new
            copy_ref[at, lanes] = new.astype(BF16)
        return carry

    lax.fori_loop(0, master_ref.shape[0] // strip, one, 0)


def run_update(filled, sums, master, moment_one, moment_two, average, nrm, gains, shifts, norm_one, norm_two):
    rows, width = master.shape
    step = rows // filled.shape[0]
    spec = pl.BlockSpec((step, width), lambda i, t: (i, 0))

    def whole(array):
        return pl.BlockSpec(array.shape, lambda i, t: (0,) * array.ndim)

    grid_spec = pltpu.PrefetchScalarGridSpec(
        num_scalar_prefetch=1,
        grid=(rows // step,),
        in_specs=[pl.BlockSpec((2, step, sums.shape[2]), lambda i, t: (0, i, 0))] + [spec] * 4
        + [whole(array) for array in (nrm, gains, shifts, norm_one, norm_two)],
        out_specs=[spec] * 6 + [whole(norm_one)] * 4,
    )
    full = jax.ShapeDtypeStruct(master.shape, F32)
    return pl.pallas_call(
        update_kernel,
        grid_spec=grid_spec,
        out_shape=[full] * 5 + [jax.ShapeDtypeStruct(master.shape, BF16)]
        + [jax.ShapeDtypeStruct(norm_one.shape, F32)] * 4,
        compiler_params=pltpu.CompilerParams(vmem_limit_bytes=24 << 20),
        name="update",
    )(filled, sums, master, moment_one, moment_two, average, nrm, gains, shifts, norm_one, norm_two)


def body(
    inputs,
    dense_inputs,
    lengths,
    owners,
    cotangent,
    master,
    moment_one,
    moment_two,
    average,
    norm_gain,
    norm_shift,
    norm_one,
    norm_two,
):
    width = inputs.shape[2]
    wides, narrows = lax.axis_size("wide"), lax.axis_size("narrow")
    depth = wides // 2
    own_rows = master.shape[0]
    block = 2 * own_rows
    capacity = own_rows * narrows // width
    places, ranking = slot_table(owners, capacity)
    act, dcv, res, block_out, input_grad, dense_grad, sums = run_chain(
        depth, block, places, lengths, master, inputs, dense_inputs, cotangent, norm_gain, norm_shift
    )
    compact = ((owners >> 2) * 2 + (owners & 1)) * capacity + ranking
    parity = (lax.axis_index("wide") // 2) % 2
    handled = jnp.where(((owners >> 1) & 1) == parity, compact, -1).astype(jnp.int32)
    kept = 2 * (lax.axis_index("wide") % 2) + lax.axis_index("narrow") // 2
    handled = jnp.concatenate([handled, kept.astype(jnp.int32)[None]])
    grads = run_grads(wides * narrows * own_rows // 2, handled, act, dcv, res)
    reduced = run_reduce(depth // 2, block, grads)

    step = min(own_rows, 256)
    first = (lax.axis_index("wide") * narrows + lax.axis_index("narrow")) * own_rows
    slot_of_step = (first + step * jnp.arange(own_rows // step, dtype=jnp.int32)) // width
    filled = jnp.any(places[None, :] == slot_of_step[:, None], axis=1).astype(jnp.int32)
    updated = run_update(
        filled, reduced, master, moment_one, moment_two, average,
        sums, norm_gain, norm_shift, norm_one.transpose(1, 0, 2), norm_two.transpose(1, 0, 2),
    )
    return (
        block_out,
        input_grad,
        dense_grad,
        *updated[:6],
        *(values.transpose(1, 0, 2) for values in updated[6:]),
    )


def solution(mesh):
    rows = P(AXES, None)
    utterances = P(AXES, None, None)
    in_specs = (
        utterances, utterances, P(AXES), P(), utterances, rows, rows, rows, rows,
        P(), P(), P(), P(),
    )
    out_specs = (
        utterances, utterances, utterances, rows, rows, rows, rows, rows, rows,
        P(), P(), P(), P(),
    )
    return jax.shard_map(body, mesh=mesh, in_specs=in_specs, out_specs=out_specs, check_vma=False)
```

```python
import functools

import jax
import jax.numpy as jnp
from jax import lax
from jax.experimental import pallas as pl
from jax.experimental.pallas import tpu as pltpu
from jax.sharding import PartitionSpec as P

WLOW = 256
WMID = 384
K = 17
SUBS = 5
SOURCES = 6
STEP = 10
MARGIN = K // 2
EDGE = 16
UNIT = 64
F32 = jnp.float32
BF16 = jnp.bfloat16
MESH = pl.DeviceIdType.MESH
AXES = ("wide", "narrow")

norm_eps = 1e-05
beta_one = 0.9
beta_two = 0.999
adam_eps = 1e-08
rate_main = 0.02
rate_norm = 0.15
decay_main = 0.01
ema_keep = 0.8

NT = (((1,), (1,)), ((), ()))


def slot_table(owners, capacity):
    number = owners.shape[0]
    same_owner = owners[:, None] == owners[None, :]
    earlier = jnp.arange(number)[None, :] < jnp.arange(number)[:, None]
    ranking = jnp.sum(jnp.where(same_owner & earlier, 1, 0), axis=1)
    return (owners * capacity + ranking).astype(jnp.int32), ranking.astype(jnp.int32)


def source_pieces(half):
    pieces = []
    start = 0
    for width in (WLOW, WLOW, WLOW, WMID, WMID):
        parts = []
        stop = start + width
        while start < stop:
            chunk, lane = divmod(start, half)
            lanes = min(half - lane, stop - start)
            parts.append((chunk, lane, lanes))
            start += lanes
        pieces.append(parts)
    return pieces


class Place:
    def __init__(self, depth):
        wide = lax.axis_index("wide")
        narrow = lax.axis_index("narrow")
        self.depth = depth
        self.core = lax.rem(narrow, 2)
        self.y = narrow // 2
        self.x = lax.rem(wide, 2)
        self.z = wide // 2
        self.groups = depth * 4
        self.me = wide * 2 + self.y

    def at(self, z, x, y, core):
        return (z * 2 + x, y * 2 + core)

    def beside(self):
        return self.at(self.z + 1 - 2 * lax.rem(self.z, 2), self.x, self.y, self.core)

    def partner(self):
        return self.at(self.z, self.x, self.y, 1 - self.core)

    def over_x(self):
        return self.at(self.z, 1 - self.x, self.y, self.core)

    def over_y(self):
        return self.at(self.z, self.x, 1 - self.y, self.core)

    def up(self):
        return self.at(self.z + 1, self.x, self.y, self.core)

    def down(self):
        return self.at(self.z - 1, self.x, self.y, self.core)

    def far(self, turn):
        z = lax.rem(self.z + 1 + turn // 4, self.depth)
        return self.at(z, lax.rem(turn // 2, 2), lax.rem(turn, 2), self.core)

    def near(self):
        return (
            self.over_x(), self.over_y(), self.at(self.z, 1 - self.x, 1 - self.y, self.core)
        )

    def enter(self):
        barrier = pltpu.get_barrier_semaphore()

        def greet(device):
            pl.semaphore_signal(barrier, inc=1, device_id=device, device_id_type=MESH)

        for device in (self.partner(), self.over_x(), self.over_y()):
            greet(device)
        above, below = self.z + 1 < self.depth, self.z >= 1
        pl.when(above)(functools.partial(greet, self.up()))
        pl.when(below)(functools.partial(greet, self.down()))
        met = 3 + above.astype(jnp.int32) + below.astype(jnp.int32)
        pl.semaphore_wait(barrier, met)


class QuadPlace(Place):
    def __init__(self, depth):
        super().__init__(depth)
        self.parity = lax.rem(self.z, 2)
        self.z = self.z // 2

    def at(self, z, x, y, core):
        return ((2 * z + self.parity) * 2 + x, y * 2 + core)


def remote(src, dst, send_sem, recv_sem, device):
    return pltpu.make_async_remote_copy(
        src_ref=src,
        dst_ref=dst,
        send_sem=send_sem,
        recv_sem=recv_sem,
        device_id=device,
        device_id_type=MESH,
    )


def when(cond, action):
    if cond is None:
        action()
    else:
        pl.when(cond)(action)


def cut(block, share):
    units = block // UNIT
    small = max(1, units // share)
    return (units - 2 * small) // 2 * UNIT, small * UNIT


def steps(depth, body, first=0):
    if depth <= 4:
        for step in range(first, depth):
            body(step)
    else:
        def looped(step, carry):
            body(step)
            return carry

        if first == 0:
            body(0)
        lax.fori_loop(max(first, 1), depth, looped, 0)


def shares(rows, number):
    units = rows // UNIT
    out = []
    first = 0
    for index in range(number):
        count = units // number + (1 if index < units % number else 0)
        if count:
            out.append((first * UNIT, count * UNIT))
        first += count
    return out


def tree_sems(depth):
    dma = pltpu.SemaphoreType.DMA
    return [
        dma((depth, 2, 2)), dma((depth, 2)), dma((depth, 2, 4)), dma((depth, 4)),
        dma((depth, 2)), dma((depth, 2)), dma((depth, 2, 2)), dma((depth, 2, 2)),
        dma((depth, 2)), dma((depth, 2)), dma((depth, 2, 2)), dma((depth, 2, 2)),
        dma((6,)), dma((6,)),
    ]


def gather_bank(place, bank, block, sems, first_idle=lambda: None, second_idle=lambda: None):
    depth, z, x, y = place.depth, place.z, place.x, place.y
    large, small = cut(block, 9)
    (zab_s, zab_r, zcd_s, zcd_r, ax_s, ax_r, ay_s, ay_r, by_s, by_r, bx_s, bx_r, cd_s, cd_r) = sems
    pieces = shares(large, 2)
    runs = range(len(pieces))

    def rows(zz, xx, yy, first, count):
        begin = ((zz * 2 + xx) * 2 + yy) * (block // UNIT) + first // UNIT
        return bank.at[pl.ds(begin, count // UNIT)]

    def move(zz, xx, yy, first, count, send_sem, recv_sem, device):
        ref = rows(zz, xx, yy, first, count)
        return remote(ref, ref, send_sem, recv_sem, device)

    start_c, start_d = 2 * large, 2 * large + small
    over_x, over_y, up, down = place.over_x(), place.over_y(), place.up(), place.down()

    def sides(step):
        out = [(z - step, z - step >= 0)]
        if not (isinstance(step, int) and step == 0):
            out.append((z + step, z + step < depth))
        return out

    def both(step, action):
        for level, cond in sides(step):
            when(cond, functools.partial(action, level))

    def z_moves(step, run):
        out = []
        low, high = z - step, z + step
        for level, cond, device, way in (
            (low, (low >= 0) & (z + 1 < depth), up, 0),
            (high, (high < depth) & (z >= 1), down, 1),
        ):
            if run is not None:
                first, count = pieces[run]
                copy = move(
                    level, x, y, 2 * first, 2 * count, zab_s.at[level, way, run], zab_r.at[level, run], device
                )
                out.append((cond, copy))
                continue
            for index in range(4):
                copy = move(
                    level, index // 2, index % 2, start_c, 2 * small, zcd_s.at[level, way, index],
                    zcd_r.at[level, index], device,
                )
                out.append((cond, copy))
        return out

    def ax(level, run):
        first, count = pieces[run]
        return move(level, x, y, 2 * first, count, ax_s.at[level, run], ax_r.at[level, run], over_x)

    def by(level, run):
        first, count = pieces[run]
        return move(level, x, y, 2 * first + count, count, by_s.at[level, run], by_r.at[level, run], over_y)

    def ay(level, run, other):
        first, count = pieces[run]
        xx = 1 - x if other else x
        return move(level, xx, y, 2 * first, count, ay_s.at[level, run, other], ay_r.at[level, run, other], over_y)

    def bx(level, run, other):
        first, count = pieces[run]
        yy = 1 - y if other else y
        return move(
            level, x, yy, 2 * first + count, count, bx_s.at[level, run, other], bx_r.at[level, run, other], over_x
        )

    plane = [
        move(z, x, y, start_c, small, cd_s.at[0], cd_r.at[0], over_x),
        move(z, x, y, start_d, small, cd_s.at[1], cd_r.at[1], over_y),
        move(z, x, y, start_c, small, cd_s.at[2], cd_r.at[2], over_y),
        move(z, 1 - x, y, start_c, small, cd_s.at[3], cd_r.at[3], over_y),
        move(z, x, y, start_d, small, cd_s.at[4], cd_r.at[4], over_x),
        move(z, x, 1 - y, start_d, small, cd_s.at[5], cd_r.at[5], over_x),
    ]

    def run_step(step):
        home = isinstance(step, int) and step == 0
        if home:
            plane[0].start()
            plane[1].start()
        for run in runs:
            first, count = pieces[run]
            if not home:
                both(
                    step,
                    lambda level, run=run, first=first, count=count: move(
                        level, x, y, 2 * first, 2 * count, zab_s.at[level, 0, run], zab_r.at[level, run], up
                    ).wait_recv(),
                )
            for cond, copy in z_moves(step, run):
                when(cond, copy.start)

            def begin(level, run=run):
                ax(level, run).start()
                by(level, run).start()

            both(step, begin)
        if home:
            first_idle()
            plane[2].start()
            plane[4].start()
            plane[0].wait_recv()
            plane[3].start()
            plane[1].wait_recv()
            plane[5].start()
            for copy in plane[2:]:
                copy.wait_recv()
            for cond, copy in z_moves(step, None):
                when(cond, copy.start)
        for run in runs:
            def across(level, run=run):
                ay(level, run, 0).start()
                bx(level, run, 0).start()
                ax(level, run).wait_recv()
                ay(level, run, 1).start()
                by(level, run).wait_recv()
                bx(level, run, 1).start()

            both(step, across)
        if not home:
            def arrived(level):
                for index in range(4):
                    move(
                        level, x, y, start_c, 2 * small, zcd_s.at[level, 0, index],
                        zcd_r.at[level, index], up,
                    ).wait_recv()

            both(step, arrived)
            for cond, copy in z_moves(step, None):
                when(cond, copy.start)
        if home:
            second_idle()

    steps(depth, run_step)

    def drain(step):
        def finish(level):
            for run in runs:
                for other in range(2):
                    ay(level, run, other).wait_recv()
                    bx(level, run, other).wait_recv()
                    ay(level, run, other).wait_send()
                    bx(level, run, other).wait_send()
                ax(level, run).wait_send()
                by(level, run).wait_send()

        both(step, finish)
        for kind in list(runs) + [None]:
            for cond, copy in z_moves(step, kind):
                when(cond, copy.wait_send)

    steps(depth, drain)
    for copy in plane:
        copy.wait_send()


def strips(rows, body, carry=0):
    strip = 64

    def one(index, carry):
        return body(pl.ds(pl.multiple_of(index * strip, strip), strip), carry)

    return lax.fori_loop(0, rows // strip, one, carry, unroll=True)


def fold(values):
    return jnp.sum(values.reshape(-1, 8, values.shape[1]), axis=0)


def chain_kernel(
    depth, block,
    slot_ref, length_ref, master, own_x, own_dense, own_cot, gain_ref, shift_ref,
    act_out, dcv_out, res_out, blk_out, ig_out, dg_out, nrm_out,
    bank, act, dense, mask, cot, raw, side, pre4, slope, upown, upsend, uprecv, dcv, dsd, res, res_x, res_y, dgrecv,
    igrecv, stage, turned, nrm, blk, blksend, keep, ex_side, ex_last, ex_sub,
    load_sem, swap_s, swap_r, act_s, act_r, up_s, up_r, ex_s, ex_r, out_sem, far_s, far_r, near_s, near_r, own_sem, edge_sem,
    *tree,
):
    place = Place(depth)
    core, other = place.core, 1 - place.core
    partner, beside = place.partner(), place.beside()
    half = bank.shape[2]
    width = 2 * half
    frames = mask.shape[1]
    rows = 2 * frames
    chunks = dense.shape[0]
    pieces = source_pieces(half)
    inner = pl.ds(EDGE, frames)
    own_rows = block // 2
    load_rows = min(own_rows, rows)
    loads_of = own_rows // load_rows

    mats_in = []
    for part in range(loads_of):
        for h in range(2):
            mats_in.append(
                pltpu.make_async_copy(
                    master.at[pl.ds(part * load_rows, load_rows), pl.ds(h * half, half)],
                    side.at[part * 2 + h, pl.ds(0, load_rows)],
                    load_sem.at[part * 2 + h],
                )
            )
    x_in = [
        pltpu.make_async_copy(
            own_x.at[0, :, pl.ds(h * half, half)], act.at[0, h, core, inner], load_sem.at[6 + h]
        )
        for h in range(2)
    ]
    dense_in = [
        pltpu.make_async_copy(
            own_dense.at[0, :, pl.ds(chunk * half, half)], dense.at[chunk, core], load_sem.at[8 + chunk]
        )
        for chunk in range(chunks)
    ]
    ours_lanes = pl.ds(pl.multiple_of(core * half, half), half)
    theirs_lanes = pl.ds(pl.multiple_of(other * half, half), half)
    cot_in = pltpu.make_async_copy(own_cot.at[0, :, ours_lanes], cot.at[core], load_sem.at[8 + chunks])
    for copy in mats_in + x_in + dense_in + [cot_in]:
        copy.start()
    place.enter()
    base = place.me * (block // UNIT) + core * (own_rows // UNIT)
    units = load_rows // UNIT
    send_mats = []
    for part in range(loads_of):
        def narrow(unit, carry, part=part):
            at = pl.ds(pl.multiple_of(unit * UNIT, UNIT), UNIT)
            stage[part * units + unit] = side[part * 2 + other, at].astype(BF16)
            return carry

        def keep_own(unit, carry, part=part):
            at = pl.ds(pl.multiple_of(unit * UNIT, UNIT), UNIT)
            bank[base + part * units + unit] = side[part * 2 + core, at].astype(BF16)
            return carry

        mats_in[2 * part].wait()
        mats_in[2 * part + 1].wait()
        lax.fori_loop(0, units, narrow, 0, unroll=2)
        copy = remote(
            stage.at[pl.ds(part * units, units)], bank.at[pl.ds(base + part * units, units)],
            swap_s.at[9 + part], swap_r.at[9 + part], partner,
        )
        copy.start()
        send_mats.append(copy)
        lax.fori_loop(0, units, keep_own, 0, unroll=2)
    mask[core] = (
        lax.broadcasted_iota(jnp.int32, (frames, 128), 0) < length_ref[0]
    ).astype(F32)
    edge_zero = jnp.zeros((EDGE, half), BF16)

    def clear(section, carry):
        for u in range(2):
            for h in range(2):
                act[section, h, u, pl.ds(0, EDGE)] = edge_zero
                act[section, h, u, pl.ds(EDGE + frames, EDGE)] = edge_zero
            dcv[section, u, pl.ds(0, EDGE)] = edge_zero
            dcv[section, u, pl.ds(EDGE + frames, EDGE)] = edge_zero
        return carry

    lax.fori_loop(0, SUBS, clear, 0)
    edges = [
        pltpu.make_async_copy(
            dcv.at[:, :, pl.ds(first, EDGE)], dcv_out.at[:, 1, :, pl.ds(first, EDGE)], edge_sem.at[index]
        )
        for index, first in enumerate((0, EDGE + frames))
    ]
    for copy in edges:
        copy.start()
    for copy in send_mats:
        copy.wait()

    def prepare():
        for copy in x_in + dense_in + [cot_in]:
            copy.wait()
        low_mask = jnp.concatenate([mask[core].astype(BF16)] * (half // 128), axis=1)
        for h in range(2):
            act[0, h, core, inner] = act[0, h, core, inner] * low_mask
        for chunk in range(chunks):
            dense[chunk, core] = dense[chunk, core] * low_mask
        own = act.at[0, :, core, inner]
        swaps = [
            remote(own, own, swap_s.at[1], swap_r.at[1], partner),
            remote(dense.at[:, core], dense.at[:, core], swap_s.at[2], swap_r.at[2], partner),
            remote(mask.at[core], mask.at[core], swap_s.at[3], swap_r.at[3], partner),
            remote(own_cot.at[0, :, theirs_lanes], cot.at[core], swap_s.at[4], swap_r.at[4], partner),
        ]
        for copy in swaps:
            copy.start()
        return swaps

    def own_act(section):
        half_of = turned.at[lax.rem(section, 2)]
        return [
            pltpu.make_async_copy(half_of, act_out.at[section, 0, core], own_sem.at[section]),
            remote(
                half_of, act_out.at[section, 0, core], near_s.at[section], near_r.at[section], partner
            ),
            remote(
                half_of, act_out.at[section, 1, core], far_s.at[section], far_r.at[section], beside
            ),
        ]

    def pass_act(section):
        ref = act_out.at[section, 1, core]
        return remote(ref, ref, near_s.at[SUBS + section], near_r.at[SUBS + section], partner)

    def turn_act(section):
        turned[lax.rem(section, 2)] = jnp.concatenate(
            [act[section, core, u, inner] for u in range(2)], axis=0
        ).T
        for copy in own_act(section)[:2]:
            copy.start()

    def free_turned(section):
        copies = own_act(section)
        copies[0].wait()
        copies[1].wait_send()
        copies[2].wait_send()

    swaps = []

    def arrived():
        for copy in swaps:
            copy.wait()
        turn_act(0)
        own_act(0)[2].start()

    gather_bank(place, bank, block, tree, lambda: swaps.extend(prepare()), arrived)

    outs = []

    def put(src, dst):
        copy = pltpu.make_async_copy(src, dst, out_sem.at[len(outs)])
        copy.start()
        outs.append(copy)

    def far_dcv(section):
        return remote(
            dcv.at[section, :, inner], dcv_out.at[section, 1, :, inner],
            far_s.at[SUBS + section], far_r.at[SUBS + section], beside,
        )

    def keep_dcv(section):
        return pltpu.make_async_copy(
            dcv.at[section], dcv_out.at[section, 0], own_sem.at[SUBS + section]
        )

    def res_over(step):
        if step == 0:
            src, dst, device = res.at[pl.ds(2 * (1 - place.x), 2)], res_x, place.over_x()
        elif step == 1:
            src, dst, device = res_x.at[1 - place.y], res_y, place.over_y()
        else:
            src, dst, device = res_y, res_out.at[1], beside
        at = 2 * SUBS + step
        return remote(src, dst, far_s.at[at], far_r.at[at], device)

    def weight(matrix, first, count):
        begin = slot_ref[matrix] * (width // UNIT) + first // UNIT
        return jnp.concatenate([bank[begin + i] for i in range(count // UNIT)], axis=0)

    def valid(at):
        return jnp.concatenate([mask_rows(at)] * (half // 128), axis=1)

    def mask_rows(at):
        return mask[at.start // frames, pl.ds(pl.multiple_of(lax.rem(at.start, frames), 64), at.size)]

    def gain(index):
        return gain_ref[pl.ds(index, 1), ours_lanes]

    def bias(index):
        return shift_ref[pl.ds(index, 1), ours_lanes]

    def share(buffer, index, values):
        buffer[place.me] = values
        mine = buffer.at[place.me]

        def go(turn, carry):
            remote(mine, mine, ex_s.at[index, 1], ex_r.at[index, 1], place.far(turn)).start()
            return carry

        lax.fori_loop(0, place.groups - 4, go, 0, unroll=place.groups <= 16)
        for device in place.near():
            remote(mine, mine, ex_s.at[index, 0], ex_r.at[index, 0], device).start()

    def shared(buffer, index, between=lambda: None):
        for kind, number in ((0, 3), (1, place.groups - 4)):
            some = buffer.at[pl.ds(0, number)]
            copy = remote(some, some, ex_s.at[index, kind], ex_r.at[index, kind], place.over_x())
            copy.wait_recv()
            copy.wait_send()
            if kind == 0:
                between()
        return buffer[...]

    def total_of(values):
        return jnp.sum(values, axis=0, keepdims=True)

    def counted():
        def add(at, carry):
            return carry + fold(valid(at))

        return total_of(strips(rows, add, jnp.zeros((8, half), F32)))

    def moments(load, count):
        pivot = load(pl.ds(0, 8))[0:1]

        def add(at, carry):
            first, second = carry
            valid_now = valid(at)
            off = (load(at) - pivot) * valid_now
            return first + fold(off), second + fold(off * off)

        zero = jnp.zeros((8, half), F32)
        first, second = strips(rows, add, (zero, zero))
        first, second = total_of(first), total_of(second)
        return first + count * pivot, jnp.maximum(second - first * first / count, 0.0)

    def merge(count, total, squares):
        frame_total = jnp.sum(count, axis=0)
        mean = jnp.sum(total, axis=0) / frame_total
        shift = total / count - mean[None]
        variance = jnp.sum(squares + count * shift * shift, axis=0) / frame_total
        return mean[None], lax.rsqrt(variance + norm_eps)[None], frame_total[None]

    def save(index, mean, inverse):
        scale = gain(index) * inverse
        keep[0, pl.ds(index, 1)] = inverse
        keep[1, pl.ds(index, 1)] = mean * inverse
        keep[2, pl.ds(index, 1)] = scale
        keep[3, pl.ds(index, 1)] = bias(index) - mean * scale

    def kept(row, index):
        return keep[row, pl.ds(index, 1)]

    count = counted()
    def side_branches():
        totals, squares = [], []
        for index in range(SOURCES):
            value = None
            if index < SOURCES - 1:
                for chunk, lane, lanes in pieces[index]:
                    left = dense[chunk].reshape(rows, half)[:, lane : lane + lanes]
                    right = weight(SUBS * K + chunk // 2, (chunk % 2) * half + lane, lanes)
                    term = jnp.dot(left, right, preferred_element_type=F32)
                    value = term if value is None else value + term
            else:
                for h in range(2):
                    left = jnp.concatenate([act[0, h, u, inner] for u in range(2)], axis=0)
                    term = jnp.dot(left, weight(SUBS * K + 3, h * half, half), preferred_element_type=F32)
                    value = term if value is None else value + term
            side[index] = value
            total, square = moments(lambda at, index=index: side[index, at], count)
            totals.append(total)
            squares.append(square)
        fill = jnp.zeros((3, half), F32)
        share(ex_side, 0, jnp.concatenate([count] + totals + squares + [fill], axis=0))

    def convolve(section, h, first):
        value = None
        for k in range(K):
            left = jnp.concatenate(
                [act[section, h, u, pl.ds(EDGE - MARGIN + k, frames)] for u in range(2)], axis=0
            )
            term = jnp.dot(
                left, weight(section * K + k, h * half, half), preferred_element_type=F32
            )
            value = term if value is None else value + term
            if k % 2 == 1 or k == K - 1:
                if first and k == 1:
                    raw[section] = value
                else:
                    raw[section] += value
                value = None

    def swap_act(section):
        own = act.at[section, core, :, inner]
        return remote(own, own, act_s.at[section], act_r.at[section], partner)

    def forward(section, last):
        convolve(section, core, True)
        if isinstance(section, int):
            if section > 0:
                swap_act(section).wait_recv()
        else:
            pl.when(section > 0)(swap_act(section).wait_recv)
        convolve(section, other, False)
        total, square = moments(lambda at: raw[section, at], count)
        buffer = ex_sub.at[lax.rem(section, 2)]
        share(buffer, 1 + section, jnp.concatenate([count, total, square, jnp.zeros_like(count)], axis=0))

        def pre_side():
            parts = shared(ex_side, 0)
            for index in range(SOURCES):
                mean, inverse, _ = merge(
                    parts[:, 0], parts[:, 1 + index], parts[:, 1 + SOURCES + index]
                )
                save(SUBS + index, mean, inverse)
            scales = [kept(2, SUBS + index) for index in range(SOURCES)]
            offset = sum(kept(3, SUBS + index) for index in range(SOURCES))

            def add(at, carry):
                before = offset
                for index in range(SOURCES):
                    before = before + side[index, at] * scales[index]
                pre4[at] = before
                return carry

            strips(rows, add)

        def background():
            own_act(section - 1)[2].wait_recv()
            pass_act(section - 1).start()
            if isinstance(section, int):
                free_turned(section - 2)
            else:
                pl.when(section > 1)(functools.partial(free_turned, section - 2))
            turn_act(section)

        if isinstance(section, int):
            background()
            parts = shared(buffer, 1 + section, own_act(section)[2].start)
        else:
            pl.when(section == 0)(side_branches)
            pl.when(section > 0)(background)
            pl.when(section == 1)(pre_side)
            parts = shared(
                buffer, 1 + section, lambda: pl.when(section > 0)(own_act(section)[2].start)
            )
        mean, inverse, frame_total = merge(parts[:, 0], parts[:, 1], parts[:, 2])
        save(section, mean, inverse)
        scale, offset = kept(2, section), kept(3, section)

        def activate(at, carry):
            before = raw[section, at] * scale + offset
            if last:
                before = before + pre4[at]
                pre4[at] = before
            hidden = (before * jax.nn.sigmoid(before) * valid(at)).astype(BF16)
            u = at.start // frames
            first = pl.multiple_of(lax.rem(at.start, frames), 64)
            if last:
                @pl.when(u == core)
                def _():
                    blk[core, pl.ds(first, at.size)] = hidden

                @pl.when(u != core)
                def _():
                    blksend[pl.ds(first, at.size)] = hidden
            else:
                act[section + 1, core, u, pl.ds(pl.multiple_of(first + EDGE, EDGE), at.size)] = hidden
            return carry

        strips(rows, activate)
        if not last:
            swap_act(section + 1).start()
        return frame_total

    def looped(section, carry):
        forward(section, False)
        return carry

    lax.fori_loop(0, SUBS - 1, looped, 0)
    frame_total = forward(SUBS - 1, True)
    blk_copy = remote(blksend, blk.at[core], swap_s.at[5], swap_r.at[5], partner)
    blk_copy.start()
    for section in range(1, SUBS):
        swap_act(section).wait_send()
    for section in (SUBS - 2, SUBS - 1):
        free_turned(section)

    def hat_of(values, index):
        return values * kept(0, index) - kept(1, index)

    def back_half(section, h):
        total = None
        value = None
        for k in range(K):
            left = jnp.concatenate(
                [dcv[section, u, pl.ds(EDGE + MARGIN - k, frames)] for u in range(2)], axis=0
            )
            term = lax.dot_general(
                left, weight(section * K + k, h * half, half), NT, preferred_element_type=F32
            )
            value = term if value is None else value + term
            if k % 2 == 1 or k == K - 1:
                total = value if total is None else total + value
                value = None
        return total

    def up_copy(section):
        slot = lax.rem(section, 2)
        return remote(upsend, uprecv.at[slot], up_s.at[slot], up_r.at[slot], partner)

    def backward(section):
        upsend[...] = back_half(section, other)
        up_copy(section).start()
        upown[...] = back_half(section, core)

    def slopes(section, upstream, before_of, others, target):
        sources = [(lambda at: raw[section, at], section)] + others

        def one(at, carry):
            before = before_of(at)
            sigmoid = jax.nn.sigmoid(before)
            now = upstream(at) * valid(at) * (sigmoid * (1.0 + before * (1.0 - sigmoid)))
            target[at] = now
            out = [carry[0] + fold(now)]
            for (load, index), so_far in zip(sources, carry[1:]):
                out.append(so_far + fold(now * hat_of(load(at), index)))
            return tuple(out)

        zero = jnp.zeros((8, half), F32)
        return [total_of(value) for value in strips(rows, one, (zero,) * (1 + len(sources)))]

    def branch(source, load, index, shift_sum, gain_sum, store):
        scale = kept(2, index)
        shift_mean, gain_mean = shift_sum / frame_total, gain_sum / frame_total

        def one(at, carry):
            value = source[at] - shift_mean - hat_of(load(at), index) * gain_mean
            store(at, (valid(at) * scale * value).astype(BF16))
            return carry

        strips(rows, one)

    def conv_branch(source, section, shift_sum, gain_sum):
        def store(at, value):
            first = pl.multiple_of(lax.rem(at.start, frames) + EDGE, EDGE)
            dcv[section, at.start // frames, pl.ds(first, at.size)] = value

        branch(source, lambda at: raw[section, at], section, shift_sum, gain_sum, store)
        far_dcv(section).start()
        keep_dcv(section).start()

    def cot_at(at):
        return cot[
            at.start // frames, pl.ds(pl.multiple_of(lax.rem(at.start, frames), 64), at.size)
        ].astype(F32)

    sums = slopes(
        SUBS - 1, cot_at, lambda at: pre4[at],
        [(lambda at, index=index: side[index, at], SUBS + index) for index in range(SOURCES)],
        pre4,
    )
    share(ex_last, SUBS + 1, jnp.concatenate(sums, axis=0))
    sums = jnp.sum(shared(ex_last, SUBS + 1), axis=0)
    shift_sum = sums[0:1]
    conv_branch(pre4, SUBS - 1, shift_sum, sums[1:2])
    nrm[core] = jnp.zeros_like(nrm[0])
    nrm[core, pl.ds(SUBS - 1, 1 + SOURCES)] = sums[1:]
    nrm[core, pl.ds(SUBS + SOURCES + SUBS - 1, 1)] = shift_sum
    backward(SUBS - 1)

    def side_grads():
        for index in range(SOURCES):
            def store(at, value, index=index):
                dsd[index, at] = value

            branch(
                pre4, lambda at, index=index: side[index, at], SUBS + index, shift_sum,
                sums[2 + index : 3 + index], store,
            )

    theirs = pl.multiple_of(other * frames, frames)
    ours = pl.multiple_of(core * frames, frames)
    dg_copy = remote(
        side.at[:, pl.ds(theirs, frames)], dgrecv, swap_s.at[6], swap_r.at[6], partner
    )

    def dense_grads():
        for index in range(SOURCES - 1):
            for chunk, lane, lanes in pieces[index]:
                right = weight(SUBS * K + chunk // 2, (chunk % 2) * half + lane, lanes)
                side[chunk, :, pl.ds(lane, lanes)] = lax.dot_general(
                    dsd[index], right, NT, preferred_element_type=F32
                )
        dg_copy.start()

    def residual_grads():
        rows_of = [[] for _ in range(chunks)]
        for index, parts in enumerate(pieces):
            for chunk, lane, lanes in parts:
                rows_of[chunk].append((lane, lanes, index))
        for chunk in range(chunks):
            turned = dense[chunk].reshape(rows, half).T
            for lane, lanes, index in rows_of[chunk]:
                res[chunk // 2, pl.ds((chunk % 2) * half + lane, lanes)] = jnp.dot(
                    turned[lane : lane + lanes], dsd[index], preferred_element_type=F32
                ).astype(BF16)
        for h in range(2):
            turned = jnp.concatenate([act[0, h, u, inner] for u in range(2)], axis=0).T
            res[3, pl.ds(h * half, half)] = jnp.dot(
                turned, dsd[SOURCES - 1], preferred_element_type=F32
            ).astype(BF16)

    dg_puts = [
        pltpu.make_async_copy(
            dgrecv.at[chunk], dg_out.at[0, :, pl.ds(chunk * half, half)], load_sem.at[chunk]
        )
        for chunk in range(chunks)
    ]

    def finish_dense():
        dg_copy.wait()
        own_valid = jnp.concatenate([mask[core]] * (half // 128), axis=1)
        for chunk in range(chunks):
            dgrecv[chunk] = (dgrecv[chunk] + side[chunk, pl.ds(ours, frames)]) * own_valid
            dg_puts[chunk].start()

    def looped_back(turn, carry):
        section = SUBS - 2 - turn
        copy = up_copy(section + 1)
        copy.wait()
        slot = lax.rem(section + 1, 2)
        scale, offset = kept(2, section), kept(3, section)
        sums_now = slopes(
            section, lambda at: upown[at] + uprecv[slot, at],
            lambda at: raw[section, at] * scale + offset, [], slope,
        )
        zero = jnp.zeros((2, half), F32)
        buffer = ex_sub.at[lax.rem(section, 2)]
        share(buffer, SUBS + 2 + section, jnp.concatenate(sums_now + [zero], axis=0))

        @pl.when(section == SUBS - 2)
        def _():
            side_grads()
            residual_grads()
            res_over(0).start()
            dense_grads()

        @pl.when(section == SUBS - 3)
        def _():
            res_over(0).wait_recv()
            for index in range(2):
                total = res[2 * place.x + index].astype(F32) + res_x[index].astype(F32)
                res_x[index] = total.astype(BF16)
            res_over(1).start()
            finish_dense()
            own_act(SUBS - 1)[2].wait_recv()
            pass_act(SUBS - 1).start()

        @pl.when(section == SUBS - 4)
        def _():
            res_over(1).wait_recv()
            res_y[...] = (res_y[...].astype(F32) + res_x[place.y].astype(F32)).astype(BF16)

        sums_now = jnp.sum(shared(buffer, SUBS + 2 + section), axis=0)
        pl.when(section == SUBS - 4)(lambda: res_over(2).start())
        conv_branch(slope, section, sums_now[0:1], sums_now[1:2])
        nrm[core, pl.ds(section, 1)] = sums_now[1:2]
        nrm[core, pl.ds(SUBS + SOURCES + section, 1)] = sums_now[0:1]

        @pl.when(section > 0)
        def _():
            backward(section)

        return carry

    lax.fori_loop(0, SUBS - 1, looped_back, 0)
    put(res_y, res_out.at[0])
    nrm_copy = remote(nrm.at[core], nrm.at[core], swap_s.at[7], swap_r.at[7], partner)
    nrm_copy.start()
    for h in range(2):
        uprecv[h] = back_half(0, h) + lax.dot_general(
            dsd[SOURCES - 1], weight(SUBS * K + 3, h * half, half), NT, preferred_element_type=F32
        )
    ig_copy = remote(
        uprecv.at[:, pl.ds(theirs, frames)], igrecv, swap_s.at[8], swap_r.at[8], partner
    )
    ig_copy.start()
    own_valid = jnp.concatenate([mask[core]] * (half // 128), axis=1)
    blk_copy.wait()
    nrm_copy.wait()
    put(nrm, nrm_out)
    ig_copy.wait()
    for h in range(2):
        igrecv[h] = (igrecv[h] + uprecv[h, pl.ds(ours, frames)]) * own_valid
        put(igrecv.at[h], ig_out.at[0, :, pl.ds(h * half, half)])
        put(blk.at[h], blk_out.at[0, :, pl.ds(h * half, half)])
    for section in range(SUBS):
        own_act(section)[1].wait_recv()
        pass_act(section).wait()
        far_dcv(section).wait()
        keep_dcv(section).wait()
    res_over(0).wait_send()
    res_over(1).wait_send()
    res_over(2).wait()
    for copy in outs + dg_puts + edges:
        copy.wait()


def run_chain(depth, block, places, lengths, master, x, dense, cot, gains, shifts):
    frames, width = x.shape[1:]
    half = width // 2
    rows = 2 * frames
    chunks = dense.shape[2] // half
    padded = frames + 2 * EDGE
    groups = depth * 4
    dma = pltpu.SemaphoreType.DMA
    anywhere = pl.BlockSpec(memory_space=pl.ANY)
    vmem = pl.BlockSpec(memory_space=pltpu.VMEM)
    smem = pl.BlockSpec(memory_space=pltpu.SMEM)
    out_shape = [
        jax.ShapeDtypeStruct((SUBS, 2, 2, half, rows), BF16),
        jax.ShapeDtypeStruct((SUBS, 2, 2, padded, half), BF16),
        jax.ShapeDtypeStruct((2, width, half), BF16),
        jax.ShapeDtypeStruct(x.shape, BF16),
        jax.ShapeDtypeStruct(x.shape, F32),
        jax.ShapeDtypeStruct(dense.shape, F32),
        jax.ShapeDtypeStruct((2, 16, half), F32),
    ]
    scratch = [
        pltpu.VMEM((groups * block // UNIT, UNIT, half), BF16),
        pltpu.VMEM((SUBS, 2, 2, padded, half), BF16),
        pltpu.VMEM((chunks, 2, frames, half), BF16),
        pltpu.VMEM((2, frames, 128), F32),
        pltpu.VMEM((2, frames, half), BF16),
        pltpu.VMEM((SUBS, rows, half), F32),
        pltpu.VMEM((SOURCES, rows, half), F32),
        pltpu.VMEM((rows, half), F32),
        pltpu.VMEM((rows, half), F32),
        pltpu.VMEM((rows, half), F32),
        pltpu.VMEM((rows, half), F32),
        pltpu.VMEM((2, rows, half), F32),
        pltpu.VMEM((SUBS, 2, padded, half), BF16),
        pltpu.VMEM((SOURCES, rows, half), BF16),
        pltpu.VMEM((4, width, half), BF16),
        pltpu.VMEM((2, width, half), BF16),
        pltpu.VMEM((width, half), BF16),
        pltpu.VMEM((chunks, frames, half), F32),
        pltpu.VMEM((2, frames, half), F32),
        pltpu.VMEM((block // 2 // UNIT, UNIT, half), BF16),
        pltpu.VMEM((2, half, rows), BF16),
        pltpu.VMEM((2, 16, half), F32),
        pltpu.VMEM((2, frames, half), BF16),
        pltpu.VMEM((frames, half), BF16),
        pltpu.VMEM((4, 16, half), F32),
        pltpu.VMEM((groups, 16, half), F32),
        pltpu.VMEM((groups, 8, half), F32),
        pltpu.VMEM((2, groups, 4, half), F32),
        dma((9 + chunks,)),
        dma((12,)), dma((12,)),
        dma((SUBS,)), dma((SUBS,)),
        dma((2,)), dma((2,)),
        dma((2 * SUBS + 1, 2)), dma((2 * SUBS + 1, 2)),
        dma((10 + chunks,)),
        dma((2 * SUBS + 3,)), dma((2 * SUBS + 3,)),
        dma((2 * SUBS,)), dma((2 * SUBS,)),
        dma((2 * SUBS,)),
        dma((2,)),
    ] + tree_sems(depth)
    return pl.pallas_call(
        functools.partial(chain_kernel, depth, block),
        out_shape=out_shape,
        in_specs=[smem] * 2 + [anywhere] * 4 + [vmem] * 2,
        out_specs=[anywhere] * len(out_shape),
        scratch_shapes=scratch,
        compiler_params=pltpu.CompilerParams(
            collective_id=1, has_side_effects=True, vmem_limit_bytes=63 << 20
        ),
        cost_estimate=pl.CostEstimate(
            flops=4 * SUBS * K * rows * width * half, bytes_accessed=16 << 20, transcendentals=0
        ),
        name="chain",
    )(places, lengths, master, x, dense, cot, gains, shifts)


def grad_kernel(slot_ref, act_ref, dcv_ref, res_ref, out_ref, stage, count, sems):
    section = pl.program_id(0)
    half = act_ref.shape[3]
    width = 2 * half
    frames = act_ref.shape[4] // 2
    ring = stage.shape[0]

    @pl.when(section == 0)
    def _():
        count[0] = 0

    def slot_copy(place, slot):
        out = out_ref.at[pl.ds(pl.multiple_of(slot * width, 16), width)]
        return pltpu.make_async_copy(stage.at[place], out, sems.at[place])

    def emit(matrix, compute):
        slot = slot_ref[matrix]

        @pl.when(slot >= 0)
        def _():
            turn = count[0]
            place = lax.rem(turn, ring)
            pl.when(turn >= ring)(slot_copy(place, 0).wait)
            stage[place] = compute().astype(BF16)
            slot_copy(place, slot).start()
            count[0] = turn + 1

    for k in range(K):
        def conv(k=k):
            total = None
            for pair in range(2):
                right = jnp.concatenate(
                    [dcv_ref[0, pair, u, pl.ds(EDGE + MARGIN - k, frames)] for u in range(2)], axis=0
                )
                left = act_ref[0, pair].reshape(width, 2 * frames)
                term = jnp.dot(left, right, preferred_element_type=F32)
                total = term if total is None else total + term
            return total

        emit(section * K + k, conv)

    @pl.when(section == SUBS - 1)
    def _():
        for index in range(4):
            here = slot_ref[SUBS * K + 4] == index
            emit(
                SUBS * K + index,
                lambda here=here: jnp.where(
                    here, res_ref[0].astype(F32) + res_ref[1].astype(F32), 0.0
                ),
            )
        turns = count[0]

        def finish(place, carry):
            pl.when(place < turns)(slot_copy(place, 0).wait)
            return carry

        lax.fori_loop(0, ring, finish, 0)


def run_grads(total_rows, places, act, dcv, res):
    half = act.shape[3]
    ring = 8
    grid_spec = pltpu.PrefetchScalarGridSpec(
        num_scalar_prefetch=1,
        grid=(SUBS,),
        in_specs=[
            pl.BlockSpec((1,) + act.shape[1:], lambda s, t: (s, 0, 0, 0, 0)),
            pl.BlockSpec((1,) + dcv.shape[1:], lambda s, t: (s, 0, 0, 0, 0)),
            pl.BlockSpec(res.shape, lambda s, t: (0, 0, 0)),
        ],
        out_specs=pl.BlockSpec(memory_space=pl.ANY),
        scratch_shapes=[
            pltpu.VMEM((ring, 2 * half, half), BF16),
            pltpu.SMEM((1,), jnp.int32),
            pltpu.SemaphoreType.DMA((ring,)),
        ],
    )
    return pl.pallas_call(
        grad_kernel,
        grid_spec=grid_spec,
        out_shape=jax.ShapeDtypeStruct((total_rows, half), BF16),
        compiler_params=pltpu.CompilerParams(vmem_limit_bytes=60 << 20),
        name="weight_grads",
    )(places, act, dcv, res)


def reduce_kernel(
    depth, block, grads, out, l_ay, l_ax, l_bx, l_by, l_zab, l_zcd, l_c, l_d,
    o_cross, o_line, o_plane, final, result,
    cross_sem, line_sem, plane_sem, out_sem, swap_s, swap_r, ay_s, ay_r, ax_s, ax_r, bx_s, bx_r, by_s, by_r,
    zab_s, zab_r, zcd_s, zcd_r, cd_s, cd_r,
):
    place = QuadPlace(depth)
    z, x, y, core = place.z, place.x, place.y, place.core
    large, small = cut(block, 16)
    start_b, start_c, start_d = large, 2 * large, 2 * large + small
    over_x, over_y, up, down = place.over_x(), place.over_y(), place.up(), place.down()
    pieces = shares(large, 2)
    runs = range(len(pieces))

    def rows(zz, xx, yy, first, count):
        begin = pl.multiple_of(((zz * 2 + xx) * 2 + yy) * block + first, 16)
        return grads.at[pl.ds(begin, count)]

    def part(run):
        return pl.ds(*pieces[run])

    def ay(level, other_x, run):
        xx = 1 - x if other_x else x
        first, count = pieces[run]
        return remote(
            rows(level, xx, 1 - y, first, count), l_ay.at[level, other_x, part(run)],
            ay_s.at[level, other_x, run], ay_r.at[level, other_x, run], over_y,
        )

    def bx(level, other_y, run):
        yy = 1 - y if other_y else y
        first, count = pieces[run]
        return remote(
            rows(level, 1 - x, yy, start_b + first, count), l_bx.at[level, other_y, part(run)],
            bx_s.at[level, other_y, run], bx_r.at[level, other_y, run], over_x,
        )

    def ax(level, run):
        return remote(
            l_ay.at[level, 1, part(run)], l_ax.at[level, part(run)],
            ax_s.at[level, run], ax_r.at[level, run], over_x,
        )

    def by(level, run):
        return remote(
            l_bx.at[level, 1, part(run)], l_by.at[level, part(run)],
            by_s.at[level, run], by_r.at[level, run], over_y,
        )

    def own_cross(level):
        return [
            pltpu.make_async_copy(rows(level, 1 - x, y, 0, large), o_cross.at[level, 0], cross_sem.at[level, 0]),
            pltpu.make_async_copy(rows(level, x, 1 - y, start_b, large), o_cross.at[level, 1], cross_sem.at[level, 1]),
        ]

    def own_line(level):
        return [
            pltpu.make_async_copy(rows(level, x, y, index * large, large), o_line.at[level, index], line_sem.at[level, index])
            for index in range(2)
        ]

    def own_plane(level):
        return [
            pltpu.make_async_copy(
                rows(level, index // 2, index % 2, start_c, 2 * small),
                o_plane.at[level, index], plane_sem.at[level, index],
            )
            for index in range(4)
        ]

    def add(target, others, count, keep=None):
        strip = UNIT

        def one(index, carry):
            at = pl.ds(pl.multiple_of(index * strip, strip), strip)
            value = target[at].astype(F32)
            for ref in others:
                value = value + ref[at].astype(F32)
            if keep is None:
                target[at] = value.astype(BF16)
            else:
                keep[at] = value
            return carry

        lax.fori_loop(0, count // strip, one, 0, unroll=4)

    def sides(step):
        out = [(z - step, z - step >= 0)]
        if not (isinstance(step, int) and step == 0):
            out.append((z + step, z + step < depth))
        return out

    def both(step, action):
        for level, cond in sides(step):
            when(cond, functools.partial(action, level))

    def backwards(body, first, last):
        if depth <= 4:
            for step in range(first, last - 1, -1):
                body(step)
        else:
            def looped(turn, carry):
                body(first - turn)
                return carry

            lax.fori_loop(0, first - last + 1, looped, 0)

    def leaf(step, other, run):
        def go(level):
            ay(level, other, run).start()
            bx(level, other, run).start()

        both(step, go)

    def fetch(step):
        def go(level):
            for copy in own_cross(level) + own_line(level):
                copy.start()

        both(step, go)

    def entry_of(level, way):
        at_home = (z - 1 == level) if way == 0 else (z + 1 == level)
        return level if way == 0 else level + (depth - level) * at_home.astype(jnp.int32)

    def beyond(way):
        return z + 1 < depth if way == 0 else z >= 1

    def zcd(level, way, index, leaf_copy):
        entry = entry_of(level, way)
        if leaf_copy:
            src = rows(level, index // 2, index % 2, start_c, 2 * small)
        else:
            src = l_zcd.at[level, index]
        return remote(
            src, l_zcd.at[entry, index], zcd_s.at[level, index], zcd_r.at[entry, index],
            down if way == 0 else up,
        )

    def zcd_arrived(entry, index):
        ref = l_zcd.at[entry, index]
        remote(ref, ref, zcd_s.at[0, index], zcd_r.at[entry, index], up).wait_recv()

    def lines(step):
        return ((0, z - step, z - step >= 0), (1, z + step, z + step < depth))

    def plane_step(step):
        for way, level, cond in lines(step):
            def go(way=way, level=level):
                @pl.when(beyond(way))
                def _():
                    copies = own_plane(level)
                    for copy in copies:
                        copy.start()
                    for index in range(4):
                        zcd_arrived(level, index)
                        copies[index].wait()
                        add(l_zcd.at[level, index], [o_plane.at[level, index]], 2 * small)
                        zcd(level, way, index, False).start()

                @pl.when(jnp.logical_not(beyond(way)))
                def _():
                    for index in range(4):
                        zcd(level, way, index, True).start()

            when(cond, go)

    def zab(level, way, run):
        entry = entry_of(level, way)
        return [
            remote(
                landing.at[level, part(run)], l_zab.at[entry, index, part(run)],
                zab_s.at[level, index, run], zab_r.at[entry, index, run], down if way == 0 else up,
            )
            for index, landing in enumerate((l_ax, l_by))
        ]

    def zab_arrived(entry, index, run):
        ref = l_zab.at[entry, index, part(run)]
        remote(ref, ref, zab_s.at[0, index, run], zab_r.at[entry, index, run], up).wait_recv()

    def across(run):
        def go(level):
            count = pieces[run][1]
            copies = own_cross(level)
            ay(level, 1, run).wait_recv()
            if run == 0:
                copies[0].wait()
            add(l_ay.at[level, 1, part(run)], [o_cross.at[level, 0, part(run)]], count)
            ax(level, run).start()
            bx(level, 1, run).wait_recv()
            if run == 0:
                copies[1].wait()
            add(l_bx.at[level, 1, part(run)], [o_cross.at[level, 1, part(run)]], count)
            by(level, run).start()

        return go

    def line_step(step, run):
        count = pieces[run][1]
        for way, level, cond in lines(step):
            def go(way=way, level=level):
                copies = own_line(level)
                hops = zab(level, way, run)
                for index, (first_hop, second_hop, first_land, second_land) in enumerate(
                    ((ay, ax, l_ay, l_ax), (bx, by, l_bx, l_by))
                ):
                    first_hop(level, 0, run).wait_recv()
                    second_hop(level, run).wait_recv()
                    if run == 0:
                        copies[index].wait()
                    target = second_land.at[level, part(run)]
                    terms = [first_land.at[level, 0, part(run)], o_line.at[level, index, part(run)]]

                    @pl.when(beyond(way))
                    def _(index=index, target=target, terms=terms):
                        zab_arrived(level, index, run)
                        add(target, terms + [l_zab.at[level, index, part(run)]], count)

                    @pl.when(jnp.logical_not(beyond(way)))
                    def _(target=target, terms=terms):
                        add(target, terms, count)

                    hops[index].start()

            when(cond, go)

    unrolled = depth <= 4
    place.enter()
    for run in runs:
        leaf(depth - 1, 1, run)
    if not unrolled:
        for run in runs:
            leaf(depth - 1, 0, run)
    fetch(depth - 1)

    def turn(step):
        plane_step(step)
        for run in runs:
            if unrolled and step == depth - 1:
                leaf(step, 0, run)
            both(step, across(run))
        for run in runs:
            leaf(step - 1, 1, run)
        fetch(step - 1)
        for run in runs:
            line_step(step, run)
            leaf(step - 1, 0, run)

    backwards(turn, depth - 1, 1)

    above, below = z + 1 < depth, z >= 1
    copies = own_plane(z)
    for copy in copies:
        copy.start()
    for index in range(4):
        pl.when(above)(functools.partial(zcd_arrived, z, index))
        pl.when(below)(functools.partial(zcd_arrived, depth, index))
        copies[index].wait()
        target = o_plane.at[z, index]
        for cond, entries in (
            (above & below, (z, depth)), (above & jnp.logical_not(below), (z,)), (jnp.logical_not(above), (depth,))
        ):
            @pl.when(cond)
            def _(entries=entries, target=target, index=index):
                add(target, [l_zcd.at[entry, index] for entry in entries], 2 * small)

    def block_at(xx, yy, first):
        return o_plane.at[z, xx * 2 + yy, pl.ds(first, small)]

    plane = [
        remote(block_at(1 - x, 1 - y, 0), l_c.at[1], cd_s.at[0], cd_r.at[0], over_y),
        remote(block_at(x, 1 - y, 0), l_c.at[0], cd_s.at[1], cd_r.at[1], over_y),
        remote(block_at(1 - x, 1 - y, small), l_d.at[1], cd_s.at[2], cd_r.at[2], over_x),
        remote(block_at(1 - x, y, small), l_d.at[0], cd_s.at[3], cd_r.at[3], over_x),
        remote(l_c.at[1], l_c.at[2], cd_s.at[4], cd_r.at[4], over_x),
        remote(l_d.at[1], l_d.at[2], cd_s.at[5], cd_r.at[5], over_y),
    ]
    for copy in plane[:4]:
        copy.start()
    for run in runs:
        both(0, across(run))
    plane[0].wait_recv()
    add(l_c.at[1], [block_at(1 - x, y, 0)], small)
    plane[4].start()
    plane[2].wait_recv()
    add(l_d.at[1], [block_at(x, 1 - y, small)], small)
    plane[5].start()

    copies = own_line(z)
    for run in runs:
        first, count = pieces[run]
        for index, (first_hop, second_hop, first_land, second_land) in enumerate(
            ((ay, ax, l_ay, l_ax), (bx, by, l_bx, l_by))
        ):
            first_hop(z, 0, run).wait_recv()
            second_hop(z, run).wait_recv()
            if run == 0:
                copies[index].wait()
            terms = [first_land.at[z, 0, part(run)], o_line.at[z, index, part(run)]]
            target = final.at[pl.ds(index * large + first, count)]
            pl.when(above)(functools.partial(zab_arrived, z, index, run))
            pl.when(below)(functools.partial(zab_arrived, depth, index, run))
            for cond, entries in (
                (above & below, (z, depth)), (above & jnp.logical_not(below), (z,)), (jnp.logical_not(above), (depth,))
            ):
                @pl.when(cond)
                def _(entries=entries, terms=terms, target=target, index=index, land=second_land, run=run, count=count):
                    more = [l_zab.at[entry, index, part(run)] for entry in entries]
                    add(land.at[z, part(run)], terms + more, count, keep=target)

    for copy in (plane[1], plane[3], plane[4], plane[5]):
        copy.wait_recv()
    add(block_at(x, y, 0), [l_c.at[0], l_c.at[2]], small, keep=final.at[pl.ds(start_c, small)])
    add(block_at(x, y, small), [l_d.at[0], l_d.at[2]], small, keep=final.at[pl.ds(start_d, small)])
    own_rows = block // 2
    theirs = final.at[pl.ds(pl.multiple_of((1 - core) * own_rows, 16), own_rows)]
    mine = final.at[pl.ds(pl.multiple_of(core * own_rows, 16), own_rows)]
    cross = remote(theirs, result, swap_s.at[0], swap_r.at[0], place.partner())
    cross.start()
    local = pltpu.make_async_copy(mine, out.at[core], out_sem.at[0])
    local.start()

    def drain(step):
        def go(level):
            for run in runs:
                for other in range(2):
                    ay(level, other, run).wait_send()
                    bx(level, other, run).wait_send()
                ax(level, run).wait_send()
                by(level, run).wait_send()

        both(step, go)
        if not (isinstance(step, int) and step == 0):
            for way, level, cond in lines(step):
                def along(way=way, level=level):
                    for index in range(4):
                        zcd(level, way, index, False).wait_send()
                    for run in runs:
                        for copy in zab(level, way, run):
                            copy.wait_send()

                when(cond, along)

    steps(depth, drain)
    for copy in plane:
        copy.wait_send()
    cross.wait()
    fetched = pltpu.make_async_copy(result, out.at[1 - core], out_sem.at[1])
    fetched.start()
    fetched.wait()
    local.wait()


def run_reduce(depth, block, grads):
    half = grads.shape[1]
    large, small = cut(block, 16)
    dma = pltpu.SemaphoreType.DMA
    anywhere = pl.BlockSpec(memory_space=pl.ANY)
    scratch = [
        pltpu.VMEM((depth, 2, large, half), BF16),
        pltpu.VMEM((depth, large, half), BF16),
        pltpu.VMEM((depth, 2, large, half), BF16),
        pltpu.VMEM((depth, large, half), BF16),
        pltpu.VMEM((depth + 1, 2, large, half), BF16),
        pltpu.VMEM((depth + 1, 4, 2 * small, half), BF16),
        pltpu.VMEM((3, small, half), BF16),
        pltpu.VMEM((3, small, half), BF16),
        pltpu.VMEM((depth, 2, large, half), BF16),
        pltpu.VMEM((depth, 2, large, half), BF16),
        pltpu.VMEM((depth, 4, 2 * small, half), BF16),
        pltpu.VMEM((block, half), F32),
        pltpu.VMEM((block // 2, half), F32),
        dma((depth, 2)), dma((depth, 2)), dma((depth, 4)), dma((2,)), dma((1,)), dma((1,)),
        dma((depth, 2, 2)), dma((depth, 2, 2)), dma((depth, 2)), dma((depth, 2)),
        dma((depth, 2, 2)), dma((depth, 2, 2)), dma((depth, 2)), dma((depth, 2)),
        dma((depth + 1, 2, 2)), dma((depth + 1, 2, 2)),
        dma((depth + 1, 4)), dma((depth + 1, 4)),
        dma((6,)), dma((6,)),
    ]
    return pl.pallas_call(
        functools.partial(reduce_kernel, depth, block),
        out_shape=jax.ShapeDtypeStruct((2, block // 2, half), F32),
        in_specs=[anywhere],
        out_specs=anywhere,
        scratch_shapes=scratch,
        compiler_params=pltpu.CompilerParams(
            collective_id=2, has_side_effects=True, vmem_limit_bytes=48 << 20
        ),
        name="reduce",
    )(grads)


def adamw(gradient, params, first_moment, second_moment, rate, decay):
    moment_new = beta_one * first_moment + (1.0 - beta_one) * gradient
    second_new = beta_two * second_moment + (1.0 - beta_two) * gradient * gradient
    direction = (
        moment_new
        / (1.0 - beta_one**STEP)
        / (jnp.sqrt(second_new / (1.0 - beta_two**STEP)) + adam_eps)
    )
    return (moment_new, second_new, params - rate * (direction + decay * params))


def update_kernel(
    filled_ref, sums_ref, master_ref, one_ref, two_ref, average_ref,
    nrm_ref, gain_ref, shift_ref, norm_one_ref, norm_two_ref,
    grad_ref, one_out, two_out, new_ref, average_out, copy_ref,
    norm_grad_ref, norm_one_out, norm_two_out, norm_new_ref,
):
    @pl.when(pl.program_id(0) == 0)
    def _():
        branches = SUBS + SOURCES
        sums = jnp.concatenate([nrm_ref[0], nrm_ref[1]], axis=1)
        shifts = sums[branches : branches + SUBS]
        both = (
            sums[:branches],
            jnp.concatenate([shifts] + [shifts[SUBS - 1 :]] * SOURCES, axis=0),
        )
        for index, (gradient, params) in enumerate(zip(both, (gain_ref, shift_ref))):
            moment, second, new = adamw(
                gradient, params[...], norm_one_ref[:, index], norm_two_ref[:, index], rate_norm, 0.0
            )
            norm_grad_ref[:, index] = gradient
            norm_one_out[:, index] = moment
            norm_two_out[:, index] = second
            norm_new_ref[:, index] = new

    filled = filled_ref[pl.program_id(0)] > 0
    half = sums_ref.shape[2]
    strip = 32

    def one(index, carry):
        at = pl.ds(pl.multiple_of(index * strip, strip), strip)
        for h in range(2):
            lanes = pl.ds(h * half, half)
            gradient = jnp.where(filled, sums_ref[h, at], 0.0)
            master = master_ref[at, lanes]
            moment, second, new = adamw(
                gradient, master, one_ref[at, lanes], two_ref[at, lanes], rate_main, decay_main
            )
            grad_ref[at, lanes] = gradient
            one_out[at, lanes] = moment
            two_out[at, lanes] = second
            new_ref[at, lanes] = new
            average_out[at, lanes] = ema_keep * average_ref[at, lanes] + (1.0 - ema_keep) * new
            copy_ref[at, lanes] = new.astype(BF16)
        return carry

    lax.fori_loop(0, master_ref.shape[0] // strip, one, 0)


def run_update(filled, sums, master, moment_one, moment_two, average, nrm, gains, shifts, norm_one, norm_two):
    rows, width = master.shape
    step = rows // filled.shape[0]
    spec = pl.BlockSpec((step, width), lambda i, t: (i, 0))

    def whole(array):
        return pl.BlockSpec(array.shape, lambda i, t: (0,) * array.ndim)

    grid_spec = pltpu.PrefetchScalarGridSpec(
        num_scalar_prefetch=1,
        grid=(rows // step,),
        in_specs=[pl.BlockSpec((2, step, sums.shape[2]), lambda i, t: (0, i, 0))] + [spec] * 4
        + [whole(array) for array in (nrm, gains, shifts, norm_one, norm_two)],
        out_specs=[spec] * 6 + [whole(norm_one)] * 4,
    )
    full = jax.ShapeDtypeStruct(master.shape, F32)
    return pl.pallas_call(
        update_kernel,
        grid_spec=grid_spec,
        out_shape=[full] * 5 + [jax.ShapeDtypeStruct(master.shape, BF16)]
        + [jax.ShapeDtypeStruct(norm_one.shape, F32)] * 4,
        compiler_params=pltpu.CompilerParams(vmem_limit_bytes=24 << 20),
        name="update",
    )(filled, sums, master, moment_one, moment_two, average, nrm, gains, shifts, norm_one, norm_two)


def body(
    inputs,
    dense_inputs,
    lengths,
    owners,
    cotangent,
    master,
    moment_one,
    moment_two,
    average,
    norm_gain,
    norm_shift,
    norm_one,
    norm_two,
):
    width = inputs.shape[2]
    wides, narrows = lax.axis_size("wide"), lax.axis_size("narrow")
    depth = wides // 2
    own_rows = master.shape[0]
    block = 2 * own_rows
    capacity = own_rows * narrows // width
    places, ranking = slot_table(owners, capacity)
    act, dcv, res, block_out, input_grad, dense_grad, sums = run_chain(
        depth, block, places, lengths, master, inputs, dense_inputs, cotangent, norm_gain, norm_shift
    )
    compact = ((owners >> 2) * 2 + (owners & 1)) * capacity + ranking
    parity = (lax.axis_index("wide") // 2) % 2
    handled = jnp.where(((owners >> 1) & 1) == parity, compact, -1).astype(jnp.int32)
    kept = 2 * (lax.axis_index("wide") % 2) + lax.axis_index("narrow") // 2
    handled = jnp.concatenate([handled, kept.astype(jnp.int32)[None]])
    grads = run_grads(wides * narrows * own_rows // 2, handled, act, dcv, res)
    reduced = run_reduce(depth // 2, block, grads)

    step = min(own_rows, 256)
    first = (lax.axis_index("wide") * narrows + lax.axis_index("narrow")) * own_rows
    slot_of_step = (first + step * jnp.arange(own_rows // step, dtype=jnp.int32)) // width
    filled = jnp.any(places[None, :] == slot_of_step[:, None], axis=1).astype(jnp.int32)
    updated = run_update(
        filled, reduced, master, moment_one, moment_two, average,
        sums, norm_gain, norm_shift, norm_one.transpose(1, 0, 2), norm_two.transpose(1, 0, 2),
    )
    return (
        block_out,
        input_grad,
        dense_grad,
        *updated[:6],
        *(values.transpose(1, 0, 2) for values in updated[6:]),
    )


def solution(mesh):
    rows = P(AXES, None)
    utterances = P(AXES, None, None)
    in_specs = (
        utterances, utterances, P(AXES), P(), utterances, rows, rows, rows, rows,
        P(), P(), P(), P(),
    )
    out_specs = (
        utterances, utterances, utterances, rows, rows, rows, rows, rows, rows,
        P(), P(), P(), P(),
    )
    return jax.shard_map(body, mesh=mesh, in_specs=in_specs, out_specs=out_specs, check_vma=False)
```

```python
import functools

import jax
import jax.numpy as jnp
from jax import lax
from jax.experimental import pallas as pl
from jax.experimental.pallas import tpu as pltpu
from jax.sharding import PartitionSpec as P

WLOW = 256
WMID = 384
K = 17
SUBS = 5
SOURCES = 6
STEP = 10
MARGIN = K // 2
EDGE = 16
UNIT = 64
F32 = jnp.float32
BF16 = jnp.bfloat16
MESH = pl.DeviceIdType.MESH
AXES = ("wide", "narrow")

norm_eps = 1e-05
beta_one = 0.9
beta_two = 0.999
adam_eps = 1e-08
rate_main = 0.02
rate_norm = 0.15
decay_main = 0.01
ema_keep = 0.8

NT = (((1,), (1,)), ((), ()))


def slot_table(owners, capacity):
    number = owners.shape[0]
    same_owner = owners[:, None] == owners[None, :]
    earlier = jnp.arange(number)[None, :] < jnp.arange(number)[:, None]
    ranking = jnp.sum(jnp.where(same_owner & earlier, 1, 0), axis=1)
    return (owners * capacity + ranking).astype(jnp.int32), ranking.astype(jnp.int32)


def source_pieces(half):
    pieces = []
    start = 0
    for width in (WLOW, WLOW, WLOW, WMID, WMID):
        parts = []
        stop = start + width
        while start < stop:
            chunk, lane = divmod(start, half)
            lanes = min(half - lane, stop - start)
            parts.append((chunk, lane, lanes))
            start += lanes
        pieces.append(parts)
    return pieces


class Place:
    def __init__(self, depth):
        wide = lax.axis_index("wide")
        narrow = lax.axis_index("narrow")
        self.depth = depth
        self.core = lax.rem(narrow, 2)
        self.y = narrow // 2
        self.x = lax.rem(wide, 2)
        self.z = wide // 2
        self.groups = depth * 4
        self.me = wide * 2 + self.y

    def at(self, z, x, y, core):
        return (z * 2 + x, y * 2 + core)

    def beside(self):
        return self.at(self.z + 1 - 2 * lax.rem(self.z, 2), self.x, self.y, self.core)

    def partner(self):
        return self.at(self.z, self.x, self.y, 1 - self.core)

    def over_x(self):
        return self.at(self.z, 1 - self.x, self.y, self.core)

    def over_y(self):
        return self.at(self.z, self.x, 1 - self.y, self.core)

    def up(self):
        return self.at(self.z + 1, self.x, self.y, self.core)

    def down(self):
        return self.at(self.z - 1, self.x, self.y, self.core)

    def far(self, turn):
        z = lax.rem(self.z + 1 + turn // 4, self.depth)
        return self.at(z, lax.rem(turn // 2, 2), lax.rem(turn, 2), self.core)

    def near(self):
        return (
            self.over_x(), self.over_y(), self.at(self.z, 1 - self.x, 1 - self.y, self.core)
        )

    def enter(self):
        barrier = pltpu.get_barrier_semaphore()

        def greet(device):
            pl.semaphore_signal(barrier, inc=1, device_id=device, device_id_type=MESH)

        for device in (self.partner(), self.over_x(), self.over_y()):
            greet(device)
        above, below = self.z + 1 < self.depth, self.z >= 1
        pl.when(above)(functools.partial(greet, self.up()))
        pl.when(below)(functools.partial(greet, self.down()))
        met = 3 + above.astype(jnp.int32) + below.astype(jnp.int32)
        pl.semaphore_wait(barrier, met)


class QuadPlace(Place):
    def __init__(self, depth):
        super().__init__(depth)
        self.parity = lax.rem(self.z, 2)
        self.z = self.z // 2

    def at(self, z, x, y, core):
        return ((2 * z + self.parity) * 2 + x, y * 2 + core)


def remote(src, dst, send_sem, recv_sem, device):
    return pltpu.make_async_remote_copy(
        src_ref=src,
        dst_ref=dst,
        send_sem=send_sem,
        recv_sem=recv_sem,
        device_id=device,
        device_id_type=MESH,
    )


def when(cond, action):
    if cond is None:
        action()
    else:
        pl.when(cond)(action)


def cut(block, share):
    units = block // UNIT
    small = max(1, units // share)
    return (units - 2 * small) // 2 * UNIT, small * UNIT


def steps(depth, body, first=0):
    if depth <= 4:
        for step in range(first, depth):
            body(step)
    else:
        def looped(step, carry):
            body(step)
            return carry

        if first == 0:
            body(0)
        lax.fori_loop(max(first, 1), depth, looped, 0)


def shares(rows, number):
    units = rows // UNIT
    out = []
    first = 0
    for index in range(number):
        count = units // number + (1 if index < units % number else 0)
        if count:
            out.append((first * UNIT, count * UNIT))
        first += count
    return out


def tree_sems(depth):
    dma = pltpu.SemaphoreType.DMA
    return [
        dma((depth, 2, 2)), dma((depth, 2)), dma((depth, 2, 4)), dma((depth, 4)),
        dma((depth, 2)), dma((depth, 2)), dma((depth, 2, 2)), dma((depth, 2, 2)),
        dma((depth, 2)), dma((depth, 2)), dma((depth, 2, 2)), dma((depth, 2, 2)),
        dma((6,)), dma((6,)),
    ]


def gather_bank(place, bank, block, sems, first_idle=lambda: None, second_idle=lambda: None):
    depth, z, x, y = place.depth, place.z, place.x, place.y
    large, small = cut(block, 9)
    (zab_s, zab_r, zcd_s, zcd_r, ax_s, ax_r, ay_s, ay_r, by_s, by_r, bx_s, bx_r, cd_s, cd_r) = sems
    pieces = shares(large, 2)
    runs = range(len(pieces))

    def rows(zz, xx, yy, first, count):
        begin = ((zz * 2 + xx) * 2 + yy) * (block // UNIT) + first // UNIT
        return bank.at[pl.ds(begin, count // UNIT)]

    def move(zz, xx, yy, first, count, send_sem, recv_sem, device):
        ref = rows(zz, xx, yy, first, count)
        return remote(ref, ref, send_sem, recv_sem, device)

    start_c, start_d = 2 * large, 2 * large + small
    over_x, over_y, up, down = place.over_x(), place.over_y(), place.up(), place.down()

    def sides(step):
        out = [(z - step, z - step >= 0)]
        if not (isinstance(step, int) and step == 0):
            out.append((z + step, z + step < depth))
        return out

    def both(step, action):
        for level, cond in sides(step):
            when(cond, functools.partial(action, level))

    def z_moves(step, run):
        out = []
        low, high = z - step, z + step
        for level, cond, device, way in (
            (low, (low >= 0) & (z + 1 < depth), up, 0),
            (high, (high < depth) & (z >= 1), down, 1),
        ):
            if run is not None:
                first, count = pieces[run]
                copy = move(
                    level, x, y, 2 * first, 2 * count, zab_s.at[level, way, run], zab_r.at[level, run], device
                )
                out.append((cond, copy))
                continue
            for index in range(4):
                copy = move(
                    level, index // 2, index % 2, start_c, 2 * small, zcd_s.at[level, way, index],
                    zcd_r.at[level, index], device,
                )
                out.append((cond, copy))
        return out

    def ax(level, run):
        first, count = pieces[run]
        return move(level, x, y, 2 * first, count, ax_s.at[level, run], ax_r.at[level, run], over_x)

    def by(level, run):
        first, count = pieces[run]
        return move(level, x, y, 2 * first + count, count, by_s.at[level, run], by_r.at[level, run], over_y)

    def ay(level, run, other):
        first, count = pieces[run]
        xx = 1 - x if other else x
        return move(level, xx, y, 2 * first, count, ay_s.at[level, run, other], ay_r.at[level, run, other], over_y)

    def bx(level, run, other):
        first, count = pieces[run]
        yy = 1 - y if other else y
        return move(
            level, x, yy, 2 * first + count, count, bx_s.at[level, run, other], bx_r.at[level, run, other], over_x
        )

    plane = [
        move(z, x, y, start_c, small, cd_s.at[0], cd_r.at[0], over_x),
        move(z, x, y, start_d, small, cd_s.at[1], cd_r.at[1], over_y),
        move(z, x, y, start_c, small, cd_s.at[2], cd_r.at[2], over_y),
        move(z, 1 - x, y, start_c, small, cd_s.at[3], cd_r.at[3], over_y),
        move(z, x, y, start_d, small, cd_s.at[4], cd_r.at[4], over_x),
        move(z, x, 1 - y, start_d, small, cd_s.at[5], cd_r.at[5], over_x),
    ]

    def run_step(step):
        home = isinstance(step, int) and step == 0
        if home:
            plane[0].start()
            plane[1].start()
        for run in runs:
            first, count = pieces[run]
            if not home:
                both(
                    step,
                    lambda level, run=run, first=first, count=count: move(
                        level, x, y, 2 * first, 2 * count, zab_s.at[level, 0, run], zab_r.at[level, run], up
                    ).wait_recv(),
                )
            for cond, copy in z_moves(step, run):
                when(cond, copy.start)

            def begin(level, run=run):
                ax(level, run).start()
                by(level, run).start()

            both(step, begin)
        if home:
            first_idle()
            plane[2].start()
            plane[4].start()
            plane[0].wait_recv()
            plane[3].start()
            plane[1].wait_recv()
            plane[5].start()
            for copy in plane[2:]:
                copy.wait_recv()
            for cond, copy in z_moves(step, None):
                when(cond, copy.start)
        for run in runs:
            def across(level, run=run):
                ay(level, run, 0).start()
                bx(level, run, 0).start()
                ax(level, run).wait_recv()
                ay(level, run, 1).start()
                by(level, run).wait_recv()
                bx(level, run, 1).start()

            both(step, across)
        if not home:
            def arrived(level):
                for index in range(4):
                    move(
                        level, x, y, start_c, 2 * small, zcd_s.at[level, 0, index],
                        zcd_r.at[level, index], up,
                    ).wait_recv()

            both(step, arrived)
            for cond, copy in z_moves(step, None):
                when(cond, copy.start)
        if home:
            second_idle()

    steps(depth, run_step)

    def drain(step):
        def finish(level):
            for run in runs:
                for other in range(2):
                    ay(level, run, other).wait_recv()
                    bx(level, run, other).wait_recv()
                    ay(level, run, other).wait_send()
                    bx(level, run, other).wait_send()
                ax(level, run).wait_send()
                by(level, run).wait_send()

        both(step, finish)
        for kind in list(runs) + [None]:
            for cond, copy in z_moves(step, kind):
                when(cond, copy.wait_send)

    steps(depth, drain)
    for copy in plane:
        copy.wait_send()


def strips(rows, body, carry=0):
    strip = 64

    def one(index, carry):
        return body(pl.ds(pl.multiple_of(index * strip, strip), strip), carry)

    return lax.fori_loop(0, rows // strip, one, carry, unroll=True)


def fold(values):
    return jnp.sum(values.reshape(-1, 8, values.shape[1]), axis=0)


def chain_kernel(
    depth, block,
    slot_ref, length_ref, master, own_x, own_dense, own_cot, gain_ref, shift_ref,
    act_out, dcv_out, res_out, blk_out, ig_out, dg_out, nrm_out,
    bank, act, dense, mask, cot, raw, side, pre4, slope, upown, upsend, uprecv, dcv, dsd, res, res_x, res_y, dgrecv,
    igrecv, stage, turned, nrm, blk, blksend, keep, ex_side, ex_last, ex_sub,
    load_sem, swap_s, swap_r, act_s, act_r, up_s, up_r, ex_s, ex_r, out_sem, far_s, far_r, near_s, near_r, own_sem, edge_sem,
    *tree,
):
    place = Place(depth)
    core, other = place.core, 1 - place.core
    partner, beside = place.partner(), place.beside()
    half = bank.shape[2]
    width = 2 * half
    frames = mask.shape[1]
    rows = 2 * frames
    chunks = dense.shape[0]
    pieces = source_pieces(half)
    inner = pl.ds(EDGE, frames)
    own_rows = block // 2
    load_rows = min(own_rows, rows)
    loads_of = own_rows // load_rows

    mats_in = []
    for part in range(loads_of):
        for h in range(2):
            mats_in.append(
                pltpu.make_async_copy(
                    master.at[pl.ds(part * load_rows, load_rows), pl.ds(h * half, half)],
                    side.at[part * 2 + h, pl.ds(0, load_rows)],
                    load_sem.at[part * 2 + h],
                )
            )
    x_in = [
        pltpu.make_async_copy(
            own_x.at[0, :, pl.ds(h * half, half)], act.at[0, h, core, inner], load_sem.at[6 + h]
        )
        for h in range(2)
    ]
    dense_in = [
        pltpu.make_async_copy(
            own_dense.at[0, :, pl.ds(chunk * half, half)], dense.at[chunk, core], load_sem.at[8 + chunk]
        )
        for chunk in range(chunks)
    ]
    ours_lanes = pl.ds(pl.multiple_of(core * half, half), half)
    theirs_lanes = pl.ds(pl.multiple_of(other * half, half), half)
    cot_in = pltpu.make_async_copy(own_cot.at[0, :, ours_lanes], cot.at[core], load_sem.at[8 + chunks])
    for copy in mats_in + x_in + dense_in + [cot_in]:
        copy.start()
    place.enter()
    base = place.me * (block // UNIT) + core * (own_rows // UNIT)
    units = load_rows // UNIT
    send_mats = []
    for part in range(loads_of):
        def narrow(unit, carry, part=part):
            at = pl.ds(pl.multiple_of(unit * UNIT, UNIT), UNIT)
            stage[part * units + unit] = side[part * 2 + other, at].astype(BF16)
            return carry

        def keep_own(unit, carry, part=part):
            at = pl.ds(pl.multiple_of(unit * UNIT, UNIT), UNIT)
            bank[base + part * units + unit] = side[part * 2 + core, at].astype(BF16)
            return carry

        mats_in[2 * part].wait()
        mats_in[2 * part + 1].wait()
        lax.fori_loop(0, units, narrow, 0, unroll=2)
        copy = remote(
            stage.at[pl.ds(part * units, units)], bank.at[pl.ds(base + part * units, units)],
            swap_s.at[9 + part], swap_r.at[9 + part], partner,
        )
        copy.start()
        send_mats.append(copy)
        lax.fori_loop(0, units, keep_own, 0, unroll=2)
    mask[core] = (
        lax.broadcasted_iota(jnp.int32, (frames, 128), 0) < length_ref[0]
    ).astype(F32)
    edge_zero = jnp.zeros((EDGE, half), BF16)

    def clear(section, carry):
        for u in range(2):
            for h in range(2):
                act[section, h, u, pl.ds(0, EDGE)] = edge_zero
                act[section, h, u, pl.ds(EDGE + frames, EDGE)] = edge_zero
            dcv[section, u, pl.ds(0, EDGE)] = edge_zero
            dcv[section, u, pl.ds(EDGE + frames, EDGE)] = edge_zero
        return carry

    lax.fori_loop(0, SUBS, clear, 0)
    edges = [
        pltpu.make_async_copy(
            dcv.at[:, :, pl.ds(first, EDGE)], dcv_out.at[:, 1, :, pl.ds(first, EDGE)], edge_sem.at[index]
        )
        for index, first in enumerate((0, EDGE + frames))
    ]
    for copy in edges:
        copy.start()
    for copy in send_mats:
        copy.wait()

    def prepare():
        for copy in x_in + dense_in + [cot_in]:
            copy.wait()
        low_mask = jnp.concatenate([mask[core].astype(BF16)] * (half // 128), axis=1)
        for h in range(2):
            act[0, h, core, inner] = act[0, h, core, inner] * low_mask
        for chunk in range(chunks):
            dense[chunk, core] = dense[chunk, core] * low_mask
        own = act.at[0, :, core, inner]
        swaps = [
            remote(own, own, swap_s.at[1], swap_r.at[1], partner),
            remote(dense.at[:, core], dense.at[:, core], swap_s.at[2], swap_r.at[2], partner),
            remote(mask.at[core], mask.at[core], swap_s.at[3], swap_r.at[3], partner),
            remote(own_cot.at[0, :, theirs_lanes], cot.at[core], swap_s.at[4], swap_r.at[4], partner),
        ]
        for copy in swaps:
            copy.start()
        return swaps

    def own_act(section):
        half_of = turned.at[lax.rem(section, 2)]
        return [
            pltpu.make_async_copy(half_of, act_out.at[section, 0, core], own_sem.at[section]),
            remote(
                half_of, act_out.at[section, 0, core], near_s.at[section], near_r.at[section], partner
            ),
            remote(
                half_of, act_out.at[section, 1, core], far_s.at[section], far_r.at[section], beside
            ),
        ]

    def pass_act(section):
        ref = act_out.at[section, 1, core]
        return remote(ref, ref, near_s.at[SUBS + section], near_r.at[SUBS + section], partner)

    def turn_act(section):
        turned[lax.rem(section, 2)] = jnp.concatenate(
            [act[section, core, u, inner] for u in range(2)], axis=0
        ).T
        for copy in own_act(section)[:2]:
            copy.start()

    def free_turned(section):
        copies = own_act(section)
        copies[0].wait()
        copies[1].wait_send()
        copies[2].wait_send()

    swaps = []

    def arrived():
        for copy in swaps:
            copy.wait()
        turn_act(0)
        own_act(0)[2].start()

    gather_bank(place, bank, block, tree, lambda: swaps.extend(prepare()), arrived)

    outs = []

    def put(src, dst):
        copy = pltpu.make_async_copy(src, dst, out_sem.at[len(outs)])
        copy.start()
        outs.append(copy)

    def far_dcv(section):
        return remote(
            dcv.at[section, :, inner], dcv_out.at[section, 1, :, inner],
            far_s.at[SUBS + section], far_r.at[SUBS + section], beside,
        )

    def keep_dcv(section):
        return pltpu.make_async_copy(
            dcv.at[section], dcv_out.at[section, 0], own_sem.at[SUBS + section]
        )

    def res_over(step):
        if step == 0:
            src, dst, device = res.at[pl.ds(2 * (1 - place.x), 2)], res_x, place.over_x()
        elif step == 1:
            src, dst, device = res_x.at[1 - place.y], res_y, place.over_y()
        else:
            src, dst, device = res_y, res_out.at[1], beside
        at = 2 * SUBS + step
        return remote(src, dst, far_s.at[at], far_r.at[at], device)

    def weight(matrix, first, count):
        begin = slot_ref[matrix] * (width // UNIT) + first // UNIT
        return jnp.concatenate([bank[begin + i] for i in range(count // UNIT)], axis=0)

    def valid(at):
        return jnp.concatenate([mask_rows(at)] * (half // 128), axis=1)

    def mask_rows(at):
        return mask[at.start // frames, pl.ds(pl.multiple_of(lax.rem(at.start, frames), 64), at.size)]

    def gain(index):
        return gain_ref[pl.ds(index, 1), ours_lanes]

    def bias(index):
        return shift_ref[pl.ds(index, 1), ours_lanes]

    def share(buffer, index, values):
        buffer[place.me] = values
        mine = buffer.at[place.me]

        def go(turn, carry):
            remote(mine, mine, ex_s.at[index, 1], ex_r.at[index, 1], place.far(turn)).start()
            return carry

        lax.fori_loop(0, place.groups - 4, go, 0, unroll=place.groups <= 16)
        for device in place.near():
            remote(mine, mine, ex_s.at[index, 0], ex_r.at[index, 0], device).start()

    def shared(buffer, index, between=lambda: None):
        sent = []
        for kind, number in ((0, 3), (1, place.groups - 4)):
            some = buffer.at[pl.ds(0, number)]
            copy = remote(some, some, ex_s.at[index, kind], ex_r.at[index, kind], place.over_x())
            copy.wait_recv()
            sent.append(copy)
            if kind == 0:
                between()
        values = buffer[...]
        for copy in sent:
            copy.wait_send()
        return values

    def total_of(values):
        return jnp.sum(values, axis=0, keepdims=True)

    def counted():
        def add(at, carry):
            return carry + fold(valid(at))

        return total_of(strips(rows, add, jnp.zeros((8, half), F32)))

    def moments(load, count):
        pivot = load(pl.ds(0, 8))[0:1]

        def add(at, carry):
            first, second = carry
            valid_now = valid(at)
            off = (load(at) - pivot) * valid_now
            return first + fold(off), second + fold(off * off)

        zero = jnp.zeros((8, half), F32)
        first, second = strips(rows, add, (zero, zero))
        first, second = total_of(first), total_of(second)
        return first + count * pivot, jnp.maximum(second - first * first / count, 0.0)

    def merge(count, total, squares):
        frame_total = jnp.sum(count, axis=0)
        mean = jnp.sum(total, axis=0) / frame_total
        shift = total / count - mean[None]
        variance = jnp.sum(squares + count * shift * shift, axis=0) / frame_total
        return mean[None], lax.rsqrt(variance + norm_eps)[None], frame_total[None]

    def save(index, mean, inverse):
        scale = gain(index) * inverse
        keep[0, pl.ds(index, 1)] = inverse
        keep[1, pl.ds(index, 1)] = mean * inverse
        keep[2, pl.ds(index, 1)] = scale
        keep[3, pl.ds(index, 1)] = bias(index) - mean * scale

    def kept(row, index):
        return keep[row, pl.ds(index, 1)]

    count = counted()
    def side_branches():
        totals, squares = [], []
        for index in range(SOURCES):
            value = None
            if index < SOURCES - 1:
                for chunk, lane, lanes in pieces[index]:
                    left = dense[chunk].reshape(rows, half)[:, lane : lane + lanes]
                    right = weight(SUBS * K + chunk // 2, (chunk % 2) * half + lane, lanes)
                    term = jnp.dot(left, right, preferred_element_type=F32)
                    value = term if value is None else value + term
            else:
                for h in range(2):
                    left = jnp.concatenate([act[0, h, u, inner] for u in range(2)], axis=0)
                    term = jnp.dot(left, weight(SUBS * K + 3, h * half, half), preferred_element_type=F32)
                    value = term if value is None else value + term
            side[index] = value
            total, square = moments(lambda at, index=index: side[index, at], count)
            totals.append(total)
            squares.append(square)
        fill = jnp.zeros((3, half), F32)
        share(ex_side, 0, jnp.concatenate([count] + totals + squares + [fill], axis=0))

    def convolve(section, h, first):
        value = None
        for k in range(K):
            left = jnp.concatenate(
                [act[section, h, u, pl.ds(EDGE - MARGIN + k, frames)] for u in range(2)], axis=0
            )
            term = jnp.dot(
                left, weight(section * K + k, h * half, half), preferred_element_type=F32
            )
            value = term if value is None else value + term
            if k % 2 == 1 or k == K - 1:
                if first and k == 1:
                    raw[section] = value
                else:
                    raw[section] += value
                value = None

    def swap_act(section):
        own = act.at[section, core, :, inner]
        return remote(own, own, act_s.at[section], act_r.at[section], partner)

    def forward(section, last):
        convolve(section, core, True)
        if isinstance(section, int):
            if section > 0:
                swap_act(section).wait_recv()
        else:
            pl.when(section > 0)(swap_act(section).wait_recv)
        convolve(section, other, False)
        total, square = moments(lambda at: raw[section, at], count)
        buffer = ex_sub.at[lax.rem(section, 2)]
        share(buffer, 1 + section, jnp.concatenate([count, total, square, jnp.zeros_like(count)], axis=0))

        def pre_side():
            parts = shared(ex_side, 0)
            for index in range(SOURCES):
                mean, inverse, _ = merge(
                    parts[:, 0], parts[:, 1 + index], parts[:, 1 + SOURCES + index]
                )
                save(SUBS + index, mean, inverse)
            scales = [kept(2, SUBS + index) for index in range(SOURCES)]
            offset = sum(kept(3, SUBS + index) for index in range(SOURCES))

            def add(at, carry):
                before = offset
                for index in range(SOURCES):
                    before = before + side[index, at] * scales[index]
                pre4[at] = before
                return carry

            strips(rows, add)

        def background():
            own_act(section - 1)[2].wait_recv()
            pass_act(section - 1).start()
            if isinstance(section, int):
                free_turned(section - 2)
            else:
                pl.when(section > 1)(functools.partial(free_turned, section - 2))
            turn_act(section)

        if isinstance(section, int):
            background()
            parts = shared(buffer, 1 + section, own_act(section)[2].start)
        else:
            pl.when(section == 0)(side_branches)
            pl.when(section > 0)(background)
            pl.when(section == 1)(pre_side)
            parts = shared(
                buffer, 1 + section, lambda: pl.when(section > 0)(own_act(section)[2].start)
            )
        mean, inverse, frame_total = merge(parts[:, 0], parts[:, 1], parts[:, 2])
        save(section, mean, inverse)
        scale, offset = kept(2, section), kept(3, section)

        def activate(at, carry):
            before = raw[section, at] * scale + offset
            if last:
                before = before + pre4[at]
                pre4[at] = before
            hidden = (before * jax.nn.sigmoid(before) * valid(at)).astype(BF16)
            u = at.start // frames
            first = pl.multiple_of(lax.rem(at.start, frames), 64)
            if last:
                @pl.when(u == core)
                def _():
                    blk[core, pl.ds(first, at.size)] = hidden

                @pl.when(u != core)
                def _():
                    blksend[pl.ds(first, at.size)] = hidden
            else:
                act[section + 1, core, u, pl.ds(pl.multiple_of(first + EDGE, EDGE), at.size)] = hidden
            return carry

        strips(rows, activate)
        if not last:
            swap_act(section + 1).start()
        return frame_total

    def looped(section, carry):
        forward(section, False)
        return carry

    lax.fori_loop(0, SUBS - 1, looped, 0)
    frame_total = forward(SUBS - 1, True)
    blk_copy = remote(blksend, blk.at[core], swap_s.at[5], swap_r.at[5], partner)
    blk_copy.start()
    for section in range(1, SUBS):
        swap_act(section).wait_send()
    for section in (SUBS - 2, SUBS - 1):
        free_turned(section)

    def hat_of(values, index):
        return values * kept(0, index) - kept(1, index)

    def back_half(section, h):
        total = None
        value = None
        for k in range(K):
            left = jnp.concatenate(
                [dcv[section, u, pl.ds(EDGE + MARGIN - k, frames)] for u in range(2)], axis=0
            )
            term = lax.dot_general(
                left, weight(section * K + k, h * half, half), NT, preferred_element_type=F32
            )
            value = term if value is None else value + term
            if k % 2 == 1 or k == K - 1:
                total = value if total is None else total + value
                value = None
        return total

    def up_copy(section):
        slot = lax.rem(section, 2)
        return remote(upsend, uprecv.at[slot], up_s.at[slot], up_r.at[slot], partner)

    def backward(section):
        upsend[...] = back_half(section, other)
        up_copy(section).start()
        upown[...] = back_half(section, core)

    def slopes(section, upstream, before_of, others, target):
        sources = [(lambda at: raw[section, at], section)] + others

        def one(at, carry):
            before = before_of(at)
            sigmoid = jax.nn.sigmoid(before)
            now = upstream(at) * valid(at) * (sigmoid * (1.0 + before * (1.0 - sigmoid)))
            target[at] = now
            out = [carry[0] + fold(now)]
            for (load, index), so_far in zip(sources, carry[1:]):
                out.append(so_far + fold(now * hat_of(load(at), index)))
            return tuple(out)

        zero = jnp.zeros((8, half), F32)
        return [total_of(value) for value in strips(rows, one, (zero,) * (1 + len(sources)))]

    def branch(source, load, index, shift_sum, gain_sum, store):
        scale = kept(2, index)
        shift_mean, gain_mean = shift_sum / frame_total, gain_sum / frame_total

        def one(at, carry):
            value = source[at] - shift_mean - hat_of(load(at), index) * gain_mean
            store(at, (valid(at) * scale * value).astype(BF16))
            return carry

        strips(rows, one)

    def conv_branch(source, section, shift_sum, gain_sum):
        def store(at, value):
            first = pl.multiple_of(lax.rem(at.start, frames) + EDGE, EDGE)
            dcv[section, at.start // frames, pl.ds(first, at.size)] = value

        branch(source, lambda at: raw[section, at], section, shift_sum, gain_sum, store)
        far_dcv(section).start()
        keep_dcv(section).start()

    def cot_at(at):
        return cot[
            at.start // frames, pl.ds(pl.multiple_of(lax.rem(at.start, frames), 64), at.size)
        ].astype(F32)

    sums = slopes(
        SUBS - 1, cot_at, lambda at: pre4[at],
        [(lambda at, index=index: side[index, at], SUBS + index) for index in range(SOURCES)],
        pre4,
    )
    share(ex_last, SUBS + 1, jnp.concatenate(sums, axis=0))
    sums = jnp.sum(shared(ex_last, SUBS + 1), axis=0)
    shift_sum = sums[0:1]
    conv_branch(pre4, SUBS - 1, shift_sum, sums[1:2])
    nrm[core] = jnp.zeros_like(nrm[0])
    nrm[core, pl.ds(SUBS - 1, 1 + SOURCES)] = sums[1:]
    nrm[core, pl.ds(SUBS + SOURCES + SUBS - 1, 1)] = shift_sum
    backward(SUBS - 1)

    def side_grads():
        for index in range(SOURCES):
            def store(at, value, index=index):
                dsd[index, at] = value

            branch(
                pre4, lambda at, index=index: side[index, at], SUBS + index, shift_sum,
                sums[2 + index : 3 + index], store,
            )

    theirs = pl.multiple_of(other * frames, frames)
    ours = pl.multiple_of(core * frames, frames)
    dg_copy = remote(
        side.at[:, pl.ds(theirs, frames)], dgrecv, swap_s.at[6], swap_r.at[6], partner
    )

    def dense_grads():
        for index in range(SOURCES - 1):
            for chunk, lane, lanes in pieces[index]:
                right = weight(SUBS * K + chunk // 2, (chunk % 2) * half + lane, lanes)
                side[chunk, :, pl.ds(lane, lanes)] = lax.dot_general(
                    dsd[index], right, NT, preferred_element_type=F32
                )
        dg_copy.start()

    def residual_grads():
        rows_of = [[] for _ in range(chunks)]
        for index, parts in enumerate(pieces):
            for chunk, lane, lanes in parts:
                rows_of[chunk].append((lane, lanes, index))
        for chunk in range(chunks):
            turned = dense[chunk].reshape(rows, half).T
            for lane, lanes, index in rows_of[chunk]:
                res[chunk // 2, pl.ds((chunk % 2) * half + lane, lanes)] = jnp.dot(
                    turned[lane : lane + lanes], dsd[index], preferred_element_type=F32
                ).astype(BF16)
        for h in range(2):
            turned = jnp.concatenate([act[0, h, u, inner] for u in range(2)], axis=0).T
            res[3, pl.ds(h * half, half)] = jnp.dot(
                turned, dsd[SOURCES - 1], preferred_element_type=F32
            ).astype(BF16)

    dg_puts = [
        pltpu.make_async_copy(
            dgrecv.at[chunk], dg_out.at[0, :, pl.ds(chunk * half, half)], load_sem.at[chunk]
        )
        for chunk in range(chunks)
    ]

    def finish_dense():
        dg_copy.wait()
        own_valid = jnp.concatenate([mask[core]] * (half // 128), axis=1)
        for chunk in range(chunks):
            dgrecv[chunk] = (dgrecv[chunk] + side[chunk, pl.ds(ours, frames)]) * own_valid
            dg_puts[chunk].start()

    def looped_back(turn, carry):
        section = SUBS - 2 - turn
        copy = up_copy(section + 1)
        copy.wait()
        slot = lax.rem(section + 1, 2)
        scale, offset = kept(2, section), kept(3, section)
        sums_now = slopes(
            section, lambda at: upown[at] + uprecv[slot, at],
            lambda at: raw[section, at] * scale + offset, [], slope,
        )
        zero = jnp.zeros((2, half), F32)
        buffer = ex_sub.at[lax.rem(section, 2)]
        share(buffer, SUBS + 2 + section, jnp.concatenate(sums_now + [zero], axis=0))

        @pl.when(section == SUBS - 2)
        def _():
            side_grads()
            residual_grads()
            res_over(0).start()
            dense_grads()

        @pl.when(section == SUBS - 3)
        def _():
            res_over(0).wait_recv()
            for index in range(2):
                total = res[2 * place.x + index].astype(F32) + res_x[index].astype(F32)
                res_x[index] = total.astype(BF16)
            res_over(1).start()
            finish_dense()
            own_act(SUBS - 1)[2].wait_recv()
            pass_act(SUBS - 1).start()

        @pl.when(section == SUBS - 4)
        def _():
            res_over(1).wait_recv()
            res_y[...] = (res_y[...].astype(F32) + res_x[place.y].astype(F32)).astype(BF16)

        sums_now = jnp.sum(shared(buffer, SUBS + 2 + section), axis=0)
        pl.when(section == SUBS - 4)(lambda: res_over(2).start())
        conv_branch(slope, section, sums_now[0:1], sums_now[1:2])
        nrm[core, pl.ds(section, 1)] = sums_now[1:2]
        nrm[core, pl.ds(SUBS + SOURCES + section, 1)] = sums_now[0:1]

        @pl.when(section > 0)
        def _():
            backward(section)

        return carry

    lax.fori_loop(0, SUBS - 1, looped_back, 0)
    put(res_y, res_out.at[0])
    nrm_copy = remote(nrm.at[core], nrm.at[core], swap_s.at[7], swap_r.at[7], partner)
    nrm_copy.start()
    for h in range(2):
        uprecv[h] = back_half(0, h) + lax.dot_general(
            dsd[SOURCES - 1], weight(SUBS * K + 3, h * half, half), NT, preferred_element_type=F32
        )
    ig_copy = remote(
        uprecv.at[:, pl.ds(theirs, frames)], igrecv, swap_s.at[8], swap_r.at[8], partner
    )
    ig_copy.start()
    own_valid = jnp.concatenate([mask[core]] * (half // 128), axis=1)
    blk_copy.wait()
    nrm_copy.wait()
    put(nrm, nrm_out)
    ig_copy.wait()
    for h in range(2):
        igrecv[h] = (igrecv[h] + uprecv[h, pl.ds(ours, frames)]) * own_valid
        put(igrecv.at[h], ig_out.at[0, :, pl.ds(h * half, half)])
        put(blk.at[h], blk_out.at[0, :, pl.ds(h * half, half)])
    for section in range(SUBS):
        own_act(section)[1].wait_recv()
        pass_act(section).wait()
        far_dcv(section).wait()
        keep_dcv(section).wait()
    res_over(0).wait_send()
    res_over(1).wait_send()
    res_over(2).wait()
    for copy in outs + dg_puts + edges:
        copy.wait()


def run_chain(depth, block, places, lengths, master, x, dense, cot, gains, shifts):
    frames, width = x.shape[1:]
    half = width // 2
    rows = 2 * frames
    chunks = dense.shape[2] // half
    padded = frames + 2 * EDGE
    groups = depth * 4
    dma = pltpu.SemaphoreType.DMA
    anywhere = pl.BlockSpec(memory_space=pl.ANY)
    vmem = pl.BlockSpec(memory_space=pltpu.VMEM)
    smem = pl.BlockSpec(memory_space=pltpu.SMEM)
    out_shape = [
        jax.ShapeDtypeStruct((SUBS, 2, 2, half, rows), BF16),
        jax.ShapeDtypeStruct((SUBS, 2, 2, padded, half), BF16),
        jax.ShapeDtypeStruct((2, width, half), BF16),
        jax.ShapeDtypeStruct(x.shape, BF16),
        jax.ShapeDtypeStruct(x.shape, F32),
        jax.ShapeDtypeStruct(dense.shape, F32),
        jax.ShapeDtypeStruct((2, 16, half), F32),
    ]
    scratch = [
        pltpu.VMEM((groups * block // UNIT, UNIT, half), BF16),
        pltpu.VMEM((SUBS, 2, 2, padded, half), BF16),
        pltpu.VMEM((chunks, 2, frames, half), BF16),
        pltpu.VMEM((2, frames, 128), F32),
        pltpu.VMEM((2, frames, half), BF16),
        pltpu.VMEM((SUBS, rows, half), F32),
        pltpu.VMEM((SOURCES, rows, half), F32),
        pltpu.VMEM((rows, half), F32),
        pltpu.VMEM((rows, half), F32),
        pltpu.VMEM((rows, half), F32),
        pltpu.VMEM((rows, half), F32),
        pltpu.VMEM((2, rows, half), F32),
        pltpu.VMEM((SUBS, 2, padded, half), BF16),
        pltpu.VMEM((SOURCES, rows, half), BF16),
        pltpu.VMEM((4, width, half), BF16),
        pltpu.VMEM((2, width, half), BF16),
        pltpu.VMEM((width, half), BF16),
        pltpu.VMEM((chunks, frames, half), F32),
        pltpu.VMEM((2, frames, half), F32),
        pltpu.VMEM((block // 2 // UNIT, UNIT, half), BF16),
        pltpu.VMEM((2, half, rows), BF16),
        pltpu.VMEM((2, 16, half), F32),
        pltpu.VMEM((2, frames, half), BF16),
        pltpu.VMEM((frames, half), BF16),
        pltpu.VMEM((4, 16, half), F32),
        pltpu.VMEM((groups, 16, half), F32),
        pltpu.VMEM((groups, 8, half), F32),
        pltpu.VMEM((2, groups, 4, half), F32),
        dma((9 + chunks,)),
        dma((12,)), dma((12,)),
        dma((SUBS,)), dma((SUBS,)),
        dma((2,)), dma((2,)),
        dma((2 * SUBS + 1, 2)), dma((2 * SUBS + 1, 2)),
        dma((10 + chunks,)),
        dma((2 * SUBS + 3,)), dma((2 * SUBS + 3,)),
        dma((2 * SUBS,)), dma((2 * SUBS,)),
        dma((2 * SUBS,)),
        dma((2,)),
    ] + tree_sems(depth)
    return pl.pallas_call(
        functools.partial(chain_kernel, depth, block),
        out_shape=out_shape,
        in_specs=[smem] * 2 + [anywhere] * 4 + [vmem] * 2,
        out_specs=[anywhere] * len(out_shape),
        scratch_shapes=scratch,
        compiler_params=pltpu.CompilerParams(
            collective_id=1, has_side_effects=True, vmem_limit_bytes=63 << 20
        ),
        cost_estimate=pl.CostEstimate(
            flops=4 * SUBS * K * rows * width * half, bytes_accessed=16 << 20, transcendentals=0
        ),
        name="chain",
    )(places, lengths, master, x, dense, cot, gains, shifts)


def grad_kernel(slot_ref, act_ref, dcv_ref, res_ref, out_ref, stage, count, sems):
    section = pl.program_id(0)
    half = act_ref.shape[3]
    width = 2 * half
    frames = act_ref.shape[4] // 2
    ring = stage.shape[0]

    @pl.when(section == 0)
    def _():
        count[0] = 0

    def slot_copy(place, slot):
        out = out_ref.at[pl.ds(pl.multiple_of(slot * width, 16), width)]
        return pltpu.make_async_copy(stage.at[place], out, sems.at[place])

    def emit(matrix, compute):
        slot = slot_ref[matrix]

        @pl.when(slot >= 0)
        def _():
            turn = count[0]
            place = lax.rem(turn, ring)
            pl.when(turn >= ring)(slot_copy(place, 0).wait)
            stage[place] = compute().astype(BF16)
            slot_copy(place, slot).start()
            count[0] = turn + 1

    for k in range(K):
        def conv(k=k):
            total = None
            for pair in range(2):
                right = jnp.concatenate(
                    [dcv_ref[0, pair, u, pl.ds(EDGE + MARGIN - k, frames)] for u in range(2)], axis=0
                )
                left = act_ref[0, pair].reshape(width, 2 * frames)
                term = jnp.dot(left, right, preferred_element_type=F32)
                total = term if total is None else total + term
            return total

        emit(section * K + k, conv)

    @pl.when(section == SUBS - 1)
    def _():
        for index in range(4):
            here = slot_ref[SUBS * K + 4] == index
            emit(
                SUBS * K + index,
                lambda here=here: jnp.where(
                    here, res_ref[0].astype(F32) + res_ref[1].astype(F32), 0.0
                ),
            )
        turns = count[0]

        def finish(place, carry):
            pl.when(place < turns)(slot_copy(place, 0).wait)
            return carry

        lax.fori_loop(0, ring, finish, 0)


def run_grads(total_rows, places, act, dcv, res):
    half = act.shape[3]
    ring = 8
    grid_spec = pltpu.PrefetchScalarGridSpec(
        num_scalar_prefetch=1,
        grid=(SUBS,),
        in_specs=[
            pl.BlockSpec((1,) + act.shape[1:], lambda s, t: (s, 0, 0, 0, 0)),
            pl.BlockSpec((1,) + dcv.shape[1:], lambda s, t: (s, 0, 0, 0, 0)),
            pl.BlockSpec(res.shape, lambda s, t: (0, 0, 0)),
        ],
        out_specs=pl.BlockSpec(memory_space=pl.ANY),
        scratch_shapes=[
            pltpu.VMEM((ring, 2 * half, half), BF16),
            pltpu.SMEM((1,), jnp.int32),
            pltpu.SemaphoreType.DMA((ring,)),
        ],
    )
    return pl.pallas_call(
        grad_kernel,
        grid_spec=grid_spec,
        out_shape=jax.ShapeDtypeStruct((total_rows, half), BF16),
        compiler_params=pltpu.CompilerParams(vmem_limit_bytes=60 << 20),
        name="weight_grads",
    )(places, act, dcv, res)


def reduce_kernel(
    depth, block, grads, out, l_ay, l_ax, l_bx, l_by, l_zab, l_zcd, l_c, l_d,
    o_cross, o_line, o_plane, final, result,
    cross_sem, line_sem, plane_sem, out_sem, swap_s, swap_r, ay_s, ay_r, ax_s, ax_r, bx_s, bx_r, by_s, by_r,
    zab_s, zab_r, zcd_s, zcd_r, cd_s, cd_r,
):
    place = QuadPlace(depth)
    z, x, y, core = place.z, place.x, place.y, place.core
    large, small = cut(block, 16)
    start_b, start_c, start_d = large, 2 * large, 2 * large + small
    over_x, over_y, up, down = place.over_x(), place.over_y(), place.up(), place.down()
    pieces = shares(large, 2)
    runs = range(len(pieces))

    def rows(zz, xx, yy, first, count):
        begin = pl.multiple_of(((zz * 2 + xx) * 2 + yy) * block + first, 16)
        return grads.at[pl.ds(begin, count)]

    def part(run):
        return pl.ds(*pieces[run])

    def ay(level, other_x, run):
        xx = 1 - x if other_x else x
        first, count = pieces[run]
        return remote(
            rows(level, xx, 1 - y, first, count), l_ay.at[level, other_x, part(run)],
            ay_s.at[level, other_x, run], ay_r.at[level, other_x, run], over_y,
        )

    def bx(level, other_y, run):
        yy = 1 - y if other_y else y
        first, count = pieces[run]
        return remote(
            rows(level, 1 - x, yy, start_b + first, count), l_bx.at[level, other_y, part(run)],
            bx_s.at[level, other_y, run], bx_r.at[level, other_y, run], over_x,
        )

    def ax(level, run):
        return remote(
            l_ay.at[level, 1, part(run)], l_ax.at[level, part(run)],
            ax_s.at[level, run], ax_r.at[level, run], over_x,
        )

    def by(level, run):
        return remote(
            l_bx.at[level, 1, part(run)], l_by.at[level, part(run)],
            by_s.at[level, run], by_r.at[level, run], over_y,
        )

    def own_cross(level):
        return [
            pltpu.make_async_copy(rows(level, 1 - x, y, 0, large), o_cross.at[level, 0], cross_sem.at[level, 0]),
            pltpu.make_async_copy(rows(level, x, 1 - y, start_b, large), o_cross.at[level, 1], cross_sem.at[level, 1]),
        ]

    def own_line(level):
        return [
            pltpu.make_async_copy(rows(level, x, y, index * large, large), o_line.at[level, index], line_sem.at[level, index])
            for index in range(2)
        ]

    def own_plane(level):
        return [
            pltpu.make_async_copy(
                rows(level, index // 2, index % 2, start_c, 2 * small),
                o_plane.at[level, index], plane_sem.at[level, index],
            )
            for index in range(4)
        ]

    def add(target, others, count, keep=None):
        strip = UNIT

        def one(index, carry):
            at = pl.ds(pl.multiple_of(index * strip, strip), strip)
            value = target[at].astype(F32)
            for ref in others:
                value = value + ref[at].astype(F32)
            if keep is None:
                target[at] = value.astype(BF16)
            else:
                keep[at] = value
            return carry

        lax.fori_loop(0, count // strip, one, 0, unroll=4)

    def sides(step):
        out = [(z - step, z - step >= 0)]
        if not (isinstance(step, int) and step == 0):
            out.append((z + step, z + step < depth))
        return out

    def both(step, action):
        for level, cond in sides(step):
            when(cond, functools.partial(action, level))

    def backwards(body, first, last):
        if depth <= 4:
            for step in range(first, last - 1, -1):
                body(step)
        else:
            def looped(turn, carry):
                body(first - turn)
                return carry

            lax.fori_loop(0, first - last + 1, looped, 0)

    def leaf(step, other, run):
        def go(level):
            ay(level, other, run).start()
            bx(level, other, run).start()

        both(step, go)

    def fetch(step):
        def go(level):
            for copy in own_cross(level) + own_line(level):
                copy.start()

        both(step, go)

    def entry_of(level, way):
        at_home = (z - 1 == level) if way == 0 else (z + 1 == level)
        return level if way == 0 else level + (depth - level) * at_home.astype(jnp.int32)

    def beyond(way):
        return z + 1 < depth if way == 0 else z >= 1

    def zcd(level, way, index, leaf_copy):
        entry = entry_of(level, way)
        if leaf_copy:
            src = rows(level, index // 2, index % 2, start_c, 2 * small)
        else:
            src = l_zcd.at[level, index]
        return remote(
            src, l_zcd.at[entry, index], zcd_s.at[level, index], zcd_r.at[entry, index],
            down if way == 0 else up,
        )

    def zcd_arrived(entry, index):
        ref = l_zcd.at[entry, index]
        remote(ref, ref, zcd_s.at[0, index], zcd_r.at[entry, index], up).wait_recv()

    def lines(step):
        return ((0, z - step, z - step >= 0), (1, z + step, z + step < depth))

    def plane_step(step):
        for way, level, cond in lines(step):
            def go(way=way, level=level):
                @pl.when(beyond(way))
                def _():
                    copies = own_plane(level)
                    for copy in copies:
                        copy.start()
                    for index in range(4):
                        zcd_arrived(level, index)
                        copies[index].wait()
                        add(l_zcd.at[level, index], [o_plane.at[level, index]], 2 * small)
                        zcd(level, way, index, False).start()

                @pl.when(jnp.logical_not(beyond(way)))
                def _():
                    for index in range(4):
                        zcd(level, way, index, True).start()

            when(cond, go)

    def zab(level, way, run):
        entry = entry_of(level, way)
        return [
            remote(
                landing.at[level, part(run)], l_zab.at[entry, index, part(run)],
                zab_s.at[level, index, run], zab_r.at[entry, index, run], down if way == 0 else up,
            )
            for index, landing in enumerate((l_ax, l_by))
        ]

    def zab_arrived(entry, index, run):
        ref = l_zab.at[entry, index, part(run)]
        remote(ref, ref, zab_s.at[0, index, run], zab_r.at[entry, index, run], up).wait_recv()

    def across(run):
        def go(level):
            count = pieces[run][1]
            copies = own_cross(level)
            ay(level, 1, run).wait_recv()
            if run == 0:
                copies[0].wait()
            add(l_ay.at[level, 1, part(run)], [o_cross.at[level, 0, part(run)]], count)
            ax(level, run).start()
            bx(level, 1, run).wait_recv()
            if run == 0:
                copies[1].wait()
            add(l_bx.at[level, 1, part(run)], [o_cross.at[level, 1, part(run)]], count)
            by(level, run).start()

        return go

    def line_step(step, run):
        count = pieces[run][1]
        for way, level, cond in lines(step):
            def go(way=way, level=level):
                copies = own_line(level)
                hops = zab(level, way, run)
                for index, (first_hop, second_hop, first_land, second_land) in enumerate(
                    ((ay, ax, l_ay, l_ax), (bx, by, l_bx, l_by))
                ):
                    first_hop(level, 0, run).wait_recv()
                    second_hop(level, run).wait_recv()
                    if run == 0:
                        copies[index].wait()
                    target = second_land.at[level, part(run)]
                    terms = [first_land.at[level, 0, part(run)], o_line.at[level, index, part(run)]]

                    @pl.when(beyond(way))
                    def _(index=index, target=target, terms=terms):
                        zab_arrived(level, index, run)
                        add(target, terms + [l_zab.at[level, index, part(run)]], count)

                    @pl.when(jnp.logical_not(beyond(way)))
                    def _(target=target, terms=terms):
                        add(target, terms, count)

                    hops[index].start()

            when(cond, go)

    unrolled = depth <= 4
    place.enter()
    for run in runs:
        leaf(depth - 1, 1, run)
    if not unrolled:
        for run in runs:
            leaf(depth - 1, 0, run)
    fetch(depth - 1)

    def turn(step):
        plane_step(step)
        for run in runs:
            if unrolled and step == depth - 1:
                leaf(step, 0, run)
            both(step, across(run))
        for run in runs:
            leaf(step - 1, 1, run)
        fetch(step - 1)
        for run in runs:
            leaf(step - 1, 0, run)
        for run in runs:
            line_step(step, run)

    backwards(turn, depth - 1, 1)

    above, below = z + 1 < depth, z >= 1
    copies = own_plane(z)
    for copy in copies:
        copy.start()
    for index in range(4):
        pl.when(above)(functools.partial(zcd_arrived, z, index))
        pl.when(below)(functools.partial(zcd_arrived, depth, index))
        copies[index].wait()
        target = o_plane.at[z, index]
        for cond, entries in (
            (above & below, (z, depth)), (above & jnp.logical_not(below), (z,)), (jnp.logical_not(above), (depth,))
        ):
            @pl.when(cond)
            def _(entries=entries, target=target, index=index):
                add(target, [l_zcd.at[entry, index] for entry in entries], 2 * small)

    def block_at(xx, yy, first):
        return o_plane.at[z, xx * 2 + yy, pl.ds(first, small)]

    plane = [
        remote(block_at(1 - x, 1 - y, 0), l_c.at[1], cd_s.at[0], cd_r.at[0], over_y),
        remote(block_at(x, 1 - y, 0), l_c.at[0], cd_s.at[1], cd_r.at[1], over_y),
        remote(block_at(1 - x, 1 - y, small), l_d.at[1], cd_s.at[2], cd_r.at[2], over_x),
        remote(block_at(1 - x, y, small), l_d.at[0], cd_s.at[3], cd_r.at[3], over_x),
        remote(l_c.at[1], l_c.at[2], cd_s.at[4], cd_r.at[4], over_x),
        remote(l_d.at[1], l_d.at[2], cd_s.at[5], cd_r.at[5], over_y),
    ]
    for copy in plane[:4]:
        copy.start()
    for run in runs:
        both(0, across(run))
    plane[0].wait_recv()
    add(l_c.at[1], [block_at(1 - x, y, 0)], small)
    plane[4].start()
    plane[2].wait_recv()
    add(l_d.at[1], [block_at(x, 1 - y, small)], small)
    plane[5].start()

    copies = own_line(z)
    for run in runs:
        first, count = pieces[run]
        for index, (first_hop, second_hop, first_land, second_land) in enumerate(
            ((ay, ax, l_ay, l_ax), (bx, by, l_bx, l_by))
        ):
            first_hop(z, 0, run).wait_recv()
            second_hop(z, run).wait_recv()
            if run == 0:
                copies[index].wait()
            terms = [first_land.at[z, 0, part(run)], o_line.at[z, index, part(run)]]
            target = final.at[pl.ds(index * large + first, count)]
            pl.when(above)(functools.partial(zab_arrived, z, index, run))
            pl.when(below)(functools.partial(zab_arrived, depth, index, run))
            for cond, entries in (
                (above & below, (z, depth)), (above & jnp.logical_not(below), (z,)), (jnp.logical_not(above), (depth,))
            ):
                @pl.when(cond)
                def _(entries=entries, terms=terms, target=target, index=index, land=second_land, run=run, count=count):
                    more = [l_zab.at[entry, index, part(run)] for entry in entries]
                    add(land.at[z, part(run)], terms + more, count, keep=target)

    for copy in (plane[1], plane[3], plane[4], plane[5]):
        copy.wait_recv()
    add(block_at(x, y, 0), [l_c.at[0], l_c.at[2]], small, keep=final.at[pl.ds(start_c, small)])
    add(block_at(x, y, small), [l_d.at[0], l_d.at[2]], small, keep=final.at[pl.ds(start_d, small)])
    own_rows = block // 2
    theirs = final.at[pl.ds(pl.multiple_of((1 - core) * own_rows, 16), own_rows)]
    mine = final.at[pl.ds(pl.multiple_of(core * own_rows, 16), own_rows)]
    cross = remote(theirs, result, swap_s.at[0], swap_r.at[0], place.partner())
    cross.start()
    local = pltpu.make_async_copy(mine, out.at[core], out_sem.at[0])
    local.start()

    def drain(step):
        def go(level):
            for run in runs:
                for other in range(2):
                    ay(level, other, run).wait_send()
                    bx(level, other, run).wait_send()
                ax(level, run).wait_send()
                by(level, run).wait_send()

        both(step, go)
        if not (isinstance(step, int) and step == 0):
            for way, level, cond in lines(step):
                def along(way=way, level=level):
                    for index in range(4):
                        zcd(level, way, index, False).wait_send()
                    for run in runs:
                        for copy in zab(level, way, run):
                            copy.wait_send()

                when(cond, along)

    steps(depth, drain)
    for copy in plane:
        copy.wait_send()
    cross.wait()
    fetched = pltpu.make_async_copy(result, out.at[1 - core], out_sem.at[1])
    fetched.start()
    fetched.wait()
    local.wait()


def run_reduce(depth, block, grads):
    half = grads.shape[1]
    large, small = cut(block, 16)
    dma = pltpu.SemaphoreType.DMA
    anywhere = pl.BlockSpec(memory_space=pl.ANY)
    scratch = [
        pltpu.VMEM((depth, 2, large, half), BF16),
        pltpu.VMEM((depth, large, half), BF16),
        pltpu.VMEM((depth, 2, large, half), BF16),
        pltpu.VMEM((depth, large, half), BF16),
        pltpu.VMEM((depth + 1, 2, large, half), BF16),
        pltpu.VMEM((depth + 1, 4, 2 * small, half), BF16),
        pltpu.VMEM((3, small, half), BF16),
        pltpu.VMEM((3, small, half), BF16),
        pltpu.VMEM((depth, 2, large, half), BF16),
        pltpu.VMEM((depth, 2, large, half), BF16),
        pltpu.VMEM((depth, 4, 2 * small, half), BF16),
        pltpu.VMEM((block, half), F32),
        pltpu.VMEM((block // 2, half), F32),
        dma((depth, 2)), dma((depth, 2)), dma((depth, 4)), dma((2,)), dma((1,)), dma((1,)),
        dma((depth, 2, 2)), dma((depth, 2, 2)), dma((depth, 2)), dma((depth, 2)),
        dma((depth, 2, 2)), dma((depth, 2, 2)), dma((depth, 2)), dma((depth, 2)),
        dma((depth + 1, 2, 2)), dma((depth + 1, 2, 2)),
        dma((depth + 1, 4)), dma((depth + 1, 4)),
        dma((6,)), dma((6,)),
    ]
    return pl.pallas_call(
        functools.partial(reduce_kernel, depth, block),
        out_shape=jax.ShapeDtypeStruct((2, block // 2, half), F32),
        in_specs=[anywhere],
        out_specs=anywhere,
        scratch_shapes=scratch,
        compiler_params=pltpu.CompilerParams(
            collective_id=2, has_side_effects=True, vmem_limit_bytes=48 << 20
        ),
        name="reduce",
    )(grads)


def adamw(gradient, params, first_moment, second_moment, rate, decay):
    moment_new = beta_one * first_moment + (1.0 - beta_one) * gradient
    second_new = beta_two * second_moment + (1.0 - beta_two) * gradient * gradient
    direction = (
        moment_new
        / (1.0 - beta_one**STEP)
        / (jnp.sqrt(second_new / (1.0 - beta_two**STEP)) + adam_eps)
    )
    return (moment_new, second_new, params - rate * (direction + decay * params))


def update_kernel(
    filled_ref, sums_ref, master_ref, one_ref, two_ref, average_ref,
    nrm_ref, gain_ref, shift_ref, norm_one_ref, norm_two_ref,
    grad_ref, one_out, two_out, new_ref, average_out, copy_ref,
    norm_grad_ref, norm_one_out, norm_two_out, norm_new_ref,
):
    @pl.when(pl.program_id(0) == 0)
    def _():
        branches = SUBS + SOURCES
        sums = jnp.concatenate([nrm_ref[0], nrm_ref[1]], axis=1)
        shifts = sums[branches : branches + SUBS]
        both = (
            sums[:branches],
            jnp.concatenate([shifts] + [shifts[SUBS - 1 :]] * SOURCES, axis=0),
        )
        for index, (gradient, params) in enumerate(zip(both, (gain_ref, shift_ref))):
            moment, second, new = adamw(
                gradient, params[...], norm_one_ref[:, index], norm_two_ref[:, index], rate_norm, 0.0
            )
            norm_grad_ref[:, index] = gradient
            norm_one_out[:, index] = moment
            norm_two_out[:, index] = second
            norm_new_ref[:, index] = new

    filled = filled_ref[pl.program_id(0)] > 0
    half = sums_ref.shape[2]
    strip = 32

    def one(index, carry):
        at = pl.ds(pl.multiple_of(index * strip, strip), strip)
        for h in range(2):
            lanes = pl.ds(h * half, half)
            gradient = jnp.where(filled, sums_ref[h, at], 0.0)
            master = master_ref[at, lanes]
            moment, second, new = adamw(
                gradient, master, one_ref[at, lanes], two_ref[at, lanes], rate_main, decay_main
            )
            grad_ref[at, lanes] = gradient
            one_out[at, lanes] = moment
            two_out[at, lanes] = second
            new_ref[at, lanes] = new
            average_out[at, lanes] = ema_keep * average_ref[at, lanes] + (1.0 - ema_keep) * new
            copy_ref[at, lanes] = new.astype(BF16)
        return carry

    lax.fori_loop(0, master_ref.shape[0] // strip, one, 0)


def run_update(filled, sums, master, moment_one, moment_two, average, nrm, gains, shifts, norm_one, norm_two):
    rows, width = master.shape
    step = rows // filled.shape[0]
    spec = pl.BlockSpec((step, width), lambda i, t: (i, 0))

    def whole(array):
        return pl.BlockSpec(array.shape, lambda i, t: (0,) * array.ndim)

    grid_spec = pltpu.PrefetchScalarGridSpec(
        num_scalar_prefetch=1,
        grid=(rows // step,),
        in_specs=[pl.BlockSpec((2, step, sums.shape[2]), lambda i, t: (0, i, 0))] + [spec] * 4
        + [whole(array) for array in (nrm, gains, shifts, norm_one, norm_two)],
        out_specs=[spec] * 6 + [whole(norm_one)] * 4,
    )
    full = jax.ShapeDtypeStruct(master.shape, F32)
    return pl.pallas_call(
        update_kernel,
        grid_spec=grid_spec,
        out_shape=[full] * 5 + [jax.ShapeDtypeStruct(master.shape, BF16)]
        + [jax.ShapeDtypeStruct(norm_one.shape, F32)] * 4,
        compiler_params=pltpu.CompilerParams(vmem_limit_bytes=24 << 20),
        name="update",
    )(filled, sums, master, moment_one, moment_two, average, nrm, gains, shifts, norm_one, norm_two)


def body(
    inputs,
    dense_inputs,
    lengths,
    owners,
    cotangent,
    master,
    moment_one,
    moment_two,
    average,
    norm_gain,
    norm_shift,
    norm_one,
    norm_two,
):
    width = inputs.shape[2]
    wides, narrows = lax.axis_size("wide"), lax.axis_size("narrow")
    depth = wides // 2
    own_rows = master.shape[0]
    block = 2 * own_rows
    capacity = own_rows * narrows // width
    places, ranking = slot_table(owners, capacity)
    act, dcv, res, block_out, input_grad, dense_grad, sums = run_chain(
        depth, block, places, lengths, master, inputs, dense_inputs, cotangent, norm_gain, norm_shift
    )
    compact = ((owners >> 2) * 2 + (owners & 1)) * capacity + ranking
    parity = (lax.axis_index("wide") // 2) % 2
    handled = jnp.where(((owners >> 1) & 1) == parity, compact, -1).astype(jnp.int32)
    kept = 2 * (lax.axis_index("wide") % 2) + lax.axis_index("narrow") // 2
    handled = jnp.concatenate([handled, kept.astype(jnp.int32)[None]])
    grads = run_grads(wides * narrows * own_rows // 2, handled, act, dcv, res)
    reduced = run_reduce(depth // 2, block, grads)

    step = min(own_rows, 256)
    first = (lax.axis_index("wide") * narrows + lax.axis_index("narrow")) * own_rows
    slot_of_step = (first + step * jnp.arange(own_rows // step, dtype=jnp.int32)) // width
    filled = jnp.any(places[None, :] == slot_of_step[:, None], axis=1).astype(jnp.int32)
    updated = run_update(
        filled, reduced, master, moment_one, moment_two, average,
        sums, norm_gain, norm_shift, norm_one.transpose(1, 0, 2), norm_two.transpose(1, 0, 2),
    )
    return (
        block_out,
        input_grad,
        dense_grad,
        *updated[:6],
        *(values.transpose(1, 0, 2) for values in updated[6:]),
    )


def solution(mesh):
    rows = P(AXES, None)
    utterances = P(AXES, None, None)
    in_specs = (
        utterances, utterances, P(AXES), P(), utterances, rows, rows, rows, rows,
        P(), P(), P(), P(),
    )
    out_specs = (
        utterances, utterances, utterances, rows, rows, rows, rows, rows, rows,
        P(), P(), P(), P(),
    )
    return jax.shard_map(body, mesh=mesh, in_specs=in_specs, out_specs=out_specs, check_vma=False)
```
